32 devices in a mesh: dp: 16 (over z, x, core), sp: 2 (over y).
Axes of the slice: x: 2, y: 2, z: 4, core: 2. Of those that a mesh axis runs over, the one named last changes fastest.
Arguments:
- features: bfloat16 [64, 32, 32, 128], P('dp', 'sp'), may hold values from -6 to 6
- target: bfloat16 [64, 32, 32, 3], P('dp', 'sp'), may hold values from -6 to 6
- pixel_mask: int32 [64, 32, 32], P('dp', 'sp'), may hold values from 0 to 1, as said below
- buckets: int32 [64], P('dp'), may hold values from 0 to 7
- conv_pair: float32 [2, 3, 3, 128, 128], replicated, may hold values from -0.1875 to 0.1875
- down_conv: float32 [3, 3, 128, 256], replicated, may hold values from -0.1875 to 0.1875
- conv_wide: float32 [3, 3, 256, 256], replicated, may hold values from -0.125 to 0.125
- skip_proj: float32 [128, 256], replicated, may hold values from -0.5 to 0.5
- attn_proj: float32 [256, 1024], replicated, may hold values from -0.375 to 0.375
- head_conv: float32 [3, 3, 256, 3], replicated, may hold values from -0.125 to 0.125
- norm_narrow: float32 [6, 128], replicated
- norm_wide: float32 [6, 256], replicated
- time_bias: float32 [8, 384], replicated, may hold values from -3 to 3
- conv_pair_mom: float32 [2, 3, 3, 128, 128], replicated, may hold values from -0.078125 to 0.078125
- down_conv_mom: float32 [3, 3, 128, 256], replicated, may hold values from -0.078125 to 0.078125
- conv_wide_mom: float32 [3, 3, 256, 256], replicated, may hold values from -0.078125 to 0.078125
- skip_proj_mom: float32 [128, 256], replicated, may hold values from -0.078125 to 0.078125
- attn_proj_mom: float32 [256, 1024], replicated, may hold values from -0.078125 to 0.078125
- head_conv_mom: float32 [3, 3, 256, 3], replicated, may hold values from -0.078125 to 0.078125
- norm_narrow_mom: float32 [6, 128], replicated, may hold values from -0.078125 to 0.078125
- norm_wide_mom: float32 [6, 256], replicated, may hold values from -0.078125 to 0.078125
- time_bias_mom: float32 [8, 384], replicated, may hold values from -0.078125 to 0.078125
- conv_pair_sq: float32 [2, 3, 3, 128, 128], replicated, as said below
- down_conv_sq: float32 [3, 3, 128, 256], replicated, as said below
- conv_wide_sq: float32 [3, 3, 256, 256], replicated, as said below
- skip_proj_sq: float32 [128, 256], replicated, as said below
- attn_proj_sq: float32 [256, 1024], replicated, as said below
- head_conv_sq: float32 [3, 3, 256, 3], replicated, as said below
- norm_narrow_sq: float32 [6, 128], replicated, as said below
- norm_wide_sq: float32 [6, 256], replicated, as said below
- time_bias_sq: float32 [8, 384], replicated, as said below
Outputs:
- loss_sum: float32 [], replicated
- bucket_counts: float32 [8], replicated
- conv_pair_new: float32 [2, 3, 3, 128, 128], replicated
- conv_pair_mom_new: float32 [2, 3, 3, 128, 128], replicated
- conv_pair_sq_new: float32 [2, 3, 3, 128, 128], replicated
- down_conv_new: float32 [3, 3, 128, 256], replicated
- down_conv_mom_new: float32 [3, 3, 128, 256], replicated
- down_conv_sq_new: float32 [3, 3, 128, 256], replicated
- conv_wide_new: float32 [3, 3, 256, 256], replicated
- conv_wide_mom_new: float32 [3, 3, 256, 256], replicated
- conv_wide_sq_new: float32 [3, 3, 256, 256], replicated
- skip_proj_new: float32 [128, 256], replicated
- skip_proj_mom_new: float32 [128, 256], replicated
- skip_proj_sq_new: float32 [128, 256], replicated
- attn_proj_new: float32 [256, 1024], replicated
- attn_proj_mom_new: float32 [256, 1024], replicated
- attn_proj_sq_new: float32 [256, 1024], replicated
- head_conv_new: float32 [3, 3, 256, 3], replicated
- head_conv_mom_new: float32 [3, 3, 256, 3], replicated
- head_conv_sq_new: float32 [3, 3, 256, 3], replicated
- norm_narrow_new: float32 [6, 128], replicated
- norm_narrow_mom_new: float32 [6, 128], replicated
- norm_narrow_sq_new: float32 [6, 128], replicated
- norm_wide_new: float32 [6, 256], replicated
- norm_wide_mom_new: float32 [6, 256], replicated
- norm_wide_sq_new: float32 [6, 256], replicated
- time_bias_new: float32 [8, 384], replicated
- time_bias_mom_new: float32 [8, 384], replicated
- time_bias_sq_new: float32 [8, 384], replicated
The draws below stay inside these ranges and needn't reach their ends.
Inputs may be any that keep to these rules, and one draw needn't show every extreme that they name: `pixel_mask`: every row of every image has at least one pixel that counts. `conv_pair_sq`: positive. `down_conv_sq`: positive. `conv_wide_sq`: positive. `skip_proj_sq`: positive. `attn_proj_sq`: positive. `head_conv_sq`: positive. `norm_narrow_sq`: positive. `norm_wide_sq`: positive. `time_bias_sq`: positive.
All inputs are finite; a program needn't handle non-finite values.
Results may differ from the reference program's by a relative error of at most 0.0013.
The reference program's roundings to bfloat16 on the way count: a program that leaves them out, or rounds other values in their place, can miss the bound.
Values may be sent and summed in bfloat16 or wider, within the bound.
A program may use at most 128 MiB of HBM per device.

```python
import math
import jax
import jax.numpy as jnp
from jax import lax

C1 = 128
HALF_CHANNELS = 256
GROUPS = 32
RES = 32
NB = 8
STEP = 10
IMAGES = 64


def draw_pixel_mask(key, part):
    image_ids = jnp.arange(IMAGES)[:, None, None]
    row_ids = jnp.arange(RES)[None, :, None]
    col_ids = jnp.arange(RES)[None, None, :]
    limit = 200 + 400 * image_ids // max(IMAGES - 1, 1) + 200 * row_ids // (RES - 1)
    drawn = jax.random.randint(key, (IMAGES, RES, RES), 0, 1000)
    forced = jax.random.randint(jax.random.fold_in(key, 7), (IMAGES, RES, 1), 0, RES)
    return ((drawn < limit) | (col_ids == forced)).astype(jnp.int32)


def norm_table(key, width):
    keys = jax.random.split(key, 2)
    gains = 1.0 + 0.3 * jax.random.uniform(keys[0], (6, width), jnp.float32, -1.0, 1.0)
    shifts = 0.3 * jax.random.normal(keys[1], (6, width), jnp.float32)
    parity = (jnp.arange(6) % 2 == 0)[:, None]
    return jnp.where(parity, gains, shifts)


def draw_norm_narrow(key, part):
    return norm_table(key, C1)


def draw_norm_wide(key, part):
    return norm_table(key, HALF_CHANNELS)


def second_moment(key, layout):
    unit = 0.016 * NB * NB / (RES * RES * IMAGES)
    return unit * jnp.exp(jax.random.uniform(key, layout, jnp.float32, 0.0, math.log(4.0)))


def draw_conv_pair_sq(key, part):
    return second_moment(key, (2, 3, 3, C1, C1))


def draw_down_conv_sq(key, part):
    return second_moment(key, (3, 3, C1, HALF_CHANNELS))


def draw_conv_wide_sq(key, part):
    return second_moment(key, (3, 3, HALF_CHANNELS, HALF_CHANNELS))


def draw_skip_proj_sq(key, part):
    return second_moment(key, (C1, HALF_CHANNELS))


def draw_attn_proj_sq(key, part):
    return second_moment(key, (HALF_CHANNELS, 4 * HALF_CHANNELS))


def draw_head_conv_sq(key, part):
    return second_moment(key, (3, 3, HALF_CHANNELS, 3))


def draw_norm_narrow_sq(key, part):
    return second_moment(key, (6, C1))


def draw_norm_wide_sq(key, part):
    return second_moment(key, (6, HALF_CHANNELS))


def draw_time_bias_sq(key, part):
    return second_moment(key, (NB, C1 + HALF_CHANNELS))


def plant(values, stream_key, smallest, high):
    longest = values.shape.index(max(values.shape))
    spots = []
    for shift in (0, 1):
        where = [jax.random.randint(jax.random.fold_in(stream_key, axis), (), 0, length) for axis, length in enumerate(values.shape)]
        where[longest] = (where[longest] + shift) % values.shape[longest]
        spots.append(tuple(where))
    return values.at[spots[0]].set(smallest).at[spots[1]].set(high)


def block_scale(stream_key, dims, shards, smallest, high):
    loudness = 1.0
    for dim, parts in shards:
        draws = jax.random.uniform(jax.random.fold_in(jax.random.fold_in(stream_key, 6), dim), (parts,), jnp.float32, smallest / len(shards), high / len(shards))
        loudness = loudness * jnp.repeat(jnp.exp(draws), dims[dim] // parts).reshape((-1,) + (1,) * (len(dims) - 1 - dim))
    return loudness


def scatter_about(key, dims, scale, bound, shards=(), dtype=jnp.bfloat16):
    values = jax.random.normal(key, dims, jnp.float32) * scale
    if len(shards) > 0:
        values = block_scale(key, dims, shards, -0.22, 0.18) * values
    return jnp.clip(values, min=-bound, max=bound).astype(dtype)


def setup_inputs(seed: int = 0) -> dict:
    seeds = jax.random.split(jax.random.key(seed), 32)
    return {
        "features": scatter_about(seeds[0], (IMAGES, RES, RES, C1), 1.0, 6.0, ((0, 16), (1, 2))),
        "target": scatter_about(seeds[1], (IMAGES, RES, RES, 3), 1.0, 6.0, ((0, 16), (1, 2))),
        "pixel_mask": draw_pixel_mask(jax.random.fold_in(seeds[31], 71), 0),
        "buckets": plant(jax.random.randint(seeds[3], (IMAGES,), 0, NB), jax.random.fold_in(seeds[3], 1), 0, NB - 1).astype(jnp.int32),
        "conv_pair": scatter_about(seeds[4], (2, 3, 3, C1, C1), (9 * C1) ** -0.5, 0.1875, (), jnp.float32),
        "down_conv": scatter_about(seeds[5], (3, 3, C1, HALF_CHANNELS), (9 * C1) ** -0.5, 0.1875, (), jnp.float32),
        "conv_wide": scatter_about(seeds[6], (3, 3, HALF_CHANNELS, HALF_CHANNELS), (9 * HALF_CHANNELS) ** -0.5, 0.125, (), jnp.float32),
        "skip_proj": scatter_about(seeds[7], (C1, HALF_CHANNELS), C1 ** -0.5, 0.5, (), jnp.float32),
        "attn_proj": scatter_about(seeds[8], (HALF_CHANNELS, 4 * HALF_CHANNELS), HALF_CHANNELS ** -0.5, 0.375, (), jnp.float32),
        "head_conv": scatter_about(seeds[9], (3, 3, HALF_CHANNELS, 3), (9 * HALF_CHANNELS) ** -0.5, 0.125, (), jnp.float32),
        "norm_narrow": draw_norm_narrow(jax.random.fold_in(seeds[31], 71), 0),
        "norm_wide": draw_norm_wide(jax.random.fold_in(seeds[31], 71), 0),
        "time_bias": scatter_about(seeds[12], (NB, C1 + HALF_CHANNELS), 0.5, 3.0, (), jnp.float32),
        "conv_pair_mom": scatter_about(seeds[13], (2, 3, 3, C1, C1), (5 * RES * RES * IMAGES // (NB * NB)) ** -0.5, 0.078125, (), jnp.float32),
        "down_conv_mom": scatter_about(seeds[14], (3, 3, C1, HALF_CHANNELS), (5 * RES * RES * IMAGES // (NB * NB)) ** -0.5, 0.078125, (), jnp.float32),
        "conv_wide_mom": scatter_about(seeds[15], (3, 3, HALF_CHANNELS, HALF_CHANNELS), (5 * RES * RES * IMAGES // (NB * NB)) ** -0.5, 0.078125, (), jnp.float32),
        "skip_proj_mom": scatter_about(seeds[16], (C1, HALF_CHANNELS), (5 * RES * RES * IMAGES // (NB * NB)) ** -0.5, 0.078125, (), jnp.float32),
        "attn_proj_mom": scatter_about(seeds[17], (HALF_CHANNELS, 4 * HALF_CHANNELS), (5 * RES * RES * IMAGES // (NB * NB)) ** -0.5, 0.078125, (), jnp.float32),
        "head_conv_mom": scatter_about(seeds[18], (3, 3, HALF_CHANNELS, 3), (5 * RES * RES * IMAGES // (NB * NB)) ** -0.5, 0.078125, (), jnp.float32),
        "norm_narrow_mom": scatter_about(seeds[19], (6, C1), (5 * RES * RES * IMAGES // (NB * NB)) ** -0.5, 0.078125, (), jnp.float32),
        "norm_wide_mom": scatter_about(seeds[20], (6, HALF_CHANNELS), (5 * RES * RES * IMAGES // (NB * NB)) ** -0.5, 0.078125, (), jnp.float32),
        "time_bias_mom": scatter_about(seeds[21], (NB, C1 + HALF_CHANNELS), (5 * RES * RES * IMAGES // (NB * NB)) ** -0.5, 0.078125, (), jnp.float32),
        "conv_pair_sq": draw_conv_pair_sq(jax.random.fold_in(seeds[31], 71), 0),
        "down_conv_sq": draw_down_conv_sq(jax.random.fold_in(seeds[31], 71), 0),
        "conv_wide_sq": draw_conv_wide_sq(jax.random.fold_in(seeds[31], 71), 0),
        "skip_proj_sq": draw_skip_proj_sq(jax.random.fold_in(seeds[31], 71), 0),
        "attn_proj_sq": draw_attn_proj_sq(jax.random.fold_in(seeds[31], 71), 0),
        "head_conv_sq": draw_head_conv_sq(jax.random.fold_in(seeds[31], 71), 0),
        "norm_narrow_sq": draw_norm_narrow_sq(jax.random.fold_in(seeds[31], 71), 0),
        "norm_wide_sq": draw_norm_wide_sq(jax.random.fold_in(seeds[31], 71), 0),
        "time_bias_sq": draw_time_bias_sq(jax.random.fold_in(seeds[31], 71), 0),
    }


@jax.custom_vjp
def lowered_values(v):
    return lax.optimization_barrier(v.astype(jnp.bfloat16)).astype(jnp.float32)

@jax.custom_vjp
def lowered_backward(v):
    return v

def low_keep(v):
    return (lowered_values(v), None)

def low_pass(kept, grad):
    return (grad,)

def back_keep(v):
    return (v, None)

def back_low(kept, grad):
    return (lowered_values(grad),)
lowered_values.defvjp(low_keep, low_pass)
lowered_backward.defvjp(back_keep, back_low)
epsilon = 1e-05
root_half = 0.7071067811865476
beta_one = 0.9
beta_two = 0.999
adam_epsilon = 1e-08
decay_rate = 0.1
rate_matrix = 0.03
rate_vector = 0.5
precision_highest = lax.Precision.HIGHEST

def silu(tensor):
    return tensor * jax.nn.sigmoid(tensor)

def gnorm(tensor, scales, shifts):
    layout = tensor.shape
    group_size = layout[-1] // GROUPS
    grouped = tensor.reshape(layout[:-1] + (GROUPS, group_size))
    counted = layout[1] * layout[2] * group_size
    average = lax.optimization_barrier(jnp.sum(grouped, axis=(1, 2, 4), keepdims=True)) / counted
    squares = lax.optimization_barrier(jnp.sum(grouped * grouped, axis=(1, 2, 4), keepdims=True)) / counted
    normed = ((grouped - average) * lax.rsqrt(squares - average * average + epsilon)).reshape(layout)
    return normed * scales + shifts

def convolve(tensor, kernel):
    return lax.conv_general_dilated(tensor, kernel, (1, 1), 'SAME', dimension_numbers=('NHWC', 'HWIO', 'NHWC'), precision=precision_highest)

def fir_table(size_in):
    rows_out = jnp.arange(size_in // 2)[:, None]
    cols_in = jnp.arange(size_in)[None, :]
    tapped = cols_in - 2 * rows_out + 1
    return jnp.where((tapped == 0) | (tapped == 3), 0.125, jnp.where((tapped == 1) | (tapped == 2), 0.375, 0.0)).astype(jnp.float32)

def fir_down(tensor):
    table = fir_table(tensor.shape[1])
    return jnp.einsum('ij,bjkc,lk->bilc', table, tensor, table, precision=precision_highest)

def forward(params, inputs, targets, weights_px, onehot):
    conv_pair, down_conv, conv_wide, skip_proj, attn_proj, head_conv, norm_narrow, norm_wide, time_bias = params
    bias_rows = jnp.dot(onehot, time_bias, precision=precision_highest)
    bias_narrow = bias_rows[:, None, None, :C1]
    bias_wide = bias_rows[:, None, None, C1:]
    hidden = lowered_backward(convolve(lowered_values(silu(gnorm(inputs, norm_narrow[0], norm_narrow[1]))), lowered_values(conv_pair[0]))) + bias_narrow
    hidden = lowered_backward(convolve(lowered_values(silu(gnorm(hidden, norm_narrow[2], norm_narrow[3]))), lowered_values(conv_pair[1])))
    first_out = (inputs + hidden) * root_half
    shared = lowered_backward(lowered_values(first_out))
    hidden = lowered_values(fir_down(silu(gnorm(shared, norm_narrow[4], norm_narrow[5]))))
    hidden = lowered_backward(convolve(hidden, lowered_values(down_conv))) + bias_wide
    hidden = lowered_backward(convolve(lowered_values(silu(gnorm(hidden, norm_wide[0], norm_wide[1]))), lowered_values(conv_wide)))
    skipped = lowered_backward(jnp.einsum('bhwi,io->bhwo', lowered_values(fir_down(shared)), lowered_values(skip_proj), precision=precision_highest))
    second_out = (skipped + hidden) * root_half
    layout = second_out.shape
    positions = layout[1] * layout[2]
    normed = lowered_values(gnorm(second_out, norm_wide[2], norm_wide[3])).reshape(layout[0], positions, HALF_CHANNELS)
    qkv = lowered_backward(lowered_values(jnp.einsum('bpc,cd->bpd', normed, lowered_values(attn_proj[:, :3 * HALF_CHANNELS]), precision=precision_highest)))
    query_rows = qkv[..., :HALF_CHANNELS]
    key_rows = qkv[..., HALF_CHANNELS:2 * HALF_CHANNELS]
    value_rows = qkv[..., 2 * HALF_CHANNELS:]
    attention_logits = lowered_backward(jnp.einsum('xjs,xos->xjo', query_rows, key_rows, precision=precision_highest) * HALF_CHANNELS ** (-0.5))
    attention_weights = jax.nn.softmax(attention_logits, axis=-1)
    attention_result = lowered_backward(lowered_values(jnp.einsum('hac,hcw->haw', lowered_values(attention_weights), value_rows, precision=precision_highest)))
    attn_out = lowered_backward(jnp.einsum('bpc,cd->bpd', attention_result, lowered_values(attn_proj[:, 3 * HALF_CHANNELS:]), precision=precision_highest))
    third_out = (second_out + attn_out.reshape(layout)) * root_half
    head_in = lowered_backward(lowered_values(silu(gnorm(third_out, norm_wide[4], norm_wide[5]))))
    upsampled = jnp.repeat(jnp.repeat(head_in, 2, axis=1), 2, axis=2)
    predicted = lowered_backward(convolve(upsampled, lowered_values(head_conv)))
    error = predicted - targets
    return jnp.sum(weights_px * lax.optimization_barrier(jnp.sum(error * error, -1)))

def adamw(weight, grad, first, second, rate):
    first = beta_one * first + (1.0 - beta_one) * grad
    second = beta_two * second + (1.0 - beta_two) * grad * grad
    corrected = first / (1.0 - beta_one ** STEP) / (jnp.sqrt(second / (1.0 - beta_two ** STEP)) + adam_epsilon)
    return (weight - rate * (corrected + decay_rate * weight), first, second)

def reference(features, target, pixel_mask, buckets, conv_pair, down_conv, conv_wide, skip_proj, attn_proj, head_conv, norm_narrow, norm_wide, time_bias, conv_pair_mom, down_conv_mom, conv_wide_mom, skip_proj_mom, attn_proj_mom, head_conv_mom, norm_narrow_mom, norm_wide_mom, time_bias_mom, conv_pair_sq, down_conv_sq, conv_wide_sq, skip_proj_sq, attn_proj_sq, head_conv_sq, norm_narrow_sq, norm_wide_sq, time_bias_sq):
    onehot = (buckets[:, None] == jnp.arange(NB)[None, :]).astype(jnp.float32)
    mask_val = pixel_mask.astype(jnp.float32)
    counts = lax.optimization_barrier(jnp.sum(onehot * lax.optimization_barrier(jnp.sum(mask_val, axis=(1, 2)))[:, None], 0))
    per_image = 1.0 / jnp.dot(onehot, counts, precision=precision_highest)
    weights_px = mask_val * per_image[:, None, None]
    params = (conv_pair, down_conv, conv_wide, skip_proj, attn_proj, head_conv, norm_narrow, norm_wide, time_bias)
    firsts = (conv_pair_mom, down_conv_mom, conv_wide_mom, skip_proj_mom, attn_proj_mom, head_conv_mom, norm_narrow_mom, norm_wide_mom, time_bias_mom)
    seconds = (conv_pair_sq, down_conv_sq, conv_wide_sq, skip_proj_sq, attn_proj_sq, head_conv_sq, norm_narrow_sq, norm_wide_sq, time_bias_sq)
    inputs = features.astype(jnp.float32)
    targets = target.astype(jnp.float32)
    loss_sum, pullback = jax.vjp(lambda weights: forward(weights, inputs, targets, weights_px, onehot), params)
    grads = pullback(jnp.ones((), jnp.float32))[0]
    results = []
    for member in range(9):
        rate = rate_matrix if member < 6 else rate_vector
        results.extend(adamw(params[member], grads[member], firsts[member], seconds[member], rate))
    return (loss_sum, counts, results[0], results[1], results[2], results[3], results[4], results[5], results[6], results[7], results[8], results[9], results[10], results[11], results[12], results[13], results[14], results[15], results[16], results[17], results[18], results[19], results[20], results[21], results[22], results[23], results[24], results[25], results[26])
```

```python
import jax
import jax.numpy as jnp
from jax import lax
from jax.sharding import PartitionSpec as P

C1 = 128
HALF_CHANNELS = 256
GROUPS = 32
NB = 8
STEP = 10


epsilon = 1e-05
root_half = 0.7071067811865476
beta_one = 0.9
beta_two = 0.999
adam_epsilon = 1e-08
decay_rate = 0.1
rate_matrix = 0.03
rate_vector = 0.5
precision_highest = lax.Precision.HIGHEST


def rounded(tensor):
    return tensor.astype(jnp.bfloat16)


def silu_both(tensor):
    sigmoid_val = jax.nn.sigmoid(tensor)
    return (tensor * sigmoid_val, sigmoid_val * (1.0 + tensor * (1.0 - sigmoid_val)))


def whole_images(tensor):
    return lax.all_to_all(tensor, "sp", split_axis=0, concat_axis=1, tiled=True)


def product(spec, first, second):
    return jnp.einsum(spec, first, second, preferred_element_type=jnp.float32)


def norm_forward(tensor, scales, shifts):
    layout = tensor.shape
    grouped = tensor.reshape(layout[:-1] + (GROUPS, layout[-1] // GROUPS))
    counted = layout[1] * layout[2] * grouped.shape[-1]
    average = jnp.sum(grouped, axis=(1, 2, 4), keepdims=True) / counted
    squares = jnp.sum(grouped * grouped, axis=(1, 2, 4), keepdims=True) / counted
    inv_std = lax.rsqrt(squares - average * average + epsilon)
    normed = ((grouped - average) * inv_std).reshape(layout)
    return (normed * scales + shifts, (normed, inv_std, counted))


def norm_backward(grad_out, scales, kept, want_input):
    normed, inv_std, counted = kept
    scale_grad = jnp.sum(grad_out * normed, axis=(0, 1, 2))
    shift_grad = jnp.sum(grad_out, axis=(0, 1, 2))
    if not want_input:
        return (None, scale_grad, shift_grad)
    layout = grad_out.shape
    inner = (grad_out * scales).reshape(layout[:-1] + (GROUPS, layout[-1] // GROUPS))
    grouped = normed.reshape(inner.shape)
    total_sum = jnp.sum(inner, axis=(1, 2, 4), keepdims=True)
    product_sum = jnp.sum(inner * grouped, axis=(1, 2, 4), keepdims=True)
    input_grad = inv_std * (inner - total_sum / counted - grouped * product_sum / counted)
    return (input_grad.reshape(layout), scale_grad, shift_grad)


def pad_image(tensor):
    return jnp.pad(tensor, ((0, 0), (1, 1), (1, 1), (0, 0)))


def conv_valid(padded, kernel):
    return lax.conv_general_dilated(
        padded,
        kernel,
        (1, 1),
        "VALID",
        dimension_numbers=("NHWC", "HWIO", "NHWC"),
        preferred_element_type=jnp.float32,
    )


def kernel_grad(padded, grad_out):
    height = grad_out.shape[1]
    across = grad_out.shape[2]
    return jnp.stack(
        [
            jnp.stack(
                [
                    jnp.einsum(
                        "bhwi,bhwo->io",
                        padded[:, down_step : down_step + height, side_step : side_step + across],
                        grad_out,
                        preferred_element_type=jnp.float32,
                    )
                    for side_step in range(3)
                ]
            )
            for down_step in range(3)
        ]
    )


def flipped(kernel):
    return jnp.swapaxes(kernel[::-1, ::-1], 2, 3)


def fir_table(size_in):
    rows_out = jnp.arange(size_in // 2)[:, None]
    cols_in = jnp.arange(size_in)[None, :]
    tapped = cols_in - 2 * rows_out + 1
    return jnp.where(
        (tapped == 0) | (tapped == 3), 0.125, jnp.where((tapped == 1) | (tapped == 2), 0.375, 0.0)
    ).astype(jnp.float32)


def fir_down(tensor):
    table = fir_table(tensor.shape[1])
    return jnp.einsum("ij,bjkc,lk->bilc", table, tensor, table, precision=precision_highest)


def fir_up(tensor):
    table = fir_table(2 * tensor.shape[1])
    return jnp.einsum("ij,bilc,lk->bjkc", table, tensor, table, precision=precision_highest)


def adamw(weight, grad, first, second, rate):
    first = beta_one * first + (1.0 - beta_one) * grad
    second = beta_two * second + (1.0 - beta_two) * grad * grad
    corrected = (
        first / (1.0 - beta_one**STEP) / (jnp.sqrt(second / (1.0 - beta_two**STEP)) + adam_epsilon)
    )
    return (weight - rate * (corrected + decay_rate * weight), first, second)


def on_device(
    features,
    target,
    pixel_mask,
    buckets,
    conv_pair,
    down_conv,
    conv_wide,
    skip_proj,
    attn_proj,
    head_conv,
    norm_narrow,
    norm_wide,
    time_bias,
    conv_pair_mom,
    down_conv_mom,
    conv_wide_mom,
    skip_proj_mom,
    attn_proj_mom,
    head_conv_mom,
    norm_narrow_mom,
    norm_wide_mom,
    time_bias_mom,
    conv_pair_sq,
    down_conv_sq,
    conv_wide_sq,
    skip_proj_sq,
    attn_proj_sq,
    head_conv_sq,
    norm_narrow_sq,
    norm_wide_sq,
    time_bias_sq,
):
    images = features.shape[0] // lax.axis_size("sp")
    features = whole_images(features)
    target_in = whole_images(target).astype(jnp.float32)
    mask_in = whole_images(pixel_mask).astype(jnp.float32)
    buckets = lax.dynamic_slice_in_dim(buckets, lax.axis_index("sp") * images, images, 0)
    onehot = (buckets[:, None] == jnp.arange(NB)[None, :]).astype(jnp.float32)
    bias_rows = jnp.dot(onehot, time_bias, precision=precision_highest)
    bias_narrow = bias_rows[:, None, None, :C1]
    bias_wide = bias_rows[:, None, None, C1:]
    local_counts = jnp.sum(onehot * jnp.sum(mask_in, axis=(1, 2))[:, None], 0)
    counts = lax.psum(local_counts, ("dp", "sp"))
    per_image = 1.0 / jnp.dot(onehot, counts, precision=precision_highest)
    weights_px = mask_in * per_image[:, None, None]
    pair_low = rounded(conv_pair)
    down_low = rounded(down_conv)
    wide_low = rounded(conv_wide)
    skip_low = rounded(skip_proj)
    qkv_low = rounded(attn_proj[:, : 3 * HALF_CHANNELS])
    out_low = rounded(attn_proj[:, 3 * HALF_CHANNELS :])
    head_low = rounded(head_conv)
    start = features.astype(jnp.float32)
    normed_a, keep_a = norm_forward(start, norm_narrow[0], norm_narrow[1])
    active_a, slope_a = silu_both(normed_a)
    padded_a = pad_image(rounded(active_a))
    hidden_b = conv_valid(padded_a, pair_low[0]) + bias_narrow
    normed_b, keep_b = norm_forward(hidden_b, norm_narrow[2], norm_narrow[3])
    active_b, slope_b = silu_both(normed_b)
    padded_b = pad_image(rounded(active_b))
    first_out = (start + conv_valid(padded_b, pair_low[1])) * root_half
    shared = rounded(first_out).astype(jnp.float32)
    normed_c, keep_c = norm_forward(shared, norm_narrow[4], norm_narrow[5])
    active_c, slope_c = silu_both(normed_c)
    padded_c = pad_image(rounded(fir_down(active_c)))
    hidden_d = conv_valid(padded_c, down_low) + bias_wide
    normed_d, keep_d = norm_forward(hidden_d, norm_wide[0], norm_wide[1])
    active_d, slope_d = silu_both(normed_d)
    padded_d = pad_image(rounded(active_d))
    skip_in = rounded(fir_down(shared))
    skip_out = product("bhwi,io->bhwo", skip_in, skip_low)
    second_out = (skip_out + conv_valid(padded_d, wide_low)) * root_half
    normed_e, keep_e = norm_forward(second_out, norm_wide[2], norm_wide[3])
    layout = second_out.shape
    positions = layout[1] * layout[2]
    attn_in = rounded(normed_e).reshape(images, positions, HALF_CHANNELS)
    qkv = rounded(product("bpc,cd->bpd", attn_in, qkv_low))
    query_rows = qkv[..., :HALF_CHANNELS]
    key_rows = qkv[..., HALF_CHANNELS : 2 * HALF_CHANNELS]
    value_rows = qkv[..., 2 * HALF_CHANNELS :]
    logit_scale = HALF_CHANNELS ** (-0.5)
    attention_logits = product("xjs,xos->xjo", query_rows, key_rows) * logit_scale
    shifted = jnp.exp(attention_logits - jnp.max(attention_logits, -1, keepdims=True))
    attention_weights = shifted / jnp.sum(shifted, -1, keepdims=True)
    lowered_weights = rounded(attention_weights)
    attention_result = rounded(product("hac,hcw->haw", lowered_weights, value_rows))
    attn_out = product("bpc,cd->bpd", attention_result, out_low)
    third_out = (second_out + attn_out.reshape(layout)) * root_half
    normed_f, keep_f = norm_forward(third_out, norm_wide[4], norm_wide[5])
    active_f, slope_f = silu_both(normed_f)
    padded_f = pad_image(jnp.repeat(jnp.repeat(rounded(active_f), 2, axis=1), 2, axis=2))
    predicted = conv_valid(padded_f, head_low)
    error = predicted - target_in
    loss_local = jnp.sum(weights_px * jnp.sum(error * error, -1))
    grad_pred = rounded(2.0 * error * weights_px[..., None])
    head_grad = kernel_grad(padded_f, grad_pred)
    grad_up = conv_valid(pad_image(grad_pred), flipped(head_low))
    up_dims = grad_up.shape
    grad_head = grad_up.reshape(
        images, up_dims[1] // 2, 2, up_dims[2] // 2, 2, HALF_CHANNELS
    ).sum(axis=(2, 4))
    grad_f = rounded(grad_head).astype(jnp.float32) * slope_f
    grad_third, gain_f, shift_f = norm_backward(grad_f, norm_wide[4], keep_f, True)
    grad_attn = rounded(grad_third * root_half).reshape(images, positions, HALF_CHANNELS)
    out_grad = product("bpc,bpd->cd", attention_result, grad_attn)
    attention_gradient = rounded(product("bpd,cd->bpc", grad_attn, out_low))
    grad_probs = product("xjs,xos->xjo", attention_gradient, value_rows)
    grad_values = product("nuo,nue->noe", lowered_weights, attention_gradient)
    scores_gradient = rounded(
        attention_weights
        * (grad_probs - jnp.sum(attention_weights * grad_probs, -1, keepdims=True))
    )
    grad_query = product("hac,hcw->haw", scores_gradient, key_rows) * logit_scale
    grad_keyed = product("nuo,nue->noe", scores_gradient, query_rows) * logit_scale
    grad_qkv = rounded(jnp.concatenate([grad_query, grad_keyed, grad_values], -1))
    qkv_grad = product("bpc,bpd->cd", attn_in, grad_qkv)
    grad_e = product("bpd,cd->bpc", grad_qkv, qkv_low).reshape(layout)
    grad_second, gain_e, shift_e = norm_backward(grad_e, norm_wide[2], keep_e, True)
    grad_second = grad_second + grad_third * root_half
    grad_branch = rounded(grad_second * root_half)
    wide_grad = kernel_grad(padded_d, grad_branch)
    grad_d = conv_valid(pad_image(grad_branch), flipped(wide_low)) * slope_d
    skip_grad = product("bhwi,bhwo->io", skip_in, grad_branch)
    grad_skip_in = product("bhwo,io->bhwi", grad_branch, skip_low)
    grad_hidden_d, gain_d, shift_d = norm_backward(grad_d, norm_wide[0], keep_d, True)
    grad_down = rounded(grad_hidden_d)
    down_grad = kernel_grad(padded_c, grad_down)
    grad_c = fir_up(conv_valid(pad_image(grad_down), flipped(down_low))) * slope_c
    grad_shared, gain_c, shift_c = norm_backward(grad_c, norm_narrow[4], keep_c, True)
    grad_first = rounded(grad_shared + fir_up(grad_skip_in)).astype(jnp.float32)
    grad_conv_b = rounded(grad_first * root_half)
    pair_grad_b = kernel_grad(padded_b, grad_conv_b)
    grad_b = conv_valid(pad_image(grad_conv_b), flipped(pair_low[1])) * slope_b
    grad_hidden_b, gain_b, shift_b = norm_backward(grad_b, norm_narrow[2], keep_b, True)
    grad_conv_a = rounded(grad_hidden_b)
    pair_grad_a = kernel_grad(padded_a, grad_conv_a)
    grad_a = conv_valid(pad_image(grad_conv_a), flipped(pair_low[0])) * slope_a
    unused, gain_a, shift_a = norm_backward(grad_a, norm_narrow[0], keep_a, False)
    bias_grad = jnp.concatenate(
        [jnp.sum(grad_hidden_b, axis=(1, 2)), jnp.sum(grad_hidden_d, axis=(1, 2))], 1
    )
    summed = lax.psum(
        (
            jnp.stack([pair_grad_a, pair_grad_b]),
            down_grad,
            wide_grad,
            skip_grad,
            jnp.concatenate([qkv_grad, out_grad], 1),
            head_grad,
            jnp.stack([gain_a, shift_a, gain_b, shift_b, gain_c, shift_c]),
            jnp.stack([gain_d, shift_d, gain_e, shift_e, gain_f, shift_f]),
            jnp.dot(onehot.T, bias_grad, precision=precision_highest),
            loss_local,
        ),
        ("dp", "sp"),
    )
    params = (
        conv_pair,
        down_conv,
        conv_wide,
        skip_proj,
        attn_proj,
        head_conv,
        norm_narrow,
        norm_wide,
        time_bias,
    )
    firsts = (
        conv_pair_mom,
        down_conv_mom,
        conv_wide_mom,
        skip_proj_mom,
        attn_proj_mom,
        head_conv_mom,
        norm_narrow_mom,
        norm_wide_mom,
        time_bias_mom,
    )
    seconds = (
        conv_pair_sq,
        down_conv_sq,
        conv_wide_sq,
        skip_proj_sq,
        attn_proj_sq,
        head_conv_sq,
        norm_narrow_sq,
        norm_wide_sq,
        time_bias_sq,
    )
    results = []
    for member in range(9):
        rate = rate_matrix if member < 6 else rate_vector
        results.extend(adamw(params[member], summed[member], firsts[member], seconds[member], rate))
    return (summed[9], counts) + tuple(results)


def solution(mesh):
    placed = (
        P("dp", "sp", None, None),
        P("dp", "sp", None, None),
        P("dp", "sp", None),
        P("dp"),
        P(),
        P(),
        P(),
        P(),
        P(),
        P(),
        P(),
        P(),
        P(),
        P(),
        P(),
        P(),
        P(),
        P(),
        P(),
        P(),
        P(),
        P(),
        P(),
        P(),
        P(),
        P(),
        P(),
        P(),
        P(),
        P(),
        P(),
    )
    return jax.shard_map(
        on_device,
        mesh=mesh,
        in_specs=placed,
        out_specs=(
            P(),
            P(),
            P(),
            P(),
            P(),
            P(),
            P(),
            P(),
            P(),
            P(),
            P(),
            P(),
            P(),
            P(),
            P(),
            P(),
            P(),
            P(),
            P(),
            P(),
            P(),
            P(),
            P(),
            P(),
            P(),
            P(),
            P(),
            P(),
            P(),
        ),
        check_vma=False,
    )
```

```python
import functools

import jax
import jax.numpy as jnp
from jax import lax
from jax.experimental import pallas as pl
from jax.experimental.pallas import tpu as pltpu
from jax.sharding import PartitionSpec as P

C1 = 128
HALF_CHANNELS = 256
GROUPS = 32
RES = 32
HALF = 16
NB = 8
STEP = 10
MESH = pl.DeviceIdType.MESH
VMEM_LIMIT = 62 * 1024 * 1024

epsilon = 1e-05
root_half = 0.7071067811865476
beta_one = 0.9
beta_two = 0.999
adam_epsilon = 1e-08
decay_rate = 0.1
rate_matrix = 0.03
rate_vector = 0.5
logit_scale = HALF_CHANNELS ** (-0.5)
ROWS = 8

bf16 = jnp.bfloat16
f32 = jnp.float32

EVEN, ODD, ODD_LEFT, EVEN_RIGHT = 0, 1, 2, 3
TAPS = ((ODD_LEFT, EVEN, ODD), (EVEN, ODD, EVEN_RIGHT))


def rounded(v):
    return v.astype(bf16).astype(f32)


def silu(t):
    return t * jax.nn.sigmoid(t)


def slope(t):
    s = jax.nn.sigmoid(t)
    return s * (1.0 + t * (1.0 - s))


def mm(a, b):
    return lax.dot_general(a, b, (((1,), (0,)), ((), ())), preferred_element_type=f32)


def mm_nt(a, b):
    return lax.dot_general(a, b, (((1,), (1,)), ((), ())), preferred_element_type=f32)


def mm_tn(a, b):
    return lax.dot_general(a, b, (((0,), (0,)), ((), ())), preferred_element_type=f32)


def fold(v):
    return jnp.sum(v.reshape(-1, 8, v.shape[-1]), axis=0)


def total(v):
    return jnp.broadcast_to(jnp.sum(v, axis=0, keepdims=True), v.shape)


def group_sum(v, size):
    lanes = v.shape[-1]
    lane = lax.broadcasted_iota(jnp.int32, v.shape, 1)
    step = 1
    while step < size:
        other = jnp.where(
            (lane & step) == 0, pltpu.roll(v, lanes - step, 1), pltpu.roll(v, step, 1)
        )
        v = v + other
        step *= 2
    return v


def norm_coefs(sums, squares, gain, shift, pixels):
    size = sums.shape[-1] // GROUPS
    count = pixels * size
    mean = group_sum(total(sums), size) / count
    power = group_sum(total(squares), size) / count
    inv = lax.rsqrt(power - mean * mean + epsilon)
    scale = inv * gain
    return scale, shift - mean * scale, mean, inv


def norm_grad_coefs(sum_dy, sum_dyv, gain, mean, inv, pixels):
    size = sum_dy.shape[-1] // GROUPS
    count = pixels * size
    first = total(sum_dy)
    second = (total(sum_dyv) - mean * first) * inv
    one = group_sum(first * gain, size) / count
    two = group_sum(second * gain, size) / count
    b = -inv * inv * two
    return second, first, inv * gain, b, -inv * one - mean * b


def shift_cols(v, step):
    col = lax.broadcasted_iota(jnp.int32, v.shape, 1)
    if step == 1:
        return jnp.where(col == 0, 0.0, pltpu.roll(v, 1, 1))
    return jnp.where(col == HALF - 1, 0.0, pltpu.roll(v, HALF - 1, 1))


def store_planes(planes, n, b, r0, v):
    rows = v.shape[0]
    v = v.astype(bf16).astype(f32)
    for plane, value in (
        (EVEN + b, v),
        (ODD_LEFT if b == 1 else EVEN_RIGHT, shift_cols(v, 1 if b == 1 else -1)),
    ):
        planes[n, plane, pl.ds(r0 + 1, rows)] = value.astype(bf16)


def store_shifted(cells, n, r0, v):
    rows = v.shape[0]
    v = v.astype(bf16).astype(f32)
    for tap, value in ((0, shift_cols(v, 1)), (1, v), (2, shift_cols(v, -1))):
        cells[n, tap, pl.ds(r0 + 1, rows)] = value.astype(bf16)


def plane_block(planes, tap, jj):
    return planes[:, tap, pl.ds(jj, HALF, stride=2)].reshape(-1, planes.shape[-1])


def pair_input(planes, b, jjs):
    return jnp.concatenate([plane_block(planes, tap, jj) for jj in jjs for tap in TAPS[b]], axis=1)


def cell_input(cells, dys):
    return jnp.concatenate(
        [
            cells[:, tap, dy : dy + HALF].reshape(-1, cells.shape[-1])
            for dy in dys
            for tap in range(3)
        ],
        axis=1,
    )


def each(count, body):
    def step(i, carry):
        body(i)
        return carry

    lax.fori_loop(0, count, step, 0)


def prepare_weights(pair, down, wide, skip, attn, head, pair_fwd, pair_bwd, down_fwd, down_bwd, wide_fwd, wide_bwd, skip_low, attn_low, head_low):
    nothing = jnp.zeros((C1, C1), bf16)
    for member in range(2):
        for jj in range(4):
            for k in range(3):
                block = (jj * 3 + k) * C1
                for a in range(2):
                    dy = jj - a
                    inside = 0 <= dy < 3
                    row = (member * 9 + dy * 3 + k) * C1
                    back = (member * 9 + (2 - dy) * 3 + (2 - k)) * C1
                    pair_fwd[member, block : block + C1, a * C1 : a * C1 + C1] = (
                        pair[row : row + C1, :].astype(bf16) if inside else nothing
                    )
                    pair_bwd[member, a * C1 : a * C1 + C1, block : block + C1] = (
                        pair[back : back + C1, :].astype(bf16) if inside else nothing
                    )
    wide_channels = HALF_CHANNELS
    for tap in range(9):
        low = down[tap * C1 : tap * C1 + C1, :].astype(bf16)
        down_fwd[tap * C1 : tap * C1 + C1, :] = low
        down_bwd[:, (8 - tap) * wide_channels : (9 - tap) * wide_channels] = low
        low = wide[tap * wide_channels : (tap + 1) * wide_channels, :].astype(bf16)
        wide_fwd[tap * wide_channels : (tap + 1) * wide_channels, :] = low
        wide_bwd[:, (8 - tap) * wide_channels : (9 - tap) * wide_channels] = low
    skip_low[...] = skip[...].astype(bf16)
    attn_low[...] = attn[...].astype(bf16)
    head_low[...] = jnp.zeros(head_low.shape, f32)
    for tap in range(9):
        head_low[tap * 8 : tap * 8 + 3, :] = rounded(head[tap])


def split_three(v):
    high = v.astype(bf16)
    rest = v - high.astype(f32)
    middle = rest.astype(bf16)
    return high, middle, (rest - middle.astype(f32)).astype(bf16)


def lane_shift(v, step):
    lane = lax.broadcasted_iota(jnp.int32, v.shape, 1)
    j = lane & (HALF - 1)
    if step == 1:
        keep = j < HALF - 1
    elif step == -1:
        keep = j > 0
    elif step == HALF:
        keep = lane < HALF * (HALF - 1)
    else:
        keep = lane >= HALF
    return jnp.where(keep, pltpu.roll(v, (-step) % v.shape[-1], 1), 0.0)


def head_forward(table):
    cols = [
        [
            lane_shift(table[dy][0], -1) + table[dy][1] + table[dy][2],
            table[dy][0] + table[dy][1] + lane_shift(table[dy][2], 1),
        ]
        for dy in range(3)
    ]
    return [
        [
            lane_shift(cols[0][b], -HALF) + cols[1][b] + cols[2][b]
            if a == 0
            else cols[0][b] + cols[1][b] + lane_shift(cols[2][b], HALF)
            for b in range(2)
        ]
        for a in range(2)
    ]


def head_backward(grad):
    rows = [
        [
            lane_shift(grad[0][b], HALF) + grad[1][b],
            grad[0][b] + grad[1][b],
            grad[0][b] + lane_shift(grad[1][b], -HALF),
        ]
        for b in range(2)
    ]
    return [
        [
            lane_shift(rows[0][dy], 1) + rows[1][dy],
            rows[0][dy] + rows[1][dy],
            rows[0][dy] + lane_shift(rows[1][dy], -1),
        ]
        for dy in range(3)
    ]


def keep_columns(ref, row, v):
    for c in range(v.shape[1] // 128):
        ref[row + c * v.shape[0] : row + (c + 1) * v.shape[0], :] = v[:, c * 128 : (c + 1) * 128]


HEAD_ROWS = 72
WIDE_NORM_ROW = 72
LOSS_ROW = 78
NARROW_NORM_ROW = 80
TIME_WIDE_ROW = 88
TIME_NARROW_ROW = 96
SMALL_ROWS = 128
SKIP_ROW = 18 * C1
PIECES = (
    (8 * HALF_CHANNELS, 128),
    (18 * HALF_CHANNELS, 128),
    (20 * C1, 128),
    (18 * C1, 128),
    (SMALL_ROWS, HALF_CHANNELS),
)


def main_kernel(
    buckets, x_in, target, mask, counts, pair, down, wide, skip, attn, head, gains_narrow, gains_wide, time_bias,
    g_attn, g_wide, g_down, g_pair, g_small,
    pair_fwd, pair_bwd, down_fwd, down_bwd, wide_fwd, wide_bwd, skip_low, attn_low, head_low,
    x_full, h1_full, xs_full, dy_full, in_a, in_b, in_g, flat,
    cells_c, cells_d, cells_g, fs_low, dfs, h3, x2, x3, n5, qkv, probs, probs_low, att, a6, dwide, dout, dqkv, dnarrow,
    coef_n, coef_w,
):
    images = x_in.shape[1]
    position = lax.axis_index("sp")
    steps = RES // ROWS
    full_pixels = RES * RES
    half_pixels = HALF * HALF
    zero_n = jnp.zeros((8, C1), f32)
    zero_w = jnp.zeros((8, HALF_CHANNELS), f32)

    def bucket(n):
        return buckets[position * images + n]

    def gain_n(row):
        return jnp.broadcast_to(gains_narrow[row : row + 1, :], (8, C1))

    def gain_w(row):
        return jnp.broadcast_to(gains_wide[row : row + 1, :], (8, HALF_CHANNELS))

    def keep_coefs(ref, which, n, values):
        for kind in range(4):
            ref[which, n, kind] = values[kind]

    def row_of(ref, which, n, kind):
        return ref[which, n, kind, 0:1, :]

    prepare_weights(pair, down, wide, skip, attn, head, pair_fwd, pair_bwd, down_fwd, down_bwd, wide_fwd, wide_bwd, skip_low, attn_low, head_low)
    g_small[...] = jnp.zeros(g_small.shape, f32)
    for planes in (in_a, in_b, in_g):
        edge = jnp.zeros((images, 4, HALF, C1), bf16)
        planes[:, :, 0] = edge
        planes[:, :, RES + 1] = edge
    for cells in (cells_c, cells_d, cells_g):
        edge = jnp.zeros((images, 3, HALF, cells.shape[-1]), bf16)
        cells[:, :, 0] = edge
        cells[:, :, HALF + 1] = edge

    def load_image(n):
        def step(i, carry):
            sums, squares = carry
            half = i // 2
            v = x_in[half, n, pl.ds((i % 2) * ROWS, ROWS)].astype(f32)
            flat[...] = v.reshape(ROWS * RES, C1)
            for b in range(2):
                w = flat[pl.ds(b, ROWS * HALF, stride=2), :].reshape(ROWS, HALF, C1)
                x_full[n, b, pl.ds(i * ROWS, ROWS)] = w
                sums = sums + fold(w)
                squares = squares + fold(w * w)
            return sums, squares

        sums, squares = lax.fori_loop(0, steps, step, (zero_n, zero_n))
        keep_coefs(coef_n, 0, n, norm_coefs(sums, squares, gain_n(0), gain_n(1), full_pixels))

    each(images, load_image)

    def activate(values, planes, which):
        def image(n):
            scale = row_of(coef_n, which, n, 0)
            offset = row_of(coef_n, which, n, 1)

            def step(i):
                for b in range(2):
                    v = values[n, b, pl.ds(i * ROWS, ROWS)]
                    store_planes(planes, n, b, i * ROWS, silu(v * scale + offset))

            each(steps, step)

        each(images, image)

    def pair_rows(result, n):
        part = result[n * half_pixels : (n + 1) * half_pixels].reshape(HALF, 1, HALF, 2 * C1)
        return jnp.concatenate([part[..., :C1], part[..., C1:]], axis=1).reshape(RES, HALF, C1)

    activate(x_full, in_a, 0)
    for b in range(2):
        out = mm(pair_input(in_a, b, range(4)), pair_fwd[0])
        for n in range(images):
            h1_full[n, b] = pair_rows(out, n)

    def first_hidden(n):
        bias = time_bias[pl.ds(bucket(n), 1), :][:, :C1]

        def step(i, carry):
            sums, squares = carry
            for b in range(2):
                v = h1_full[n, b, pl.ds(i * ROWS, ROWS)] + bias
                h1_full[n, b, pl.ds(i * ROWS, ROWS)] = v
                sums = sums + fold(v)
                squares = squares + fold(v * v)
            return sums, squares

        sums, squares = lax.fori_loop(0, steps, step, (zero_n, zero_n))
        keep_coefs(coef_n, 1, n, norm_coefs(sums, squares, gain_n(2), gain_n(3), full_pixels))

    each(images, first_hidden)
    activate(h1_full, in_b, 1)
    for b in range(2):
        out = mm(pair_input(in_b, b, range(4)), pair_fwd[1])
        for n in range(images):
            xs_full[n, b] = pair_rows(out, n)

    def first_out(n):
        def step(i, carry):
            sums, squares = carry
            for b in range(2):
                v = xs_full[n, b, pl.ds(i * ROWS, ROWS)]
                v = rounded((x_full[n, b, pl.ds(i * ROWS, ROWS)] + v) * root_half)
                xs_full[n, b, pl.ds(i * ROWS, ROWS)] = v
                sums = sums + fold(v)
                squares = squares + fold(v * v)
            return sums, squares

        sums, squares = lax.fori_loop(0, steps, step, (zero_n, zero_n))
        keep_coefs(coef_n, 2, n, norm_coefs(sums, squares, gain_n(4), gain_n(5), full_pixels))

    each(images, first_out)

    def fir_down_image(n):
        scale = row_of(coef_n, 2, n, 0)
        offset = row_of(coef_n, 2, n, 1)
        for b in range(2):
            dy_full[n, b, 0] = jnp.zeros((HALF, C1), f32)
            dy_full[n, b, RES + 1] = jnp.zeros((HALF, C1), f32)

        def act_step(i):
            for b in range(2):
                v = xs_full[n, b, pl.ds(i * ROWS, ROWS)]
                dy_full[n, b, pl.ds(i * ROWS + 1, ROWS)] = silu(v * scale + offset)

        each(steps, act_step)

        def columns(rows):
            even, odd = rows
            return (
                0.125 * (shift_cols(odd, 1) + shift_cols(even, -1)) + 0.375 * (even + odd)
            )

        def taps(ref, b, r0, size):
            return [ref[n, b, pl.ds(r0 + t, size, stride=2)] for t in range(4)]

        def down_step(i):
            size = HALF // 2
            rows = []
            for b in range(2):
                t = taps(dy_full, b, 2 * size * i, size)
                rows.append(0.125 * (t[0] + t[3]) + 0.375 * (t[1] + t[2]))
            store_shifted(cells_c, n, i * size, columns(rows))

        each(2, down_step)
        for b in range(2):
            dy_full[n, b, pl.ds(1, RES)] = xs_full[n, b]

        def skip_step(i):
            size = HALF // 2
            rows = []
            for b in range(2):
                t = taps(dy_full, b, 2 * size * i, size)
                rows.append(0.125 * (t[0] + t[3]) + 0.375 * (t[1] + t[2]))
            fs_low[n, pl.ds(i * size * HALF, size * HALF)] = (
                columns(rows).reshape(size * HALF, C1).astype(bf16)
            )

        each(2, skip_step)

    each(images, fir_down_image)

    def wide_stats(v, which, n, row):
        values = norm_coefs(fold(v), fold(v * v), gain_w(row), gain_w(row + 1), half_pixels)
        keep_coefs(coef_w, which, n, values)
        return values[0][0:1, :], values[1][0:1, :]

    out = mm(cell_input(cells_c, range(3)), down_fwd[...])
    for n in range(images):
        v = out[n * half_pixels : (n + 1) * half_pixels] + time_bias[pl.ds(bucket(n), 1), :][:, C1:]
        h3[n] = v
        scale, offset = wide_stats(v, 0, n, 0)
        store_shifted(cells_d, n, 0, silu(v * scale + offset).reshape(HALF, HALF, HALF_CHANNELS))
    out = mm(cell_input(cells_d, range(3)), wide_fwd[...])
    out = out + mm(fs_low[...].reshape(-1, C1), skip_low[...])
    for n in range(images):
        v = out[n * half_pixels : (n + 1) * half_pixels] * root_half
        x2[n] = v
        scale, offset = wide_stats(v, 1, n, 2)
        n5[n] = (v * scale + offset).astype(bf16)
        qkv[n] = mm(n5[n], attn_low[:, : 3 * HALF_CHANNELS]).astype(bf16)
        q = qkv[n, :, :HALF_CHANNELS]
        k = qkv[n, :, HALF_CHANNELS : 2 * HALF_CHANNELS]
        w = qkv[n, :, 2 * HALF_CHANNELS :]
        logits = mm_nt(q, k) * logit_scale
        powers = jnp.exp(logits - jnp.max(logits, axis=1, keepdims=True))
        weights = powers / jnp.sum(powers, axis=1, keepdims=True)
        probs[n] = weights
        probs_low[n] = weights.astype(bf16)
        att[n] = mm(probs_low[n], w).astype(bf16)
        v = (v + mm(att[n], attn_low[:, 3 * HALF_CHANNELS :])) * root_half
        x3[n] = v
        scale, offset = wide_stats(v, 2, n, 4)
        a6[n] = silu(v * scale + offset).astype(bf16)

    lane = lax.broadcasted_iota(jnp.int32, (RES, 2 * half_pixels), 1)
    source = lax.broadcasted_iota(jnp.int32, (RES, 2 * half_pixels), 0)
    picks = (source == 2 * (lane & (HALF - 1)) + (lane >> 8)).astype(bf16)
    row_lane = (lax.broadcasted_iota(jnp.int32, (HALF, 2 * half_pixels), 1) & (half_pixels - 1)) >> 4
    row_source = lax.broadcasted_iota(jnp.int32, (HALF, 2 * half_pixels), 0)
    component = lax.broadcasted_iota(jnp.int32, (8, half_pixels), 0)

    def spread(halves):
        moved = [mm(half, picks) for half in halves]
        rows = []
        for a in range(2):
            picked = sum(
                jnp.where(2 * row_lane + a == row_source + HALF * h, moved[h], 0.0)
                for h in range(2)
            )
            row = jnp.sum(picked, axis=0, keepdims=True)
            rows.append([row[:, :half_pixels], row[:, half_pixels:]])
        return rows

    loss = jnp.zeros((1, half_pixels), f32)
    head_grad = jnp.zeros((HEAD_ROWS, HALF_CHANNELS), f32)
    for n in range(images):
        moved = mm_nt(head_low[...].astype(bf16), a6[n])
        pred = head_forward(
            [[moved[(dy * 3 + dx) * 8 : (dy * 3 + dx) * 8 + 8] for dx in range(3)] for dy in range(3)]
        )
        wanted = [spread([target[h, n, c] for h in range(2)]) for c in range(3)]
        counted = spread([mask[h, n].astype(f32).astype(bf16) for h in range(2)])
        per_image = 1.0 / counts[pl.ds(bucket(n), 1), :]
        per_image = jnp.concatenate([per_image, per_image], axis=1)
        grad_pred = [[None, None], [None, None]]
        for a in range(2):
            for b in range(2):
                goal = jnp.zeros((8, half_pixels), f32)
                for c in range(3):
                    goal = jnp.where(component == c, wanted[c][a][b], goal)
                error = pred[a][b] - goal
                weight = counted[a][b] * per_image
                loss = loss + weight * jnp.sum(error * error, axis=0, keepdims=True)
                grad_pred[a][b] = rounded(2.0 * error * weight)
        table = head_backward(grad_pred)
        table = jnp.concatenate([table[dy][dx] for dy in range(3) for dx in range(3)], axis=0)
        parts = split_three(table)
        for part in parts:
            head_grad = head_grad + mm(part, a6[n])
        head_rows = head_low[...].astype(bf16)
        grad = sum(mm_tn(part, head_rows) for part in parts)
        v = x3[n]
        values = [coef_w[2, n, kind] for kind in range(4)]
        dy = rounded(grad) * slope(v * values[0][0:1, :] + values[1][0:1, :])
        gain, shift, ca, cb, cd = norm_grad_coefs(
            fold(dy), fold(dy * v), gain_w(4), values[2], values[3], half_pixels
        )
        g_small[WIDE_NORM_ROW + 4 : WIDE_NORM_ROW + 5, :] += gain[0:1, :]
        g_small[WIDE_NORM_ROW + 5 : WIDE_NORM_ROW + 6, :] += shift[0:1, :]
        grad_third = dy * ca[0:1, :] + v * cb[0:1, :] + cd[0:1, :]
        dwide[n] = grad_third
    g_small[0:HEAD_ROWS, :] = head_grad
    g_small[LOSS_ROW : LOSS_ROW + 1, :] = jnp.broadcast_to(
        jnp.sum(loss, axis=1, keepdims=True), (1, HALF_CHANNELS)
    )

    for n in range(images):
        grad_attn = (dwide[n] * root_half).astype(bf16)
        dout[n] = grad_attn
        grad_att = mm_nt(grad_attn, attn_low[:, 3 * HALF_CHANNELS :]).astype(bf16)
        q = qkv[n, :, :HALF_CHANNELS]
        k = qkv[n, :, HALF_CHANNELS : 2 * HALF_CHANNELS]
        w = qkv[n, :, 2 * HALF_CHANNELS :]
        grad_probs = mm_nt(grad_att, w)
        weights = probs[n]
        inner = jnp.sum(weights * grad_probs, axis=1, keepdims=True)
        grad_scores = (weights * (grad_probs - inner)).astype(bf16)
        dqkv[n, :, :HALF_CHANNELS] = (mm(grad_scores, k) * logit_scale).astype(bf16)
        dqkv[n, :, HALF_CHANNELS : 2 * HALF_CHANNELS] = (mm_tn(grad_scores, q) * logit_scale).astype(bf16)
        dqkv[n, :, 2 * HALF_CHANNELS :] = mm_tn(probs_low[n], grad_att).astype(bf16)
    keep_columns(
        g_attn, 0, mm_tn(n5[...].reshape(-1, HALF_CHANNELS), dqkv[...].reshape(-1, 3 * HALF_CHANNELS))
    )
    keep_columns(
        g_attn,
        6 * HALF_CHANNELS,
        mm_tn(att[...].reshape(-1, HALF_CHANNELS), dout[...].reshape(-1, HALF_CHANNELS)),
    )
    for n in range(images):
        dy = mm_nt(dqkv[n], attn_low[:, : 3 * HALF_CHANNELS])
        v = x2[n]
        gain, shift, ca, cb, cd = norm_grad_coefs(
            fold(dy), fold(dy * v), gain_w(2), coef_w[1, n, 2], coef_w[1, n, 3], half_pixels
        )
        g_small[WIDE_NORM_ROW + 2 : WIDE_NORM_ROW + 3, :] += gain[0:1, :]
        g_small[WIDE_NORM_ROW + 3 : WIDE_NORM_ROW + 4, :] += shift[0:1, :]
        grad = dy * ca[0:1, :] + v * cb[0:1, :] + cd[0:1, :] + dwide[n] * root_half
        store_shifted(cells_g, n, 0, (grad * root_half).reshape(HALF, HALF, HALF_CHANNELS))

    center = cells_g[:, 1, 1 : HALF + 1].reshape(-1, HALF_CHANNELS)
    for dy in range(3):
        product = mm_tn(cell_input(cells_d, [dy]), center)
        for k in range(3):
            keep_columns(
                g_wide,
                (dy * 3 + k) * 2 * HALF_CHANNELS,
                product[k * HALF_CHANNELS : (k + 1) * HALF_CHANNELS],
            )
    keep_columns(g_down, SKIP_ROW, mm_tn(fs_low[...].reshape(-1, C1), center))
    dfs[...] = mm_nt(center, skip_low[...]).reshape(dfs.shape)
    out = mm_nt(cell_input(cells_g, range(3)), wide_bwd[...])
    bucket_rows = lax.broadcasted_iota(jnp.int32, (NB, HALF_CHANNELS), 0)
    time_wide = jnp.zeros((NB, HALF_CHANNELS), f32)
    for n in range(images):
        v = h3[n]
        dy = out[n * half_pixels : (n + 1) * half_pixels] * slope(
            v * row_of(coef_w, 0, n, 0) + row_of(coef_w, 0, n, 1)
        )
        gain, shift, ca, cb, cd = norm_grad_coefs(
            fold(dy), fold(dy * v), gain_w(0), coef_w[0, n, 2], coef_w[0, n, 3], half_pixels
        )
        g_small[WIDE_NORM_ROW : WIDE_NORM_ROW + 1, :] += gain[0:1, :]
        g_small[WIDE_NORM_ROW + 1 : WIDE_NORM_ROW + 2, :] += shift[0:1, :]
        grad = dy * ca[0:1, :] + v * cb[0:1, :] + cd[0:1, :]
        time_wide = time_wide + jnp.where(bucket_rows == bucket(n), total(fold(grad)), 0.0)
        store_shifted(cells_g, n, 0, grad.reshape(HALF, HALF, HALF_CHANNELS))
    g_small[TIME_WIDE_ROW : TIME_WIDE_ROW + NB, :] = time_wide

    center = cells_g[:, 1, 1 : HALF + 1].reshape(-1, HALF_CHANNELS)
    for dy in range(3):
        product = mm_tn(cell_input(cells_c, [dy]), center)
        for k in range(3):
            keep_columns(g_down, (dy * 3 + k) * 2 * C1, product[k * C1 : (k + 1) * C1])
    dnarrow[...] = mm_nt(cell_input(cells_g, range(3)), down_bwd[...]).reshape(dnarrow.shape)

    def up_parts(ref, n, i, size):
        here = pl.ds(i * size * HALF, size * HALF)
        g = ref[n, here].reshape(size, HALF, C1)
        lane_rows = lax.broadcasted_iota(jnp.int32, g.shape, 0) + i * size
        above = ref[n, pl.ds(jnp.maximum(i * size - 1, 0) * HALF, HALF)].reshape(1, HALF, C1)
        below = ref[n, pl.ds(jnp.minimum((i + 1) * size, HALF - 1) * HALF, HALF)].reshape(1, HALF, C1)
        above = jnp.where(lane_rows == 0, 0.0, jnp.concatenate([above, g[:-1]], axis=0))
        below = jnp.where(lane_rows == HALF - 1, 0.0, jnp.concatenate([g[1:], below], axis=0))
        result = []
        for rows in (0.375 * g + 0.125 * above, 0.375 * g + 0.125 * below):
            result.append(
                (
                    0.375 * rows + 0.125 * shift_cols(rows, 1),
                    0.375 * rows + 0.125 * shift_cols(rows, -1),
                )
            )
        return result

    def third_norm(n):
        size = HALF // 4
        scale = row_of(coef_n, 2, n, 0)
        offset = row_of(coef_n, 2, n, 1)

        def step(i, carry):
            sum_dy, sum_dyv = carry
            parts = up_parts(dnarrow, n, i, size)
            for b in range(2):
                g = jnp.stack([parts[0][b], parts[1][b]], axis=1).reshape(2 * size, HALF, C1)
                v = xs_full[n, b, pl.ds(i * 2 * size, 2 * size)]
                dy = g * slope(v * scale + offset)
                dy_full[n, b, pl.ds(i * 2 * size, 2 * size)] = dy
                sum_dy = sum_dy + fold(dy)
                sum_dyv = sum_dyv + fold(dy * v)
            return sum_dy, sum_dyv

        sum_dy, sum_dyv = lax.fori_loop(0, 4, step, (zero_n, zero_n))
        gain, shift, ca, cb, cd = norm_grad_coefs(
            sum_dy, sum_dyv, gain_n(4), coef_n[2, n, 2], coef_n[2, n, 3], full_pixels
        )
        g_small[NARROW_NORM_ROW + 4 : NARROW_NORM_ROW + 5, :C1] += gain[0:1, :]
        g_small[NARROW_NORM_ROW + 5 : NARROW_NORM_ROW + 6, :C1] += shift[0:1, :]

        def finish(i):
            parts = up_parts(dfs, n, i, size)
            for b in range(2):
                g = jnp.stack([parts[0][b], parts[1][b]], axis=1).reshape(2 * size, HALF, C1)
                here = pl.ds(i * 2 * size, 2 * size)
                v = xs_full[n, b, here]
                g = g + dy_full[n, b, here] * ca[0:1, :] + v * cb[0:1, :] + cd[0:1, :]
                store_planes(in_g, n, b, i * 2 * size, rounded(g) * root_half)

        each(4, finish)

    each(images, third_norm)

    def pair_gradient(planes, member):
        products = None
        for b in range(2):
            grads = jnp.concatenate([plane_block(in_g, EVEN + b, a + 1) for a in range(2)], axis=1)
            part = [mm_tn(grads, pair_input(planes, b, jjs)) for jjs in ((0, 1), (2, 3))]
            products = part if products is None else [p + q for p, q in zip(products, part)]
        for dy in range(3):
            blocks = []
            for a in range(2):
                jj = dy + a
                wide_part = products[jj // 2][a * C1 : (a + 1) * C1]
                blocks.append(wide_part[:, (jj % 2) * 3 * C1 : (jj % 2 + 1) * 3 * C1])
            both = blocks[0] + blocks[1]
            for k in range(3):
                row = (member * 9 + dy * 3 + k) * C1
                g_pair[row : row + C1, :] = both[:, k * C1 : (k + 1) * C1].T

    def back_through(member, values, which, gain_row, last):
        for b in range(2):
            out = mm_nt(pair_input(in_g, b, range(4)), pair_bwd[member])
            for n in range(images):
                dy_full[n, b, pl.ds(0, RES)] = pair_rows(out, n)
        bucket_rows = lax.broadcasted_iota(jnp.int32, (NB, C1), 0)

        def image(n):
            scale = row_of(coef_n, which, n, 0)
            offset = row_of(coef_n, which, n, 1)

            def step(i, carry):
                sum_dy, sum_dyv = carry
                here = pl.ds(i * ROWS, ROWS)
                for b in range(2):
                    v = values[n, b, here]
                    dy = dy_full[n, b, here] * slope(v * scale + offset)
                    if not last:
                        dy_full[n, b, here] = dy
                    sum_dy = sum_dy + fold(dy)
                    sum_dyv = sum_dyv + fold(dy * v)
                return sum_dy, sum_dyv

            sum_dy, sum_dyv = lax.fori_loop(0, steps, step, (zero_n, zero_n))
            gain, shift, ca, cb, cd = norm_grad_coefs(
                sum_dy, sum_dyv, gain_n(gain_row), coef_n[which, n, 2], coef_n[which, n, 3], full_pixels
            )
            row = NARROW_NORM_ROW + gain_row
            g_small[row : row + 1, :C1] += gain[0:1, :]
            g_small[row + 1 : row + 2, :C1] += shift[0:1, :]
            if last:
                return

            def finish(i, carry):
                here = pl.ds(i * ROWS, ROWS)
                for b in range(2):
                    v = values[n, b, here]
                    g = dy_full[n, b, here] * ca[0:1, :] + v * cb[0:1, :] + cd[0:1, :]
                    carry = carry + fold(g)
                    store_planes(in_g, n, b, i * ROWS, g)
                return carry

            sums = total(lax.fori_loop(0, steps, finish, zero_n))
            g_small[TIME_NARROW_ROW : TIME_NARROW_ROW + NB, :C1] += jnp.where(
                bucket_rows == bucket(n), sums, 0.0
            )

        each(images, image)

    pair_gradient(in_b, 1)
    back_through(1, h1_full, 1, 2, False)
    pair_gradient(in_a, 0)
    back_through(0, x_full, 0, 0, True)


def main_call(images, *operands):
    n = images
    vm = pltpu.VMEM
    full = (n, 2, RES, HALF, C1)
    planes = (n, 4, RES + 2, HALF, C1)
    wide = HALF_CHANNELS
    square = (n, HALF * HALF, wide)
    scratch = [
        vm((2, 12 * C1, 2 * C1), bf16),
        vm((2, 2 * C1, 12 * C1), bf16),
        vm((9 * C1, wide), bf16),
        vm((C1, 9 * wide), bf16),
        vm((9 * wide, wide), bf16),
        vm((wide, 9 * wide), bf16),
        vm((C1, wide), bf16),
        vm((wide, 4 * wide), bf16),
        vm((HEAD_ROWS, wide), f32),
        vm(full, f32),
        vm(full, f32),
        vm(full, f32),
        vm((n, 2, RES + 2, HALF, C1), f32),
        vm(planes, bf16),
        vm(planes, bf16),
        vm(planes, bf16),
        vm((ROWS * RES, C1), f32),
        vm((n, 3, HALF + 2, HALF, C1), bf16),
        vm((n, 3, HALF + 2, HALF, wide), bf16),
        vm((n, 3, HALF + 2, HALF, wide), bf16),
        vm((n, HALF * HALF, C1), bf16),
        vm((n, HALF * HALF, C1), f32),
        vm(square, f32),
        vm(square, f32),
        vm(square, f32),
        vm(square, bf16),
        vm((n, HALF * HALF, 3 * wide), bf16),
        vm(square, f32),
        vm(square, bf16),
        vm(square, bf16),
        vm(square, bf16),
        vm(square, f32),
        vm(square, bf16),
        vm((n, HALF * HALF, 3 * wide), bf16),
        vm((n, HALF * HALF, C1), f32),
        vm((3, n, 4, 8, C1), f32),
        vm((3, n, 4, 8, wide), f32),
    ]
    whole = pl.BlockSpec(memory_space=pltpu.VMEM)
    return pl.pallas_call(
        main_kernel,
        out_shape=[
            jax.ShapeDtypeStruct(shape, f32)
            for shape in PIECES
        ],
        in_specs=[pl.BlockSpec(memory_space=pltpu.SMEM)] + [whole] * 13,
        out_specs=[whole] * 5,
        scratch_shapes=scratch,
        compiler_params=pltpu.CompilerParams(vmem_limit_bytes=VMEM_LIMIT),
        cost_estimate=pl.CostEstimate(flops=8 * 10**9, bytes_accessed=12 * 10**6, transcendentals=0),
    )(*operands)


def partners(dp_size):
    dp = lax.axis_index("dp")
    sp = lax.axis_index("sp")

    def flip(k):
        unit = 1 << k
        side = (dp // unit) % 2
        return side, (dp + unit * (1 - 2 * side), sp)

    core, near = flip(0), flip(1)
    second = core[0]

    def pick(first, other):
        return first + second * (other - first)

    stages = [
        core,
        (pick(near[0], sp), (pick(near[1][0], dp), pick(sp, 1 - sp))),
        (pick(sp, near[0]), (pick(dp, near[1][0]), pick(1 - sp, sp))),
    ]
    for k in range(2, (dp_size - 1).bit_length()):
        stages.append(flip(k))
    return stages


def greet(stages):
    barrier = pltpu.get_barrier_semaphore()
    for _, other in stages:
        pl.semaphore_signal(barrier, inc=1, device_id=other, device_id_type=MESH)
    pl.semaphore_wait(barrier, len(stages))


def send(source, target, sems, index, other):
    return pltpu.make_async_remote_copy(
        src_ref=source,
        dst_ref=target,
        send_sem=sems.at[0, index],
        recv_sem=sems.at[1, index],
        device_id=other,
        device_id_type=MESH,
    )


def images_kernel(
    dp_size, buckets, features, target, mask, mask_in, x_out, target_out, mask_out, counts_out,
    totals, arrived, sems, local_sems, count_sems,
):
    stages = partners(dp_size)
    dp = lax.axis_index("dp")
    sp = lax.axis_index("sp")
    greet(stages)
    copies = [
        send(source.at[1 - sp], out.at[sp], sems, i, (dp, 1 - sp))
        for i, (source, out) in enumerate(((features, x_out), (target, target_out), (mask, mask_out)))
    ]
    for copy in copies:
        copy.start()
    keeps = [
        pltpu.make_async_copy(source.at[sp], out.at[sp], local_sems.at[i])
        for i, (source, out) in enumerate(((features, x_out), (target, target_out), (mask, mask_out)))
    ]
    for copy in keeps:
        copy.start()
    rows = lax.broadcasted_iota(jnp.int32, (NB, 128), 0)
    counted = jnp.zeros((NB, 128), f32)
    images = mask_in.shape[1]
    for i in range(2 * images):
        pixels = mask_in[i // images, i % images].astype(f32)
        number = jnp.sum(jnp.sum(pixels, axis=0, keepdims=True), axis=1, keepdims=True)
        counted = counted + jnp.where(rows == buckets[i], number, 0.0)
    totals[0] = counted
    for s, (_, other) in enumerate(stages):
        copy = send(totals.at[s], arrived.at[s], count_sems, s, other)
        copy.start()
        copy.wait()
        totals[s + 1] = totals[s] + arrived[s]
    counts_out[...] = totals[len(stages)]
    for copy in keeps + copies:
        copy.wait()


def images_call(dp_size, buckets, features, target, mask):
    stages = (dp_size - 1).bit_length() + 1
    anywhere = pl.BlockSpec(memory_space=pl.ANY)
    whole = pl.BlockSpec(memory_space=pltpu.VMEM)
    shapes = [jax.ShapeDtypeStruct(v.shape, v.dtype) for v in (features, target, mask)]
    return pl.pallas_call(
        functools.partial(images_kernel, dp_size),
        out_shape=shapes + [jax.ShapeDtypeStruct((NB, 128), f32)],
        in_specs=[pl.BlockSpec(memory_space=pltpu.SMEM)] + [anywhere] * 3 + [whole],
        out_specs=[anywhere] * 3 + [whole],
        scratch_shapes=[
            pltpu.VMEM((stages + 1, NB, 128), f32),
            pltpu.VMEM((stages, NB, 128), f32),
            pltpu.SemaphoreType.DMA((2, 3)),
            pltpu.SemaphoreType.DMA((3,)),
            pltpu.SemaphoreType.DMA((2, stages)),
        ],
        compiler_params=pltpu.CompilerParams(collective_id=0, has_side_effects=True),
    )(buckets, features, target, mask, mask)


def chunk_of(rows):
    return next(c for c in (128, 96, 72, 64, 48, 40, 32, 24, 16, 8) if rows % c == 0)


def add_rows(target, base, source, offset, rows):
    size = chunk_of(rows)

    def step(i):
        here = pl.ds(pl.multiple_of(base + i * size, 8), size)
        target[here, :] = target[here, :] + source[pl.ds(pl.multiple_of(offset + i * size, 8), size), :]

    each(rows // size, step)


class Piece:
    def __init__(self, source, arrived, out, sems, stages):
        self.source, self.arrived, self.out, self.sems, self.stages = source, arrived, out, sems, stages
        rows = source.shape[0]
        self.plan = []
        base = 0
        lowest = 0
        for side, other in stages:
            halved = rows % 16 == 0
            rows = rows // 2 if halved else rows
            self.plan.append((side, other, halved, rows, base, lowest))
            lowest = lowest + side * rows if halved else lowest
            base += rows
        self.rows, self.lowest = rows, lowest
        self.copies = {}

    def region(self, s, side):
        halved, rows = self.plan[s][2:4]
        if s == 0:
            ref, base = self.source, 0
        else:
            ref, base = self.arrived, self.plan[s - 1][4]
        return ref, (base + side * rows if halved else base)

    def scatter_start(self, s):
        side, other, halved, rows, base, _ = self.plan[s]
        ref, first = self.region(s, 1 - side)
        copy = send(
            ref.at[pl.ds(pl.multiple_of(first, 8), rows)],
            self.arrived.at[pl.ds(base, rows)],
            self.sems,
            s,
            other,
        )
        copy.start()
        self.copies[s] = copy

    def scatter_end(self, s):
        side, other, halved, rows, base, _ = self.plan[s]
        self.copies[s].wait()
        ref, first = self.region(s, side)
        add_rows(self.arrived, base, ref, first, rows)
        if s + 1 == len(self.stages):
            self.out[pl.ds(pl.multiple_of(self.lowest, 8), rows), :] = self.arrived[base : base + rows, :]

    def gather_start(self, s):
        side, other, halved, rows, base, lowest = self.plan[s]
        if halved:
            here = pl.ds(pl.multiple_of(lowest + side * rows, 8), rows)
            copy = send(self.out.at[here], self.out.at[here], self.sems, len(self.stages) + s, other)
            copy.start()
            self.copies[len(self.stages) + s] = copy

    def gather_end(self, s):
        if self.plan[s][2]:
            self.copies[len(self.stages) + s].wait()

    def step(self, t):
        count = len(self.stages)
        if 0 < t <= count:
            self.scatter_end(t - 1)
        elif t > count:
            self.gather_end(2 * count - t)
        if t < count:
            self.scatter_start(t)
        elif t < 2 * count:
            self.gather_start(2 * count - 1 - t)


def arrived_rows(rows, stages):
    needed = 0
    for _ in range(stages):
        rows = rows // 2 if rows % 16 == 0 else rows
        needed += rows
    return needed


def sum_kernel(dp_size, *refs):
    count = len(PIECES)
    sources, outs, arrived, sems = (refs[i * count : (i + 1) * count] for i in range(4))
    stages = partners(dp_size)
    greet(stages)
    pieces = [Piece(*parts, stages) for parts in zip(sources, arrived, outs, sems)]
    last = 2 * len(stages)
    for t in range(last + count):
        for i, piece in enumerate(pieces):
            if 0 <= t - i <= last:
                piece.step(t - i)


def sum_call(dp_size, partial):
    stages = (dp_size - 1).bit_length() + 1
    whole = pl.BlockSpec(memory_space=pltpu.VMEM)
    return pl.pallas_call(
        functools.partial(sum_kernel, dp_size),
        out_shape=[jax.ShapeDtypeStruct(shape, f32) for shape in PIECES],
        in_specs=[whole] * len(PIECES),
        out_specs=[whole] * len(PIECES),
        scratch_shapes=[pltpu.VMEM((arrived_rows(rows, stages), lanes), f32) for rows, lanes in PIECES]
        + [pltpu.SemaphoreType.DMA((2, 2 * stages)) for _ in PIECES],
        compiler_params=pltpu.CompilerParams(
            collective_id=1, has_side_effects=True, vmem_limit_bytes=VMEM_LIMIT
        ),
    )(*partial)


def adamw(weight, grad, first, second, rate):
    first = beta_one * first + (1.0 - beta_one) * grad
    second = beta_two * second + (1.0 - beta_two) * grad * grad
    scale = rate / (1.0 - beta_one**STEP)
    root = jnp.sqrt(second * (1.0 / (1.0 - beta_two**STEP))) + adam_epsilon
    return weight * (1.0 - rate * decay_rate) - scale * first / root, first, second


def update_kernel(*refs):
    g_attn, g_wide, g_down, g_pair, g_small = refs[:5]
    members = [refs[5 + 3 * i : 8 + 3 * i] for i in range(9)]
    outs = [refs[32 + 3 * i : 35 + 3 * i] for i in range(9)]
    loss_out = refs[59]

    def blocks(member, grad, block_rows, base, count):
        size = 64

        def step(i):
            block = i // (block_rows // size)
            row = (i % (block_rows // size)) * size
            here = pl.ds(pl.multiple_of(block * block_rows + row, 8), size)
            columns = members[member][0].shape[1] // 128
            for c in range(columns):
                lanes = slice(c * 128, (c + 1) * 128)
                g = grad[pl.ds(pl.multiple_of(base + (block * columns + c) * block_rows + row, 8), size), :]
                w, m, v = (ref[here, lanes] for ref in members[member])
                for out, value in zip(outs[member], adamw(w, g, m, v, rate_matrix)):
                    out[here, lanes] = value

        each(count * block_rows // size, step)

    def single(member, index, grad, rate):
        w, m, v = (ref[index] for ref in members[member])
        for out, value in zip(outs[member], adamw(w, grad, m, v, rate)):
            out[index] = value

    blocks(0, g_pair, C1, 0, 18)
    blocks(1, g_down, C1, 0, 9)
    blocks(2, g_wide, HALF_CHANNELS, 0, 9)
    blocks(3, g_down, C1, SKIP_ROW, 1)
    blocks(4, g_attn, HALF_CHANNELS, 0, 1)
    for tap in range(9):
        single(5, (tap,), g_small[tap * 8 : tap * 8 + 3, :], rate_matrix)
    single(6, (slice(None), slice(None)), g_small[NARROW_NORM_ROW : NARROW_NORM_ROW + 6, :C1], rate_vector)
    single(7, (slice(None), slice(None)), g_small[WIDE_NORM_ROW : WIDE_NORM_ROW + 6, :], rate_vector)
    single(
        8, (slice(None), slice(0, C1)), g_small[TIME_NARROW_ROW : TIME_NARROW_ROW + NB, :C1], rate_vector
    )
    single(
        8, (slice(None), slice(C1, None)), g_small[TIME_WIDE_ROW : TIME_WIDE_ROW + NB, :], rate_vector
    )
    loss_out[...] = g_small[LOSS_ROW : LOSS_ROW + 1, :128]


def update_call(grads, members):
    whole = pl.BlockSpec(memory_space=pltpu.VMEM)
    flat = [v for member in members for v in member]
    return pl.pallas_call(
        update_kernel,
        out_shape=[jax.ShapeDtypeStruct(v.shape, f32) for v in flat]
        + [jax.ShapeDtypeStruct((1, 128), f32)],
        in_specs=[whole] * (5 + len(flat)),
        out_specs=[whole] * (len(flat) + 1),
        compiler_params=pltpu.CompilerParams(vmem_limit_bytes=VMEM_LIMIT),
    )(*grads, *flat)


def on_device(
    features,
    target,
    pixel_mask,
    buckets,
    conv_pair,
    down_conv,
    conv_wide,
    skip_proj,
    attn_proj,
    head_conv,
    norm_narrow,
    norm_wide,
    time_bias,
    conv_pair_mom,
    down_conv_mom,
    conv_wide_mom,
    skip_proj_mom,
    attn_proj_mom,
    head_conv_mom,
    norm_narrow_mom,
    norm_wide_mom,
    time_bias_mom,
    conv_pair_sq,
    down_conv_sq,
    conv_wide_sq,
    skip_proj_sq,
    attn_proj_sq,
    head_conv_sq,
    norm_narrow_sq,
    norm_wide_sq,
    time_bias_sq,
):
    dp_size = lax.axis_size("dp")
    images = features.shape[0] // 2

    def halves(tensor):
        return tensor.reshape((2, images) + tensor.shape[1:])

    def flat(tensor):
        return tensor.reshape(-1, tensor.shape[-1])

    def head_rows(tensor):
        return jnp.transpose(tensor, (0, 1, 3, 2)).reshape(9, 3, HALF_CHANNELS)

    images_in = images_call(
        dp_size,
        buckets,
        halves(features),
        halves(jnp.transpose(target, (0, 3, 1, 2))),
        halves(pixel_mask),
    )
    params = (
        flat(conv_pair),
        flat(down_conv),
        flat(conv_wide),
        skip_proj,
        attn_proj,
        head_rows(head_conv),
        norm_narrow,
        norm_wide,
        time_bias,
    )
    firsts = (
        flat(conv_pair_mom),
        flat(down_conv_mom),
        flat(conv_wide_mom),
        skip_proj_mom,
        attn_proj_mom,
        head_rows(head_conv_mom),
        norm_narrow_mom,
        norm_wide_mom,
        time_bias_mom,
    )
    seconds = (
        flat(conv_pair_sq),
        flat(down_conv_sq),
        flat(conv_wide_sq),
        skip_proj_sq,
        attn_proj_sq,
        head_rows(head_conv_sq),
        norm_narrow_sq,
        norm_wide_sq,
        time_bias_sq,
    )
    partial = main_call(images, buckets, *images_in, *params)
    summed = sum_call(dp_size, partial)
    results = update_call(summed, list(zip(params, firsts, seconds)))
    shaped = []
    for member, like in enumerate((conv_pair, down_conv, conv_wide, skip_proj, attn_proj)):
        shaped.extend(v.reshape(like.shape) for v in results[3 * member : 3 * member + 3])
    for v in results[15:18]:
        shaped.append(jnp.transpose(v.reshape(3, 3, 3, HALF_CHANNELS), (0, 1, 3, 2)))
    shaped.extend(results[18:27])
    return (results[27][0, 0], images_in[3][:, 0]) + tuple(shaped)


def solution(mesh):
    placed = (
        P("dp", "sp", None, None),
        P("dp", "sp", None, None),
        P("dp", "sp", None),
        P("dp"),
        P(),
        P(),
        P(),
        P(),
        P(),
        P(),
        P(),
        P(),
        P(),
        P(),
        P(),
        P(),
        P(),
        P(),
        P(),
        P(),
        P(),
        P(),
        P(),
        P(),
        P(),
        P(),
        P(),
        P(),
        P(),
        P(),
        P(),
    )
    return jax.shard_map(
        on_device,
        mesh=mesh,
        in_specs=placed,
        out_specs=(
            P(),
            P(),
            P(),
            P(),
            P(),
            P(),
            P(),
            P(),
            P(),
            P(),
            P(),
            P(),
            P(),
            P(),
            P(),
            P(),
            P(),
            P(),
            P(),
            P(),
            P(),
            P(),
            P(),
            P(),
            P(),
            P(),
            P(),
            P(),
            P(),
        ),
        check_vma=False,
    )
```

```python
import functools

import jax
import jax.numpy as jnp
from jax import lax
from jax.experimental import pallas as pl
from jax.experimental.pallas import tpu as pltpu
from jax.sharding import PartitionSpec as P

C1 = 128
HALF_CHANNELS = 256
GROUPS = 32
RES = 32
HALF = 16
NB = 8
STEP = 10
MESH = pl.DeviceIdType.MESH
VMEM_LIMIT = 62 * 1024 * 1024

epsilon = 1e-05
root_half = 0.7071067811865476
beta_one = 0.9
beta_two = 0.999
adam_epsilon = 1e-08
decay_rate = 0.1
rate_matrix = 0.03
rate_vector = 0.5
logit_scale = HALF_CHANNELS ** (-0.5)
ROWS = 8

bf16 = jnp.bfloat16
f32 = jnp.float32

EVEN, ODD, ODD_LEFT, EVEN_RIGHT = 0, 1, 2, 3
TAPS = ((ODD_LEFT, EVEN, ODD), (EVEN, ODD, EVEN_RIGHT))


def rounded(v):
    return v.astype(bf16).astype(f32)


def silu(t):
    return t * jax.nn.sigmoid(t)


def slope(t):
    s = jax.nn.sigmoid(t)
    return s * (1.0 + t * (1.0 - s))


def mm(a, b):
    return lax.dot_general(a, b, (((1,), (0,)), ((), ())), preferred_element_type=f32)


def mm_nt(a, b):
    return lax.dot_general(a, b, (((1,), (1,)), ((), ())), preferred_element_type=f32)


def mm_tn(a, b):
    return lax.dot_general(a, b, (((0,), (0,)), ((), ())), preferred_element_type=f32)


def fold(v):
    return jnp.sum(v.reshape(-1, 8, v.shape[-1]), axis=0)


def total(v):
    return jnp.broadcast_to(jnp.sum(v, axis=0, keepdims=True), v.shape)


def group_sum(v, size):
    lanes = v.shape[-1]
    lane = lax.broadcasted_iota(jnp.int32, v.shape, 1)
    step = 1
    while step < size:
        other = jnp.where(
            (lane & step) == 0, pltpu.roll(v, lanes - step, 1), pltpu.roll(v, step, 1)
        )
        v = v + other
        step *= 2
    return v


def norm_coefs(sums, squares, gain, shift, pixels):
    size = sums.shape[-1] // GROUPS
    count = pixels * size
    mean = group_sum(total(sums), size) / count
    power = group_sum(total(squares), size) / count
    inv = lax.rsqrt(power - mean * mean + epsilon)
    scale = inv * gain
    return scale, shift - mean * scale, mean, inv


def norm_grad_coefs(sum_dy, sum_dyv, gain, mean, inv, pixels):
    size = sum_dy.shape[-1] // GROUPS
    count = pixels * size
    first = total(sum_dy)
    second = (total(sum_dyv) - mean * first) * inv
    one = group_sum(first * gain, size) / count
    two = group_sum(second * gain, size) / count
    b = -inv * inv * two
    return second, first, inv * gain, b, -inv * one - mean * b


def shift_cols(v, step):
    col = lax.broadcasted_iota(jnp.int32, v.shape, 1)
    if step == 1:
        return jnp.where(col == 0, 0.0, pltpu.roll(v, 1, 1))
    return jnp.where(col == HALF - 1, 0.0, pltpu.roll(v, HALF - 1, 1))


def store_planes(planes, n, b, r0, v):
    rows = v.shape[0]
    v = v.astype(bf16).astype(f32)
    for plane, value in (
        (EVEN + b, v),
        (ODD_LEFT if b == 1 else EVEN_RIGHT, shift_cols(v, 1 if b == 1 else -1)),
    ):
        planes[n, plane, pl.ds(r0 + 1, rows)] = value.astype(bf16)


def store_shifted(cells, n, r0, v):
    rows = v.shape[0]
    v = v.astype(bf16).astype(f32)
    for tap, value in ((0, shift_cols(v, 1)), (1, v), (2, shift_cols(v, -1))):
        cells[n, tap, pl.ds(r0 + 1, rows)] = value.astype(bf16)


def plane_block(planes, tap, jj):
    return planes[:, tap, pl.ds(jj, HALF, stride=2)].reshape(-1, planes.shape[-1])


def pair_input(planes, b, jjs):
    return jnp.concatenate([plane_block(planes, tap, jj) for jj in jjs for tap in TAPS[b]], axis=1)


def cell_input(cells, dys):
    return jnp.concatenate(
        [
            cells[:, tap, dy : dy + HALF].reshape(-1, cells.shape[-1])
            for dy in dys
            for tap in range(3)
        ],
        axis=1,
    )


def each(count, body):
    def step(i, carry):
        body(i)
        return carry

    lax.fori_loop(0, count, step, 0)


def prepare_weights(pair, down, wide, skip, attn, head, pair_fwd, pair_bwd, down_fwd, down_bwd, wide_fwd, wide_bwd, skip_low, attn_low, head_low):
    nothing = jnp.zeros((C1, C1), bf16)
    for member in range(2):
        for jj in range(4):
            for k in range(3):
                block = (jj * 3 + k) * C1
                for a in range(2):
                    dy = jj - a
                    inside = 0 <= dy < 3
                    row = (member * 9 + dy * 3 + k) * C1
                    back = (member * 9 + (2 - dy) * 3 + (2 - k)) * C1
                    pair_fwd[member, block : block + C1, a * C1 : a * C1 + C1] = (
                        pair[row : row + C1, :].astype(bf16) if inside else nothing
                    )
                    pair_bwd[member, a * C1 : a * C1 + C1, block : block + C1] = (
                        pair[back : back + C1, :].astype(bf16) if inside else nothing
                    )
    wide_channels = HALF_CHANNELS
    for tap in range(9):
        low = down[tap * C1 : tap * C1 + C1, :].astype(bf16)
        down_fwd[tap * C1 : tap * C1 + C1, :] = low
        down_bwd[:, (8 - tap) * wide_channels : (9 - tap) * wide_channels] = low
        low = wide[tap * wide_channels : (tap + 1) * wide_channels, :].astype(bf16)
        wide_fwd[tap * wide_channels : (tap + 1) * wide_channels, :] = low
        wide_bwd[:, (8 - tap) * wide_channels : (9 - tap) * wide_channels] = low
    skip_low[...] = skip[...].astype(bf16)
    attn_low[...] = attn[...].astype(bf16)
    head_low[...] = jnp.zeros(head_low.shape, f32)
    for tap in range(9):
        head_low[tap * 8 : tap * 8 + 3, :] = rounded(head[tap])


def split_three(v):
    high = v.astype(bf16)
    rest = v - high.astype(f32)
    middle = rest.astype(bf16)
    return high, middle, (rest - middle.astype(f32)).astype(bf16)


def lane_shift(v, step):
    lane = lax.broadcasted_iota(jnp.int32, v.shape, 1)
    j = lane & (HALF - 1)
    if step == 1:
        keep = j < HALF - 1
    elif step == -1:
        keep = j > 0
    elif step == HALF:
        keep = lane < HALF * (HALF - 1)
    else:
        keep = lane >= HALF
    return jnp.where(keep, pltpu.roll(v, (-step) % v.shape[-1], 1), 0.0)


def head_forward(table):
    cols = [
        [
            lane_shift(table[dy][0], -1) + table[dy][1] + table[dy][2],
            table[dy][0] + table[dy][1] + lane_shift(table[dy][2], 1),
        ]
        for dy in range(3)
    ]
    return [
        [
            lane_shift(cols[0][b], -HALF) + cols[1][b] + cols[2][b]
            if a == 0
            else cols[0][b] + cols[1][b] + lane_shift(cols[2][b], HALF)
            for b in range(2)
        ]
        for a in range(2)
    ]


def head_backward(grad):
    rows = [
        [
            lane_shift(grad[0][b], HALF) + grad[1][b],
            grad[0][b] + grad[1][b],
            grad[0][b] + lane_shift(grad[1][b], -HALF),
        ]
        for b in range(2)
    ]
    return [
        [
            lane_shift(rows[0][dy], 1) + rows[1][dy],
            rows[0][dy] + rows[1][dy],
            rows[0][dy] + lane_shift(rows[1][dy], -1),
        ]
        for dy in range(3)
    ]


def keep_columns(ref, row, v):
    for c in range(v.shape[1] // 128):
        ref[row + c * v.shape[0] : row + (c + 1) * v.shape[0], :] = v[:, c * 128 : (c + 1) * 128]


HEAD_ROWS = 72
WIDE_NORM_ROW = 72
LOSS_ROW = 78
NARROW_NORM_ROW = 80
TIME_WIDE_ROW = 88
TIME_NARROW_ROW = 96
SMALL_ROWS = 128
SKIP_ROW = 18 * C1
PIECES = (
    (8 * HALF_CHANNELS, 128),
    (18 * HALF_CHANNELS, 128),
    (20 * C1, 128),
    (18 * C1, 128),
    (SMALL_ROWS, HALF_CHANNELS),
)


def main_kernel(
    dp_size,
    buckets, features, target_rows, mask_rows, mask_local, pair_all, down_all, wide_all, skip_all, attn_all, head_all,
    gains_narrow, gains_wide, time_bias,
    sum_attn, sum_wide, sum_down, sum_pair, sum_small, counts,
    x_in, target, mask, pair, down, wide, skip, attn, head, g_attn, g_wide, g_down, g_pair, g_small,
    arrived_attn, arrived_wide, arrived_down, arrived_pair, arrived_small,
    sems_attn, sems_wide, sems_down, sems_pair, sems_small,
    totals, arrived_totals, image_sems, local_sems, count_sems, weight_sems,
    pair_fwd, pair_bwd, down_fwd, down_bwd, wide_fwd, wide_bwd, skip_low, attn_low, head_low,
    x_full, h1_full, xs_full, dy_full, in_a, in_b, in_g, flat,
    cells_c, cells_d, cells_g, fs_low, dfs, h3, x2, x3, n5, qkv, probs, probs_low, att, a6, dwide, dout, dqkv, dnarrow,
    coef_n, coef_w,
):
    loads = [
        pltpu.make_async_copy(source, ref, weight_sems.at[i])
        for i, (source, ref) in enumerate(
            (
                (pair_all, pair),
                (down_all, down),
                (wide_all, wide),
                (skip_all, skip),
                (attn_all, attn),
                (head_all, head),
            )
        )
    ]
    stages = partners(dp_size)
    greet(stages)
    here = (lax.axis_index("dp"), 1 - lax.axis_index("sp"))
    moved = ((features, x_in), (target_rows, target), (mask_rows, mask))
    side = lax.axis_index("sp")
    arrivals = [
        send(source.at[1 - side], out.at[side], image_sems, i, here) for i, (source, out) in enumerate(moved)
    ]
    for copy in arrivals:
        copy.start()
    keeps = [
        pltpu.make_async_copy(source.at[side], out.at[side], local_sems.at[i])
        for i, (source, out) in enumerate(moved)
    ]
    for copy in keeps + loads:
        copy.start()
    images = x_in.shape[1]
    position = lax.axis_index("sp")
    steps = RES // ROWS
    full_pixels = RES * RES
    half_pixels = HALF * HALF
    zero_n = jnp.zeros((8, C1), f32)
    zero_w = jnp.zeros((8, HALF_CHANNELS), f32)

    def bucket(n):
        return buckets[position * images + n]

    def gain_n(row):
        return jnp.broadcast_to(gains_narrow[row : row + 1, :], (8, C1))

    def gain_w(row):
        return jnp.broadcast_to(gains_wide[row : row + 1, :], (8, HALF_CHANNELS))

    def keep_coefs(ref, which, n, values):
        for kind in range(4):
            ref[which, n, kind] = values[kind]

    def row_of(ref, which, n, kind):
        return ref[which, n, kind, 0:1, :]

    counting = Counting(buckets, mask_local, totals, arrived_totals, count_sems, stages)
    counting.step()
    for copy in loads:
        copy.wait()
    prepare_weights(pair, down, wide, skip, attn, head, pair_fwd, pair_bwd, down_fwd, down_bwd, wide_fwd, wide_bwd, skip_low, attn_low, head_low)
    g_small[...] = jnp.zeros(g_small.shape, f32)
    for planes in (in_a, in_b, in_g):
        edge = jnp.zeros((images, 4, HALF, C1), bf16)
        planes[:, :, 0] = edge
        planes[:, :, RES + 1] = edge
    for cells in (cells_c, cells_d, cells_g):
        edge = jnp.zeros((images, 3, HALF, cells.shape[-1]), bf16)
        cells[:, :, 0] = edge
        cells[:, :, HALF + 1] = edge

    for copy in keeps + arrivals:
        copy.wait()
    counting.step()

    def load_image(n):
        def step(i, carry):
            sums, squares = carry
            half = i // 2
            v = x_in[half, n, pl.ds((i % 2) * ROWS, ROWS)].astype(f32)
            flat[...] = v.reshape(ROWS * RES, C1)
            for b in range(2):
                w = flat[pl.ds(b, ROWS * HALF, stride=2), :].reshape(ROWS, HALF, C1)
                x_full[n, b, pl.ds(i * ROWS, ROWS)] = w
                sums = sums + fold(w)
                squares = squares + fold(w * w)
            return sums, squares

        sums, squares = lax.fori_loop(0, steps, step, (zero_n, zero_n))
        keep_coefs(coef_n, 0, n, norm_coefs(sums, squares, gain_n(0), gain_n(1), full_pixels))

    each(images, load_image)

    def activate(values, planes, which):
        def image(n):
            scale = row_of(coef_n, which, n, 0)
            offset = row_of(coef_n, which, n, 1)

            def step(i):
                for b in range(2):
                    v = values[n, b, pl.ds(i * ROWS, ROWS)]
                    store_planes(planes, n, b, i * ROWS, silu(v * scale + offset))

            each(steps, step)

        each(images, image)

    def pair_rows(result, n):
        part = result[n * half_pixels : (n + 1) * half_pixels].reshape(HALF, 1, HALF, 2 * C1)
        return jnp.concatenate([part[..., :C1], part[..., C1:]], axis=1).reshape(RES, HALF, C1)

    activate(x_full, in_a, 0)
    counting.step()
    for b in range(2):
        out = mm(pair_input(in_a, b, range(4)), pair_fwd[0])
        for n in range(images):
            h1_full[n, b] = pair_rows(out, n)

    def first_hidden(n):
        bias = time_bias[pl.ds(bucket(n), 1), :][:, :C1]

        def step(i, carry):
            sums, squares = carry
            for b in range(2):
                v = h1_full[n, b, pl.ds(i * ROWS, ROWS)] + bias
                h1_full[n, b, pl.ds(i * ROWS, ROWS)] = v
                sums = sums + fold(v)
                squares = squares + fold(v * v)
            return sums, squares

        sums, squares = lax.fori_loop(0, steps, step, (zero_n, zero_n))
        keep_coefs(coef_n, 1, n, norm_coefs(sums, squares, gain_n(2), gain_n(3), full_pixels))

    each(images, first_hidden)
    activate(h1_full, in_b, 1)
    counting.step()
    for b in range(2):
        out = mm(pair_input(in_b, b, range(4)), pair_fwd[1])
        for n in range(images):
            xs_full[n, b] = pair_rows(out, n)

    def first_out(n):
        def step(i, carry):
            sums, squares = carry
            for b in range(2):
                v = xs_full[n, b, pl.ds(i * ROWS, ROWS)]
                v = rounded((x_full[n, b, pl.ds(i * ROWS, ROWS)] + v) * root_half)
                xs_full[n, b, pl.ds(i * ROWS, ROWS)] = v
                sums = sums + fold(v)
                squares = squares + fold(v * v)
            return sums, squares

        sums, squares = lax.fori_loop(0, steps, step, (zero_n, zero_n))
        keep_coefs(coef_n, 2, n, norm_coefs(sums, squares, gain_n(4), gain_n(5), full_pixels))

    each(images, first_out)

    counting.step()

    def fir_down_image(n):
        scale = row_of(coef_n, 2, n, 0)
        offset = row_of(coef_n, 2, n, 1)
        for b in range(2):
            dy_full[n, b, 0] = jnp.zeros((HALF, C1), f32)
            dy_full[n, b, RES + 1] = jnp.zeros((HALF, C1), f32)

        def act_step(i):
            for b in range(2):
                v = xs_full[n, b, pl.ds(i * ROWS, ROWS)]
                dy_full[n, b, pl.ds(i * ROWS + 1, ROWS)] = silu(v * scale + offset)

        each(steps, act_step)

        def columns(rows):
            even, odd = rows
            return (
                0.125 * (shift_cols(odd, 1) + shift_cols(even, -1)) + 0.375 * (even + odd)
            )

        def taps(ref, b, r0, size):
            return [ref[n, b, pl.ds(r0 + t, size, stride=2)] for t in range(4)]

        def down_step(i):
            size = HALF // 2
            rows = []
            for b in range(2):
                t = taps(dy_full, b, 2 * size * i, size)
                rows.append(0.125 * (t[0] + t[3]) + 0.375 * (t[1] + t[2]))
            store_shifted(cells_c, n, i * size, columns(rows))

        each(2, down_step)
        for b in range(2):
            dy_full[n, b, pl.ds(1, RES)] = xs_full[n, b]

        def skip_step(i):
            size = HALF // 2
            rows = []
            for b in range(2):
                t = taps(dy_full, b, 2 * size * i, size)
                rows.append(0.125 * (t[0] + t[3]) + 0.375 * (t[1] + t[2]))
            fs_low[n, pl.ds(i * size * HALF, size * HALF)] = (
                columns(rows).reshape(size * HALF, C1).astype(bf16)
            )

        each(2, skip_step)

    each(images, fir_down_image)

    def wide_stats(v, which, n, row):
        values = norm_coefs(fold(v), fold(v * v), gain_w(row), gain_w(row + 1), half_pixels)
        keep_coefs(coef_w, which, n, values)
        return values[0][0:1, :], values[1][0:1, :]

    out = mm(cell_input(cells_c, range(3)), down_fwd[...])
    for n in range(images):
        v = out[n * half_pixels : (n + 1) * half_pixels] + time_bias[pl.ds(bucket(n), 1), :][:, C1:]
        h3[n] = v
        scale, offset = wide_stats(v, 0, n, 0)
        store_shifted(cells_d, n, 0, silu(v * scale + offset).reshape(HALF, HALF, HALF_CHANNELS))
    out = mm(cell_input(cells_d, range(3)), wide_fwd[...])
    out = out + mm(fs_low[...].reshape(-1, C1), skip_low[...])
    for n in range(images):
        v = out[n * half_pixels : (n + 1) * half_pixels] * root_half
        x2[n] = v
        scale, offset = wide_stats(v, 1, n, 2)
        n5[n] = (v * scale + offset).astype(bf16)
        qkv[n] = mm(n5[n], attn_low[:, : 3 * HALF_CHANNELS]).astype(bf16)
        q = qkv[n, :, :HALF_CHANNELS]
        k = qkv[n, :, HALF_CHANNELS : 2 * HALF_CHANNELS]
        w = qkv[n, :, 2 * HALF_CHANNELS :]
        logits = mm_nt(q, k) * logit_scale
        powers = jnp.exp(logits - jnp.max(logits, axis=1, keepdims=True))
        weights = powers / jnp.sum(powers, axis=1, keepdims=True)
        probs[n] = weights
        probs_low[n] = weights.astype(bf16)
        att[n] = mm(probs_low[n], w).astype(bf16)
        v = (v + mm(att[n], attn_low[:, 3 * HALF_CHANNELS :])) * root_half
        x3[n] = v
        scale, offset = wide_stats(v, 2, n, 4)
        a6[n] = silu(v * scale + offset).astype(bf16)

    counting.finish(counts)

    lane = lax.broadcasted_iota(jnp.int32, (RES, 2 * half_pixels), 1)
    source = lax.broadcasted_iota(jnp.int32, (RES, 2 * half_pixels), 0)
    picks = (source == 2 * (lane & (HALF - 1)) + (lane >> 8)).astype(bf16)
    row_lane = (lax.broadcasted_iota(jnp.int32, (HALF, 2 * half_pixels), 1) & (half_pixels - 1)) >> 4
    row_source = lax.broadcasted_iota(jnp.int32, (HALF, 2 * half_pixels), 0)
    component = lax.broadcasted_iota(jnp.int32, (8, half_pixels), 0)

    def spread(halves):
        moved = [mm(half, picks) for half in halves]
        rows = []
        for a in range(2):
            picked = sum(
                jnp.where(2 * row_lane + a == row_source + HALF * h, moved[h], 0.0)
                for h in range(2)
            )
            row = jnp.sum(picked, axis=0, keepdims=True)
            rows.append([row[:, :half_pixels], row[:, half_pixels:]])
        return rows

    loss = jnp.zeros((1, half_pixels), f32)
    head_grad = jnp.zeros((HEAD_ROWS, HALF_CHANNELS), f32)
    for n in range(images):
        moved = mm_nt(head_low[...].astype(bf16), a6[n])
        pred = head_forward(
            [[moved[(dy * 3 + dx) * 8 : (dy * 3 + dx) * 8 + 8] for dx in range(3)] for dy in range(3)]
        )
        wanted = [spread([target[h, n, c] for h in range(2)]) for c in range(3)]
        counted = spread([mask[h, n].astype(f32).astype(bf16) for h in range(2)])
        per_image = 1.0 / counts[pl.ds(bucket(n), 1), :]
        per_image = jnp.concatenate([per_image, per_image], axis=1)
        grad_pred = [[None, None], [None, None]]
        for a in range(2):
            for b in range(2):
                goal = jnp.zeros((8, half_pixels), f32)
                for c in range(3):
                    goal = jnp.where(component == c, wanted[c][a][b], goal)
                error = pred[a][b] - goal
                weight = counted[a][b] * per_image
                loss = loss + weight * jnp.sum(error * error, axis=0, keepdims=True)
                grad_pred[a][b] = rounded(2.0 * error * weight)
        table = head_backward(grad_pred)
        table = jnp.concatenate([table[dy][dx] for dy in range(3) for dx in range(3)], axis=0)
        parts = split_three(table)
        for part in parts:
            head_grad = head_grad + mm(part, a6[n])
        head_rows = head_low[...].astype(bf16)
        grad = sum(mm_tn(part, head_rows) for part in parts)
        v = x3[n]
        values = [coef_w[2, n, kind] for kind in range(4)]
        dy = rounded(grad) * slope(v * values[0][0:1, :] + values[1][0:1, :])
        gain, shift, ca, cb, cd = norm_grad_coefs(
            fold(dy), fold(dy * v), gain_w(4), values[2], values[3], half_pixels
        )
        g_small[WIDE_NORM_ROW + 4 : WIDE_NORM_ROW + 5, :] += gain[0:1, :]
        g_small[WIDE_NORM_ROW + 5 : WIDE_NORM_ROW + 6, :] += shift[0:1, :]
        grad_third = dy * ca[0:1, :] + v * cb[0:1, :] + cd[0:1, :]
        dwide[n] = grad_third
    g_small[0:HEAD_ROWS, :] = head_grad
    g_small[LOSS_ROW : LOSS_ROW + 1, :] = jnp.broadcast_to(
        jnp.sum(loss, axis=1, keepdims=True), (1, HALF_CHANNELS)
    )

    for n in range(images):
        grad_attn = (dwide[n] * root_half).astype(bf16)
        dout[n] = grad_attn
        grad_att = mm_nt(grad_attn, attn_low[:, 3 * HALF_CHANNELS :]).astype(bf16)
        q = qkv[n, :, :HALF_CHANNELS]
        k = qkv[n, :, HALF_CHANNELS : 2 * HALF_CHANNELS]
        w = qkv[n, :, 2 * HALF_CHANNELS :]
        grad_probs = mm_nt(grad_att, w)
        weights = probs[n]
        inner = jnp.sum(weights * grad_probs, axis=1, keepdims=True)
        grad_scores = (weights * (grad_probs - inner)).astype(bf16)
        dqkv[n, :, :HALF_CHANNELS] = (mm(grad_scores, k) * logit_scale).astype(bf16)
        dqkv[n, :, HALF_CHANNELS : 2 * HALF_CHANNELS] = (mm_tn(grad_scores, q) * logit_scale).astype(bf16)
        dqkv[n, :, 2 * HALF_CHANNELS :] = mm_tn(probs_low[n], grad_att).astype(bf16)
    keep_columns(
        g_attn, 0, mm_tn(n5[...].reshape(-1, HALF_CHANNELS), dqkv[...].reshape(-1, 3 * HALF_CHANNELS))
    )
    keep_columns(
        g_attn,
        6 * HALF_CHANNELS,
        mm_tn(att[...].reshape(-1, HALF_CHANNELS), dout[...].reshape(-1, HALF_CHANNELS)),
    )
    for n in range(images):
        dy = mm_nt(dqkv[n], attn_low[:, : 3 * HALF_CHANNELS])
        v = x2[n]
        gain, shift, ca, cb, cd = norm_grad_coefs(
            fold(dy), fold(dy * v), gain_w(2), coef_w[1, n, 2], coef_w[1, n, 3], half_pixels
        )
        g_small[WIDE_NORM_ROW + 2 : WIDE_NORM_ROW + 3, :] += gain[0:1, :]
        g_small[WIDE_NORM_ROW + 3 : WIDE_NORM_ROW + 4, :] += shift[0:1, :]
        grad = dy * ca[0:1, :] + v * cb[0:1, :] + cd[0:1, :] + dwide[n] * root_half
        store_shifted(cells_g, n, 0, (grad * root_half).reshape(HALF, HALF, HALF_CHANNELS))

    center = cells_g[:, 1, 1 : HALF + 1].reshape(-1, HALF_CHANNELS)
    for dy in range(3):
        product = mm_tn(cell_input(cells_d, [dy]), center)
        for k in range(3):
            keep_columns(
                g_wide,
                (dy * 3 + k) * 2 * HALF_CHANNELS,
                product[k * HALF_CHANNELS : (k + 1) * HALF_CHANNELS],
            )
    keep_columns(g_down, SKIP_ROW, mm_tn(fs_low[...].reshape(-1, C1), center))
    dfs[...] = mm_nt(center, skip_low[...]).reshape(dfs.shape)
    out = mm_nt(cell_input(cells_g, range(3)), wide_bwd[...])
    bucket_rows = lax.broadcasted_iota(jnp.int32, (NB, HALF_CHANNELS), 0)
    time_wide = jnp.zeros((NB, HALF_CHANNELS), f32)
    for n in range(images):
        v = h3[n]
        dy = out[n * half_pixels : (n + 1) * half_pixels] * slope(
            v * row_of(coef_w, 0, n, 0) + row_of(coef_w, 0, n, 1)
        )
        gain, shift, ca, cb, cd = norm_grad_coefs(
            fold(dy), fold(dy * v), gain_w(0), coef_w[0, n, 2], coef_w[0, n, 3], half_pixels
        )
        g_small[WIDE_NORM_ROW : WIDE_NORM_ROW + 1, :] += gain[0:1, :]
        g_small[WIDE_NORM_ROW + 1 : WIDE_NORM_ROW + 2, :] += shift[0:1, :]
        grad = dy * ca[0:1, :] + v * cb[0:1, :] + cd[0:1, :]
        time_wide = time_wide + jnp.where(bucket_rows == bucket(n), total(fold(grad)), 0.0)
        store_shifted(cells_g, n, 0, grad.reshape(HALF, HALF, HALF_CHANNELS))
    g_small[TIME_WIDE_ROW : TIME_WIDE_ROW + NB, :] = time_wide

    center = cells_g[:, 1, 1 : HALF + 1].reshape(-1, HALF_CHANNELS)
    for dy in range(3):
        product = mm_tn(cell_input(cells_c, [dy]), center)
        for k in range(3):
            keep_columns(g_down, (dy * 3 + k) * 2 * C1, product[k * C1 : (k + 1) * C1])
    dnarrow[...] = mm_nt(cell_input(cells_g, range(3)), down_bwd[...]).reshape(dnarrow.shape)

    def up_parts(ref, n, i, size):
        here = pl.ds(i * size * HALF, size * HALF)
        g = ref[n, here].reshape(size, HALF, C1)
        lane_rows = lax.broadcasted_iota(jnp.int32, g.shape, 0) + i * size
        above = ref[n, pl.ds(jnp.maximum(i * size - 1, 0) * HALF, HALF)].reshape(1, HALF, C1)
        below = ref[n, pl.ds(jnp.minimum((i + 1) * size, HALF - 1) * HALF, HALF)].reshape(1, HALF, C1)
        above = jnp.where(lane_rows == 0, 0.0, jnp.concatenate([above, g[:-1]], axis=0))
        below = jnp.where(lane_rows == HALF - 1, 0.0, jnp.concatenate([g[1:], below], axis=0))
        result = []
        for rows in (0.375 * g + 0.125 * above, 0.375 * g + 0.125 * below):
            result.append(
                (
                    0.375 * rows + 0.125 * shift_cols(rows, 1),
                    0.375 * rows + 0.125 * shift_cols(rows, -1),
                )
            )
        return result

    def third_norm(n):
        size = HALF // 4
        scale = row_of(coef_n, 2, n, 0)
        offset = row_of(coef_n, 2, n, 1)

        def step(i, carry):
            sum_dy, sum_dyv = carry
            parts = up_parts(dnarrow, n, i, size)
            for b in range(2):
                g = jnp.stack([parts[0][b], parts[1][b]], axis=1).reshape(2 * size, HALF, C1)
                v = xs_full[n, b, pl.ds(i * 2 * size, 2 * size)]
                dy = g * slope(v * scale + offset)
                dy_full[n, b, pl.ds(i * 2 * size, 2 * size)] = dy
                sum_dy = sum_dy + fold(dy)
                sum_dyv = sum_dyv + fold(dy * v)
            return sum_dy, sum_dyv

        sum_dy, sum_dyv = lax.fori_loop(0, 4, step, (zero_n, zero_n))
        gain, shift, ca, cb, cd = norm_grad_coefs(
            sum_dy, sum_dyv, gain_n(4), coef_n[2, n, 2], coef_n[2, n, 3], full_pixels
        )
        g_small[NARROW_NORM_ROW + 4 : NARROW_NORM_ROW + 5, :C1] += gain[0:1, :]
        g_small[NARROW_NORM_ROW + 5 : NARROW_NORM_ROW + 6, :C1] += shift[0:1, :]

        def finish(i):
            parts = up_parts(dfs, n, i, size)
            for b in range(2):
                g = jnp.stack([parts[0][b], parts[1][b]], axis=1).reshape(2 * size, HALF, C1)
                here = pl.ds(i * 2 * size, 2 * size)
                v = xs_full[n, b, here]
                g = g + dy_full[n, b, here] * ca[0:1, :] + v * cb[0:1, :] + cd[0:1, :]
                store_planes(in_g, n, b, i * 2 * size, rounded(g) * root_half)

        each(4, finish)

    each(images, third_norm)

    def pair_gradient(planes, member):
        products = None
        for b in range(2):
            grads = jnp.concatenate([plane_block(in_g, EVEN + b, a + 1) for a in range(2)], axis=1)
            part = [mm_tn(grads, pair_input(planes, b, jjs)) for jjs in ((0, 1), (2, 3))]
            products = part if products is None else [p + q for p, q in zip(products, part)]
        for dy in range(3):
            blocks = []
            for a in range(2):
                jj = dy + a
                wide_part = products[jj // 2][a * C1 : (a + 1) * C1]
                blocks.append(wide_part[:, (jj % 2) * 3 * C1 : (jj % 2 + 1) * 3 * C1])
            both = blocks[0] + blocks[1]
            for k in range(3):
                row = (member * 9 + dy * 3 + k) * C1
                g_pair[row : row + C1, :] = both[:, k * C1 : (k + 1) * C1].T

    def back_through(member, values, which, gain_row, last):
        for b in range(2):
            out = mm_nt(pair_input(in_g, b, range(4)), pair_bwd[member])
            for n in range(images):
                dy_full[n, b, pl.ds(0, RES)] = pair_rows(out, n)
        bucket_rows = lax.broadcasted_iota(jnp.int32, (NB, C1), 0)

        def image(n):
            scale = row_of(coef_n, which, n, 0)
            offset = row_of(coef_n, which, n, 1)

            def step(i, carry):
                sum_dy, sum_dyv = carry
                here = pl.ds(i * ROWS, ROWS)
                for b in range(2):
                    v = values[n, b, here]
                    dy = dy_full[n, b, here] * slope(v * scale + offset)
                    if not last:
                        dy_full[n, b, here] = dy
                    sum_dy = sum_dy + fold(dy)
                    sum_dyv = sum_dyv + fold(dy * v)
                return sum_dy, sum_dyv

            sum_dy, sum_dyv = lax.fori_loop(0, steps, step, (zero_n, zero_n))
            gain, shift, ca, cb, cd = norm_grad_coefs(
                sum_dy, sum_dyv, gain_n(gain_row), coef_n[which, n, 2], coef_n[which, n, 3], full_pixels
            )
            row = NARROW_NORM_ROW + gain_row
            g_small[row : row + 1, :C1] += gain[0:1, :]
            g_small[row + 1 : row + 2, :C1] += shift[0:1, :]
            if last:
                return

            def finish(i, carry):
                here = pl.ds(i * ROWS, ROWS)
                for b in range(2):
                    v = values[n, b, here]
                    g = dy_full[n, b, here] * ca[0:1, :] + v * cb[0:1, :] + cd[0:1, :]
                    carry = carry + fold(g)
                    store_planes(in_g, n, b, i * ROWS, g)
                return carry

            sums = total(lax.fori_loop(0, steps, finish, zero_n))
            g_small[TIME_NARROW_ROW : TIME_NARROW_ROW + NB, :C1] += jnp.where(
                bucket_rows == bucket(n), sums, 0.0
            )

        each(images, image)

    pair_gradient(in_b, 1)
    back_through(1, h1_full, 1, 2, False)
    pair_gradient(in_a, 0)
    back_through(0, x_full, 0, 0, True)
    sources = (g_attn, g_wide, g_down, g_pair, g_small)
    arrived = (arrived_attn, arrived_wide, arrived_down, arrived_pair, arrived_small)
    outs = (sum_attn, sum_wide, sum_down, sum_pair, sum_small)
    sems = (sems_attn, sems_wide, sems_down, sems_pair, sems_small)
    pieces = [Piece(*parts, stages) for parts in zip(sources, arrived, outs, sems)]
    last = 2 * len(stages)
    for t in range(last + len(pieces)):
        for i, piece in enumerate(pieces):
            if 0 <= t - i <= last:
                piece.step(t - i)


def main_call(dp_size, *operands):
    n = operands[1].shape[1]
    stages = (dp_size - 1).bit_length() + 1
    vm = pltpu.VMEM
    full = (n, 2, RES, HALF, C1)
    planes = (n, 4, RES + 2, HALF, C1)
    wide = HALF_CHANNELS
    square = (n, HALF * HALF, wide)
    moved = [vm(v.shape, v.dtype) for v in operands[1:4] + operands[5:11]]
    scratch = moved + [vm(shape, f32) for shape in PIECES]
    scratch += [vm((arrived_rows(rows, stages), lanes), f32) for rows, lanes in PIECES]
    scratch += [pltpu.SemaphoreType.DMA((2, 2 * stages)) for _ in PIECES]
    scratch += [
        vm((stages + 1, NB, 128), f32),
        vm((stages, NB, 128), f32),
        pltpu.SemaphoreType.DMA((2, 3)),
        pltpu.SemaphoreType.DMA((3,)),
        pltpu.SemaphoreType.DMA((2, stages)),
        pltpu.SemaphoreType.DMA((6,)),
        vm((2, 12 * C1, 2 * C1), bf16),
        vm((2, 2 * C1, 12 * C1), bf16),
        vm((9 * C1, wide), bf16),
        vm((C1, 9 * wide), bf16),
        vm((9 * wide, wide), bf16),
        vm((wide, 9 * wide), bf16),
        vm((C1, wide), bf16),
        vm((wide, 4 * wide), bf16),
        vm((HEAD_ROWS, wide), f32),
        vm(full, f32),
        vm(full, f32),
        vm(full, f32),
        vm((n, 2, RES + 2, HALF, C1), f32),
        vm(planes, bf16),
        vm(planes, bf16),
        vm(planes, bf16),
        vm((ROWS * RES, C1), f32),
        vm((n, 3, HALF + 2, HALF, C1), bf16),
        vm((n, 3, HALF + 2, HALF, wide), bf16),
        vm((n, 3, HALF + 2, HALF, wide), bf16),
        vm((n, HALF * HALF, C1), bf16),
        vm((n, HALF * HALF, C1), f32),
        vm(square, f32),
        vm(square, f32),
        vm(square, f32),
        vm(square, bf16),
        vm((n, HALF * HALF, 3 * wide), bf16),
        vm(square, f32),
        vm(square, bf16),
        vm(square, bf16),
        vm(square, bf16),
        vm(square, f32),
        vm(square, bf16),
        vm((n, HALF * HALF, 3 * wide), bf16),
        vm((n, HALF * HALF, C1), f32),
        vm((3, n, 4, 8, C1), f32),
        vm((3, n, 4, 8, wide), f32),
    ]
    whole = pl.BlockSpec(memory_space=pltpu.VMEM)
    anywhere = pl.BlockSpec(memory_space=pl.ANY)
    return pl.pallas_call(
        functools.partial(main_kernel, dp_size),
        out_shape=[jax.ShapeDtypeStruct(shape, f32) for shape in PIECES + ((NB, 128),)],
        in_specs=[pl.BlockSpec(memory_space=pltpu.SMEM)]
        + [anywhere] * 3
        + [whole]
        + [anywhere] * 6
        + [whole] * 3,
        out_specs=[whole] * (len(PIECES) + 1),
        scratch_shapes=scratch,
        compiler_params=pltpu.CompilerParams(
            collective_id=0, has_side_effects=True, vmem_limit_bytes=VMEM_LIMIT
        ),
        cost_estimate=pl.CostEstimate(flops=8 * 10**9, bytes_accessed=12 * 10**6, transcendentals=0),
    )(*operands)


def partners(dp_size):
    dp = lax.axis_index("dp")
    sp = lax.axis_index("sp")

    def flip(k):
        unit = 1 << k
        side = (dp // unit) % 2
        return side, (dp + unit * (1 - 2 * side), sp)

    core, near = flip(0), flip(1)
    second = core[0]

    def pick(first, other):
        return first + second * (other - first)

    stages = [
        core,
        (pick(near[0], sp), (pick(near[1][0], dp), pick(sp, 1 - sp))),
        (pick(sp, near[0]), (pick(dp, near[1][0]), pick(1 - sp, sp))),
    ]
    for k in range(2, (dp_size - 1).bit_length()):
        stages.append(flip(k))
    return stages


def greet(stages):
    barrier = pltpu.get_barrier_semaphore()
    for _, other in stages:
        pl.semaphore_signal(barrier, inc=1, device_id=other, device_id_type=MESH)
    pl.semaphore_wait(barrier, len(stages))


def send(source, target, sems, index, other):
    return pltpu.make_async_remote_copy(
        src_ref=source,
        dst_ref=target,
        send_sem=sems.at[0, index],
        recv_sem=sems.at[1, index],
        device_id=other,
        device_id_type=MESH,
    )


class Counting:
    def __init__(self, buckets, mask, totals, arrived, sems, stages):
        rows = lax.broadcasted_iota(jnp.int32, (NB, 128), 0)
        counted = jnp.zeros((NB, 128), f32)
        images = mask.shape[1]
        for i in range(2 * images):
            pixels = mask[i // images, i % images].astype(f32)
            number = jnp.sum(jnp.sum(pixels, axis=0, keepdims=True), axis=1, keepdims=True)
            counted = counted + jnp.where(rows == buckets[i], number, 0.0)
        totals[0] = counted
        self.totals, self.arrived, self.sems, self.stages = totals, arrived, sems, stages
        self.copies = []

    def step(self):
        done = len(self.copies)
        if done:
            self.copies[-1].wait()
            self.totals[done] = self.totals[done - 1] + self.arrived[done - 1]
        if done < len(self.stages):
            copy = send(self.totals.at[done], self.arrived.at[done], self.sems, done, self.stages[done][1])
            copy.start()
            self.copies.append(copy)

    def finish(self, counts):
        while len(self.copies) < len(self.stages):
            self.step()
        self.step()
        counts[...] = self.totals[len(self.stages)]


def chunk_of(rows):
    return next(c for c in (128, 96, 72, 64, 48, 40, 32, 24, 16, 8) if rows % c == 0)


def add_rows(target, base, source, offset, rows):
    size = chunk_of(rows)

    def step(i):
        here = pl.ds(pl.multiple_of(base + i * size, 8), size)
        target[here, :] = target[here, :] + source[pl.ds(pl.multiple_of(offset + i * size, 8), size), :]

    each(rows // size, step)


class Piece:
    def __init__(self, source, arrived, out, sems, stages):
        self.source, self.arrived, self.out, self.sems, self.stages = source, arrived, out, sems, stages
        rows = source.shape[0]
        self.plan = []
        base = 0
        lowest = 0
        for side, other in stages:
            halved = rows % 16 == 0
            rows = rows // 2 if halved else rows
            self.plan.append((side, other, halved, rows, base, lowest))
            lowest = lowest + side * rows if halved else lowest
            base += rows
        self.rows, self.lowest = rows, lowest
        self.copies = {}

    def region(self, s, side):
        halved, rows = self.plan[s][2:4]
        if s == 0:
            ref, base = self.source, 0
        else:
            ref, base = self.arrived, self.plan[s - 1][4]
        return ref, (base + side * rows if halved else base)

    def scatter_start(self, s):
        side, other, halved, rows, base, _ = self.plan[s]
        ref, first = self.region(s, 1 - side)
        copy = send(
            ref.at[pl.ds(pl.multiple_of(first, 8), rows)],
            self.arrived.at[pl.ds(base, rows)],
            self.sems,
            s,
            other,
        )
        copy.start()
        self.copies[s] = copy

    def scatter_end(self, s):
        side, other, halved, rows, base, _ = self.plan[s]
        self.copies[s].wait()
        ref, first = self.region(s, side)
        add_rows(self.arrived, base, ref, first, rows)
        if s + 1 == len(self.stages):
            self.out[pl.ds(pl.multiple_of(self.lowest, 8), rows), :] = self.arrived[base : base + rows, :]

    def gather_start(self, s):
        side, other, halved, rows, base, lowest = self.plan[s]
        if halved:
            here = pl.ds(pl.multiple_of(lowest + side * rows, 8), rows)
            copy = send(self.out.at[here], self.out.at[here], self.sems, len(self.stages) + s, other)
            copy.start()
            self.copies[len(self.stages) + s] = copy

    def gather_end(self, s):
        if self.plan[s][2]:
            self.copies[len(self.stages) + s].wait()

    def step(self, t):
        count = len(self.stages)
        if 0 < t <= count:
            self.scatter_end(t - 1)
        elif t > count:
            self.gather_end(2 * count - t)
        if t < count:
            self.scatter_start(t)
        elif t < 2 * count:
            self.gather_start(2 * count - 1 - t)


def arrived_rows(rows, stages):
    needed = 0
    for _ in range(stages):
        rows = rows // 2 if rows % 16 == 0 else rows
        needed += rows
    return needed


def adamw(weight, grad, first, second, rate):
    first = beta_one * first + (1.0 - beta_one) * grad
    second = beta_two * second + (1.0 - beta_two) * grad * grad
    scale = rate / (1.0 - beta_one**STEP)
    root = jnp.sqrt(second * (1.0 / (1.0 - beta_two**STEP))) + adam_epsilon
    return weight * (1.0 - rate * decay_rate) - scale * first / root, first, second


def update_kernel(*refs):
    g_attn, g_wide, g_down, g_pair, g_small = refs[:5]
    members = [refs[5 + 3 * i : 8 + 3 * i] for i in range(9)]
    outs = [refs[32 + 3 * i : 35 + 3 * i] for i in range(9)]
    loss_out = refs[59]

    def blocks(member, grad, block_rows, base, count):
        size = 64

        def step(i):
            block = i // (block_rows // size)
            row = (i % (block_rows // size)) * size
            here = pl.ds(pl.multiple_of(block * block_rows + row, 8), size)
            columns = members[member][0].shape[1] // 128
            for c in range(columns):
                lanes = slice(c * 128, (c + 1) * 128)
                g = grad[pl.ds(pl.multiple_of(base + (block * columns + c) * block_rows + row, 8), size), :]
                w, m, v = (ref[here, lanes] for ref in members[member])
                for out, value in zip(outs[member], adamw(w, g, m, v, rate_matrix)):
                    out[here, lanes] = value

        each(count * block_rows // size, step)

    def single(member, index, grad, rate):
        w, m, v = (ref[index] for ref in members[member])
        for out, value in zip(outs[member], adamw(w, grad, m, v, rate)):
            out[index] = value

    blocks(0, g_pair, C1, 0, 18)
    blocks(1, g_down, C1, 0, 9)
    blocks(2, g_wide, HALF_CHANNELS, 0, 9)
    blocks(3, g_down, C1, SKIP_ROW, 1)
    blocks(4, g_attn, HALF_CHANNELS, 0, 1)
    for tap in range(9):
        single(5, (tap,), g_small[tap * 8 : tap * 8 + 3, :], rate_matrix)
    single(6, (slice(None), slice(None)), g_small[NARROW_NORM_ROW : NARROW_NORM_ROW + 6, :C1], rate_vector)
    single(7, (slice(None), slice(None)), g_small[WIDE_NORM_ROW : WIDE_NORM_ROW + 6, :], rate_vector)
    single(
        8, (slice(None), slice(0, C1)), g_small[TIME_NARROW_ROW : TIME_NARROW_ROW + NB, :C1], rate_vector
    )
    single(
        8, (slice(None), slice(C1, None)), g_small[TIME_WIDE_ROW : TIME_WIDE_ROW + NB, :], rate_vector
    )
    loss_out[...] = g_small[LOSS_ROW : LOSS_ROW + 1, :128]


def update_call(grads, members):
    whole = pl.BlockSpec(memory_space=pltpu.VMEM)
    flat = [v for member in members for v in member]
    return pl.pallas_call(
        update_kernel,
        out_shape=[jax.ShapeDtypeStruct(v.shape, f32) for v in flat]
        + [jax.ShapeDtypeStruct((1, 128), f32)],
        in_specs=[whole] * (5 + len(flat)),
        out_specs=[whole] * (len(flat) + 1),
        compiler_params=pltpu.CompilerParams(vmem_limit_bytes=VMEM_LIMIT),
    )(*grads, *flat)


def on_device(
    features,
    target,
    pixel_mask,
    buckets,
    conv_pair,
    down_conv,
    conv_wide,
    skip_proj,
    attn_proj,
    head_conv,
    norm_narrow,
    norm_wide,
    time_bias,
    conv_pair_mom,
    down_conv_mom,
    conv_wide_mom,
    skip_proj_mom,
    attn_proj_mom,
    head_conv_mom,
    norm_narrow_mom,
    norm_wide_mom,
    time_bias_mom,
    conv_pair_sq,
    down_conv_sq,
    conv_wide_sq,
    skip_proj_sq,
    attn_proj_sq,
    head_conv_sq,
    norm_narrow_sq,
    norm_wide_sq,
    time_bias_sq,
):
    dp_size = lax.axis_size("dp")
    images = features.shape[0] // 2

    def halves(tensor):
        return tensor.reshape((2, images) + tensor.shape[1:])

    def flat(tensor):
        return tensor.reshape(-1, tensor.shape[-1])

    def head_rows(tensor):
        return jnp.transpose(tensor, (0, 1, 3, 2)).reshape(9, 3, HALF_CHANNELS)

    params = (
        flat(conv_pair),
        flat(down_conv),
        flat(conv_wide),
        skip_proj,
        attn_proj,
        head_rows(head_conv),
        norm_narrow,
        norm_wide,
        time_bias,
    )
    firsts = (
        flat(conv_pair_mom),
        flat(down_conv_mom),
        flat(conv_wide_mom),
        skip_proj_mom,
        attn_proj_mom,
        head_rows(head_conv_mom),
        norm_narrow_mom,
        norm_wide_mom,
        time_bias_mom,
    )
    seconds = (
        flat(conv_pair_sq),
        flat(down_conv_sq),
        flat(conv_wide_sq),
        skip_proj_sq,
        attn_proj_sq,
        head_rows(head_conv_sq),
        norm_narrow_sq,
        norm_wide_sq,
        time_bias_sq,
    )
    masks = halves(pixel_mask)
    *summed, counts = main_call(
        dp_size,
        buckets,
        halves(features),
        halves(jnp.transpose(target, (0, 3, 1, 2))),
        masks,
        masks,
        *params,
    )
    results = update_call(summed, list(zip(params, firsts, seconds)))
    shaped = []
    for member, like in enumerate((conv_pair, down_conv, conv_wide, skip_proj, attn_proj)):
        shaped.extend(v.reshape(like.shape) for v in results[3 * member : 3 * member + 3])
    for v in results[15:18]:
        shaped.append(jnp.transpose(v.reshape(3, 3, 3, HALF_CHANNELS), (0, 1, 3, 2)))
    shaped.extend(results[18:27])
    return (results[27][0, 0], counts[:, 0]) + tuple(shaped)


def solution(mesh):
    placed = (
        P("dp", "sp", None, None),
        P("dp", "sp", None, None),
        P("dp", "sp", None),
        P("dp"),
        P(),
        P(),
        P(),
        P(),
        P(),
        P(),
        P(),
        P(),
        P(),
        P(),
        P(),
        P(),
        P(),
        P(),
        P(),
        P(),
        P(),
        P(),
        P(),
        P(),
        P(),
        P(),
        P(),
        P(),
        P(),
        P(),
        P(),
    )
    return jax.shard_map(
        on_device,
        mesh=mesh,
        in_specs=placed,
        out_specs=(
            P(),
            P(),
            P(),
            P(),
            P(),
            P(),
            P(),
            P(),
            P(),
            P(),
            P(),
            P(),
            P(),
            P(),
            P(),
            P(),
            P(),
            P(),
            P(),
            P(),
            P(),
            P(),
            P(),
            P(),
            P(),
            P(),
            P(),
            P(),
            P(),
        ),
        check_vma=False,
    )
```

```python
import functools

import jax
import jax.numpy as jnp
from jax import lax
from jax.experimental import pallas as pl
from jax.experimental.pallas import tpu as pltpu
from jax.sharding import PartitionSpec as P

C1 = 128
HALF_CHANNELS = 256
GROUPS = 32
RES = 32
HALF = 16
NB = 8
STEP = 10
MESH = pl.DeviceIdType.MESH
VMEM_LIMIT = 62 * 1024 * 1024

epsilon = 1e-05
root_half = 0.7071067811865476
beta_one = 0.9
beta_two = 0.999
adam_epsilon = 1e-08
decay_rate = 0.1
rate_matrix = 0.03
rate_vector = 0.5
logit_scale = HALF_CHANNELS ** (-0.5)
ROWS = 8

bf16 = jnp.bfloat16
f32 = jnp.float32

EVEN, ODD, ODD_LEFT, EVEN_RIGHT = 0, 1, 2, 3
TAPS = ((ODD_LEFT, EVEN, ODD), (EVEN, ODD, EVEN_RIGHT))


def rounded(v):
    return v.astype(bf16).astype(f32)


def silu(t):
    return t * jax.nn.sigmoid(t)


def slope(t):
    s = jax.nn.sigmoid(t)
    return s * (1.0 + t * (1.0 - s))


def mm(a, b):
    return lax.dot_general(a, b, (((1,), (0,)), ((), ())), preferred_element_type=f32)


def mm_nt(a, b):
    return lax.dot_general(a, b, (((1,), (1,)), ((), ())), preferred_element_type=f32)


def mm_tn(a, b):
    return lax.dot_general(a, b, (((0,), (0,)), ((), ())), preferred_element_type=f32)


def fold(v):
    return jnp.sum(v.reshape(-1, 8, v.shape[-1]), axis=0)


def total(v):
    return jnp.broadcast_to(jnp.sum(v, axis=0, keepdims=True), v.shape)


def group_sum(v, size):
    lanes = v.shape[-1]
    lane = lax.broadcasted_iota(jnp.int32, v.shape, 1)
    step = 1
    while step < size:
        other = jnp.where(
            (lane & step) == 0, pltpu.roll(v, lanes - step, 1), pltpu.roll(v, step, 1)
        )
        v = v + other
        step *= 2
    return v


def norm_coefs(sums, squares, gain, shift, pixels):
    size = sums.shape[-1] // GROUPS
    count = pixels * size
    mean = group_sum(total(sums), size) / count
    power = group_sum(total(squares), size) / count
    inv = lax.rsqrt(power - mean * mean + epsilon)
    scale = inv * gain
    return scale, shift - mean * scale, mean, inv


def norm_grad_coefs(sum_dy, sum_dyv, gain, mean, inv, pixels):
    size = sum_dy.shape[-1] // GROUPS
    count = pixels * size
    first = total(sum_dy)
    second = (total(sum_dyv) - mean * first) * inv
    one = group_sum(first * gain, size) / count
    two = group_sum(second * gain, size) / count
    b = -inv * inv * two
    return second, first, inv * gain, b, -inv * one - mean * b


def shift_cols(v, step):
    col = lax.broadcasted_iota(jnp.int32, v.shape, 1)
    if step == 1:
        return jnp.where(col == 0, 0.0, pltpu.roll(v, 1, 1))
    return jnp.where(col == HALF - 1, 0.0, pltpu.roll(v, HALF - 1, 1))


def store_planes(planes, n, b, r0, v):
    rows = v.shape[0]
    v = v.astype(bf16).astype(f32)
    for plane, value in (
        (EVEN + b, v),
        (ODD_LEFT if b == 1 else EVEN_RIGHT, shift_cols(v, 1 if b == 1 else -1)),
    ):
        planes[n, plane, pl.ds(r0 + 1, rows)] = value.astype(bf16)


def store_shifted(cells, n, r0, v):
    rows = v.shape[0]
    v = v.astype(bf16).astype(f32)
    for tap, value in ((0, shift_cols(v, 1)), (1, v), (2, shift_cols(v, -1))):
        cells[n, tap, pl.ds(r0 + 1, rows)] = value.astype(bf16)


def plane_block(planes, tap, jj):
    return planes[:, tap, pl.ds(jj, HALF, stride=2)].reshape(-1, planes.shape[-1])


def pair_input(planes, b, jjs):
    return jnp.concatenate([plane_block(planes, tap, jj) for jj in jjs for tap in TAPS[b]], axis=1)


def cell_input(cells, dys):
    return jnp.concatenate(
        [
            cells[:, tap, dy : dy + HALF].reshape(-1, cells.shape[-1])
            for dy in dys
            for tap in range(3)
        ],
        axis=1,
    )


def each(count, body):
    def step(i, carry):
        body(i)
        return carry

    lax.fori_loop(0, count, step, 0)


def prepare_weights(pair, down, wide, skip, attn, head, pair_fwd, pair_bwd, down_fwd, down_bwd, wide_fwd, wide_bwd, skip_low, attn_low, head_low):
    nothing = jnp.zeros((C1, C1), bf16)
    for member in range(2):
        for jj in range(4):
            for k in range(3):
                block = (jj * 3 + k) * C1
                for a in range(2):
                    dy = jj - a
                    inside = 0 <= dy < 3
                    row = (member * 9 + dy * 3 + k) * C1
                    back = (member * 9 + (2 - dy) * 3 + (2 - k)) * C1
                    pair_fwd[member, block : block + C1, a * C1 : a * C1 + C1] = (
                        pair[row : row + C1, :].astype(bf16) if inside else nothing
                    )
                    pair_bwd[member, a * C1 : a * C1 + C1, block : block + C1] = (
                        pair[back : back + C1, :].astype(bf16) if inside else nothing
                    )
    wide_channels = HALF_CHANNELS
    for tap in range(9):
        low = down[tap * C1 : tap * C1 + C1, :].astype(bf16)
        down_fwd[tap * C1 : tap * C1 + C1, :] = low
        down_bwd[:, (8 - tap) * wide_channels : (9 - tap) * wide_channels] = low
        low = wide[tap * wide_channels : (tap + 1) * wide_channels, :].astype(bf16)
        wide_fwd[tap * wide_channels : (tap + 1) * wide_channels, :] = low
        wide_bwd[:, (8 - tap) * wide_channels : (9 - tap) * wide_channels] = low
    skip_low[...] = skip[...].astype(bf16)
    attn_low[...] = attn[...].astype(bf16)
    head_low[...] = jnp.zeros(head_low.shape, f32)
    for tap in range(9):
        head_low[tap * 8 : tap * 8 + 3, :] = rounded(head[tap])


def split_three(v):
    high = v.astype(bf16)
    rest = v - high.astype(f32)
    middle = rest.astype(bf16)
    return high, middle, (rest - middle.astype(f32)).astype(bf16)


def lane_shift(v, step):
    lane = lax.broadcasted_iota(jnp.int32, v.shape, 1)
    j = lane & (HALF - 1)
    if step == 1:
        keep = j < HALF - 1
    elif step == -1:
        keep = j > 0
    elif step == HALF:
        keep = lane < HALF * (HALF - 1)
    else:
        keep = lane >= HALF
    return jnp.where(keep, pltpu.roll(v, (-step) % v.shape[-1], 1), 0.0)


def head_forward(table):
    cols = [
        [
            lane_shift(table[dy][0], -1) + table[dy][1] + table[dy][2],
            table[dy][0] + table[dy][1] + lane_shift(table[dy][2], 1),
        ]
        for dy in range(3)
    ]
    return [
        [
            lane_shift(cols[0][b], -HALF) + cols[1][b] + cols[2][b]
            if a == 0
            else cols[0][b] + cols[1][b] + lane_shift(cols[2][b], HALF)
            for b in range(2)
        ]
        for a in range(2)
    ]


def head_backward(grad):
    rows = [
        [
            lane_shift(grad[0][b], HALF) + grad[1][b],
            grad[0][b] + grad[1][b],
            grad[0][b] + lane_shift(grad[1][b], -HALF),
        ]
        for b in range(2)
    ]
    return [
        [
            lane_shift(rows[0][dy], 1) + rows[1][dy],
            rows[0][dy] + rows[1][dy],
            rows[0][dy] + lane_shift(rows[1][dy], -1),
        ]
        for dy in range(3)
    ]


def keep_columns(ref, row, v):
    for c in range(v.shape[1] // 128):
        ref[row + c * v.shape[0] : row + (c + 1) * v.shape[0], :] = v[:, c * 128 : (c + 1) * 128]


HEAD_ROWS = 72
WIDE_NORM_ROW = 72
LOSS_ROW = 78
TIME_WIDE_ROW = 80
SMALL_ROWS = 96
TIME_NARROW_ROW = 8
LATE_ROWS = 16
SKIP_ROW = 18 * C1
ATTN_ROWS = 8 * HALF_CHANNELS
WIDE_ROWS = 18 * HALF_CHANNELS
DOWN_ROWS = 20 * C1
PAIR_ROWS = 9 * C1
GRADS = (ATTN_ROWS, WIDE_ROWS, DOWN_ROWS, PAIR_ROWS, PAIR_ROWS)
TILE = 16


def padded(rows, devices, tile):
    return -(-rows // (devices * tile)) * devices * tile


def coded_rows(rows, devices):
    return padded(rows, devices, TILE) + devices * TILE


def main_kernel(
    dp_size,
    buckets, features, target_rows, mask_rows, mask_local, pair_all, down_all, wide_all, skip_all, attn_all, head_all,
    gains_narrow, gains_wide, time_bias,
    sum_attn, sum_wide, sum_down, sum_pair_b, sum_pair_a, sum_small, sum_late, counts,
    x_in, target, mask, pair, down, wide, skip, attn, head,
    g_attn, g_wide, g_down, g_pair_b, g_pair_a, g_rows,
    out_attn, out_wide, out_down, out_pair_b, out_pair_a,
    in_attn, in_wide, in_down, in_pair_b, in_pair_a, in_small,
    sems_attn, sems_wide, sems_down, sems_pair_b, sems_pair_a, sems_small,
    g_small, g_late,
    totals, arrived_totals, late_totals, arrived_late, image_sems, local_sems, count_sems, late_sems, weight_sems,
    pair_fwd, pair_bwd, down_fwd, down_bwd, wide_fwd, wide_bwd, skip_low, attn_low, head_low,
    x_full, h1_full, xs_full, dy_full, in_a, in_b, in_g, flat,
    cells_c, cells_d, cells_g, fs_low, dfs, h3, x2, x3, n5, qkv, probs, probs_low, att, a6, dwide, dout, dqkv, dnarrow,
    coef_n, coef_w,
):
    loads = [
        pltpu.make_async_copy(source, ref, weight_sems.at[i])
        for i, (source, ref) in enumerate(
            (
                (pair_all, pair),
                (down_all, down),
                (wide_all, wide),
                (skip_all, skip),
                (attn_all, attn),
                (head_all, head),
            )
        )
    ]
    links = Links(dp_size)
    links.greet()
    here = (lax.axis_index("dp"), 1 - lax.axis_index("sp"))
    moved = ((features, x_in), (target_rows, target), (mask_rows, mask))
    side = lax.axis_index("sp")
    arrivals = [
        send(source.at[1 - side], out.at[side], image_sems, i, i, here) for i, (source, out) in enumerate(moved)
    ]
    for copy in arrivals:
        copy.start()
    keeps = [
        pltpu.make_async_copy(source.at[side], out.at[side], local_sems.at[i])
        for i, (source, out) in enumerate(moved)
    ]
    for copy in keeps + loads:
        copy.start()
    images = x_in.shape[1]
    position = lax.axis_index("sp")
    steps = RES // ROWS
    full_pixels = RES * RES
    half_pixels = HALF * HALF
    zero_n = jnp.zeros((8, C1), f32)
    zero_w = jnp.zeros((8, HALF_CHANNELS), f32)

    def bucket(n):
        return buckets[position * images + n]

    def gain_n(row):
        return jnp.broadcast_to(gains_narrow[row : row + 1, :], (8, C1))

    def gain_w(row):
        return jnp.broadcast_to(gains_wide[row : row + 1, :], (8, HALF_CHANNELS))

    def keep_coefs(ref, which, n, values):
        for kind in range(4):
            ref[which, n, kind] = values[kind]

    def row_of(ref, which, n, kind):
        return ref[which, n, kind, 0:1, :]

    counting = Exchange(count_pixels(buckets, mask_local), totals, arrived_totals, count_sems, links.brief)
    counting.step()
    sources = (g_attn, g_wide, g_down, g_pair_b, g_pair_a, g_rows)
    outgoing = (out_attn, out_wide, out_down, out_pair_b, out_pair_a, None)
    incoming = (in_attn, in_wide, in_down, in_pair_b, in_pair_a, in_small)
    outs = (sum_attn, sum_wide, sum_down, sum_pair_b, sum_pair_a, sum_small)
    sems = (sems_attn, sems_wide, sems_down, sems_pair_b, sems_pair_a, sems_small)
    orders = (links.brief, links.full, links.brief, links.brief, links.brief, links.brief)
    pieces = dict(zip(PIECE_NAMES, (Piece(*parts) for parts in zip(sources, outgoing, incoming, outs, sems, orders))))

    def advance(point):
        for name in SCHEDULE.get(point, ()):
            pieces[name].step()

    for rows, ref in zip(GRADS + (2 * SMALL_ROWS,), sources):
        if ref.shape[0] > rows:
            ref[rows:, :] = jnp.zeros((ref.shape[0] - rows, 128), f32)
    for copy in loads:
        copy.wait()
    prepare_weights(pair, down, wide, skip, attn, head, pair_fwd, pair_bwd, down_fwd, down_bwd, wide_fwd, wide_bwd, skip_low, attn_low, head_low)
    g_small[...] = jnp.zeros(g_small.shape, f32)
    g_late[...] = jnp.zeros(g_late.shape, f32)
    for planes in (in_a, in_b, in_g):
        edge = jnp.zeros((images, 4, HALF, C1), bf16)
        planes[:, :, 0] = edge
        planes[:, :, RES + 1] = edge
    for cells in (cells_c, cells_d, cells_g):
        edge = jnp.zeros((images, 3, HALF, cells.shape[-1]), bf16)
        cells[:, :, 0] = edge
        cells[:, :, HALF + 1] = edge

    for copy in keeps + arrivals:
        copy.wait()
    counting.step()

    def load_image(n):
        def step(i, carry):
            sums, squares = carry
            half = i // 2
            v = x_in[half, n, pl.ds((i % 2) * ROWS, ROWS)].astype(f32)
            flat[...] = v.reshape(ROWS * RES, C1)
            for b in range(2):
                w = flat[pl.ds(b, ROWS * HALF, stride=2), :].reshape(ROWS, HALF, C1)
                x_full[n, b, pl.ds(i * ROWS, ROWS)] = w
                sums = sums + fold(w)
                squares = squares + fold(w * w)
            return sums, squares

        sums, squares = lax.fori_loop(0, steps, step, (zero_n, zero_n))
        keep_coefs(coef_n, 0, n, norm_coefs(sums, squares, gain_n(0), gain_n(1), full_pixels))

    each(images, load_image)

    def activate(values, planes, which):
        def image(n):
            scale = row_of(coef_n, which, n, 0)
            offset = row_of(coef_n, which, n, 1)

            def step(i):
                for b in range(2):
                    v = values[n, b, pl.ds(i * ROWS, ROWS)]
                    store_planes(planes, n, b, i * ROWS, silu(v * scale + offset))

            each(steps, step)

        each(images, image)

    def pair_rows(result, n):
        part = result[n * half_pixels : (n + 1) * half_pixels].reshape(HALF, 1, HALF, 2 * C1)
        return jnp.concatenate([part[..., :C1], part[..., C1:]], axis=1).reshape(RES, HALF, C1)

    activate(x_full, in_a, 0)
    counting.step()
    for b in range(2):
        out = mm(pair_input(in_a, b, range(4)), pair_fwd[0])
        for n in range(images):
            h1_full[n, b] = pair_rows(out, n)

    def first_hidden(n):
        bias = time_bias[pl.ds(bucket(n), 1), :][:, :C1]

        def step(i, carry):
            sums, squares = carry
            for b in range(2):
                v = h1_full[n, b, pl.ds(i * ROWS, ROWS)] + bias
                h1_full[n, b, pl.ds(i * ROWS, ROWS)] = v
                sums = sums + fold(v)
                squares = squares + fold(v * v)
            return sums, squares

        sums, squares = lax.fori_loop(0, steps, step, (zero_n, zero_n))
        keep_coefs(coef_n, 1, n, norm_coefs(sums, squares, gain_n(2), gain_n(3), full_pixels))

    each(images, first_hidden)
    activate(h1_full, in_b, 1)
    counting.step()
    for b in range(2):
        out = mm(pair_input(in_b, b, range(4)), pair_fwd[1])
        for n in range(images):
            xs_full[n, b] = pair_rows(out, n)

    def first_out(n):
        def step(i, carry):
            sums, squares = carry
            for b in range(2):
                v = xs_full[n, b, pl.ds(i * ROWS, ROWS)]
                v = rounded((x_full[n, b, pl.ds(i * ROWS, ROWS)] + v) * root_half)
                xs_full[n, b, pl.ds(i * ROWS, ROWS)] = v
                sums = sums + fold(v)
                squares = squares + fold(v * v)
            return sums, squares

        sums, squares = lax.fori_loop(0, steps, step, (zero_n, zero_n))
        keep_coefs(coef_n, 2, n, norm_coefs(sums, squares, gain_n(4), gain_n(5), full_pixels))

    each(images, first_out)

    counting.step()

    def fir_down_image(n):
        scale = row_of(coef_n, 2, n, 0)
        offset = row_of(coef_n, 2, n, 1)
        for b in range(2):
            dy_full[n, b, 0] = jnp.zeros((HALF, C1), f32)
            dy_full[n, b, RES + 1] = jnp.zeros((HALF, C1), f32)

        def act_step(i):
            for b in range(2):
                v = xs_full[n, b, pl.ds(i * ROWS, ROWS)]
                dy_full[n, b, pl.ds(i * ROWS + 1, ROWS)] = silu(v * scale + offset)

        each(steps, act_step)

        def columns(rows):
            even, odd = rows
            return (
                0.125 * (shift_cols(odd, 1) + shift_cols(even, -1)) + 0.375 * (even + odd)
            )

        def taps(ref, b, r0, size):
            return [ref[n, b, pl.ds(r0 + t, size, stride=2)] for t in range(4)]

        def down_step(i):
            size = HALF // 2
            rows = []
            for b in range(2):
                t = taps(dy_full, b, 2 * size * i, size)
                rows.append(0.125 * (t[0] + t[3]) + 0.375 * (t[1] + t[2]))
            store_shifted(cells_c, n, i * size, columns(rows))

        each(2, down_step)
        for b in range(2):
            dy_full[n, b, pl.ds(1, RES)] = xs_full[n, b]

        def skip_step(i):
            size = HALF // 2
            rows = []
            for b in range(2):
                t = taps(dy_full, b, 2 * size * i, size)
                rows.append(0.125 * (t[0] + t[3]) + 0.375 * (t[1] + t[2]))
            fs_low[n, pl.ds(i * size * HALF, size * HALF)] = (
                columns(rows).reshape(size * HALF, C1).astype(bf16)
            )

        each(2, skip_step)

    each(images, fir_down_image)

    def wide_stats(v, which, n, row):
        values = norm_coefs(fold(v), fold(v * v), gain_w(row), gain_w(row + 1), half_pixels)
        keep_coefs(coef_w, which, n, values)
        return values[0][0:1, :], values[1][0:1, :]

    out = mm(cell_input(cells_c, range(3)), down_fwd[...])
    for n in range(images):
        v = out[n * half_pixels : (n + 1) * half_pixels] + time_bias[pl.ds(bucket(n), 1), :][:, C1:]
        h3[n] = v
        scale, offset = wide_stats(v, 0, n, 0)
        store_shifted(cells_d, n, 0, silu(v * scale + offset).reshape(HALF, HALF, HALF_CHANNELS))
    out = mm(cell_input(cells_d, range(3)), wide_fwd[...])
    out = out + mm(fs_low[...].reshape(-1, C1), skip_low[...])
    for n in range(images):
        v = out[n * half_pixels : (n + 1) * half_pixels] * root_half
        x2[n] = v
        scale, offset = wide_stats(v, 1, n, 2)
        n5[n] = (v * scale + offset).astype(bf16)
        qkv[n] = mm(n5[n], attn_low[:, : 3 * HALF_CHANNELS]).astype(bf16)
        q = qkv[n, :, :HALF_CHANNELS]
        k = qkv[n, :, HALF_CHANNELS : 2 * HALF_CHANNELS]
        w = qkv[n, :, 2 * HALF_CHANNELS :]
        logits = mm_nt(q, k) * logit_scale
        powers = jnp.exp(logits - jnp.max(logits, axis=1, keepdims=True))
        weights = powers / jnp.sum(powers, axis=1, keepdims=True)
        probs[n] = weights
        probs_low[n] = weights.astype(bf16)
        att[n] = mm(probs_low[n], w).astype(bf16)
        v = (v + mm(att[n], attn_low[:, 3 * HALF_CHANNELS :])) * root_half
        x3[n] = v
        scale, offset = wide_stats(v, 2, n, 4)
        a6[n] = silu(v * scale + offset).astype(bf16)

    counting.finish(counts)

    lane = lax.broadcasted_iota(jnp.int32, (RES, 2 * half_pixels), 1)
    source = lax.broadcasted_iota(jnp.int32, (RES, 2 * half_pixels), 0)
    picks = (source == 2 * (lane & (HALF - 1)) + (lane >> 8)).astype(bf16)
    row_lane = (lax.broadcasted_iota(jnp.int32, (HALF, 2 * half_pixels), 1) & (half_pixels - 1)) >> 4
    row_source = lax.broadcasted_iota(jnp.int32, (HALF, 2 * half_pixels), 0)
    component = lax.broadcasted_iota(jnp.int32, (8, half_pixels), 0)

    def spread(halves):
        moved = [mm(half, picks) for half in halves]
        rows = []
        for a in range(2):
            picked = sum(
                jnp.where(2 * row_lane + a == row_source + HALF * h, moved[h], 0.0)
                for h in range(2)
            )
            row = jnp.sum(picked, axis=0, keepdims=True)
            rows.append([row[:, :half_pixels], row[:, half_pixels:]])
        return rows

    loss = jnp.zeros((1, half_pixels), f32)
    head_grad = jnp.zeros((HEAD_ROWS, HALF_CHANNELS), f32)
    for n in range(images):
        moved = mm_nt(head_low[...].astype(bf16), a6[n])
        pred = head_forward(
            [[moved[(dy * 3 + dx) * 8 : (dy * 3 + dx) * 8 + 8] for dx in range(3)] for dy in range(3)]
        )
        wanted = [spread([target[h, n, c] for h in range(2)]) for c in range(3)]
        counted = spread([mask[h, n].astype(f32).astype(bf16) for h in range(2)])
        per_image = 1.0 / counts[pl.ds(bucket(n), 1), :]
        per_image = jnp.concatenate([per_image, per_image], axis=1)
        grad_pred = [[None, None], [None, None]]
        for a in range(2):
            for b in range(2):
                goal = jnp.zeros((8, half_pixels), f32)
                for c in range(3):
                    goal = jnp.where(component == c, wanted[c][a][b], goal)
                error = pred[a][b] - goal
                weight = counted[a][b] * per_image
                loss = loss + weight * jnp.sum(error * error, axis=0, keepdims=True)
                grad_pred[a][b] = rounded(2.0 * error * weight)
        table = head_backward(grad_pred)
        table = jnp.concatenate([table[dy][dx] for dy in range(3) for dx in range(3)], axis=0)
        parts = split_three(table)
        for part in parts:
            head_grad = head_grad + mm(part, a6[n])
        head_rows = head_low[...].astype(bf16)
        grad = sum(mm_tn(part, head_rows) for part in parts)
        v = x3[n]
        values = [coef_w[2, n, kind] for kind in range(4)]
        dy = rounded(grad) * slope(v * values[0][0:1, :] + values[1][0:1, :])
        gain, shift, ca, cb, cd = norm_grad_coefs(
            fold(dy), fold(dy * v), gain_w(4), values[2], values[3], half_pixels
        )
        g_small[WIDE_NORM_ROW + 4 : WIDE_NORM_ROW + 5, :] += gain[0:1, :]
        g_small[WIDE_NORM_ROW + 5 : WIDE_NORM_ROW + 6, :] += shift[0:1, :]
        grad_third = dy * ca[0:1, :] + v * cb[0:1, :] + cd[0:1, :]
        dwide[n] = grad_third
    g_small[0:HEAD_ROWS, :] = head_grad
    g_small[LOSS_ROW : LOSS_ROW + 1, :] = jnp.broadcast_to(
        jnp.sum(loss, axis=1, keepdims=True), (1, HALF_CHANNELS)
    )

    for n in range(images):
        grad_attn = (dwide[n] * root_half).astype(bf16)
        dout[n] = grad_attn
        grad_att = mm_nt(grad_attn, attn_low[:, 3 * HALF_CHANNELS :]).astype(bf16)
        q = qkv[n, :, :HALF_CHANNELS]
        k = qkv[n, :, HALF_CHANNELS : 2 * HALF_CHANNELS]
        w = qkv[n, :, 2 * HALF_CHANNELS :]
        grad_probs = mm_nt(grad_att, w)
        weights = probs[n]
        inner = jnp.sum(weights * grad_probs, axis=1, keepdims=True)
        grad_scores = (weights * (grad_probs - inner)).astype(bf16)
        dqkv[n, :, :HALF_CHANNELS] = (mm(grad_scores, k) * logit_scale).astype(bf16)
        dqkv[n, :, HALF_CHANNELS : 2 * HALF_CHANNELS] = (mm_tn(grad_scores, q) * logit_scale).astype(bf16)
        dqkv[n, :, 2 * HALF_CHANNELS :] = mm_tn(probs_low[n], grad_att).astype(bf16)
    keep_columns(
        g_attn, 0, mm_tn(n5[...].reshape(-1, HALF_CHANNELS), dqkv[...].reshape(-1, 3 * HALF_CHANNELS))
    )
    keep_columns(
        g_attn,
        6 * HALF_CHANNELS,
        mm_tn(att[...].reshape(-1, HALF_CHANNELS), dout[...].reshape(-1, HALF_CHANNELS)),
    )
    advance("attn")
    for n in range(images):
        dy = mm_nt(dqkv[n], attn_low[:, : 3 * HALF_CHANNELS])
        v = x2[n]
        gain, shift, ca, cb, cd = norm_grad_coefs(
            fold(dy), fold(dy * v), gain_w(2), coef_w[1, n, 2], coef_w[1, n, 3], half_pixels
        )
        g_small[WIDE_NORM_ROW + 2 : WIDE_NORM_ROW + 3, :] += gain[0:1, :]
        g_small[WIDE_NORM_ROW + 3 : WIDE_NORM_ROW + 4, :] += shift[0:1, :]
        grad = dy * ca[0:1, :] + v * cb[0:1, :] + cd[0:1, :] + dwide[n] * root_half
        store_shifted(cells_g, n, 0, (grad * root_half).reshape(HALF, HALF, HALF_CHANNELS))

    center = cells_g[:, 1, 1 : HALF + 1].reshape(-1, HALF_CHANNELS)
    for dy in range(3):
        product = mm_tn(cell_input(cells_d, [dy]), center)
        for k in range(3):
            keep_columns(
                g_wide,
                (dy * 3 + k) * 2 * HALF_CHANNELS,
                product[k * HALF_CHANNELS : (k + 1) * HALF_CHANNELS],
            )
    keep_columns(g_down, SKIP_ROW, mm_tn(fs_low[...].reshape(-1, C1), center))
    advance("wide")
    dfs[...] = mm_nt(center, skip_low[...]).reshape(dfs.shape)
    out = mm_nt(cell_input(cells_g, range(3)), wide_bwd[...])
    advance("conv_d")
    bucket_rows = lax.broadcasted_iota(jnp.int32, (NB, HALF_CHANNELS), 0)
    time_wide = jnp.zeros((NB, HALF_CHANNELS), f32)
    for n in range(images):
        v = h3[n]
        dy = out[n * half_pixels : (n + 1) * half_pixels] * slope(
            v * row_of(coef_w, 0, n, 0) + row_of(coef_w, 0, n, 1)
        )
        gain, shift, ca, cb, cd = norm_grad_coefs(
            fold(dy), fold(dy * v), gain_w(0), coef_w[0, n, 2], coef_w[0, n, 3], half_pixels
        )
        g_small[WIDE_NORM_ROW : WIDE_NORM_ROW + 1, :] += gain[0:1, :]
        g_small[WIDE_NORM_ROW + 1 : WIDE_NORM_ROW + 2, :] += shift[0:1, :]
        grad = dy * ca[0:1, :] + v * cb[0:1, :] + cd[0:1, :]
        time_wide = time_wide + jnp.where(bucket_rows == bucket(n), total(fold(grad)), 0.0)
        store_shifted(cells_g, n, 0, grad.reshape(HALF, HALF, HALF_CHANNELS))
    g_small[TIME_WIDE_ROW : TIME_WIDE_ROW + NB, :] = time_wide

    for c in range(2):
        g_rows[c * SMALL_ROWS : (c + 1) * SMALL_ROWS, :] = g_small[:, c * 128 : (c + 1) * 128]
    advance("gn_d")

    center = cells_g[:, 1, 1 : HALF + 1].reshape(-1, HALF_CHANNELS)
    for dy in range(3):
        product = mm_tn(cell_input(cells_c, [dy]), center)
        for k in range(3):
            keep_columns(g_down, (dy * 3 + k) * 2 * C1, product[k * C1 : (k + 1) * C1])
    advance("down")
    dnarrow[...] = mm_nt(cell_input(cells_g, range(3)), down_bwd[...]).reshape(dnarrow.shape)

    def up_parts(ref, n, i, size):
        here = pl.ds(i * size * HALF, size * HALF)
        g = ref[n, here].reshape(size, HALF, C1)
        lane_rows = lax.broadcasted_iota(jnp.int32, g.shape, 0) + i * size
        above = ref[n, pl.ds(jnp.maximum(i * size - 1, 0) * HALF, HALF)].reshape(1, HALF, C1)
        below = ref[n, pl.ds(jnp.minimum((i + 1) * size, HALF - 1) * HALF, HALF)].reshape(1, HALF, C1)
        above = jnp.where(lane_rows == 0, 0.0, jnp.concatenate([above, g[:-1]], axis=0))
        below = jnp.where(lane_rows == HALF - 1, 0.0, jnp.concatenate([g[1:], below], axis=0))
        result = []
        for rows in (0.375 * g + 0.125 * above, 0.375 * g + 0.125 * below):
            result.append(
                (
                    0.375 * rows + 0.125 * shift_cols(rows, 1),
                    0.375 * rows + 0.125 * shift_cols(rows, -1),
                )
            )
        return result

    def third_norm(n):
        size = HALF // 4
        scale = row_of(coef_n, 2, n, 0)
        offset = row_of(coef_n, 2, n, 1)

        def step(i, carry):
            sum_dy, sum_dyv = carry
            parts = up_parts(dnarrow, n, i, size)
            for b in range(2):
                g = jnp.stack([parts[0][b], parts[1][b]], axis=1).reshape(2 * size, HALF, C1)
                v = xs_full[n, b, pl.ds(i * 2 * size, 2 * size)]
                dy = g * slope(v * scale + offset)
                dy_full[n, b, pl.ds(i * 2 * size, 2 * size)] = dy
                sum_dy = sum_dy + fold(dy)
                sum_dyv = sum_dyv + fold(dy * v)
            return sum_dy, sum_dyv

        sum_dy, sum_dyv = lax.fori_loop(0, 4, step, (zero_n, zero_n))
        gain, shift, ca, cb, cd = norm_grad_coefs(
            sum_dy, sum_dyv, gain_n(4), coef_n[2, n, 2], coef_n[2, n, 3], full_pixels
        )
        g_late[4:5, :] += gain[0:1, :]
        g_late[5:6, :] += shift[0:1, :]
        advance("t%da" % n)

        def finish(i):
            parts = up_parts(dfs, n, i, size)
            for b in range(2):
                g = jnp.stack([parts[0][b], parts[1][b]], axis=1).reshape(2 * size, HALF, C1)
                here = pl.ds(i * 2 * size, 2 * size)
                v = xs_full[n, b, here]
                g = g + dy_full[n, b, here] * ca[0:1, :] + v * cb[0:1, :] + cd[0:1, :]
                store_planes(in_g, n, b, i * 2 * size, rounded(g) * root_half)

        each(4, finish)

    advance("narrow")
    for n in range(images):
        third_norm(n)
        advance("t%db" % n)

    def pair_gradient(planes, member):
        products = None
        for b in range(2):
            grads = jnp.concatenate([plane_block(in_g, EVEN + b, a + 1) for a in range(2)], axis=1)
            part = [mm_tn(grads, pair_input(planes, b, jjs)) for jjs in ((0, 1), (2, 3))]
            products = part if products is None else [p + q for p, q in zip(products, part)]
        for dy in range(3):
            blocks = []
            for a in range(2):
                jj = dy + a
                wide_part = products[jj // 2][a * C1 : (a + 1) * C1]
                blocks.append(wide_part[:, (jj % 2) * 3 * C1 : (jj % 2 + 1) * 3 * C1])
            both = blocks[0] + blocks[1]
            for k in range(3):
                row = (dy * 3 + k) * C1
                (g_pair_b if member else g_pair_a)[row : row + C1, :] = both[:, k * C1 : (k + 1) * C1].T

    def back_through(member, values, which, gain_row, last):
        for b in range(2):
            out = mm_nt(pair_input(in_g, b, range(4)), pair_bwd[member])
            for n in range(images):
                dy_full[n, b, pl.ds(0, RES)] = pair_rows(out, n)
        advance("b%dc" % member)
        bucket_rows = lax.broadcasted_iota(jnp.int32, (NB, C1), 0)

        def image(n):
            scale = row_of(coef_n, which, n, 0)
            offset = row_of(coef_n, which, n, 1)

            def step(i, carry):
                sum_dy, sum_dyv = carry
                here = pl.ds(i * ROWS, ROWS)
                for b in range(2):
                    v = values[n, b, here]
                    dy = dy_full[n, b, here] * slope(v * scale + offset)
                    if not last:
                        dy_full[n, b, here] = dy
                    sum_dy = sum_dy + fold(dy)
                    sum_dyv = sum_dyv + fold(dy * v)
                return sum_dy, sum_dyv

            sum_dy, sum_dyv = lax.fori_loop(0, steps, step, (zero_n, zero_n))
            gain, shift, ca, cb, cd = norm_grad_coefs(
                sum_dy, sum_dyv, gain_n(gain_row), coef_n[which, n, 2], coef_n[which, n, 3], full_pixels
            )
            g_late[gain_row : gain_row + 1, :] += gain[0:1, :]
            g_late[gain_row + 1 : gain_row + 2, :] += shift[0:1, :]
            if last:
                return

            def finish(i, carry):
                here = pl.ds(i * ROWS, ROWS)
                for b in range(2):
                    v = values[n, b, here]
                    g = dy_full[n, b, here] * ca[0:1, :] + v * cb[0:1, :] + cd[0:1, :]
                    carry = carry + fold(g)
                    store_planes(in_g, n, b, i * ROWS, g)
                return carry

            sums = total(lax.fori_loop(0, steps, finish, zero_n))
            g_late[TIME_NARROW_ROW : TIME_NARROW_ROW + NB, :] += jnp.where(
                bucket_rows == bucket(n), sums, 0.0
            )

        for n in range(images):
            image(n)
            advance("b%di%d" % (member, n))

    pair_gradient(in_b, 1)
    advance("pair_b")
    back_through(1, h1_full, 1, 2, False)
    pair_gradient(in_a, 0)
    advance("pair_a")
    back_through(0, x_full, 0, 0, True)
    pieces["late"] = Exchange(g_late[...], late_totals, arrived_late, late_sems, links.brief)
    advance("end")
    while any(piece.left() for piece in pieces.values()):
        for name, piece in pieces.items():
            if piece.left():
                piece.step()
    sum_late[...] = late_totals[len(links.brief)]


def main_call(dp_size, *operands):
    n = operands[1].shape[1]
    devices = 2 * dp_size
    counts = group_sizes(dp_size)
    orders = (counts[1], counts[0]) + (counts[1],) * 4
    grads = [padded(rows, devices, TILE) for rows in GRADS]
    sums = [(coded_rows(rows, devices), jnp.int16) for rows in GRADS]
    sums.append((padded(2 * SMALL_ROWS, devices, 8), f32))
    spaces = [message_rows(rows, order, TILE) for rows, order in zip(grads, orders)]
    small_space = message_rows(sums[-1][0], orders[-1], 0)
    stages = sum(size - 1 for size in counts[1])
    vm = pltpu.VMEM
    full = (n, 2, RES, HALF, C1)
    planes = (n, 4, RES + 2, HALF, C1)
    wide = HALF_CHANNELS
    square = (n, HALF * HALF, wide)
    moved = [vm(v.shape, v.dtype) for v in operands[1:4] + operands[5:11]]
    scratch = moved + [vm((rows, 128), f32) for rows in grads + [sums[-1][0]]]
    scratch += [vm((rows, 128), jnp.int16) for rows in spaces]
    scratch += [vm((rows, 128), jnp.int16) for rows in spaces] + [vm((small_space, 128), f32)]
    scratch += [pltpu.SemaphoreType.DMA((2, 2 * sum(size - 1 for size in order))) for order in orders]
    scratch += [
        vm((SMALL_ROWS, wide), f32),
        vm((LATE_ROWS, C1), f32),
        vm((len(counts[1]) + 1, NB, 128), f32),
        vm((sum(counts[1]), NB, 128), f32),
        vm((len(counts[1]) + 1, LATE_ROWS, 128), f32),
        vm((sum(counts[1]), LATE_ROWS, 128), f32),
        pltpu.SemaphoreType.DMA((2, 3)),
        pltpu.SemaphoreType.DMA((3,)),
        pltpu.SemaphoreType.DMA((2, stages)),
        pltpu.SemaphoreType.DMA((2, stages)),
        pltpu.SemaphoreType.DMA((6,)),
        vm((2, 12 * C1, 2 * C1), bf16),
        vm((2, 2 * C1, 12 * C1), bf16),
        vm((9 * C1, wide), bf16),
        vm((C1, 9 * wide), bf16),
        vm((9 * wide, wide), bf16),
        vm((wide, 9 * wide), bf16),
        vm((C1, wide), bf16),
        vm((wide, 4 * wide), bf16),
        vm((HEAD_ROWS, wide), f32),
        vm(full, f32),
        vm(full, f32),
        vm(full, f32),
        vm((n, 2, RES + 2, HALF, C1), f32),
        vm(planes, bf16),
        vm(planes, bf16),
        vm(planes, bf16),
        vm((ROWS * RES, C1), f32),
        vm((n, 3, HALF + 2, HALF, C1), bf16),
        vm((n, 3, HALF + 2, HALF, wide), bf16),
        vm((n, 3, HALF + 2, HALF, wide), bf16),
        vm((n, HALF * HALF, C1), bf16),
        vm((n, HALF * HALF, C1), f32),
        vm(square, f32),
        vm(square, f32),
        vm(square, f32),
        vm(square, bf16),
        vm((n, HALF * HALF, 3 * wide), bf16),
        vm(square, f32),
        vm(square, bf16),
        vm(square, bf16),
        vm(square, bf16),
        vm(square, f32),
        vm(square, bf16),
        vm((n, HALF * HALF, 3 * wide), bf16),
        vm((n, HALF * HALF, C1), f32),
        vm((3, n, 4, 8, C1), f32),
        vm((3, n, 4, 8, wide), f32),
    ]
    whole = pl.BlockSpec(memory_space=pltpu.VMEM)
    anywhere = pl.BlockSpec(memory_space=pl.ANY)
    return pl.pallas_call(
        functools.partial(main_kernel, dp_size),
        out_shape=[jax.ShapeDtypeStruct((rows, 128), dtype) for rows, dtype in sums + [(LATE_ROWS, f32), (NB, f32)]],
        in_specs=[pl.BlockSpec(memory_space=pltpu.SMEM)]
        + [anywhere] * 3
        + [whole]
        + [anywhere] * 6
        + [whole] * 3,
        out_specs=[whole] * (len(sums) + 2),
        scratch_shapes=scratch,
        compiler_params=pltpu.CompilerParams(
            collective_id=0, has_side_effects=True, vmem_limit_bytes=VMEM_LIMIT
        ),
        cost_estimate=pl.CostEstimate(flops=8 * 10**9, bytes_accessed=12 * 10**6, transcendentals=0),
    )(*operands)


PIECE_NAMES = ("attn", "wide", "down", "pair_b", "pair_a", "small")
SCHEDULE = {
    "attn": ("attn",),
    "wide": ("wide", "attn"),
    "gn_d": ("small", "wide"),
    "down": ("down", "small"),
    "t0a": ("down", "attn"),
    "t1a": ("wide",),
    "t1b": ("small",),
    "pair_b": ("pair_b",),
    "b1c": ("attn",),
    "b1i0": ("pair_b", "down", "small", "wide"),
    "pair_a": ("pair_a",),
    "b0c": ("attn",),
    "b0i0": ("pair_a", "pair_b"),
    "end": ("late", "down", "small", "late", "wide", "attn", "pair_b", "attn", "pair_a", "down", "small", "late", "small", "wide", "pair_b", "pair_a", "down", "late", "wide", "down", "pair_a", "pair_b", "pair_b", "wide", "wide", "pair_a", "pair_a"),
}


def group_sizes(dp_size):
    bits = (dp_size - 1).bit_length()
    far = []
    k = 2
    while k < bits:
        far.append(1 << min(2, bits - k))
        k += 2
    return [2, 2, 2] + far, [2, 4] + far


class Links:
    def __init__(self, dp_size):
        dp = lax.axis_index("dp")
        sp = lax.axis_index("sp")
        core = dp % 2
        near = (dp // 2) % 2

        def along(unit, size):
            place = (dp // unit) % size
            return place, [(dp + unit * ((place + r) % size - place), sp) for r in range(1, size)]

        def pick(first, other):
            return first + core * (other - first)

        across = (dp, 1 - sp)
        beside = (dp + 2 * (1 - 2 * near), sp)
        second = (pick(near, sp), [(pick(beside[0], dp), pick(sp, 1 - sp))])
        third = (pick(sp, near), [(pick(dp, beside[0]), pick(1 - sp, sp))])
        place = 2 * near + sp
        square = []
        for r in range(1, 4):
            member = (place + r) % 4
            square.append((dp + 2 * (member // 2 - near), member % 2))
        far = []
        unit = 4
        for size in group_sizes(dp_size)[1][2:]:
            far.append(along(unit, size))
            unit *= size
        self.full = [along(1, 2), second, third] + far
        self.brief = [along(1, 2), (place, square)] + far
        self.all = [other for _, others in self.brief for other in others]

    def greet(self):
        barrier = pltpu.get_barrier_semaphore()
        for other in self.all:
            pl.semaphore_signal(barrier, inc=1, device_id=other, device_id_type=MESH)
        pl.semaphore_wait(barrier, len(self.all))


def send(source, target, sems, index, landing, other):
    return pltpu.make_async_remote_copy(
        src_ref=source,
        dst_ref=target,
        send_sem=sems.at[0, index],
        recv_sem=sems.at[1, landing],
        device_id=other,
        device_id_type=MESH,
    )


class Exchange:
    def __init__(self, value, totals, arrived, sems, stages):
        totals[0] = value
        self.totals, self.arrived, self.sems, self.stages = totals, arrived, sems, stages
        self.t = self.base = self.index = 0
        self.copies = []

    def left(self):
        return self.t <= len(self.stages)

    def step(self):
        if self.copies:
            for copy in self.copies:
                copy.wait()
            size = len(self.copies) + 1
            total_now = self.arrived[self.base]
            for m in range(1, size):
                total_now = total_now + self.arrived[self.base + m]
            self.totals[self.t] = total_now
            self.base += size
            self.index += size - 1
            self.copies = []
        if self.t < len(self.stages):
            place, others = self.stages[self.t]
            mine = self.totals.at[self.t]
            landing = self.arrived.at[self.base + place]
            for r, other in enumerate(others):
                copy = send(mine, landing, self.sems, self.index + r, self.index + len(others) - 1 - r, other)
                copy.start()
                self.copies.append(copy)
            self.arrived[self.base + place] = self.totals[self.t]
        self.t += 1

    def finish(self, out):
        while self.left():
            self.step()
        out[...] = self.totals[len(self.stages)]


def count_pixels(buckets, mask):
    rows = lax.broadcasted_iota(jnp.int32, (NB, 128), 0)
    counted = jnp.zeros((NB, 128), f32)
    images = mask.shape[1]
    for i in range(2 * images):
        pixels = mask[i // images, i % images].astype(f32)
        number = jnp.sum(jnp.sum(pixels, axis=0, keepdims=True), axis=1, keepdims=True)
        counted = counted + jnp.where(rows == buckets[i], number, 0.0)
    return counted


def chunk_of(rows):
    return next(c for c in (128, 96, 80, 64, 48, 32, 16, 8) if rows % c == 0)


def aligned(row, tile):
    return row if isinstance(row, int) else pl.multiple_of(row, tile)


def encode(source, first, rows, target, base):
    size = chunk_of(rows)

    def largest(i, carry):
        v = jnp.abs(source[pl.ds(aligned(first + i * size, 8), size), :])
        return jnp.maximum(carry, jnp.max(v.reshape(-1, 8, 128), axis=0))

    bound = lax.fori_loop(0, rows // size, largest, jnp.zeros((8, 128), f32))
    bound = jnp.max(bound, axis=0, keepdims=True)
    power = jnp.floor(jnp.log2(jnp.maximum(bound, 1e-30))) + 1.0
    scale = jnp.exp2(15.0 - power)

    def step(i):
        v = source[pl.ds(aligned(first + i * size, 8), size), :] * scale
        v = jnp.clip(jnp.round(v), -32767.0, 32767.0)
        target[pl.ds(aligned(base + i * size, TILE), size), :] = v.astype(jnp.int32).astype(jnp.int16)

    each(rows // size, step)
    target[pl.ds(aligned(base + rows, TILE), TILE), :] = jnp.broadcast_to(
        power.astype(jnp.int32), (TILE, 128)
    ).astype(jnp.int16)


def decode(source, base, rows):
    power = source[pl.ds(aligned(base + rows, TILE), TILE), :].astype(jnp.int32).astype(f32)
    return jnp.exp2(power[0:1, :] - 15.0)


def message_rows(rows, sizes, tile):
    needed = 0
    for size in sizes:
        rows //= size
        needed += (size - 1) * (rows + tile)
    return needed


class Piece:
    def __init__(self, source, outgoing, arrived, out, sems, stages):
        self.source, self.outgoing, self.arrived, self.out, self.sems = source, outgoing, arrived, out, sems
        self.stages = stages
        self.tile = 0 if outgoing is None else TILE
        self.rows = source.shape[0]
        self.first = 0
        self.base = self.index = self.t = 0
        self.copies = []
        self.share = self.rows
        for _, others in stages:
            self.share //= len(others) + 1

    def left(self):
        return self.t <= 2 * len(self.stages)

    def step(self):
        count = len(self.stages)
        if 0 < self.t <= count:
            self.scatter_end(self.stages[self.t - 1])
        elif self.t > count:
            self.gather_end(self.stages[2 * count - self.t])
        if self.t == count:
            self.keep()
        if self.t < count:
            self.scatter_start(self.stages[self.t])
        elif self.t < 2 * count:
            self.gather_start(self.stages[2 * count - 1 - self.t])
        self.t += 1

    def scatter_start(self, stage):
        place, others = stage
        size = len(others) + 1
        rows = self.rows // size
        block = rows + self.tile
        for r, other in enumerate(others):
            part = self.first + ((place + r + 1) % size) * rows
            if self.tile:
                mine = self.base + r * block
                encode(self.source, part, rows, self.outgoing, mine)
                message = self.outgoing.at[pl.ds(mine, block)]
            else:
                message = self.source.at[pl.ds(aligned(part, 8), rows)]
            landing = size - 2 - r
            copy = send(
                message,
                self.arrived.at[pl.ds(self.base + landing * block, block)],
                self.sems,
                self.index + r,
                self.index + landing,
                other,
            )
            copy.start()
            self.copies.append(copy)

    def scatter_end(self, stage):
        place, others = stage
        size = len(others) + 1
        rows = self.rows // size
        block = rows + self.tile
        for copy in self.copies:
            copy.wait()
        first = self.first + place * rows
        scales = [decode(self.arrived, self.base + r * block, rows) if self.tile else 1.0 for r in range(size - 1)]
        chunk = chunk_of(rows)

        def add(i):
            here = pl.ds(aligned(first + i * chunk, 8), chunk)
            v = self.source[here, :]
            for r, scale in enumerate(scales):
                more = self.arrived[pl.ds(aligned(self.base + r * block + i * chunk, self.tile or 8), chunk), :]
                v = v + (more.astype(jnp.int32).astype(f32) * scale if self.tile else more)
            self.source[here, :] = v

        each(rows // chunk, add)
        self.first, self.rows = first, rows
        self.base += (size - 1) * block
        self.index += size - 1
        self.copies = []

    def keep(self):
        block = self.share + self.tile
        self.place = 0
        for place, others in self.stages:
            self.place = self.place * (len(others) + 1) + place
        self.first = self.place * block
        self.rows = block
        if self.tile:
            encode(self.source, self.place * self.share, self.share, self.out, self.first)
        else:
            self.out[pl.ds(aligned(self.first, 8), block), :] = self.source[
                pl.ds(aligned(self.first, 8), block), :
            ]

    def gather_start(self, stage):
        place, others = stage
        here = self.out.at[pl.ds(aligned(self.first, self.tile or 8), self.rows)]
        for r, other in enumerate(others):
            copy = send(here, here, self.sems, self.index + r, self.index + len(others) - 1 - r, other)
            copy.start()
            self.copies.append(copy)

    def gather_end(self, stage):
        place, others = stage
        size = len(others) + 1
        for copy in self.copies:
            copy.wait()
        self.copies = []
        self.index += size - 1
        self.first = self.first - place * self.rows
        self.rows = self.rows * size


def adamw(weight, grad, first, second, rate):
    first = beta_one * first + (1.0 - beta_one) * grad
    second = beta_two * second + (1.0 - beta_two) * grad * grad
    scale = rate / (1.0 - beta_one**STEP)
    root = jnp.sqrt(second * (1.0 / (1.0 - beta_two**STEP))) + adam_epsilon
    return weight * (1.0 - rate * decay_rate) - scale * first / root, first, second


def update_kernel(devices, *refs):
    count = len(GRADS)
    coded, (g_small, g_late, counts), refs = refs[:count], refs[count : count + 3], refs[count + 3 :]
    members = [refs[3 * i : 3 + 3 * i] for i in range(9)]
    outs = [refs[27 + 3 * i : 30 + 3 * i] for i in range(9)]
    loss_out, counts_out = refs[54:56]
    grads = refs[56:]
    g_attn, g_wide, g_down, g_pair_b, g_pair_a = grads
    for source, grad in zip(coded, grads):
        share = grad.shape[0] // devices

        def shares(i, source=source, grad=grad, share=share):
            base = i * (share + TILE)
            v = source[pl.ds(aligned(base, TILE), share), :].astype(jnp.int32).astype(f32)
            grad[pl.ds(aligned(i * share, 8), share), :] = v * decode(source, base, share)

        each(devices, shares)

    def small(row, rows, lanes):
        parts = [g_small[c * SMALL_ROWS + row : c * SMALL_ROWS + row + rows, :] for c in range(lanes // 128)]
        return parts[0] if len(parts) == 1 else jnp.concatenate(parts, axis=1)

    def blocks(member, grad, block_rows, base, count, start=0):
        size = 64

        def step(i):
            block = i // (block_rows // size)
            row = (i % (block_rows // size)) * size
            here = pl.ds(pl.multiple_of(start + block * block_rows + row, 8), size)
            columns = members[member][0].shape[1] // 128
            for c in range(columns):
                lanes = slice(c * 128, (c + 1) * 128)
                g = grad[pl.ds(pl.multiple_of(base + (block * columns + c) * block_rows + row, 8), size), :]
                w, m, v = (ref[here, lanes] for ref in members[member])
                for out, value in zip(outs[member], adamw(w, g, m, v, rate_matrix)):
                    out[here, lanes] = value

        each(count * block_rows // size, step)

    def single(member, index, grad, rate):
        w, m, v = (ref[index] for ref in members[member])
        for out, value in zip(outs[member], adamw(w, grad, m, v, rate)):
            out[index] = value

    blocks(0, g_pair_a, C1, 0, 9)
    blocks(0, g_pair_b, C1, 0, 9, 9 * C1)
    blocks(1, g_down, C1, 0, 9)
    blocks(2, g_wide, HALF_CHANNELS, 0, 9)
    blocks(3, g_down, C1, SKIP_ROW, 1)
    blocks(4, g_attn, HALF_CHANNELS, 0, 1)
    for tap in range(9):
        single(5, (tap,), small(tap * 8, 3, HALF_CHANNELS), rate_matrix)
    every = slice(None)
    single(6, (every, every), g_late[:6, :], rate_vector)
    single(7, (every, every), small(WIDE_NORM_ROW, 6, HALF_CHANNELS), rate_vector)
    single(8, (every, slice(0, C1)), g_late[TIME_NARROW_ROW : TIME_NARROW_ROW + NB, :], rate_vector)
    single(8, (every, slice(C1, None)), small(TIME_WIDE_ROW, NB, HALF_CHANNELS), rate_vector)
    loss_out[...] = g_small[LOSS_ROW : LOSS_ROW + 1, :]
    diagonal = lax.broadcasted_iota(jnp.int32, (NB, 128), 0) == lax.broadcasted_iota(jnp.int32, (NB, 128), 1)
    counts_out[...] = jnp.sum(jnp.where(diagonal, counts[...], 0.0), axis=0, keepdims=True)[:, :NB]


def update_call(devices, grads, members):
    whole = pl.BlockSpec(memory_space=pltpu.VMEM)
    flat = [v for member in members for v in member]
    return pl.pallas_call(
        functools.partial(update_kernel, devices),
        out_shape=[jax.ShapeDtypeStruct(v.shape, f32) for v in flat]
        + [jax.ShapeDtypeStruct((1, 128), f32), jax.ShapeDtypeStruct((1, NB), f32)],
        in_specs=[whole] * (len(grads) + len(flat)),
        out_specs=[whole] * (len(flat) + 2),
        scratch_shapes=[pltpu.VMEM((padded(rows, devices, TILE), 128), f32) for rows in GRADS],
        compiler_params=pltpu.CompilerParams(vmem_limit_bytes=VMEM_LIMIT),
    )(*grads, *flat)


def on_device(
    features,
    target,
    pixel_mask,
    buckets,
    conv_pair,
    down_conv,
    conv_wide,
    skip_proj,
    attn_proj,
    head_conv,
    norm_narrow,
    norm_wide,
    time_bias,
    conv_pair_mom,
    down_conv_mom,
    conv_wide_mom,
    skip_proj_mom,
    attn_proj_mom,
    head_conv_mom,
    norm_narrow_mom,
    norm_wide_mom,
    time_bias_mom,
    conv_pair_sq,
    down_conv_sq,
    conv_wide_sq,
    skip_proj_sq,
    attn_proj_sq,
    head_conv_sq,
    norm_narrow_sq,
    norm_wide_sq,
    time_bias_sq,
):
    dp_size = lax.axis_size("dp")
    images = features.shape[0] // 2

    def halves(tensor):
        return tensor.reshape((2, images) + tensor.shape[1:])

    def flat(tensor):
        return tensor.reshape(-1, tensor.shape[-1])

    def head_rows(tensor):
        return jnp.transpose(tensor, (0, 1, 3, 2)).reshape(9, 3, HALF_CHANNELS)

    params = (
        flat(conv_pair),
        flat(down_conv),
        flat(conv_wide),
        skip_proj,
        attn_proj,
        head_rows(head_conv),
        norm_narrow,
        norm_wide,
        time_bias,
    )
    firsts = (
        flat(conv_pair_mom),
        flat(down_conv_mom),
        flat(conv_wide_mom),
        skip_proj_mom,
        attn_proj_mom,
        head_rows(head_conv_mom),
        norm_narrow_mom,
        norm_wide_mom,
        time_bias_mom,
    )
    seconds = (
        flat(conv_pair_sq),
        flat(down_conv_sq),
        flat(conv_wide_sq),
        skip_proj_sq,
        attn_proj_sq,
        head_rows(head_conv_sq),
        norm_narrow_sq,
        norm_wide_sq,
        time_bias_sq,
    )
    masks = halves(pixel_mask)
    summed = main_call(
        dp_size,
        buckets,
        halves(features),
        halves(jnp.transpose(target, (0, 3, 1, 2))),
        masks,
        masks,
        *params,
    )
    results = update_call(2 * dp_size, summed, list(zip(params, firsts, seconds)))
    shaped = []
    for member, like in enumerate((conv_pair, down_conv, conv_wide, skip_proj, attn_proj)):
        shaped.extend(v.reshape(like.shape) for v in results[3 * member : 3 * member + 3])
    for v in results[15:18]:
        shaped.append(jnp.transpose(v.reshape(3, 3, 3, HALF_CHANNELS), (0, 1, 3, 2)))
    shaped.extend(results[18:27])
    return (results[27][0, 0], results[28].reshape(NB)) + tuple(shaped)


def solution(mesh):
    placed = (
        P("dp", "sp", None, None),
        P("dp", "sp", None, None),
        P("dp", "sp", None),
        P("dp"),
        P(),
        P(),
        P(),
        P(),
        P(),
        P(),
        P(),
        P(),
        P(),
        P(),
        P(),
        P(),
        P(),
        P(),
        P(),
        P(),
        P(),
        P(),
        P(),
        P(),
        P(),
        P(),
        P(),
        P(),
        P(),
        P(),
        P(),
    )
    return jax.shard_map(
        on_device,
        mesh=mesh,
        in_specs=placed,
        out_specs=(
            P(),
            P(),
            P(),
            P(),
            P(),
            P(),
            P(),
            P(),
            P(),
            P(),
            P(),
            P(),
            P(),
            P(),
            P(),
            P(),
            P(),
            P(),
            P(),
            P(),
            P(),
            P(),
            P(),
            P(),
            P(),
            P(),
            P(),
            P(),
            P(),
        ),
        check_vma=False,
    )
```

```python
import functools

import jax
import jax.numpy as jnp
from jax import lax
from jax.experimental import pallas as pl
from jax.experimental.pallas import tpu as pltpu
from jax.sharding import PartitionSpec as P

C1 = 128
HALF_CHANNELS = 256
GROUPS = 32
RES = 32
HALF = 16
NB = 8
STEP = 10
MESH = pl.DeviceIdType.MESH
MAIN_LIMIT = 41 * 1024 * 1024
UPDATE_LIMIT = 26 * 1024 * 1024

epsilon = 1e-05
root_half = 0.7071067811865476
beta_one = 0.9
beta_two = 0.999
adam_epsilon = 1e-08
decay_rate = 0.1
rate_matrix = 0.03
rate_vector = 0.5
logit_scale = HALF_CHANNELS ** (-0.5)
ROWS = 8

bf16 = jnp.bfloat16
f32 = jnp.float32

EVEN, ODD, ODD_LEFT, EVEN_RIGHT = 0, 1, 2, 3
TAPS = ((ODD_LEFT, EVEN, ODD), (EVEN, ODD, EVEN_RIGHT))


def rounded(v):
    return v.astype(bf16).astype(f32)


def silu(t):
    return t * jax.nn.sigmoid(t)


def slope(t):
    s = jax.nn.sigmoid(t)
    return s * (1.0 + t * (1.0 - s))


def mm(a, b):
    return lax.dot_general(a, b, (((1,), (0,)), ((), ())), preferred_element_type=f32)


def mm_nt(a, b):
    return lax.dot_general(a, b, (((1,), (1,)), ((), ())), preferred_element_type=f32)


def mm_tn(a, b):
    return lax.dot_general(a, b, (((0,), (0,)), ((), ())), preferred_element_type=f32)


def fold(v):
    return jnp.sum(v.reshape(-1, 8, v.shape[-1]), axis=0)


def total(v):
    return jnp.broadcast_to(jnp.sum(v, axis=0, keepdims=True), v.shape)


def group_sum(v, size):
    lanes = v.shape[-1]
    lane = lax.broadcasted_iota(jnp.int32, v.shape, 1)
    step = 1
    while step < size:
        other = jnp.where(
            (lane & step) == 0, pltpu.roll(v, lanes - step, 1), pltpu.roll(v, step, 1)
        )
        v = v + other
        step *= 2
    return v


def norm_coefs(sums, squares, gain, shift, pixels):
    size = sums.shape[-1] // GROUPS
    count = pixels * size
    mean = group_sum(total(sums), size) / count
    power = group_sum(total(squares), size) / count
    inv = lax.rsqrt(power - mean * mean + epsilon)
    scale = inv * gain
    return scale, shift - mean * scale, mean, inv


def norm_grad_coefs(sum_dy, sum_dyv, gain, mean, inv, pixels):
    size = sum_dy.shape[-1] // GROUPS
    count = pixels * size
    first = total(sum_dy)
    second = (total(sum_dyv) - mean * first) * inv
    one = group_sum(first * gain, size) / count
    two = group_sum(second * gain, size) / count
    b = -inv * inv * two
    return second, first, inv * gain, b, -inv * one - mean * b


def shift_cols(v, step):
    col = lax.broadcasted_iota(jnp.int32, v.shape, 1)
    if step == 1:
        return jnp.where(col == 0, 0.0, pltpu.roll(v, 1, 1))
    return jnp.where(col == HALF - 1, 0.0, pltpu.roll(v, HALF - 1, 1))


def store_planes(planes, n, b, r0, v):
    rows = v.shape[0]
    v = v.astype(bf16).astype(f32)
    for plane, value in (
        (EVEN + b, v),
        (ODD_LEFT if b == 1 else EVEN_RIGHT, shift_cols(v, 1 if b == 1 else -1)),
    ):
        planes[n, plane, pl.ds(r0 + 1, rows)] = value.astype(bf16)


def store_shifted(cells, n, r0, v):
    rows = v.shape[0]
    v = v.astype(bf16).astype(f32)
    for tap, value in ((0, shift_cols(v, 1)), (1, v), (2, shift_cols(v, -1))):
        cells[n, tap, pl.ds(r0 + 1, rows)] = value.astype(bf16)


def plane_block(planes, tap, jj):
    return planes[:, tap, pl.ds(jj, HALF, stride=2)].reshape(-1, planes.shape[-1])


def pair_input(planes, b, jjs):
    return jnp.concatenate([plane_block(planes, tap, jj) for jj in jjs for tap in TAPS[b]], axis=1)


def cell_input(cells, dys):
    return jnp.concatenate(
        [
            cells[:, tap, dy : dy + HALF].reshape(-1, cells.shape[-1])
            for dy in dys
            for tap in range(3)
        ],
        axis=1,
    )


def each(count, body):
    def step(i, carry):
        body(i)
        return carry

    lax.fori_loop(0, count, step, 0)


def prepare_weights(pair, down, wide, skip, attn, head, pair_fwd, pair_bwd, down_fwd, down_bwd, wide_fwd, wide_bwd, skip_low, attn_low, head_low):
    nothing = jnp.zeros((C1, C1), bf16)
    for member in range(2):
        for jj in range(4):
            for k in range(3):
                block = (jj * 3 + k) * C1
                for a in range(2):
                    dy = jj - a
                    inside = 0 <= dy < 3
                    row = (dy * 3 + k) * C1
                    back = ((2 - dy) * 3 + (2 - k)) * C1
                    pair_fwd[member, block : block + C1, a * C1 : a * C1 + C1] = (
                        pair[member][row : row + C1, :].astype(bf16) if inside else nothing
                    )
                    pair_bwd[member, a * C1 : a * C1 + C1, block : block + C1] = (
                        pair[member][back : back + C1, :].astype(bf16) if inside else nothing
                    )
    wide_channels = HALF_CHANNELS
    for tap in range(9):
        low = down[tap * C1 : tap * C1 + C1, :].astype(bf16)
        down_fwd[tap * C1 : tap * C1 + C1, :] = low
        down_bwd[:, (8 - tap) * wide_channels : (9 - tap) * wide_channels] = low
        low = wide[tap * wide_channels : (tap + 1) * wide_channels, :].astype(bf16)
        wide_fwd[tap * wide_channels : (tap + 1) * wide_channels, :] = low
        wide_bwd[:, (8 - tap) * wide_channels : (9 - tap) * wide_channels] = low
    skip_low[...] = skip[...].astype(bf16)
    attn_low[...] = attn[...].astype(bf16)
    head_low[...] = jnp.zeros(head_low.shape, f32)
    for tap in range(9):
        head_low[tap * 8 : tap * 8 + 3, :] = rounded(head[tap])


def split_three(v):
    high = v.astype(bf16)
    rest = v - high.astype(f32)
    middle = rest.astype(bf16)
    return high, middle, (rest - middle.astype(f32)).astype(bf16)


def lane_shift(v, step):
    lane = lax.broadcasted_iota(jnp.int32, v.shape, 1)
    j = lane & (HALF - 1)
    if step == 1:
        keep = j < HALF - 1
    elif step == -1:
        keep = j > 0
    elif step == HALF:
        keep = lane < HALF * (HALF - 1)
    else:
        keep = lane >= HALF
    return jnp.where(keep, pltpu.roll(v, (-step) % v.shape[-1], 1), 0.0)


def head_forward(table):
    cols = [
        [
            lane_shift(table[dy][0], -1) + table[dy][1] + table[dy][2],
            table[dy][0] + table[dy][1] + lane_shift(table[dy][2], 1),
        ]
        for dy in range(3)
    ]
    return [
        [
            lane_shift(cols[0][b], -HALF) + cols[1][b] + cols[2][b]
            if a == 0
            else cols[0][b] + cols[1][b] + lane_shift(cols[2][b], HALF)
            for b in range(2)
        ]
        for a in range(2)
    ]


def head_backward(grad):
    rows = [
        [
            lane_shift(grad[0][b], HALF) + grad[1][b],
            grad[0][b] + grad[1][b],
            grad[0][b] + lane_shift(grad[1][b], -HALF),
        ]
        for b in range(2)
    ]
    return [
        [
            lane_shift(rows[0][dy], 1) + rows[1][dy],
            rows[0][dy] + rows[1][dy],
            rows[0][dy] + lane_shift(rows[1][dy], -1),
        ]
        for dy in range(3)
    ]


def keep_columns(ref, row, v):
    for c in range(v.shape[1] // 128):
        ref[row + c * v.shape[0] : row + (c + 1) * v.shape[0], :] = v[:, c * 128 : (c + 1) * 128]


HEAD_ROWS = 72
WIDE_NORM_ROW = 72
LOSS_ROW = 78
TIME_WIDE_ROW = 80
SMALL_ROWS = 96
TIME_NARROW_ROW = 8
LATE_ROWS = 16
SKIP_ROW = 18 * C1
ATTN_ROWS = 8 * HALF_CHANNELS
WIDE_ROWS = 18 * HALF_CHANNELS
DOWN_ROWS = 20 * C1
PAIR_ROWS = 9 * C1
GRADS = (ATTN_ROWS, WIDE_ROWS, DOWN_ROWS, PAIR_ROWS, PAIR_ROWS)
TILE = 16


def padded(rows, devices, tile):
    return -(-rows // (devices * tile)) * devices * tile


def coded_rows(rows, devices):
    return padded(rows, devices, TILE) + devices * TILE


def main_kernel(
    dp_size,
    buckets, features, target_rows, mask_rows, pair_all, down_all, wide_all, skip_all, attn_all, head_all,
    narrow_all, gains_all, time_all,
    sum_attn, sum_wide, sum_down, sum_pair_b, sum_pair_a, sum_small, sum_late, counts,
    x_in, target, mask, down, wide, skip, attn, head, gains_narrow, gains_wide, time_bias, mask_local,
    g_attn, g_wide, g_down, g_pair_b, g_pair_a, g_rows,
    out_attn, out_wide, out_down, out_pair_b, out_pair_a,
    in_attn, in_wide, in_down, in_pair_b, in_pair_a, in_small,
    sems_attn, sems_wide, sems_down, sems_pair_b, sems_pair_a, sems_small,
    g_small, g_late,
    totals, arrived_totals, late_totals, arrived_late, image_sems, local_sems, count_sems, late_sems, weight_sems,
    pair_fwd, pair_bwd, down_fwd, down_bwd, wide_fwd, wide_bwd, skip_low, attn_low, head_low,
    x_full, h1_full, xs_full, dy_full, in_a, in_b, in_g, flat,
    cells_c, cells_d, cells_g, fs_low, dfs, h3, x2, x3, n5, qkv, probs, probs_low, att, a6, dwide, dout, dqkv, dnarrow,
    coef_n, coef_w,
):
    loads = [
        pltpu.make_async_copy(source, ref, weight_sems.at[i])
        for i, (source, ref) in enumerate(
            (
                (pair_all.at[:PAIR_ROWS], g_pair_a.at[:PAIR_ROWS]),
                (pair_all.at[PAIR_ROWS:], g_pair_b.at[:PAIR_ROWS]),
                (down_all, down),
                (wide_all, wide),
                (skip_all, skip),
                (attn_all, attn),
                (head_all, head),
                (narrow_all, gains_narrow),
                (gains_all, gains_wide),
                (time_all, time_bias),
                (mask_rows, mask_local),
            )
        )
    ]
    links = Links(dp_size)
    links.greet()
    for copy in loads[::-1]:
        copy.start()
    loads.pop().wait()
    counted = count_pixels(buckets, mask_local)
    links.meet()
    here = (lax.axis_index("dp"), 1 - lax.axis_index("sp"))
    moved = ((features, x_in), (target_rows, target), (mask_rows, mask))
    side = lax.axis_index("sp")
    arrivals = [
        send(source.at[1 - side], out.at[side], image_sems, i, i, here) for i, (source, out) in enumerate(moved)
    ]
    for copy in arrivals:
        copy.start()
    keeps = [
        pltpu.make_async_copy(source.at[side], out.at[side], local_sems.at[i])
        for i, (source, out) in enumerate(moved)
    ]
    for copy in keeps:
        copy.start()
    images = x_in.shape[1]
    position = lax.axis_index("sp")
    steps = RES // ROWS
    full_pixels = RES * RES
    half_pixels = HALF * HALF
    zero_n = jnp.zeros((8, C1), f32)
    zero_w = jnp.zeros((8, HALF_CHANNELS), f32)

    def bucket(n):
        return buckets[position * images + n]

    def gain_n(row):
        return jnp.broadcast_to(gains_narrow[row : row + 1, :], (8, C1))

    def gain_w(row):
        return jnp.broadcast_to(gains_wide[row : row + 1, :], (8, HALF_CHANNELS))

    def keep_coefs(ref, which, n, values):
        for kind in range(4):
            ref[which, n, kind] = values[kind]

    def row_of(ref, which, n, kind):
        return ref[which, n, kind, 0:1, :]

    counting = Exchange(counted, totals, arrived_totals, count_sems, links.brief)
    counting.step()
    sources = (g_attn, g_wide, g_down, g_pair_b, g_pair_a, g_rows)
    outgoing = (out_attn, out_wide, out_down, out_pair_b, out_pair_a, None)
    incoming = (in_attn, in_wide, in_down, in_pair_b, in_pair_a, in_small)
    outs = (sum_attn, sum_wide, sum_down, sum_pair_b, sum_pair_a, sum_small)
    sems = (sems_attn, sems_wide, sems_down, sems_pair_b, sems_pair_a, sems_small)
    orders = (links.brief, links.full, links.brief, links.brief, links.brief, links.brief)
    pieces = dict(zip(PIECE_NAMES, (Piece(*parts) for parts in zip(sources, outgoing, incoming, outs, sems, orders))))

    def advance(point):
        for name in SCHEDULE.get(point, ()):
            pieces[name].step()

    for rows, ref in zip(GRADS + (2 * SMALL_ROWS,), sources):
        if ref.shape[0] > rows:
            ref[rows:, :] = jnp.zeros((ref.shape[0] - rows, 128), f32)
    for copy in loads:
        copy.wait()
    prepare_weights((g_pair_a, g_pair_b), down, wide, skip, attn, head, pair_fwd, pair_bwd, down_fwd, down_bwd, wide_fwd, wide_bwd, skip_low, attn_low, head_low)
    g_small[...] = jnp.zeros(g_small.shape, f32)
    g_late[...] = jnp.zeros(g_late.shape, f32)
    for planes in (in_a, in_b, in_g):
        edge = jnp.zeros((images, 4, HALF, C1), bf16)
        planes[:, :, 0] = edge
        planes[:, :, RES + 1] = edge
    for cells in (cells_c, cells_d, cells_g):
        edge = jnp.zeros((images, 3, HALF, cells.shape[-1]), bf16)
        cells[:, :, 0] = edge
        cells[:, :, HALF + 1] = edge

    for copy in keeps + arrivals:
        copy.wait()
    counting.step()

    def load_image(n):
        def step(i, carry):
            sums, squares = carry
            half = i // 2
            v = x_in[half, n, pl.ds((i % 2) * ROWS, ROWS)].astype(f32)
            flat[...] = v.reshape(ROWS * RES, C1)
            for b in range(2):
                w = flat[pl.ds(b, ROWS * HALF, stride=2), :].reshape(ROWS, HALF, C1)
                x_full[n, b, pl.ds(i * ROWS, ROWS)] = w
                sums = sums + fold(w)
                squares = squares + fold(w * w)
            return sums, squares

        sums, squares = lax.fori_loop(0, steps, step, (zero_n, zero_n))
        keep_coefs(coef_n, 0, n, norm_coefs(sums, squares, gain_n(0), gain_n(1), full_pixels))

    each(images, load_image)

    def activate(values, planes, which):
        def image(n):
            scale = row_of(coef_n, which, n, 0)
            offset = row_of(coef_n, which, n, 1)

            def step(i):
                for b in range(2):
                    v = values[n, b, pl.ds(i * ROWS, ROWS)]
                    store_planes(planes, n, b, i * ROWS, silu(v * scale + offset))

            each(steps, step)

        each(images, image)

    def pair_rows(result, n):
        part = result[n * half_pixels : (n + 1) * half_pixels].reshape(HALF, 1, HALF, 2 * C1)
        return jnp.concatenate([part[..., :C1], part[..., C1:]], axis=1).reshape(RES, HALF, C1)

    activate(x_full, in_a, 0)
    counting.step()
    for b in range(2):
        out = mm(pair_input(in_a, b, range(4)), pair_fwd[0])
        for n in range(images):
            h1_full[n, b] = pair_rows(out, n)

    def first_hidden(n):
        bias = time_bias[pl.ds(bucket(n), 1), :][:, :C1]

        def step(i, carry):
            sums, squares = carry
            for b in range(2):
                v = h1_full[n, b, pl.ds(i * ROWS, ROWS)] + bias
                h1_full[n, b, pl.ds(i * ROWS, ROWS)] = v
                sums = sums + fold(v)
                squares = squares + fold(v * v)
            return sums, squares

        sums, squares = lax.fori_loop(0, steps, step, (zero_n, zero_n))
        keep_coefs(coef_n, 1, n, norm_coefs(sums, squares, gain_n(2), gain_n(3), full_pixels))

    each(images, first_hidden)
    activate(h1_full, in_b, 1)
    counting.step()
    for b in range(2):
        out = mm(pair_input(in_b, b, range(4)), pair_fwd[1])
        for n in range(images):
            xs_full[n, b] = pair_rows(out, n)

    def first_out(n):
        def step(i, carry):
            sums, squares = carry
            for b in range(2):
                v = xs_full[n, b, pl.ds(i * ROWS, ROWS)]
                v = rounded((x_full[n, b, pl.ds(i * ROWS, ROWS)] + v) * root_half)
                xs_full[n, b, pl.ds(i * ROWS, ROWS)] = v
                sums = sums + fold(v)
                squares = squares + fold(v * v)
            return sums, squares

        sums, squares = lax.fori_loop(0, steps, step, (zero_n, zero_n))
        keep_coefs(coef_n, 2, n, norm_coefs(sums, squares, gain_n(4), gain_n(5), full_pixels))

    each(images, first_out)

    counting.step()

    def fir_down_image(n):
        scale = row_of(coef_n, 2, n, 0)
        offset = row_of(coef_n, 2, n, 1)
        for b in range(2):
            dy_full[n, b, 0] = jnp.zeros((HALF, C1), f32)
            dy_full[n, b, RES + 1] = jnp.zeros((HALF, C1), f32)

        def act_step(i):
            for b in range(2):
                v = xs_full[n, b, pl.ds(i * ROWS, ROWS)]
                dy_full[n, b, pl.ds(i * ROWS + 1, ROWS)] = silu(v * scale + offset)

        each(steps, act_step)

        def columns(rows):
            even, odd = rows
            return (
                0.125 * (shift_cols(odd, 1) + shift_cols(even, -1)) + 0.375 * (even + odd)
            )

        def taps(ref, b, r0, size):
            return [ref[n, b, pl.ds(r0 + t, size, stride=2)] for t in range(4)]

        def down_step(i):
            size = HALF // 2
            rows = []
            for b in range(2):
                t = taps(dy_full, b, 2 * size * i, size)
                rows.append(0.125 * (t[0] + t[3]) + 0.375 * (t[1] + t[2]))
            store_shifted(cells_c, n, i * size, columns(rows))

        each(2, down_step)
        for b in range(2):
            dy_full[n, b, pl.ds(1, RES)] = xs_full[n, b]

        def skip_step(i):
            size = HALF // 2
            rows = []
            for b in range(2):
                t = taps(dy_full, b, 2 * size * i, size)
                rows.append(0.125 * (t[0] + t[3]) + 0.375 * (t[1] + t[2]))
            fs_low[n, pl.ds(i * size * HALF, size * HALF)] = (
                columns(rows).reshape(size * HALF, C1).astype(bf16)
            )

        each(2, skip_step)

    each(images, fir_down_image)

    def wide_stats(v, which, n, row):
        values = norm_coefs(fold(v), fold(v * v), gain_w(row), gain_w(row + 1), half_pixels)
        keep_coefs(coef_w, which, n, values)
        return values[0][0:1, :], values[1][0:1, :]

    out = mm(cell_input(cells_c, range(3)), down_fwd[...])
    for n in range(images):
        v = out[n * half_pixels : (n + 1) * half_pixels] + time_bias[pl.ds(bucket(n), 1), :][:, C1:]
        h3[n] = v
        scale, offset = wide_stats(v, 0, n, 0)
        store_shifted(cells_d, n, 0, silu(v * scale + offset).reshape(HALF, HALF, HALF_CHANNELS))
    out = mm(cell_input(cells_d, range(3)), wide_fwd[...])
    out = out + mm(fs_low[...].reshape(-1, C1), skip_low[...])
    for n in range(images):
        v = out[n * half_pixels : (n + 1) * half_pixels] * root_half
        x2[n] = v
        scale, offset = wide_stats(v, 1, n, 2)
        n5[n] = (v * scale + offset).astype(bf16)
        qkv[n] = mm(n5[n], attn_low[:, : 3 * HALF_CHANNELS]).astype(bf16)
        q = qkv[n, :, :HALF_CHANNELS]
        k = qkv[n, :, HALF_CHANNELS : 2 * HALF_CHANNELS]
        w = qkv[n, :, 2 * HALF_CHANNELS :]
        logits = mm_nt(q, k) * logit_scale
        powers = jnp.exp(logits - jnp.max(logits, axis=1, keepdims=True))
        weights = powers / jnp.sum(powers, axis=1, keepdims=True)
        probs[n] = weights
        probs_low[n] = weights.astype(bf16)
        att[n] = mm(probs_low[n], w).astype(bf16)
        v = (v + mm(att[n], attn_low[:, 3 * HALF_CHANNELS :])) * root_half
        x3[n] = v
        scale, offset = wide_stats(v, 2, n, 4)
        a6[n] = silu(v * scale + offset).astype(bf16)

    counting.finish(counts)

    lane = lax.broadcasted_iota(jnp.int32, (RES, 2 * half_pixels), 1)
    source = lax.broadcasted_iota(jnp.int32, (RES, 2 * half_pixels), 0)
    picks = (source == 2 * (lane & (HALF - 1)) + (lane >> 8)).astype(bf16)
    row_lane = (lax.broadcasted_iota(jnp.int32, (HALF, 2 * half_pixels), 1) & (half_pixels - 1)) >> 4
    row_source = lax.broadcasted_iota(jnp.int32, (HALF, 2 * half_pixels), 0)
    component = lax.broadcasted_iota(jnp.int32, (8, half_pixels), 0)

    def spread(halves):
        moved = [mm(half, picks) for half in halves]
        rows = []
        for a in range(2):
            picked = sum(
                jnp.where(2 * row_lane + a == row_source + HALF * h, moved[h], 0.0)
                for h in range(2)
            )
            row = jnp.sum(picked, axis=0, keepdims=True)
            rows.append([row[:, :half_pixels], row[:, half_pixels:]])
        return rows

    loss = jnp.zeros((1, half_pixels), f32)
    head_grad = jnp.zeros((HEAD_ROWS, HALF_CHANNELS), f32)
    for n in range(images):
        moved = mm_nt(head_low[...].astype(bf16), a6[n])
        pred = head_forward(
            [[moved[(dy * 3 + dx) * 8 : (dy * 3 + dx) * 8 + 8] for dx in range(3)] for dy in range(3)]
        )
        wanted = [spread([target[h, n, c] for h in range(2)]) for c in range(3)]
        counted = spread([mask[h, n].astype(f32).astype(bf16) for h in range(2)])
        per_image = 1.0 / counts[pl.ds(bucket(n), 1), :]
        per_image = jnp.concatenate([per_image, per_image], axis=1)
        grad_pred = [[None, None], [None, None]]
        for a in range(2):
            for b in range(2):
                goal = jnp.zeros((8, half_pixels), f32)
                for c in range(3):
                    goal = jnp.where(component == c, wanted[c][a][b], goal)
                error = pred[a][b] - goal
                weight = counted[a][b] * per_image
                loss = loss + weight * jnp.sum(error * error, axis=0, keepdims=True)
                grad_pred[a][b] = rounded(2.0 * error * weight)
        table = head_backward(grad_pred)
        table = jnp.concatenate([table[dy][dx] for dy in range(3) for dx in range(3)], axis=0)
        parts = split_three(table)
        for part in parts:
            head_grad = head_grad + mm(part, a6[n])
        head_rows = head_low[...].astype(bf16)
        grad = sum(mm_tn(part, head_rows) for part in parts)
        v = x3[n]
        values = [coef_w[2, n, kind] for kind in range(4)]
        dy = rounded(grad) * slope(v * values[0][0:1, :] + values[1][0:1, :])
        gain, shift, ca, cb, cd = norm_grad_coefs(
            fold(dy), fold(dy * v), gain_w(4), values[2], values[3], half_pixels
        )
        g_small[WIDE_NORM_ROW + 4 : WIDE_NORM_ROW + 5, :] += gain[0:1, :]
        g_small[WIDE_NORM_ROW + 5 : WIDE_NORM_ROW + 6, :] += shift[0:1, :]
        grad_third = dy * ca[0:1, :] + v * cb[0:1, :] + cd[0:1, :]
        dwide[n] = grad_third
    g_small[0:HEAD_ROWS, :] = head_grad
    g_small[LOSS_ROW : LOSS_ROW + 1, :] = jnp.broadcast_to(
        jnp.sum(loss, axis=1, keepdims=True), (1, HALF_CHANNELS)
    )

    for n in range(images):
        grad_attn = (dwide[n] * root_half).astype(bf16)
        dout[n] = grad_attn
        grad_att = mm_nt(grad_attn, attn_low[:, 3 * HALF_CHANNELS :]).astype(bf16)
        q = qkv[n, :, :HALF_CHANNELS]
        k = qkv[n, :, HALF_CHANNELS : 2 * HALF_CHANNELS]
        w = qkv[n, :, 2 * HALF_CHANNELS :]
        grad_probs = mm_nt(grad_att, w)
        weights = probs[n]
        inner = jnp.sum(weights * grad_probs, axis=1, keepdims=True)
        grad_scores = (weights * (grad_probs - inner)).astype(bf16)
        dqkv[n, :, :HALF_CHANNELS] = (mm(grad_scores, k) * logit_scale).astype(bf16)
        dqkv[n, :, HALF_CHANNELS : 2 * HALF_CHANNELS] = (mm_tn(grad_scores, q) * logit_scale).astype(bf16)
        dqkv[n, :, 2 * HALF_CHANNELS :] = mm_tn(probs_low[n], grad_att).astype(bf16)
    keep_columns(
        g_attn, 0, mm_tn(n5[...].reshape(-1, HALF_CHANNELS), dqkv[...].reshape(-1, 3 * HALF_CHANNELS))
    )
    keep_columns(
        g_attn,
        6 * HALF_CHANNELS,
        mm_tn(att[...].reshape(-1, HALF_CHANNELS), dout[...].reshape(-1, HALF_CHANNELS)),
    )
    advance("attn")
    for n in range(images):
        dy = mm_nt(dqkv[n], attn_low[:, : 3 * HALF_CHANNELS])
        v = x2[n]
        gain, shift, ca, cb, cd = norm_grad_coefs(
            fold(dy), fold(dy * v), gain_w(2), coef_w[1, n, 2], coef_w[1, n, 3], half_pixels
        )
        g_small[WIDE_NORM_ROW + 2 : WIDE_NORM_ROW + 3, :] += gain[0:1, :]
        g_small[WIDE_NORM_ROW + 3 : WIDE_NORM_ROW + 4, :] += shift[0:1, :]
        grad = dy * ca[0:1, :] + v * cb[0:1, :] + cd[0:1, :] + dwide[n] * root_half
        store_shifted(cells_g, n, 0, (grad * root_half).reshape(HALF, HALF, HALF_CHANNELS))

    center = cells_g[:, 1, 1 : HALF + 1].reshape(-1, HALF_CHANNELS)
    for dy in range(3):
        product = mm_tn(cell_input(cells_d, [dy]), center)
        for k in range(3):
            keep_columns(
                g_wide,
                (dy * 3 + k) * 2 * HALF_CHANNELS,
                product[k * HALF_CHANNELS : (k + 1) * HALF_CHANNELS],
            )
    keep_columns(g_down, SKIP_ROW, mm_tn(fs_low[...].reshape(-1, C1), center))
    advance("wide")
    dfs[...] = mm_nt(center, skip_low[...]).reshape(dfs.shape)
    out = mm_nt(cell_input(cells_g, range(3)), wide_bwd[...])
    advance("conv_d")
    bucket_rows = lax.broadcasted_iota(jnp.int32, (NB, HALF_CHANNELS), 0)
    time_wide = jnp.zeros((NB, HALF_CHANNELS), f32)
    for n in range(images):
        v = h3[n]
        dy = out[n * half_pixels : (n + 1) * half_pixels] * slope(
            v * row_of(coef_w, 0, n, 0) + row_of(coef_w, 0, n, 1)
        )
        gain, shift, ca, cb, cd = norm_grad_coefs(
            fold(dy), fold(dy * v), gain_w(0), coef_w[0, n, 2], coef_w[0, n, 3], half_pixels
        )
        g_small[WIDE_NORM_ROW : WIDE_NORM_ROW + 1, :] += gain[0:1, :]
        g_small[WIDE_NORM_ROW + 1 : WIDE_NORM_ROW + 2, :] += shift[0:1, :]
        grad = dy * ca[0:1, :] + v * cb[0:1, :] + cd[0:1, :]
        time_wide = time_wide + jnp.where(bucket_rows == bucket(n), total(fold(grad)), 0.0)
        store_shifted(cells_g, n, 0, grad.reshape(HALF, HALF, HALF_CHANNELS))
    g_small[TIME_WIDE_ROW : TIME_WIDE_ROW + NB, :] = time_wide

    for c in range(2):
        g_rows[c * SMALL_ROWS : (c + 1) * SMALL_ROWS, :] = g_small[:, c * 128 : (c + 1) * 128]
    advance("gn_d")

    center = cells_g[:, 1, 1 : HALF + 1].reshape(-1, HALF_CHANNELS)
    for dy in range(3):
        product = mm_tn(cell_input(cells_c, [dy]), center)
        for k in range(3):
            keep_columns(g_down, (dy * 3 + k) * 2 * C1, product[k * C1 : (k + 1) * C1])
    advance("down")
    dnarrow[...] = mm_nt(cell_input(cells_g, range(3)), down_bwd[...]).reshape(dnarrow.shape)

    def up_parts(ref, n, i, size):
        here = pl.ds(i * size * HALF, size * HALF)
        g = ref[n, here].reshape(size, HALF, C1)
        lane_rows = lax.broadcasted_iota(jnp.int32, g.shape, 0) + i * size
        above = ref[n, pl.ds(jnp.maximum(i * size - 1, 0) * HALF, HALF)].reshape(1, HALF, C1)
        below = ref[n, pl.ds(jnp.minimum((i + 1) * size, HALF - 1) * HALF, HALF)].reshape(1, HALF, C1)
        above = jnp.where(lane_rows == 0, 0.0, jnp.concatenate([above, g[:-1]], axis=0))
        below = jnp.where(lane_rows == HALF - 1, 0.0, jnp.concatenate([g[1:], below], axis=0))
        result = []
        for rows in (0.375 * g + 0.125 * above, 0.375 * g + 0.125 * below):
            result.append(
                (
                    0.375 * rows + 0.125 * shift_cols(rows, 1),
                    0.375 * rows + 0.125 * shift_cols(rows, -1),
                )
            )
        return result

    def third_norm(n):
        size = HALF // 4
        scale = row_of(coef_n, 2, n, 0)
        offset = row_of(coef_n, 2, n, 1)

        def step(i, carry):
            sum_dy, sum_dyv = carry
            parts = up_parts(dnarrow, n, i, size)
            for b in range(2):
                g = jnp.stack([parts[0][b], parts[1][b]], axis=1).reshape(2 * size, HALF, C1)
                v = xs_full[n, b, pl.ds(i * 2 * size, 2 * size)]
                dy = g * slope(v * scale + offset)
                dy_full[n, b, pl.ds(i * 2 * size, 2 * size)] = dy
                sum_dy = sum_dy + fold(dy)
                sum_dyv = sum_dyv + fold(dy * v)
            return sum_dy, sum_dyv

        sum_dy, sum_dyv = lax.fori_loop(0, 4, step, (zero_n, zero_n))
        gain, shift, ca, cb, cd = norm_grad_coefs(
            sum_dy, sum_dyv, gain_n(4), coef_n[2, n, 2], coef_n[2, n, 3], full_pixels
        )
        g_late[4:5, :] += gain[0:1, :]
        g_late[5:6, :] += shift[0:1, :]
        advance("t%da" % n)

        def finish(i):
            parts = up_parts(dfs, n, i, size)
            for b in range(2):
                g = jnp.stack([parts[0][b], parts[1][b]], axis=1).reshape(2 * size, HALF, C1)
                here = pl.ds(i * 2 * size, 2 * size)
                v = xs_full[n, b, here]
                g = g + dy_full[n, b, here] * ca[0:1, :] + v * cb[0:1, :] + cd[0:1, :]
                store_planes(in_g, n, b, i * 2 * size, rounded(g) * root_half)

        each(4, finish)

    advance("narrow")
    for n in range(images):
        third_norm(n)
        advance("t%db" % n)

    def pair_gradient(planes, member):
        products = None
        for b in range(2):
            grads = jnp.concatenate([plane_block(in_g, EVEN + b, a + 1) for a in range(2)], axis=1)
            part = [mm_tn(grads, pair_input(planes, b, jjs)) for jjs in ((0, 1), (2, 3))]
            products = part if products is None else [p + q for p, q in zip(products, part)]
        for dy in range(3):
            blocks = []
            for a in range(2):
                jj = dy + a
                wide_part = products[jj // 2][a * C1 : (a + 1) * C1]
                blocks.append(wide_part[:, (jj % 2) * 3 * C1 : (jj % 2 + 1) * 3 * C1])
            both = blocks[0] + blocks[1]
            for k in range(3):
                row = (dy * 3 + k) * C1
                (g_pair_b if member else g_pair_a)[row : row + C1, :] = both[:, k * C1 : (k + 1) * C1].T

    def back_through(member, values, which, gain_row, last):
        for b in range(2):
            out = mm_nt(pair_input(in_g, b, range(4)), pair_bwd[member])
            for n in range(images):
                dy_full[n, b, pl.ds(0, RES)] = pair_rows(out, n)
        advance("b%dc" % member)
        bucket_rows = lax.broadcasted_iota(jnp.int32, (NB, C1), 0)

        def image(n):
            scale = row_of(coef_n, which, n, 0)
            offset = row_of(coef_n, which, n, 1)

            def step(i, carry):
                sum_dy, sum_dyv = carry
                here = pl.ds(i * ROWS, ROWS)
                for b in range(2):
                    v = values[n, b, here]
                    dy = dy_full[n, b, here] * slope(v * scale + offset)
                    if not last:
                        dy_full[n, b, here] = dy
                    sum_dy = sum_dy + fold(dy)
                    sum_dyv = sum_dyv + fold(dy * v)
                return sum_dy, sum_dyv

            sum_dy, sum_dyv = lax.fori_loop(0, steps, step, (zero_n, zero_n))
            gain, shift, ca, cb, cd = norm_grad_coefs(
                sum_dy, sum_dyv, gain_n(gain_row), coef_n[which, n, 2], coef_n[which, n, 3], full_pixels
            )
            g_late[gain_row : gain_row + 1, :] += gain[0:1, :]
            g_late[gain_row + 1 : gain_row + 2, :] += shift[0:1, :]
            if last:
                return

            def finish(i, carry):
                here = pl.ds(i * ROWS, ROWS)
                for b in range(2):
                    v = values[n, b, here]
                    g = dy_full[n, b, here] * ca[0:1, :] + v * cb[0:1, :] + cd[0:1, :]
                    carry = carry + fold(g)
                    store_planes(in_g, n, b, i * ROWS, g)
                return carry

            sums = total(lax.fori_loop(0, steps, finish, zero_n))
            g_late[TIME_NARROW_ROW : TIME_NARROW_ROW + NB, :] += jnp.where(
                bucket_rows == bucket(n), sums, 0.0
            )

        for n in range(images):
            image(n)
            advance("b%di%d" % (member, n))

    pair_gradient(in_b, 1)
    advance("pair_b")
    back_through(1, h1_full, 1, 2, False)
    pair_gradient(in_a, 0)
    advance("pair_a")
    back_through(0, x_full, 0, 0, True)
    pieces["late"] = Exchange(g_late[...], late_totals, arrived_late, late_sems, links.brief)
    advance("end")
    while any(piece.left() for piece in pieces.values()):
        for name, piece in pieces.items():
            if piece.left():
                piece.step()
    sum_late[...] = late_totals[len(links.brief)]


def main_call(dp_size, *operands):
    n = operands[1].shape[1]
    devices = 2 * dp_size
    counts = group_sizes(dp_size)
    orders = (counts[1], counts[0]) + (counts[1],) * 4
    grads = [padded(rows, devices, TILE) for rows in GRADS]
    sums = [(coded_rows(rows, devices), jnp.int16) for rows in GRADS]
    sums.append((padded(2 * SMALL_ROWS, devices, 8), f32))
    spaces = [message_rows(rows, order, TILE) for rows, order in zip(grads, orders)]
    small_space = message_rows(sums[-1][0], orders[-1], 0)
    stages = sum(size - 1 for size in counts[1])
    vm = pltpu.VMEM
    full = (n, 2, RES, HALF, C1)
    planes = (n, 4, RES + 2, HALF, C1)
    wide = HALF_CHANNELS
    square = (n, HALF * HALF, wide)
    moved = [vm(v.shape, v.dtype) for v in operands[1:4] + operands[5:] + operands[3:4]]
    scratch = moved + [vm((rows, 128), f32) for rows in grads + [sums[-1][0]]]
    scratch += [vm((rows, 128), jnp.int16) for rows in spaces]
    scratch += [vm((rows, 128), jnp.int16) for rows in spaces] + [vm((small_space, 128), f32)]
    scratch += [pltpu.SemaphoreType.DMA((2, 2 * sum(size - 1 for size in order))) for order in orders]
    scratch += [
        vm((SMALL_ROWS, wide), f32),
        vm((LATE_ROWS, C1), f32),
        vm((len(counts[1]) + 1, NB, 128), f32),
        vm((sum(counts[1]), NB, 128), f32),
        vm((len(counts[1]) + 1, LATE_ROWS, 128), f32),
        vm((sum(counts[1]), LATE_ROWS, 128), f32),
        pltpu.SemaphoreType.DMA((2, 3)),
        pltpu.SemaphoreType.DMA((3,)),
        pltpu.SemaphoreType.DMA((2, stages)),
        pltpu.SemaphoreType.DMA((2, stages)),
        pltpu.SemaphoreType.DMA((11,)),
        vm((2, 12 * C1, 2 * C1), bf16),
        vm((2, 2 * C1, 12 * C1), bf16),
        vm((9 * C1, wide), bf16),
        vm((C1, 9 * wide), bf16),
        vm((9 * wide, wide), bf16),
        vm((wide, 9 * wide), bf16),
        vm((C1, wide), bf16),
        vm((wide, 4 * wide), bf16),
        vm((HEAD_ROWS, wide), f32),
        vm(full, f32),
        vm(full, f32),
        vm(full, f32),
        vm((n, 2, RES + 2, HALF, C1), f32),
        vm(planes, bf16),
        vm(planes, bf16),
        vm(planes, bf16),
        vm((ROWS * RES, C1), f32),
        vm((n, 3, HALF + 2, HALF, C1), bf16),
        vm((n, 3, HALF + 2, HALF, wide), bf16),
        vm((n, 3, HALF + 2, HALF, wide), bf16),
        vm((n, HALF * HALF, C1), bf16),
        vm((n, HALF * HALF, C1), f32),
        vm(square, f32),
        vm(square, f32),
        vm(square, f32),
        vm(square, bf16),
        vm((n, HALF * HALF, 3 * wide), bf16),
        vm(square, f32),
        vm(square, bf16),
        vm(square, bf16),
        vm(square, bf16),
        vm(square, f32),
        vm(square, bf16),
        vm((n, HALF * HALF, 3 * wide), bf16),
        vm((n, HALF * HALF, C1), f32),
        vm((3, n, 4, 8, C1), f32),
        vm((3, n, 4, 8, wide), f32),
    ]
    whole = pl.BlockSpec(memory_space=pltpu.VMEM)
    anywhere = pl.BlockSpec(memory_space=pltpu.HBM)
    return pl.pallas_call(
        functools.partial(main_kernel, dp_size),
        out_shape=[jax.ShapeDtypeStruct((rows, 128), dtype) for rows, dtype in sums + [(LATE_ROWS, f32), (NB, f32)]],
        in_specs=[pl.BlockSpec(memory_space=pltpu.SMEM)] + [anywhere] * 12,
        out_specs=[whole] * (len(sums) + 2),
        scratch_shapes=scratch,
        compiler_params=pltpu.CompilerParams(
            collective_id=0, has_side_effects=True, vmem_limit_bytes=MAIN_LIMIT + 1536 * (sum(grads) - sum(GRADS))
        ),
        cost_estimate=pl.CostEstimate(flops=8 * 10**9, bytes_accessed=12 * 10**6, transcendentals=0),
    )(*[pltpu.with_memory_space_constraint(v, pltpu.HBM) for v in operands])


PIECE_NAMES = ("attn", "wide", "down", "pair_b", "pair_a", "small")
SCHEDULE = {
    "attn": ("attn",),
    "wide": ("wide", "attn"),
    "gn_d": ("small", "wide"),
    "down": ("down", "small"),
    "t0a": ("down", "attn"),
    "t1a": ("wide",),
    "t1b": ("small",),
    "pair_b": ("pair_b",),
    "b1c": ("attn",),
    "b1i0": ("pair_b", "down", "small", "wide"),
    "pair_a": ("pair_a",),
    "b0c": ("attn",),
    "b0i0": ("pair_a", "pair_b"),
    "end": ("late", "down", "small", "late", "wide", "attn", "pair_b", "attn", "pair_a", "down", "small", "late", "small", "wide", "pair_b", "pair_a", "down", "late", "wide", "down", "pair_a", "pair_b", "pair_b", "wide", "wide", "pair_a", "pair_a"),
}


def group_sizes(dp_size):
    bits = (dp_size - 1).bit_length()
    far = []
    k = 2
    while k < bits:
        far.append(1 << min(2, bits - k))
        k += 2
    return [2, 2, 2] + far, [2, 4] + far


class Links:
    def __init__(self, dp_size):
        dp = lax.axis_index("dp")
        sp = lax.axis_index("sp")
        core = dp % 2
        near = (dp // 2) % 2

        def along(unit, size):
            place = (dp // unit) % size
            return place, [(dp + unit * ((place + r) % size - place), sp) for r in range(1, size)]

        def pick(first, other):
            return first + core * (other - first)

        across = (dp, 1 - sp)
        beside = (dp + 2 * (1 - 2 * near), sp)
        second = (pick(near, sp), [(pick(beside[0], dp), pick(sp, 1 - sp))])
        third = (pick(sp, near), [(pick(dp, beside[0]), pick(1 - sp, sp))])
        place = 2 * near + sp
        square = []
        for r in range(1, 4):
            member = (place + r) % 4
            square.append((dp + 2 * (member // 2 - near), member % 2))
        far = []
        unit = 4
        for size in group_sizes(dp_size)[1][2:]:
            far.append(along(unit, size))
            unit *= size
        self.full = [along(1, 2), second, third] + far
        self.brief = [along(1, 2), (place, square)] + far
        self.all = [other for _, others in self.brief for other in others]

    def greet(self):
        barrier = pltpu.get_barrier_semaphore()
        for other in self.all:
            pl.semaphore_signal(barrier, inc=1, device_id=other, device_id_type=MESH)

    def meet(self):
        pl.semaphore_wait(pltpu.get_barrier_semaphore(), len(self.all))


def send(source, target, sems, index, landing, other):
    return pltpu.make_async_remote_copy(
        src_ref=source,
        dst_ref=target,
        send_sem=sems.at[0, index],
        recv_sem=sems.at[1, landing],
        device_id=other,
        device_id_type=MESH,
    )


class Exchange:
    def __init__(self, value, totals, arrived, sems, stages):
        totals[0] = value
        self.totals, self.arrived, self.sems, self.stages = totals, arrived, sems, stages
        self.t = self.base = self.index = 0
        self.copies = []

    def left(self):
        return self.t <= len(self.stages)

    def step(self):
        if self.copies:
            for copy in self.copies:
                copy.wait()
            size = len(self.copies) + 1
            total_now = self.arrived[self.base]
            for m in range(1, size):
                total_now = total_now + self.arrived[self.base + m]
            self.totals[self.t] = total_now
            self.base += size
            self.index += size - 1
            self.copies = []
        if self.t < len(self.stages):
            place, others = self.stages[self.t]
            mine = self.totals.at[self.t]
            landing = self.arrived.at[self.base + place]
            for r, other in enumerate(others):
                copy = send(mine, landing, self.sems, self.index + r, self.index + len(others) - 1 - r, other)
                copy.start()
                self.copies.append(copy)
            self.arrived[self.base + place] = self.totals[self.t]
        self.t += 1

    def finish(self, out):
        while self.left():
            self.step()
        out[...] = self.totals[len(self.stages)]


def count_pixels(buckets, mask):
    rows = lax.broadcasted_iota(jnp.int32, (NB, 128), 0)
    counted = jnp.zeros((NB, 128), f32)
    images = mask.shape[1]
    for i in range(2 * images):
        pixels = mask[i // images, i % images].astype(f32)
        number = jnp.sum(jnp.sum(pixels, axis=0, keepdims=True), axis=1, keepdims=True)
        counted = counted + jnp.where(rows == buckets[i], number, 0.0)
    return counted


def chunk_of(rows):
    return next(c for c in (128, 96, 80, 64, 48, 32, 16, 8) if rows % c == 0)


def aligned(row, tile):
    return row if isinstance(row, int) else pl.multiple_of(row, tile)


def encode(source, first, rows, target, base):
    size = chunk_of(rows)

    def largest(i, carry):
        v = jnp.abs(source[pl.ds(aligned(first + i * size, 8), size), :])
        return jnp.maximum(carry, jnp.max(v.reshape(-1, 8, 128), axis=0))

    bound = lax.fori_loop(0, rows // size, largest, jnp.zeros((8, 128), f32))
    bound = jnp.max(bound, axis=0, keepdims=True)
    power = jnp.floor(jnp.log2(jnp.maximum(bound, 1e-30))) + 1.0
    scale = jnp.exp2(15.0 - power)

    def step(i):
        v = source[pl.ds(aligned(first + i * size, 8), size), :] * scale
        v = jnp.clip(jnp.round(v), -32767.0, 32767.0)
        target[pl.ds(aligned(base + i * size, TILE), size), :] = v.astype(jnp.int32).astype(jnp.int16)

    each(rows // size, step)
    target[pl.ds(aligned(base + rows, TILE), TILE), :] = jnp.broadcast_to(
        power.astype(jnp.int32), (TILE, 128)
    ).astype(jnp.int16)


def decode(source, base, rows):
    power = source[pl.ds(aligned(base + rows, TILE), TILE), :].astype(jnp.int32).astype(f32)
    return jnp.exp2(power[0:1, :] - 15.0)


def message_rows(rows, sizes, tile):
    needed = 0
    for size in sizes:
        rows //= size
        needed += (size - 1) * (rows + tile)
    return needed


class Piece:
    def __init__(self, source, outgoing, arrived, out, sems, stages):
        self.source, self.outgoing, self.arrived, self.out, self.sems = source, outgoing, arrived, out, sems
        self.stages = stages
        self.tile = 0 if outgoing is None else TILE
        self.rows = source.shape[0]
        self.first = 0
        self.base = self.index = self.t = 0
        self.copies = []
        self.share = self.rows
        for _, others in stages:
            self.share //= len(others) + 1

    def left(self):
        return self.t <= 2 * len(self.stages)

    def step(self):
        count = len(self.stages)
        if 0 < self.t <= count:
            self.scatter_end(self.stages[self.t - 1])
        elif self.t > count:
            self.gather_end(self.stages[2 * count - self.t])
        if self.t == count:
            self.keep()
        if self.t < count:
            self.scatter_start(self.stages[self.t])
        elif self.t < 2 * count:
            self.gather_start(self.stages[2 * count - 1 - self.t])
        self.t += 1

    def scatter_start(self, stage):
        place, others = stage
        size = len(others) + 1
        rows = self.rows // size
        block = rows + self.tile
        for r, other in enumerate(others):
            part = self.first + ((place + r + 1) % size) * rows
            if self.tile:
                mine = self.base + r * block
                encode(self.source, part, rows, self.outgoing, mine)
                message = self.outgoing.at[pl.ds(mine, block)]
            else:
                message = self.source.at[pl.ds(aligned(part, 8), rows)]
            landing = size - 2 - r
            copy = send(
                message,
                self.arrived.at[pl.ds(self.base + landing * block, block)],
                self.sems,
                self.index + r,
                self.index + landing,
                other,
            )
            copy.start()
            self.copies.append(copy)

    def scatter_end(self, stage):
        place, others = stage
        size = len(others) + 1
        rows = self.rows // size
        block = rows + self.tile
        for copy in self.copies:
            copy.wait()
        first = self.first + place * rows
        scales = [decode(self.arrived, self.base + r * block, rows) if self.tile else 1.0 for r in range(size - 1)]
        chunk = chunk_of(rows)

        def add(i):
            here = pl.ds(aligned(first + i * chunk, 8), chunk)
            v = self.source[here, :]
            for r, scale in enumerate(scales):
                more = self.arrived[pl.ds(aligned(self.base + r * block + i * chunk, self.tile or 8), chunk), :]
                v = v + (more.astype(jnp.int32).astype(f32) * scale if self.tile else more)
            self.source[here, :] = v

        each(rows // chunk, add)
        self.first, self.rows = first, rows
        self.base += (size - 1) * block
        self.index += size - 1
        self.copies = []

    def keep(self):
        block = self.share + self.tile
        self.place = 0
        for place, others in self.stages:
            self.place = self.place * (len(others) + 1) + place
        self.first = self.place * block
        self.rows = block
        if self.tile:
            encode(self.source, self.place * self.share, self.share, self.out, self.first)
        else:
            self.out[pl.ds(aligned(self.first, 8), block), :] = self.source[
                pl.ds(aligned(self.first, 8), block), :
            ]

    def gather_start(self, stage):
        place, others = stage
        here = self.out.at[pl.ds(aligned(self.first, self.tile or 8), self.rows)]
        for r, other in enumerate(others):
            copy = send(here, here, self.sems, self.index + r, self.index + len(others) - 1 - r, other)
            copy.start()
            self.copies.append(copy)

    def gather_end(self, stage):
        place, others = stage
        size = len(others) + 1
        for copy in self.copies:
            copy.wait()
        self.copies = []
        self.index += size - 1
        self.first = self.first - place * self.rows
        self.rows = self.rows * size


def adamw(weight, grad, first, second, rate):
    first = beta_one * first + (1.0 - beta_one) * grad
    second = beta_two * second + (1.0 - beta_two) * grad * grad
    power = jnp.maximum(second * (1.0 / (1.0 - beta_two**STEP)), 1e-36)
    root = power * lax.rsqrt(power) + adam_epsilon
    scale = rate / (1.0 - beta_one**STEP)
    return weight * (1.0 - rate * decay_rate) - scale * first / root, first, second


PARTS = (
    (2, 1, HALF_CHANNELS, 0, 3, 0),
    (2, 1, HALF_CHANNELS, 6 * HALF_CHANNELS, 3, 3 * HALF_CHANNELS),
    (2, 1, HALF_CHANNELS, 12 * HALF_CHANNELS, 3, 6 * HALF_CHANNELS),
    (4, 0, HALF_CHANNELS, 0, 1, 0),
    (1, 2, C1, 0, 9, 0),
    (3, 2, C1, 18 * C1, 1, 0),
    (0, 3, C1, 0, 9, 9 * C1),
    (0, 4, C1, 0, 9, 0),
)
LARGE = 5


def update_kernel(devices, *refs):
    count = len(GRADS)
    coded, (g_small, g_late, counts), refs = refs[:count], refs[count : count + 3], refs[count + 3 :]
    members = [refs[3 * i : 3 + 3 * i] for i in range(9)]
    outs = [refs[27 + 3 * i : 30 + 3 * i] for i in range(9)]
    loss_out, counts_out = refs[54:56]
    refs = refs[56:]
    grads, refs = refs[:count], refs[count:]
    staged = [refs[3 * i : 3 * i + 3] for i in range(LARGE)]
    store_sems = refs[3 * LARGE]

    def small(row, rows, lanes):
        parts = [g_small[c * SMALL_ROWS + row : c * SMALL_ROWS + row + rows, :] for c in range(lanes // 128)]
        return parts[0] if len(parts) == 1 else jnp.concatenate(parts, axis=1)

    def single(member, index, grad, rate):
        w, m, v = (ref[index] for ref in members[member])
        for out, value in zip(outs[member], adamw(w, grad, m, v, rate)):
            out[index] = value

    def unpack(source, grad):
        share = grad.shape[0] // devices

        def shares(i):
            base = i * (share + TILE)
            v = source[pl.ds(aligned(base, TILE), share), :].astype(jnp.int32).astype(f32)
            grad[pl.ds(aligned(i * share, 8), share), :] = v * decode(source, base, share)

        each(devices, shares)

    def update(part):
        member, which, block_rows, base, blocks, start = part
        size = 64
        grad = grads[which]
        columns = staged[member][0].shape[1] // 128

        def step(i):
            block = i // (block_rows // size)
            row = (i % (block_rows // size)) * size
            here = pl.ds(aligned(start + block * block_rows + row, 8), size)
            for c in range(columns):
                lanes = slice(c * 128, (c + 1) * 128)
                g = grad[pl.ds(aligned(base + (block * columns + c) * block_rows + row, 8), size), :]
                w, m, v = (ref[here, lanes] for ref in members[member])
                for out, value in zip(staged[member], adamw(w, g, m, v, rate_matrix)):
                    out[here, lanes] = value

        each(blocks * block_rows // size, step)

    stores = []
    seen = set()
    for i, part in enumerate(PARTS):
        member, which, block_rows, _, blocks, start = part
        if which not in seen:
            unpack(coded[which], grads[which])
            seen.add(which)
        update(part)
        here = pl.ds(start, block_rows * blocks)
        for kind in range(3):
            copy = pltpu.make_async_copy(
                staged[member][kind].at[here], outs[member][kind].at[here], store_sems.at[i, kind]
            )
            copy.start()
            stores.append(copy)
    for tap in range(9):
        single(5, (tap,), small(tap * 8, 3, HALF_CHANNELS), rate_matrix)
    every = slice(None)
    single(6, (every, every), g_late[:6, :], rate_vector)
    single(7, (every, every), small(WIDE_NORM_ROW, 6, HALF_CHANNELS), rate_vector)
    single(8, (every, slice(0, C1)), g_late[TIME_NARROW_ROW : TIME_NARROW_ROW + NB, :], rate_vector)
    single(8, (every, slice(C1, None)), small(TIME_WIDE_ROW, NB, HALF_CHANNELS), rate_vector)
    loss_out[...] = g_small[LOSS_ROW : LOSS_ROW + 1, :]
    diagonal = lax.broadcasted_iota(jnp.int32, (NB, 128), 0) == lax.broadcasted_iota(jnp.int32, (NB, 128), 1)
    counts_out[...] = jnp.sum(jnp.where(diagonal, counts[...], 0.0), axis=0, keepdims=True)[:, :NB]
    for copy in stores:
        copy.wait()


def update_call(devices, grads, members):
    whole = pl.BlockSpec(memory_space=pltpu.VMEM)
    outside = pl.BlockSpec(memory_space=pltpu.HBM)
    flat = [v for member in members for v in member]
    large = [v.shape for v in flat[: 3 * LARGE]]
    return pl.pallas_call(
        functools.partial(update_kernel, devices),
        out_shape=[jax.ShapeDtypeStruct(v.shape, f32) for v in flat]
        + [jax.ShapeDtypeStruct((1, 128), f32), jax.ShapeDtypeStruct((1, NB), f32)],
        in_specs=[whole] * (len(grads) + len(flat)),
        out_specs=[outside] * (3 * LARGE) + [whole] * (len(flat) - 3 * LARGE + 2),
        scratch_shapes=[pltpu.VMEM((padded(rows, devices, TILE), 128), f32) for rows in GRADS]
        + [pltpu.VMEM(shape, f32) for shape in large]
        + [pltpu.SemaphoreType.DMA((len(PARTS), 3))],
        compiler_params=pltpu.CompilerParams(vmem_limit_bytes=UPDATE_LIMIT),
        cost_estimate=pl.CostEstimate(flops=30 * 10**6, bytes_accessed=40 * 10**6, transcendentals=0),
    )(*grads, *flat)


def on_device(
    features,
    target,
    pixel_mask,
    buckets,
    conv_pair,
    down_conv,
    conv_wide,
    skip_proj,
    attn_proj,
    head_conv,
    norm_narrow,
    norm_wide,
    time_bias,
    conv_pair_mom,
    down_conv_mom,
    conv_wide_mom,
    skip_proj_mom,
    attn_proj_mom,
    head_conv_mom,
    norm_narrow_mom,
    norm_wide_mom,
    time_bias_mom,
    conv_pair_sq,
    down_conv_sq,
    conv_wide_sq,
    skip_proj_sq,
    attn_proj_sq,
    head_conv_sq,
    norm_narrow_sq,
    norm_wide_sq,
    time_bias_sq,
):
    dp_size = lax.axis_size("dp")
    images = features.shape[0] // 2

    def halves(tensor):
        return tensor.reshape((2, images) + tensor.shape[1:])

    def flat(tensor):
        return tensor.reshape(-1, tensor.shape[-1])

    def head_rows(tensor):
        return jnp.transpose(tensor, (0, 1, 3, 2)).reshape(9, 3, HALF_CHANNELS)

    params = (
        flat(conv_pair),
        flat(down_conv),
        flat(conv_wide),
        skip_proj,
        attn_proj,
        head_rows(head_conv),
        norm_narrow,
        norm_wide,
        time_bias,
    )
    firsts = (
        flat(conv_pair_mom),
        flat(down_conv_mom),
        flat(conv_wide_mom),
        skip_proj_mom,
        attn_proj_mom,
        head_rows(head_conv_mom),
        norm_narrow_mom,
        norm_wide_mom,
        time_bias_mom,
    )
    seconds = (
        flat(conv_pair_sq),
        flat(down_conv_sq),
        flat(conv_wide_sq),
        skip_proj_sq,
        attn_proj_sq,
        head_rows(head_conv_sq),
        norm_narrow_sq,
        norm_wide_sq,
        time_bias_sq,
    )
    summed = main_call(
        dp_size,
        buckets,
        halves(features),
        halves(jnp.transpose(target, (0, 3, 1, 2))),
        halves(pixel_mask),
        *params,
    )
    results = update_call(2 * dp_size, summed, list(zip(params, firsts, seconds)))
    shaped = []
    for member, like in enumerate((conv_pair, down_conv, conv_wide, skip_proj, attn_proj)):
        shaped.extend(v.reshape(like.shape) for v in results[3 * member : 3 * member + 3])
    for v in results[15:18]:
        shaped.append(jnp.transpose(v.reshape(3, 3, 3, HALF_CHANNELS), (0, 1, 3, 2)))
    shaped.extend(results[18:27])
    return (results[27][0, 0], results[28].reshape(NB)) + tuple(shaped)


def solution(mesh):
    placed = (
        P("dp", "sp", None, None),
        P("dp", "sp", None, None),
        P("dp", "sp", None),
        P("dp"),
        P(),
        P(),
        P(),
        P(),
        P(),
        P(),
        P(),
        P(),
        P(),
        P(),
        P(),
        P(),
        P(),
        P(),
        P(),
        P(),
        P(),
        P(),
        P(),
        P(),
        P(),
        P(),
        P(),
        P(),
        P(),
        P(),
        P(),
    )
    return jax.shard_map(
        on_device,
        mesh=mesh,
        in_specs=placed,
        out_specs=(
            P(),
            P(),
            P(),
            P(),
            P(),
            P(),
            P(),
            P(),
            P(),
            P(),
            P(),
            P(),
            P(),
            P(),
            P(),
            P(),
            P(),
            P(),
            P(),
            P(),
            P(),
            P(),
            P(),
            P(),
            P(),
            P(),
            P(),
            P(),
            P(),
        ),
        check_vma=False,
    )
```

```python
import functools

import jax
import jax.numpy as jnp
from jax import lax
from jax.experimental import pallas as pl
from jax.experimental.pallas import tpu as pltpu
from jax.sharding import PartitionSpec as P

C1 = 128
HALF_CHANNELS = 256
GROUPS = 32
RES = 32
HALF = 16
NB = 8
STEP = 10
MESH = pl.DeviceIdType.MESH
MAIN_LIMIT = 41 * 1024 * 1024
UPDATE_LIMIT = 26 * 1024 * 1024

epsilon = 1e-05
root_half = 0.7071067811865476
beta_one = 0.9
beta_two = 0.999
adam_epsilon = 1e-08
decay_rate = 0.1
rate_matrix = 0.03
rate_vector = 0.5
logit_scale = HALF_CHANNELS ** (-0.5)
ROWS = 8

bf16 = jnp.bfloat16
f32 = jnp.float32

EVEN, ODD, ODD_LEFT, EVEN_RIGHT = 0, 1, 2, 3
TAPS = ((ODD_LEFT, EVEN, ODD), (EVEN, ODD, EVEN_RIGHT))


def rounded(v):
    return v.astype(bf16).astype(f32)


def silu(t):
    return t * jax.nn.sigmoid(t)


def slope(t):
    s = jax.nn.sigmoid(t)
    return s * (1.0 + t * (1.0 - s))


def mm(a, b):
    return lax.dot_general(a, b, (((1,), (0,)), ((), ())), preferred_element_type=f32)


def mm_nt(a, b):
    return lax.dot_general(a, b, (((1,), (1,)), ((), ())), preferred_element_type=f32)


def mm_tn(a, b):
    return lax.dot_general(a, b, (((0,), (0,)), ((), ())), preferred_element_type=f32)


def fold(v):
    return jnp.sum(v.reshape(-1, 8, v.shape[-1]), axis=0)


def total(v):
    return jnp.broadcast_to(jnp.sum(v, axis=0, keepdims=True), v.shape)


def group_sum(v, size):
    lanes = v.shape[-1]
    lane = lax.broadcasted_iota(jnp.int32, v.shape, 1)
    step = 1
    while step < size:
        other = jnp.where(
            (lane & step) == 0, pltpu.roll(v, lanes - step, 1), pltpu.roll(v, step, 1)
        )
        v = v + other
        step *= 2
    return v


def norm_coefs(sums, squares, gain, shift, pixels):
    size = sums.shape[-1] // GROUPS
    count = pixels * size
    mean = group_sum(total(sums), size) / count
    power = group_sum(total(squares), size) / count
    inv = lax.rsqrt(power - mean * mean + epsilon)
    scale = inv * gain
    return scale, shift - mean * scale, mean, inv


def norm_grad_coefs(sum_dy, sum_dyv, gain, mean, inv, pixels):
    size = sum_dy.shape[-1] // GROUPS
    count = pixels * size
    first = total(sum_dy)
    second = (total(sum_dyv) - mean * first) * inv
    one = group_sum(first * gain, size) / count
    two = group_sum(second * gain, size) / count
    b = -inv * inv * two
    return second, first, inv * gain, b, -inv * one - mean * b


def shift_cols(v, step):
    col = lax.broadcasted_iota(jnp.int32, v.shape, 1)
    if step == 1:
        return jnp.where(col == 0, 0.0, pltpu.roll(v, 1, 1))
    return jnp.where(col == HALF - 1, 0.0, pltpu.roll(v, HALF - 1, 1))


def store_planes(planes, n, b, r0, v):
    rows = v.shape[0]
    v = v.astype(bf16).astype(f32)
    for plane, value in (
        (EVEN + b, v),
        (ODD_LEFT if b == 1 else EVEN_RIGHT, shift_cols(v, 1 if b == 1 else -1)),
    ):
        planes[n, plane, pl.ds(r0 + 1, rows)] = value.astype(bf16)


def store_shifted(cells, n, r0, v):
    rows = v.shape[0]
    v = v.astype(bf16).astype(f32)
    for tap, value in ((0, shift_cols(v, 1)), (1, v), (2, shift_cols(v, -1))):
        cells[n, tap, pl.ds(r0 + 1, rows)] = value.astype(bf16)


def plane_block(planes, tap, jj):
    return planes[:, tap, pl.ds(jj, HALF, stride=2)].reshape(-1, planes.shape[-1])


def pair_input(planes, b, jjs):
    return jnp.concatenate([plane_block(planes, tap, jj) for jj in jjs for tap in TAPS[b]], axis=1)


def cell_input(cells, dys):
    return jnp.concatenate(
        [
            cells[:, tap, dy : dy + HALF].reshape(-1, cells.shape[-1])
            for dy in dys
            for tap in range(3)
        ],
        axis=1,
    )


def each(count, body):
    def step(i, carry):
        body(i)
        return carry

    lax.fori_loop(0, count, step, 0)


def prepare_weights(pair, down, wide, skip, attn, head, pair_fwd, pair_bwd, down_fwd, down_bwd, wide_fwd, wide_bwd, skip_low, attn_low, head_low):
    nothing = jnp.zeros((C1, C1), bf16)
    for member in range(2):
        for jj in range(4):
            for k in range(3):
                block = (jj * 3 + k) * C1
                for a in range(2):
                    dy = jj - a
                    inside = 0 <= dy < 3
                    row = (dy * 3 + k) * C1
                    back = ((2 - dy) * 3 + (2 - k)) * C1
                    pair_fwd[member, block : block + C1, a * C1 : a * C1 + C1] = (
                        pair[member][row : row + C1, :].astype(bf16) if inside else nothing
                    )
                    pair_bwd[member, a * C1 : a * C1 + C1, block : block + C1] = (
                        pair[member][back : back + C1, :].astype(bf16) if inside else nothing
                    )
    wide_channels = HALF_CHANNELS
    for tap in range(9):
        low = down[tap * C1 : tap * C1 + C1, :].astype(bf16)
        down_fwd[tap * C1 : tap * C1 + C1, :] = low
        down_bwd[:, (8 - tap) * wide_channels : (9 - tap) * wide_channels] = low
        low = wide[tap * wide_channels : (tap + 1) * wide_channels, :].astype(bf16)
        wide_fwd[tap * wide_channels : (tap + 1) * wide_channels, :] = low
        wide_bwd[:, (8 - tap) * wide_channels : (9 - tap) * wide_channels] = low
    skip_low[...] = skip[...].astype(bf16)
    attn_low[...] = attn[...].astype(bf16)
    head_low[...] = jnp.zeros(head_low.shape, f32)
    for tap in range(9):
        head_low[tap * 8 : tap * 8 + 3, :] = rounded(head[tap])


def split_three(v):
    high = v.astype(bf16)
    rest = v - high.astype(f32)
    middle = rest.astype(bf16)
    return high, middle, (rest - middle.astype(f32)).astype(bf16)


def lane_shift(v, step):
    lane = lax.broadcasted_iota(jnp.int32, v.shape, 1)
    j = lane & (HALF - 1)
    if step == 1:
        keep = j < HALF - 1
    elif step == -1:
        keep = j > 0
    elif step == HALF:
        keep = lane < HALF * (HALF - 1)
    else:
        keep = lane >= HALF
    return jnp.where(keep, pltpu.roll(v, (-step) % v.shape[-1], 1), 0.0)


def head_forward(table):
    cols = [
        [
            lane_shift(table[dy][0], -1) + table[dy][1] + table[dy][2],
            table[dy][0] + table[dy][1] + lane_shift(table[dy][2], 1),
        ]
        for dy in range(3)
    ]
    return [
        [
            lane_shift(cols[0][b], -HALF) + cols[1][b] + cols[2][b]
            if a == 0
            else cols[0][b] + cols[1][b] + lane_shift(cols[2][b], HALF)
            for b in range(2)
        ]
        for a in range(2)
    ]


def head_backward(grad):
    rows = [
        [
            lane_shift(grad[0][b], HALF) + grad[1][b],
            grad[0][b] + grad[1][b],
            grad[0][b] + lane_shift(grad[1][b], -HALF),
        ]
        for b in range(2)
    ]
    return [
        [
            lane_shift(rows[0][dy], 1) + rows[1][dy],
            rows[0][dy] + rows[1][dy],
            rows[0][dy] + lane_shift(rows[1][dy], -1),
        ]
        for dy in range(3)
    ]


def keep_columns(ref, row, v):
    for c in range(v.shape[1] // 128):
        ref[row + c * v.shape[0] : row + (c + 1) * v.shape[0], :] = v[:, c * 128 : (c + 1) * 128]


HEAD_ROWS = 72
WIDE_NORM_ROW = 72
LOSS_ROW = 78
TIME_WIDE_ROW = 80
SMALL_ROWS = 96
TIME_NARROW_ROW = 8
LATE_ROWS = 16
SKIP_ROW = 18 * C1
ATTN_ROWS = 8 * HALF_CHANNELS
WIDE_ROWS = 18 * HALF_CHANNELS
DOWN_ROWS = 20 * C1
PAIR_ROWS = 9 * C1
GRADS = (ATTN_ROWS, WIDE_ROWS, DOWN_ROWS, PAIR_ROWS, PAIR_ROWS)
TILE = 16


def padded(rows, devices, tile):
    return -(-rows // (devices * tile)) * devices * tile


def coded_rows(rows, devices):
    return padded(rows, devices, TILE) + devices * TILE


def main_kernel(
    dp_size,
    buckets, features, target_rows, mask_rows, pair_all, down_all, wide_all, skip_all, attn_all, head_all,
    narrow_all, gains_all, time_all,
    sum_attn, sum_wide, sum_down, sum_pair_b, sum_pair_a, sum_small, sum_late, counts,
    x_in, target, mask, down, wide, skip, attn, head, gains_narrow, gains_wide, time_bias, mask_local,
    g_attn, g_wide, g_down, g_pair_b, g_pair_a, g_rows,
    out_attn, out_wide, out_down, out_pair_b, out_pair_a,
    half_attn, half_wide, half_down, half_pair_b, half_pair_a,
    in_attn, in_wide, in_down, in_pair_b, in_pair_a, in_small,
    sems_attn, sems_wide, sems_down, sems_pair_b, sems_pair_a, sems_small,
    g_small, g_late,
    totals, arrived_totals, late_totals, arrived_late, image_sems, local_sems, count_sems, late_sems, weight_sems,
    pair_fwd, pair_bwd, down_fwd, down_bwd, wide_fwd, wide_bwd, skip_low, attn_low, head_low,
    x_full, h1_full, xs_full, dy_full, in_a, in_b, in_g, flat,
    cells_c, cells_d, cells_g, fs_low, dfs, h3, x2, x3, n5, qkv, probs, probs_low, att, a6, dwide, dout, dqkv, dnarrow,
    coef_n, coef_w,
):
    loads = [
        pltpu.make_async_copy(source, ref, weight_sems.at[i])
        for i, (source, ref) in enumerate(
            (
                (pair_all.at[:PAIR_ROWS], g_pair_a.at[:PAIR_ROWS]),
                (pair_all.at[PAIR_ROWS:], g_pair_b.at[:PAIR_ROWS]),
                (down_all, down),
                (wide_all, wide),
                (skip_all, skip),
                (attn_all, attn),
                (head_all, head),
                (narrow_all, gains_narrow),
                (gains_all, gains_wide),
                (time_all, time_bias),
                (mask_rows, mask_local),
            )
        )
    ]
    links = Links(dp_size)
    links.greet()
    for copy in loads[::-1]:
        copy.start()
    loads.pop().wait()
    counted = count_pixels(buckets, mask_local)
    links.meet()
    here = (lax.axis_index("dp"), 1 - lax.axis_index("sp"))
    moved = ((features, x_in), (target_rows, target), (mask_rows, mask))
    side = lax.axis_index("sp")
    arrivals = [
        send(source.at[1 - side], out.at[side], image_sems, i, i, here) for i, (source, out) in enumerate(moved)
    ]
    for copy in arrivals:
        copy.start()
    keeps = [
        pltpu.make_async_copy(source.at[side], out.at[side], local_sems.at[i])
        for i, (source, out) in enumerate(moved)
    ]
    for copy in keeps:
        copy.start()
    images = x_in.shape[1]
    position = lax.axis_index("sp")
    steps = RES // ROWS
    full_pixels = RES * RES
    half_pixels = HALF * HALF
    zero_n = jnp.zeros((8, C1), f32)
    zero_w = jnp.zeros((8, HALF_CHANNELS), f32)

    def bucket(n):
        return buckets[position * images + n]

    def gain_n(row):
        return jnp.broadcast_to(gains_narrow[row : row + 1, :], (8, C1))

    def gain_w(row):
        return jnp.broadcast_to(gains_wide[row : row + 1, :], (8, HALF_CHANNELS))

    def keep_coefs(ref, which, n, values):
        for kind in range(4):
            ref[which, n, kind] = values[kind]

    def row_of(ref, which, n, kind):
        return ref[which, n, kind, 0:1, :]

    counting = Exchange(counted, totals, arrived_totals, count_sems, links.brief)
    counting.step()
    sources = (g_attn, g_wide, g_down, g_pair_b, g_pair_a, g_rows)
    outgoing = (out_attn, out_wide, out_down, out_pair_b, out_pair_a, None)
    halves = (half_attn, half_wide, half_down, half_pair_b, half_pair_a, None)
    incoming = (in_attn, in_wide, in_down, in_pair_b, in_pair_a, in_small)
    outs = (sum_attn, sum_wide, sum_down, sum_pair_b, sum_pair_a, sum_small)
    sems = (sems_attn, sems_wide, sems_down, sems_pair_b, sems_pair_a, sems_small)
    orders = (links.brief, links.brief, links.brief, links.brief, links.brief, links.brief)
    pieces = dict(zip(PIECE_NAMES, (Piece(*parts) for parts in zip(sources, outgoing, halves, incoming, outs, sems, orders))))

    def advance(point):
        for name in SCHEDULE.get(point, ()):
            pieces[name].step()

    for rows, ref in zip(GRADS + (2 * SMALL_ROWS,), sources):
        if ref.shape[0] > rows:
            ref[rows:, :] = jnp.zeros((ref.shape[0] - rows, 128), f32)
    for copy in loads:
        copy.wait()
    prepare_weights((g_pair_a, g_pair_b), down, wide, skip, attn, head, pair_fwd, pair_bwd, down_fwd, down_bwd, wide_fwd, wide_bwd, skip_low, attn_low, head_low)
    g_small[...] = jnp.zeros(g_small.shape, f32)
    g_late[...] = jnp.zeros(g_late.shape, f32)
    for planes in (in_a, in_b, in_g):
        edge = jnp.zeros((images, 4, HALF, C1), bf16)
        planes[:, :, 0] = edge
        planes[:, :, RES + 1] = edge
    for cells in (cells_c, cells_d, cells_g):
        edge = jnp.zeros((images, 3, HALF, cells.shape[-1]), bf16)
        cells[:, :, 0] = edge
        cells[:, :, HALF + 1] = edge

    for copy in keeps + arrivals:
        copy.wait()
    counting.step()

    def load_image(n):
        def step(i, carry):
            sums, squares = carry
            half = i // 2
            v = x_in[half, n, pl.ds((i % 2) * ROWS, ROWS)].astype(f32)
            flat[...] = v.reshape(ROWS * RES, C1)
            for b in range(2):
                w = flat[pl.ds(b, ROWS * HALF, stride=2), :].reshape(ROWS, HALF, C1)
                x_full[n, b, pl.ds(i * ROWS, ROWS)] = w
                sums = sums + fold(w)
                squares = squares + fold(w * w)
            return sums, squares

        sums, squares = lax.fori_loop(0, steps, step, (zero_n, zero_n))
        keep_coefs(coef_n, 0, n, norm_coefs(sums, squares, gain_n(0), gain_n(1), full_pixels))

    each(images, load_image)

    def activate(values, planes, which):
        def image(n):
            scale = row_of(coef_n, which, n, 0)
            offset = row_of(coef_n, which, n, 1)

            def step(i):
                for b in range(2):
                    v = values[n, b, pl.ds(i * ROWS, ROWS)]
                    store_planes(planes, n, b, i * ROWS, silu(v * scale + offset))

            each(steps, step)

        each(images, image)

    def pair_rows(result, n):
        part = result[n * half_pixels : (n + 1) * half_pixels].reshape(HALF, 1, HALF, 2 * C1)
        return jnp.concatenate([part[..., :C1], part[..., C1:]], axis=1).reshape(RES, HALF, C1)

    activate(x_full, in_a, 0)
    counting.step()
    for b in range(2):
        out = mm(pair_input(in_a, b, range(4)), pair_fwd[0])
        for n in range(images):
            h1_full[n, b] = pair_rows(out, n)

    def first_hidden(n):
        bias = time_bias[pl.ds(bucket(n), 1), :][:, :C1]

        def step(i, carry):
            sums, squares = carry
            for b in range(2):
                v = h1_full[n, b, pl.ds(i * ROWS, ROWS)] + bias
                h1_full[n, b, pl.ds(i * ROWS, ROWS)] = v
                sums = sums + fold(v)
                squares = squares + fold(v * v)
            return sums, squares

        sums, squares = lax.fori_loop(0, steps, step, (zero_n, zero_n))
        keep_coefs(coef_n, 1, n, norm_coefs(sums, squares, gain_n(2), gain_n(3), full_pixels))

    each(images, first_hidden)
    activate(h1_full, in_b, 1)
    counting.step()
    for b in range(2):
        out = mm(pair_input(in_b, b, range(4)), pair_fwd[1])
        for n in range(images):
            xs_full[n, b] = pair_rows(out, n)

    def first_out(n):
        def step(i, carry):
            sums, squares = carry
            for b in range(2):
                v = xs_full[n, b, pl.ds(i * ROWS, ROWS)]
                v = rounded((x_full[n, b, pl.ds(i * ROWS, ROWS)] + v) * root_half)
                xs_full[n, b, pl.ds(i * ROWS, ROWS)] = v
                sums = sums + fold(v)
                squares = squares + fold(v * v)
            return sums, squares

        sums, squares = lax.fori_loop(0, steps, step, (zero_n, zero_n))
        keep_coefs(coef_n, 2, n, norm_coefs(sums, squares, gain_n(4), gain_n(5), full_pixels))

    each(images, first_out)

    counting.step()

    def fir_down_image(n):
        scale = row_of(coef_n, 2, n, 0)
        offset = row_of(coef_n, 2, n, 1)
        for b in range(2):
            dy_full[n, b, 0] = jnp.zeros((HALF, C1), f32)
            dy_full[n, b, RES + 1] = jnp.zeros((HALF, C1), f32)

        def act_step(i):
            for b in range(2):
                v = xs_full[n, b, pl.ds(i * ROWS, ROWS)]
                dy_full[n, b, pl.ds(i * ROWS + 1, ROWS)] = silu(v * scale + offset)

        each(steps, act_step)

        def columns(rows):
            even, odd = rows
            return (
                0.125 * (shift_cols(odd, 1) + shift_cols(even, -1)) + 0.375 * (even + odd)
            )

        def taps(ref, b, r0, size):
            return [ref[n, b, pl.ds(r0 + t, size, stride=2)] for t in range(4)]

        def down_step(i):
            size = HALF // 2
            rows = []
            for b in range(2):
                t = taps(dy_full, b, 2 * size * i, size)
                rows.append(0.125 * (t[0] + t[3]) + 0.375 * (t[1] + t[2]))
            store_shifted(cells_c, n, i * size, columns(rows))

        each(2, down_step)
        for b in range(2):
            dy_full[n, b, pl.ds(1, RES)] = xs_full[n, b]

        def skip_step(i):
            size = HALF // 2
            rows = []
            for b in range(2):
                t = taps(dy_full, b, 2 * size * i, size)
                rows.append(0.125 * (t[0] + t[3]) + 0.375 * (t[1] + t[2]))
            fs_low[n, pl.ds(i * size * HALF, size * HALF)] = (
                columns(rows).reshape(size * HALF, C1).astype(bf16)
            )

        each(2, skip_step)

    each(images, fir_down_image)

    def wide_stats(v, which, n, row):
        values = norm_coefs(fold(v), fold(v * v), gain_w(row), gain_w(row + 1), half_pixels)
        keep_coefs(coef_w, which, n, values)
        return values[0][0:1, :], values[1][0:1, :]

    out = mm(cell_input(cells_c, range(3)), down_fwd[...])
    for n in range(images):
        v = out[n * half_pixels : (n + 1) * half_pixels] + time_bias[pl.ds(bucket(n), 1), :][:, C1:]
        h3[n] = v
        scale, offset = wide_stats(v, 0, n, 0)
        store_shifted(cells_d, n, 0, silu(v * scale + offset).reshape(HALF, HALF, HALF_CHANNELS))
    out = mm(cell_input(cells_d, range(3)), wide_fwd[...])
    out = out + mm(fs_low[...].reshape(-1, C1), skip_low[...])
    for n in range(images):
        v = out[n * half_pixels : (n + 1) * half_pixels] * root_half
        x2[n] = v
        scale, offset = wide_stats(v, 1, n, 2)
        n5[n] = (v * scale + offset).astype(bf16)
        qkv[n] = mm(n5[n], attn_low[:, : 3 * HALF_CHANNELS]).astype(bf16)
        q = qkv[n, :, :HALF_CHANNELS]
        k = qkv[n, :, HALF_CHANNELS : 2 * HALF_CHANNELS]
        w = qkv[n, :, 2 * HALF_CHANNELS :]
        logits = mm_nt(q, k) * logit_scale
        powers = jnp.exp(logits - jnp.max(logits, axis=1, keepdims=True))
        weights = powers / jnp.sum(powers, axis=1, keepdims=True)
        probs[n] = weights
        probs_low[n] = weights.astype(bf16)
        att[n] = mm(probs_low[n], w).astype(bf16)
        v = (v + mm(att[n], attn_low[:, 3 * HALF_CHANNELS :])) * root_half
        x3[n] = v
        scale, offset = wide_stats(v, 2, n, 4)
        a6[n] = silu(v * scale + offset).astype(bf16)

    counting.finish(counts)

    lane = lax.broadcasted_iota(jnp.int32, (RES, 2 * half_pixels), 1)
    source = lax.broadcasted_iota(jnp.int32, (RES, 2 * half_pixels), 0)
    picks = (source == 2 * (lane & (HALF - 1)) + (lane >> 8)).astype(bf16)
    row_lane = (lax.broadcasted_iota(jnp.int32, (HALF, 2 * half_pixels), 1) & (half_pixels - 1)) >> 4
    row_source = lax.broadcasted_iota(jnp.int32, (HALF, 2 * half_pixels), 0)
    component = lax.broadcasted_iota(jnp.int32, (8, half_pixels), 0)

    def spread(halves):
        moved = [mm(half, picks) for half in halves]
        rows = []
        for a in range(2):
            picked = sum(
                jnp.where(2 * row_lane + a == row_source + HALF * h, moved[h], 0.0)
                for h in range(2)
            )
            row = jnp.sum(picked, axis=0, keepdims=True)
            rows.append([row[:, :half_pixels], row[:, half_pixels:]])
        return rows

    loss = jnp.zeros((1, half_pixels), f32)
    head_grad = jnp.zeros((HEAD_ROWS, HALF_CHANNELS), f32)
    for n in range(images):
        moved = mm_nt(head_low[...].astype(bf16), a6[n])
        pred = head_forward(
            [[moved[(dy * 3 + dx) * 8 : (dy * 3 + dx) * 8 + 8] for dx in range(3)] for dy in range(3)]
        )
        wanted = [spread([target[h, n, c] for h in range(2)]) for c in range(3)]
        counted = spread([mask[h, n].astype(f32).astype(bf16) for h in range(2)])
        per_image = 1.0 / counts[pl.ds(bucket(n), 1), :]
        per_image = jnp.concatenate([per_image, per_image], axis=1)
        grad_pred = [[None, None], [None, None]]
        for a in range(2):
            for b in range(2):
                goal = jnp.zeros((8, half_pixels), f32)
                for c in range(3):
                    goal = jnp.where(component == c, wanted[c][a][b], goal)
                error = pred[a][b] - goal
                weight = counted[a][b] * per_image
                loss = loss + weight * jnp.sum(error * error, axis=0, keepdims=True)
                grad_pred[a][b] = rounded(2.0 * error * weight)
        table = head_backward(grad_pred)
        table = jnp.concatenate([table[dy][dx] for dy in range(3) for dx in range(3)], axis=0)
        parts = split_three(table)
        for part in parts:
            head_grad = head_grad + mm(part, a6[n])
        head_rows = head_low[...].astype(bf16)
        grad = sum(mm_tn(part, head_rows) for part in parts)
        v = x3[n]
        values = [coef_w[2, n, kind] for kind in range(4)]
        dy = rounded(grad) * slope(v * values[0][0:1, :] + values[1][0:1, :])
        gain, shift, ca, cb, cd = norm_grad_coefs(
            fold(dy), fold(dy * v), gain_w(4), values[2], values[3], half_pixels
        )
        g_small[WIDE_NORM_ROW + 4 : WIDE_NORM_ROW + 5, :] += gain[0:1, :]
        g_small[WIDE_NORM_ROW + 5 : WIDE_NORM_ROW + 6, :] += shift[0:1, :]
        grad_third = dy * ca[0:1, :] + v * cb[0:1, :] + cd[0:1, :]
        dwide[n] = grad_third
    g_small[0:HEAD_ROWS, :] = head_grad
    g_small[LOSS_ROW : LOSS_ROW + 1, :] = jnp.broadcast_to(
        jnp.sum(loss, axis=1, keepdims=True), (1, HALF_CHANNELS)
    )

    for n in range(images):
        grad_attn = (dwide[n] * root_half).astype(bf16)
        dout[n] = grad_attn
        grad_att = mm_nt(grad_attn, attn_low[:, 3 * HALF_CHANNELS :]).astype(bf16)
        q = qkv[n, :, :HALF_CHANNELS]
        k = qkv[n, :, HALF_CHANNELS : 2 * HALF_CHANNELS]
        w = qkv[n, :, 2 * HALF_CHANNELS :]
        grad_probs = mm_nt(grad_att, w)
        weights = probs[n]
        inner = jnp.sum(weights * grad_probs, axis=1, keepdims=True)
        grad_scores = (weights * (grad_probs - inner)).astype(bf16)
        dqkv[n, :, :HALF_CHANNELS] = (mm(grad_scores, k) * logit_scale).astype(bf16)
        dqkv[n, :, HALF_CHANNELS : 2 * HALF_CHANNELS] = (mm_tn(grad_scores, q) * logit_scale).astype(bf16)
        dqkv[n, :, 2 * HALF_CHANNELS :] = mm_tn(probs_low[n], grad_att).astype(bf16)
    keep_columns(
        g_attn, 0, mm_tn(n5[...].reshape(-1, HALF_CHANNELS), dqkv[...].reshape(-1, 3 * HALF_CHANNELS))
    )
    keep_columns(
        g_attn,
        6 * HALF_CHANNELS,
        mm_tn(att[...].reshape(-1, HALF_CHANNELS), dout[...].reshape(-1, HALF_CHANNELS)),
    )
    advance("attn")
    for n in range(images):
        dy = mm_nt(dqkv[n], attn_low[:, : 3 * HALF_CHANNELS])
        v = x2[n]
        gain, shift, ca, cb, cd = norm_grad_coefs(
            fold(dy), fold(dy * v), gain_w(2), coef_w[1, n, 2], coef_w[1, n, 3], half_pixels
        )
        g_small[WIDE_NORM_ROW + 2 : WIDE_NORM_ROW + 3, :] += gain[0:1, :]
        g_small[WIDE_NORM_ROW + 3 : WIDE_NORM_ROW + 4, :] += shift[0:1, :]
        grad = dy * ca[0:1, :] + v * cb[0:1, :] + cd[0:1, :] + dwide[n] * root_half
        store_shifted(cells_g, n, 0, (grad * root_half).reshape(HALF, HALF, HALF_CHANNELS))
        advance("gn_e%d" % n)

    center = cells_g[:, 1, 1 : HALF + 1].reshape(-1, HALF_CHANNELS)
    for dy in range(3):
        product = mm_tn(cell_input(cells_d, [dy]), center)
        for k in range(3):
            keep_columns(
                g_wide,
                (dy * 3 + k) * 2 * HALF_CHANNELS,
                product[k * HALF_CHANNELS : (k + 1) * HALF_CHANNELS],
            )
    keep_columns(g_down, SKIP_ROW, mm_tn(fs_low[...].reshape(-1, C1), center))
    advance("wide")
    dfs[...] = mm_nt(center, skip_low[...]).reshape(dfs.shape)
    out = mm_nt(cell_input(cells_g, range(3)), wide_bwd[...])
    advance("conv_d")
    bucket_rows = lax.broadcasted_iota(jnp.int32, (NB, HALF_CHANNELS), 0)
    time_wide = jnp.zeros((NB, HALF_CHANNELS), f32)
    for n in range(images):
        v = h3[n]
        dy = out[n * half_pixels : (n + 1) * half_pixels] * slope(
            v * row_of(coef_w, 0, n, 0) + row_of(coef_w, 0, n, 1)
        )
        gain, shift, ca, cb, cd = norm_grad_coefs(
            fold(dy), fold(dy * v), gain_w(0), coef_w[0, n, 2], coef_w[0, n, 3], half_pixels
        )
        g_small[WIDE_NORM_ROW : WIDE_NORM_ROW + 1, :] += gain[0:1, :]
        g_small[WIDE_NORM_ROW + 1 : WIDE_NORM_ROW + 2, :] += shift[0:1, :]
        grad = dy * ca[0:1, :] + v * cb[0:1, :] + cd[0:1, :]
        time_wide = time_wide + jnp.where(bucket_rows == bucket(n), total(fold(grad)), 0.0)
        store_shifted(cells_g, n, 0, grad.reshape(HALF, HALF, HALF_CHANNELS))
        advance("gn_d%d" % n)
    g_small[TIME_WIDE_ROW : TIME_WIDE_ROW + NB, :] = time_wide

    for c in range(2):
        g_rows[c * SMALL_ROWS : (c + 1) * SMALL_ROWS, :] = g_small[:, c * 128 : (c + 1) * 128]
    advance("gn_d")

    center = cells_g[:, 1, 1 : HALF + 1].reshape(-1, HALF_CHANNELS)
    for dy in range(3):
        product = mm_tn(cell_input(cells_c, [dy]), center)
        for k in range(3):
            keep_columns(g_down, (dy * 3 + k) * 2 * C1, product[k * C1 : (k + 1) * C1])
    advance("down")
    dnarrow[...] = mm_nt(cell_input(cells_g, range(3)), down_bwd[...]).reshape(dnarrow.shape)

    def up_parts(ref, n, i, size):
        here = pl.ds(i * size * HALF, size * HALF)
        g = ref[n, here].reshape(size, HALF, C1)
        lane_rows = lax.broadcasted_iota(jnp.int32, g.shape, 0) + i * size
        above = ref[n, pl.ds(jnp.maximum(i * size - 1, 0) * HALF, HALF)].reshape(1, HALF, C1)
        below = ref[n, pl.ds(jnp.minimum((i + 1) * size, HALF - 1) * HALF, HALF)].reshape(1, HALF, C1)
        above = jnp.where(lane_rows == 0, 0.0, jnp.concatenate([above, g[:-1]], axis=0))
        below = jnp.where(lane_rows == HALF - 1, 0.0, jnp.concatenate([g[1:], below], axis=0))
        result = []
        for rows in (0.375 * g + 0.125 * above, 0.375 * g + 0.125 * below):
            result.append(
                (
                    0.375 * rows + 0.125 * shift_cols(rows, 1),
                    0.375 * rows + 0.125 * shift_cols(rows, -1),
                )
            )
        return result

    def third_norm(n):
        size = HALF // 4
        scale = row_of(coef_n, 2, n, 0)
        offset = row_of(coef_n, 2, n, 1)

        def step(i, carry):
            sum_dy, sum_dyv = carry
            parts = up_parts(dnarrow, n, i, size)
            for b in range(2):
                g = jnp.stack([parts[0][b], parts[1][b]], axis=1).reshape(2 * size, HALF, C1)
                v = xs_full[n, b, pl.ds(i * 2 * size, 2 * size)]
                dy = g * slope(v * scale + offset)
                dy_full[n, b, pl.ds(i * 2 * size, 2 * size)] = dy
                sum_dy = sum_dy + fold(dy)
                sum_dyv = sum_dyv + fold(dy * v)
            return sum_dy, sum_dyv

        carry = (zero_n, zero_n)
        for part in range(2):
            carry = lax.fori_loop(2 * part, 2 * part + 2, step, carry)
            if part == 0:
                advance("t%da0" % n)
        sum_dy, sum_dyv = carry
        gain, shift, ca, cb, cd = norm_grad_coefs(
            sum_dy, sum_dyv, gain_n(4), coef_n[2, n, 2], coef_n[2, n, 3], full_pixels
        )
        g_late[4:5, :] += gain[0:1, :]
        g_late[5:6, :] += shift[0:1, :]
        advance("t%da1" % n)

        def finish(i):
            parts = up_parts(dfs, n, i, size)
            for b in range(2):
                g = jnp.stack([parts[0][b], parts[1][b]], axis=1).reshape(2 * size, HALF, C1)
                here = pl.ds(i * 2 * size, 2 * size)
                v = xs_full[n, b, here]
                g = g + dy_full[n, b, here] * ca[0:1, :] + v * cb[0:1, :] + cd[0:1, :]
                store_planes(in_g, n, b, i * 2 * size, rounded(g) * root_half)

        for part in range(2):
            each(2, lambda i: finish(2 * part + i))
            advance("t%db%d" % (n, part))

    advance("narrow")
    for n in range(images):
        third_norm(n)

    def pair_gradient(planes, member):
        products = None
        for b in range(2):
            grads = jnp.concatenate([plane_block(in_g, EVEN + b, a + 1) for a in range(2)], axis=1)
            part = [mm_tn(grads, pair_input(planes, b, jjs)) for jjs in ((0, 1), (2, 3))]
            products = part if products is None else [p + q for p, q in zip(products, part)]
        for dy in range(3):
            blocks = []
            for a in range(2):
                jj = dy + a
                wide_part = products[jj // 2][a * C1 : (a + 1) * C1]
                blocks.append(wide_part[:, (jj % 2) * 3 * C1 : (jj % 2 + 1) * 3 * C1])
            both = blocks[0] + blocks[1]
            for k in range(3):
                row = (dy * 3 + k) * C1
                (g_pair_b if member else g_pair_a)[row : row + C1, :] = both[:, k * C1 : (k + 1) * C1].T

    def back_through(member, values, which, gain_row, last):
        for b in range(2):
            out = mm_nt(pair_input(in_g, b, range(4)), pair_bwd[member])
            for n in range(images):
                dy_full[n, b, pl.ds(0, RES)] = pair_rows(out, n)
            advance("b%dc" % member if b else "b%dc0" % member)
        bucket_rows = lax.broadcasted_iota(jnp.int32, (NB, C1), 0)

        def image(n):
            scale = row_of(coef_n, which, n, 0)
            offset = row_of(coef_n, which, n, 1)

            def step(i, carry):
                sum_dy, sum_dyv = carry
                here = pl.ds(i * ROWS, ROWS)
                for b in range(2):
                    v = values[n, b, here]
                    dy = dy_full[n, b, here] * slope(v * scale + offset)
                    if not last:
                        dy_full[n, b, here] = dy
                    sum_dy = sum_dy + fold(dy)
                    sum_dyv = sum_dyv + fold(dy * v)
                return sum_dy, sum_dyv

            sum_dy, sum_dyv = lax.fori_loop(0, steps, step, (zero_n, zero_n))
            gain, shift, ca, cb, cd = norm_grad_coefs(
                sum_dy, sum_dyv, gain_n(gain_row), coef_n[which, n, 2], coef_n[which, n, 3], full_pixels
            )
            g_late[gain_row : gain_row + 1, :] += gain[0:1, :]
            g_late[gain_row + 1 : gain_row + 2, :] += shift[0:1, :]
            if last:
                return
            advance("b%di%da" % (member, n))

            def finish(i, carry):
                here = pl.ds(i * ROWS, ROWS)
                for b in range(2):
                    v = values[n, b, here]
                    g = dy_full[n, b, here] * ca[0:1, :] + v * cb[0:1, :] + cd[0:1, :]
                    carry = carry + fold(g)
                    store_planes(in_g, n, b, i * ROWS, g)
                return carry

            sums = total(lax.fori_loop(0, steps, finish, zero_n))
            g_late[TIME_NARROW_ROW : TIME_NARROW_ROW + NB, :] += jnp.where(
                bucket_rows == bucket(n), sums, 0.0
            )

        for n in range(images):
            image(n)
            advance("b%di%d" % (member, n))

    pair_gradient(in_b, 1)
    advance("pair_b")
    back_through(1, h1_full, 1, 2, False)
    pair_gradient(in_a, 0)
    advance("pair_a")
    back_through(0, x_full, 0, 0, True)
    pieces["late"] = Exchange(g_late[...], late_totals, arrived_late, late_sems, links.brief)
    advance("end")
    while any(piece.left() for piece in pieces.values()):
        for name, piece in pieces.items():
            if piece.left():
                piece.step()
    sum_late[...] = late_totals[len(links.brief)]


def main_call(dp_size, *operands):
    n = operands[1].shape[1]
    devices = 2 * dp_size
    counts = group_sizes(dp_size)
    orders = (counts[1], counts[1], counts[1], counts[1], counts[1], counts[1])
    grads = [padded(rows, devices, TILE) for rows in GRADS]
    sums = [(coded_rows(rows, devices), jnp.int16) for rows in GRADS]
    sums.append((padded(2 * SMALL_ROWS, devices, 8), f32))
    spaces = [message_rows(rows // 2, order[1:], TILE) for rows, order in zip(grads, orders)]
    sent = [message_rows(rows // 2, order[1:], TILE, 1) for rows, order in zip(grads, orders)]
    small_space = message_rows(sums[-1][0], orders[-1], 0)
    stages = sum(size - 1 for size in counts[1])
    vm = pltpu.VMEM
    full = (n, 2, RES, HALF, C1)
    planes = (n, 4, RES + 2, HALF, C1)
    wide = HALF_CHANNELS
    square = (n, HALF * HALF, wide)
    moved = [vm(v.shape, v.dtype) for v in operands[1:4] + operands[5:] + operands[3:4]]
    scratch = moved + [vm((rows, 128), f32) for rows in grads + [sums[-1][0]]]
    scratch += [vm((rows, 128), jnp.int16) for rows in sent]
    scratch += [vm((rows // 2, 128), f32) for rows in grads]
    scratch += [vm((rows, 128), jnp.int16) for rows in spaces] + [vm((small_space, 128), f32)]
    scratch += [pltpu.SemaphoreType.DMA((2, 2 * sum(size - 1 for size in order))) for order in orders]
    scratch += [
        vm((SMALL_ROWS, wide), f32),
        vm((LATE_ROWS, C1), f32),
        vm((len(counts[1]) + 1, NB, 128), f32),
        vm((sum(counts[1]), NB, 128), f32),
        vm((len(counts[1]) + 1, LATE_ROWS, 128), f32),
        vm((sum(counts[1]), LATE_ROWS, 128), f32),
        pltpu.SemaphoreType.DMA((2, 3)),
        pltpu.SemaphoreType.DMA((3,)),
        pltpu.SemaphoreType.DMA((2, stages)),
        pltpu.SemaphoreType.DMA((2, stages)),
        pltpu.SemaphoreType.DMA((11,)),
        vm((2, 12 * C1, 2 * C1), bf16),
        vm((2, 2 * C1, 12 * C1), bf16),
        vm((9 * C1, wide), bf16),
        vm((C1, 9 * wide), bf16),
        vm((9 * wide, wide), bf16),
        vm((wide, 9 * wide), bf16),
        vm((C1, wide), bf16),
        vm((wide, 4 * wide), bf16),
        vm((HEAD_ROWS, wide), f32),
        vm(full, f32),
        vm(full, f32),
        vm(full, f32),
        vm((n, 2, RES + 2, HALF, C1), f32),
        vm(planes, bf16),
        vm(planes, bf16),
        vm(planes, bf16),
        vm((ROWS * RES, C1), f32),
        vm((n, 3, HALF + 2, HALF, C1), bf16),
        vm((n, 3, HALF + 2, HALF, wide), bf16),
        vm((n, 3, HALF + 2, HALF, wide), bf16),
        vm((n, HALF * HALF, C1), bf16),
        vm((n, HALF * HALF, C1), f32),
        vm(square, f32),
        vm(square, f32),
        vm(square, f32),
        vm(square, bf16),
        vm((n, HALF * HALF, 3 * wide), bf16),
        vm(square, f32),
        vm(square, bf16),
        vm(square, bf16),
        vm(square, bf16),
        vm(square, f32),
        vm(square, bf16),
        vm((n, HALF * HALF, 3 * wide), bf16),
        vm((n, HALF * HALF, C1), f32),
        vm((3, n, 4, 8, C1), f32),
        vm((3, n, 4, 8, wide), f32),
    ]
    whole = pl.BlockSpec(memory_space=pltpu.VMEM)
    anywhere = pl.BlockSpec(memory_space=pltpu.HBM)
    return pl.pallas_call(
        functools.partial(main_kernel, dp_size),
        out_shape=[jax.ShapeDtypeStruct((rows, 128), dtype) for rows, dtype in sums + [(LATE_ROWS, f32), (NB, f32)]],
        in_specs=[pl.BlockSpec(memory_space=pltpu.SMEM)] + [anywhere] * 12,
        out_specs=[whole] * (len(sums) + 2),
        scratch_shapes=scratch,
        compiler_params=pltpu.CompilerParams(
            collective_id=0, has_side_effects=True, vmem_limit_bytes=MAIN_LIMIT + 1536 * (sum(grads) - sum(GRADS))
        ),
        cost_estimate=pl.CostEstimate(flops=8 * 10**9, bytes_accessed=12 * 10**6, transcendentals=0),
    )(*[pltpu.with_memory_space_constraint(v, pltpu.HBM) for v in operands])


PIECE_NAMES = ("attn", "wide", "down", "pair_b", "pair_a", "small")
SCHEDULE = {
    "attn": ("attn",),
    "wide": ("wide",),
    "conv_d": ("attn",),
    "gn_d": ("small",),
    "down": ("down",),
    "t0a0": ("wide", "small",),
    "t0a1": ("down", "attn",),
    "pair_b": ("pair_b", "attn",),
    "b1i0a": ("wide", "small", "pair_b",),
    "b1i1a": ("attn",),
    "pair_a": ("pair_a", "down",),
    "b0c": ("wide", "small", "pair_b", "pair_a",),
    "end": (
        "late", "down", "attn", "late", "pair_a", "wide", "attn", "small",
        "pair_b", "late", "down", "pair_a", "pair_b", "late", "wide", "small",
        "pair_a", "wide", "small", "down", "down", "pair_b", "pair_b", "pair_a",
        "pair_a",
    ),
}


def group_sizes(dp_size):
    bits = (dp_size - 1).bit_length()
    far = []
    k = 2
    while k < bits:
        far.append(1 << min(2, bits - k))
        k += 2
    return [2, 2, 2] + far, [2, 4] + far, [2] + far + [4]


class Links:
    def __init__(self, dp_size):
        dp = lax.axis_index("dp")
        sp = lax.axis_index("sp")
        core = dp % 2
        near = (dp // 2) % 2

        def along(unit, size):
            place = (dp // unit) % size
            return place, [(dp + unit * ((place + r) % size - place), sp) for r in range(1, size)]

        def pick(first, other):
            return first + core * (other - first)

        across = (dp, 1 - sp)
        beside = (dp + 2 * (1 - 2 * near), sp)
        second = (pick(near, sp), [(pick(beside[0], dp), pick(sp, 1 - sp))])
        third = (pick(sp, near), [(pick(dp, beside[0]), pick(1 - sp, sp))])
        place = 2 * near + sp
        square = []
        for r in range(1, 4):
            member = (place + r) % 4
            square.append((dp + 2 * (member // 2 - near), member % 2))
        far = []
        unit = 4
        for size in group_sizes(dp_size)[1][2:]:
            far.append(along(unit, size))
            unit *= size
        self.full = [along(1, 2), second, third] + far
        self.brief = [along(1, 2), (place, square)] + far
        self.far_first = [along(1, 2)] + far + [(place, square)]
        self.all = [other for _, others in self.brief for other in others]

    def greet(self):
        barrier = pltpu.get_barrier_semaphore()
        for other in self.all:
            pl.semaphore_signal(barrier, inc=1, device_id=other, device_id_type=MESH)

    def meet(self):
        pl.semaphore_wait(pltpu.get_barrier_semaphore(), len(self.all))


def send(source, target, sems, index, landing, other):
    return pltpu.make_async_remote_copy(
        src_ref=source,
        dst_ref=target,
        send_sem=sems.at[0, index],
        recv_sem=sems.at[1, landing],
        device_id=other,
        device_id_type=MESH,
    )


class Exchange:
    def __init__(self, value, totals, arrived, sems, stages):
        totals[0] = value
        self.totals, self.arrived, self.sems, self.stages = totals, arrived, sems, stages
        self.t = self.base = self.index = 0
        self.copies = []

    def left(self):
        return self.t <= len(self.stages)

    def step(self):
        if self.copies:
            for copy in self.copies:
                copy.wait()
            size = len(self.copies) + 1
            total_now = self.arrived[self.base]
            for m in range(1, size):
                total_now = total_now + self.arrived[self.base + m]
            self.totals[self.t] = total_now
            self.base += size
            self.index += size - 1
            self.copies = []
        if self.t < len(self.stages):
            place, others = self.stages[self.t]
            mine = self.totals.at[self.t]
            landing = self.arrived.at[self.base + place]
            for r, other in enumerate(others):
                copy = send(mine, landing, self.sems, self.index + r, self.index + len(others) - 1 - r, other)
                copy.start()
                self.copies.append(copy)
            self.arrived[self.base + place] = self.totals[self.t]
        self.t += 1

    def finish(self, out):
        while self.left():
            self.step()
        out[...] = self.totals[len(self.stages)]


def count_pixels(buckets, mask):
    rows = lax.broadcasted_iota(jnp.int32, (NB, 128), 0)
    counted = jnp.zeros((NB, 128), f32)
    images = mask.shape[1]
    for i in range(2 * images):
        pixels = mask[i // images, i % images].astype(f32)
        number = jnp.sum(jnp.sum(pixels, axis=0, keepdims=True), axis=1, keepdims=True)
        counted = counted + jnp.where(rows == buckets[i], number, 0.0)
    return counted


def chunk_of(rows):
    return next(c for c in (128, 96, 80, 64, 48, 32, 16, 8) if rows % c == 0)


def aligned(row, tile):
    return row if isinstance(row, int) else pl.multiple_of(row, tile)


def encode(source, first, rows, parts, target, base):
    part = rows // parts
    size = chunk_of(part)
    per_part = part // size

    def largest(i, carry):
        v = jnp.abs(source[pl.ds(aligned(first + i * size, 8), size), :])
        return jnp.maximum(carry, jnp.max(v.reshape(-1, 8, 128), axis=0))

    bound = lax.fori_loop(0, rows // size, largest, jnp.zeros((8, 128), f32))
    bound = jnp.max(bound, axis=0, keepdims=True)
    power = jnp.floor(jnp.log2(jnp.maximum(bound, 1e-30))) + 1.0
    scale = jnp.exp2(15.0 - power)

    def step(i):
        v = source[pl.ds(aligned(first + i * size, 8), size), :] * scale
        v = jnp.clip(jnp.round(v), -32767.0, 32767.0).astype(jnp.int32).astype(jnp.int16)
        row = base + i * size + (i // per_part) * TILE
        target[pl.ds(aligned(row, TILE), size), :] = v

    each(rows // size, step)
    tile = jnp.broadcast_to(power.astype(jnp.int32), (TILE, 128)).astype(jnp.int16)
    for m in range(parts):
        target[pl.ds(aligned(base + m * (part + TILE) + part, TILE), TILE), :] = tile


def decode(source, base, rows):
    power = source[pl.ds(aligned(base + rows, TILE), TILE), :].astype(jnp.int32).astype(f32)
    return jnp.exp2(power[0:1, :] - 15.0)


def message_rows(rows, sizes, tile, own=0):
    needed = 0
    for size in sizes:
        rows //= size
        needed += (size - 1 + (own if size > 2 else 0)) * (rows + tile)
    return needed


class Piece:
    def __init__(self, source, outgoing, half, arrived, out, sems, stages):
        self.source, self.outgoing, self.half, self.arrived = source, outgoing, half, arrived
        self.out, self.sems = out, sems
        self.stages = stages
        self.tile = 0 if outgoing is None else TILE
        self.rows = source.shape[0]
        self.first = 0
        self.base = self.sent = self.index = self.t = 0
        self.copies = []
        self.share = self.rows
        for _, others in stages:
            self.share //= len(others) + 1

    def left(self):
        return self.t <= 2 * len(self.stages)

    def step(self):
        count = len(self.stages)
        if 0 < self.t <= count:
            self.scatter_end(self.stages[self.t - 1])
        elif self.t > count:
            self.gather_end(self.stages[2 * count - self.t])
        if self.t == count:
            self.keep()
        if self.t < count:
            self.scatter_start(self.stages[self.t])
        elif self.t < 2 * count:
            self.gather_start(self.stages[2 * count - 1 - self.t])
        self.t += 1

    def scatter_start(self, stage):
        place, others = stage
        size = len(others) + 1
        rows = self.rows // size
        raw = self.half is not None and self.t == 0
        tile = 0 if raw else self.tile
        block = rows + tile
        arrived = self.half if raw else self.arrived
        if tile and size > 2:
            encode(self.source, self.first, self.rows, size, self.outgoing, self.sent)
        for r, other in enumerate(others):
            member = (place + r + 1) % size
            part = self.first + member * rows
            if tile and size > 2:
                message = self.outgoing.at[pl.ds(aligned(self.sent + member * block, TILE), block)]
            elif tile:
                encode(self.source, part, rows, 1, self.outgoing, self.sent)
                message = self.outgoing.at[pl.ds(self.sent, block)]
            else:
                message = self.source.at[pl.ds(aligned(part, 8), rows)]
            landing = size - 2 - r
            copy = send(
                message,
                arrived.at[pl.ds(self.base + landing * block, block)],
                self.sems,
                self.index + r,
                self.index + landing,
                other,
            )
            copy.start()
            self.copies.append(copy)

    def scatter_end(self, stage):
        place, others = stage
        size = len(others) + 1
        rows = self.rows // size
        raw = self.half is not None and self.t == 1
        tile = 0 if raw else self.tile
        block = rows + tile
        arrived = self.half if raw else self.arrived
        for copy in self.copies:
            copy.wait()
        first = self.first + place * rows
        scales = [decode(arrived, self.base + r * block, rows) if tile else 1.0 for r in range(size - 1)]
        chunk = chunk_of(rows)

        def add(i):
            here = pl.ds(aligned(first + i * chunk, 8), chunk)
            v = self.source[here, :]
            for r, scale in enumerate(scales):
                more = arrived[pl.ds(aligned(self.base + r * block + i * chunk, tile or 8), chunk), :]
                v = v + (more.astype(jnp.int32).astype(f32) * scale if tile else more)
            self.source[here, :] = v

        each(rows // chunk, add)
        self.first, self.rows = first, rows
        if not raw:
            self.base += (size - 1) * block
            self.sent += (size if size > 2 else 1) * block
        self.index += size - 1
        self.copies = []

    def keep(self):
        block = self.share + self.tile
        self.place = 0
        for place, others in self.stages:
            self.place = self.place * (len(others) + 1) + place
        self.first = self.place * block
        self.rows = block
        if self.tile:
            encode(self.source, self.place * self.share, self.share, 1, self.out, self.first)
        else:
            self.out[pl.ds(aligned(self.first, 8), block), :] = self.source[
                pl.ds(aligned(self.first, 8), block), :
            ]

    def gather_start(self, stage):
        place, others = stage
        here = self.out.at[pl.ds(aligned(self.first, self.tile or 8), self.rows)]
        for r, other in enumerate(others):
            copy = send(here, here, self.sems, self.index + r, self.index + len(others) - 1 - r, other)
            copy.start()
            self.copies.append(copy)

    def gather_end(self, stage):
        place, others = stage
        size = len(others) + 1
        for copy in self.copies:
            copy.wait()
        self.copies = []
        self.index += size - 1
        self.first = self.first - place * self.rows
        self.rows = self.rows * size


def adamw(weight, grad, first, second, rate):
    first = beta_one * first + (1.0 - beta_one) * grad
    second = beta_two * second + (1.0 - beta_two) * grad * grad
    power = jnp.maximum(second * (1.0 / (1.0 - beta_two**STEP)), 1e-36)
    root = power * lax.rsqrt(power) + adam_epsilon
    scale = rate / (1.0 - beta_one**STEP)
    return weight * (1.0 - rate * decay_rate) - scale * first / root, first, second


PARTS = (
    (2, 1, HALF_CHANNELS, 0, 3, 0),
    (2, 1, HALF_CHANNELS, 6 * HALF_CHANNELS, 3, 3 * HALF_CHANNELS),
    (2, 1, HALF_CHANNELS, 12 * HALF_CHANNELS, 3, 6 * HALF_CHANNELS),
    (4, 0, HALF_CHANNELS, 0, 1, 0),
    (1, 2, C1, 0, 9, 0),
    (3, 2, C1, 18 * C1, 1, 0),
    (0, 3, C1, 0, 9, 9 * C1),
    (0, 4, C1, 0, 9, 0),
)
LARGE = 5


def update_kernel(devices, *refs):
    count = len(GRADS)
    coded, (g_small, g_late, counts), refs = refs[:count], refs[count : count + 3], refs[count + 3 :]
    members = [refs[3 * i : 3 + 3 * i] for i in range(9)]
    outs = [refs[27 + 3 * i : 30 + 3 * i] for i in range(9)]
    loss_out, counts_out = refs[54:56]
    refs = refs[56:]
    grads, refs = refs[:count], refs[count:]
    staged = [refs[3 * i : 3 * i + 3] for i in range(LARGE)]
    store_sems = refs[3 * LARGE]

    def small(row, rows, lanes):
        parts = [g_small[c * SMALL_ROWS + row : c * SMALL_ROWS + row + rows, :] for c in range(lanes // 128)]
        return parts[0] if len(parts) == 1 else jnp.concatenate(parts, axis=1)

    def single(member, index, grad, rate):
        w, m, v = (ref[index] for ref in members[member])
        for out, value in zip(outs[member], adamw(w, grad, m, v, rate)):
            out[index] = value

    def unpack(source, grad):
        share = grad.shape[0] // devices

        def shares(i):
            base = i * (share + TILE)
            v = source[pl.ds(aligned(base, TILE), share), :].astype(jnp.int32).astype(f32)
            grad[pl.ds(aligned(i * share, 8), share), :] = v * decode(source, base, share)

        each(devices, shares)

    def update(part):
        member, which, block_rows, base, blocks, start = part
        size = 64
        grad = grads[which]
        columns = staged[member][0].shape[1] // 128

        def step(i):
            block = i // (block_rows // size)
            row = (i % (block_rows // size)) * size
            here = pl.ds(aligned(start + block * block_rows + row, 8), size)
            for c in range(columns):
                lanes = slice(c * 128, (c + 1) * 128)
                g = grad[pl.ds(aligned(base + (block * columns + c) * block_rows + row, 8), size), :]
                w, m, v = (ref[here, lanes] for ref in members[member])
                for out, value in zip(staged[member], adamw(w, g, m, v, rate_matrix)):
                    out[here, lanes] = value

        each(blocks * block_rows // size, step)

    stores = []
    seen = set()
    for i, part in enumerate(PARTS):
        member, which, block_rows, _, blocks, start = part
        if which not in seen:
            unpack(coded[which], grads[which])
            seen.add(which)
        update(part)
        here = pl.ds(start, block_rows * blocks)
        for kind in range(3):
            copy = pltpu.make_async_copy(
                staged[member][kind].at[here], outs[member][kind].at[here], store_sems.at[i, kind]
            )
            copy.start()
            stores.append(copy)
    for tap in range(9):
        single(5, (tap,), small(tap * 8, 3, HALF_CHANNELS), rate_matrix)
    every = slice(None)
    single(6, (every, every), g_late[:6, :], rate_vector)
    single(7, (every, every), small(WIDE_NORM_ROW, 6, HALF_CHANNELS), rate_vector)
    single(8, (every, slice(0, C1)), g_late[TIME_NARROW_ROW : TIME_NARROW_ROW + NB, :], rate_vector)
    single(8, (every, slice(C1, None)), small(TIME_WIDE_ROW, NB, HALF_CHANNELS), rate_vector)
    loss_out[...] = g_small[LOSS_ROW : LOSS_ROW + 1, :]
    diagonal = lax.broadcasted_iota(jnp.int32, (NB, 128), 0) == lax.broadcasted_iota(jnp.int32, (NB, 128), 1)
    counts_out[...] = jnp.sum(jnp.where(diagonal, counts[...], 0.0), axis=0, keepdims=True)[:, :NB]
    for copy in stores:
        copy.wait()


def update_call(devices, grads, members):
    whole = pl.BlockSpec(memory_space=pltpu.VMEM)
    outside = pl.BlockSpec(memory_space=pltpu.HBM)
    flat = [v for member in members for v in member]
    large = [v.shape for v in flat[: 3 * LARGE]]
    return pl.pallas_call(
        functools.partial(update_kernel, devices),
        out_shape=[jax.ShapeDtypeStruct(v.shape, f32) for v in flat]
        + [jax.ShapeDtypeStruct((1, 128), f32), jax.ShapeDtypeStruct((1, NB), f32)],
        in_specs=[whole] * (len(grads) + len(flat)),
        out_specs=[outside] * (3 * LARGE) + [whole] * (len(flat) - 3 * LARGE + 2),
        scratch_shapes=[pltpu.VMEM((padded(rows, devices, TILE), 128), f32) for rows in GRADS]
        + [pltpu.VMEM(shape, f32) for shape in large]
        + [pltpu.SemaphoreType.DMA((len(PARTS), 3))],
        compiler_params=pltpu.CompilerParams(vmem_limit_bytes=UPDATE_LIMIT),
        cost_estimate=pl.CostEstimate(flops=30 * 10**6, bytes_accessed=40 * 10**6, transcendentals=0),
    )(*grads, *flat)


def on_device(
    features,
    target,
    pixel_mask,
    buckets,
    conv_pair,
    down_conv,
    conv_wide,
    skip_proj,
    attn_proj,
    head_conv,
    norm_narrow,
    norm_wide,
    time_bias,
    conv_pair_mom,
    down_conv_mom,
    conv_wide_mom,
    skip_proj_mom,
    attn_proj_mom,
    head_conv_mom,
    norm_narrow_mom,
    norm_wide_mom,
    time_bias_mom,
    conv_pair_sq,
    down_conv_sq,
    conv_wide_sq,
    skip_proj_sq,
    attn_proj_sq,
    head_conv_sq,
    norm_narrow_sq,
    norm_wide_sq,
    time_bias_sq,
):
    dp_size = lax.axis_size("dp")
    images = features.shape[0] // 2

    def halves(tensor):
        return tensor.reshape((2, images) + tensor.shape[1:])

    def flat(tensor):
        return tensor.reshape(-1, tensor.shape[-1])

    def head_rows(tensor):
        return jnp.transpose(tensor, (0, 1, 3, 2)).reshape(9, 3, HALF_CHANNELS)

    params = (
        flat(conv_pair),
        flat(down_conv),
        flat(conv_wide),
        skip_proj,
        attn_proj,
        head_rows(head_conv),
        norm_narrow,
        norm_wide,
        time_bias,
    )
    firsts = (
        flat(conv_pair_mom),
        flat(down_conv_mom),
        flat(conv_wide_mom),
        skip_proj_mom,
        attn_proj_mom,
        head_rows(head_conv_mom),
        norm_narrow_mom,
        norm_wide_mom,
        time_bias_mom,
    )
    seconds = (
        flat(conv_pair_sq),
        flat(down_conv_sq),
        flat(conv_wide_sq),
        skip_proj_sq,
        attn_proj_sq,
        head_rows(head_conv_sq),
        norm_narrow_sq,
        norm_wide_sq,
        time_bias_sq,
    )
    summed = main_call(
        dp_size,
        buckets,
        halves(features),
        halves(jnp.transpose(target, (0, 3, 1, 2))),
        halves(pixel_mask),
        *params,
    )
    results = update_call(2 * dp_size, summed, list(zip(params, firsts, seconds)))
    shaped = []
    for member, like in enumerate((conv_pair, down_conv, conv_wide, skip_proj, attn_proj)):
        shaped.extend(v.reshape(like.shape) for v in results[3 * member : 3 * member + 3])
    for v in results[15:18]:
        shaped.append(jnp.transpose(v.reshape(3, 3, 3, HALF_CHANNELS), (0, 1, 3, 2)))
    shaped.extend(results[18:27])
    return (results[27][0, 0], results[28].reshape(NB)) + tuple(shaped)


def solution(mesh):
    placed = (
        P("dp", "sp", None, None),
        P("dp", "sp", None, None),
        P("dp", "sp", None),
        P("dp"),
        P(),
        P(),
        P(),
        P(),
        P(),
        P(),
        P(),
        P(),
        P(),
        P(),
        P(),
        P(),
        P(),
        P(),
        P(),
        P(),
        P(),
        P(),
        P(),
        P(),
        P(),
        P(),
        P(),
        P(),
        P(),
        P(),
        P(),
    )
    return jax.shard_map(
        on_device,
        mesh=mesh,
        in_specs=placed,
        out_specs=(
            P(),
            P(),
            P(),
            P(),
            P(),
            P(),
            P(),
            P(),
            P(),
            P(),
            P(),
            P(),
            P(),
            P(),
            P(),
            P(),
            P(),
            P(),
            P(),
            P(),
            P(),
            P(),
            P(),
            P(),
            P(),
            P(),
            P(),
            P(),
            P(),
        ),
        check_vma=False,
    )
```

```python
import functools

import jax
import jax.numpy as jnp
from jax import lax
from jax.experimental import pallas as pl
from jax.experimental.pallas import tpu as pltpu
from jax.sharding import PartitionSpec as P

C1 = 128
HALF_CHANNELS = 256
GROUPS = 32
RES = 32
HALF = 16
NB = 8
STEP = 10
MESH = pl.DeviceIdType.MESH
MAIN_LIMIT = 41 * 1024 * 1024
UPDATE_LIMIT = 26 * 1024 * 1024

epsilon = 1e-05
root_half = 0.7071067811865476
beta_one = 0.9
beta_two = 0.999
adam_epsilon = 1e-08
decay_rate = 0.1
rate_matrix = 0.03
rate_vector = 0.5
logit_scale = HALF_CHANNELS ** (-0.5)
ROWS = 8

bf16 = jnp.bfloat16
f32 = jnp.float32

EVEN, ODD, ODD_LEFT, EVEN_RIGHT = 0, 1, 2, 3
TAPS = ((ODD_LEFT, EVEN, ODD), (EVEN, ODD, EVEN_RIGHT))


def rounded(v):
    return v.astype(bf16).astype(f32)


def silu(t):
    return t * jax.nn.sigmoid(t)


def slope(t):
    s = jax.nn.sigmoid(t)
    return s * (1.0 + t * (1.0 - s))


def mm(a, b):
    return lax.dot_general(a, b, (((1,), (0,)), ((), ())), preferred_element_type=f32)


def mm_nt(a, b):
    return lax.dot_general(a, b, (((1,), (1,)), ((), ())), preferred_element_type=f32)


def mm_tn(a, b):
    return lax.dot_general(a, b, (((0,), (0,)), ((), ())), preferred_element_type=f32)


def fold(v):
    return jnp.sum(v.reshape(-1, 8, v.shape[-1]), axis=0)


def total(v):
    return jnp.broadcast_to(jnp.sum(v, axis=0, keepdims=True), v.shape)


def group_sum(v, size):
    lanes = v.shape[-1]
    lane = lax.broadcasted_iota(jnp.int32, v.shape, 1)
    step = 1
    while step < size:
        other = jnp.where(
            (lane & step) == 0, pltpu.roll(v, lanes - step, 1), pltpu.roll(v, step, 1)
        )
        v = v + other
        step *= 2
    return v


def norm_coefs(sums, squares, gain, shift, pixels):
    size = sums.shape[-1] // GROUPS
    count = pixels * size
    mean = group_sum(total(sums), size) / count
    power = group_sum(total(squares), size) / count
    inv = lax.rsqrt(power - mean * mean + epsilon)
    scale = inv * gain
    return scale, shift - mean * scale, mean, inv


def norm_grad_coefs(sum_dy, sum_dyv, gain, mean, inv, pixels):
    size = sum_dy.shape[-1] // GROUPS
    count = pixels * size
    first = total(sum_dy)
    second = (total(sum_dyv) - mean * first) * inv
    one = group_sum(first * gain, size) / count
    two = group_sum(second * gain, size) / count
    b = -inv * inv * two
    return second, first, inv * gain, b, -inv * one - mean * b


def shift_cols(v, step):
    col = lax.broadcasted_iota(jnp.int32, v.shape, 1)
    if step == 1:
        return jnp.where(col == 0, 0.0, pltpu.roll(v, 1, 1))
    return jnp.where(col == HALF - 1, 0.0, pltpu.roll(v, HALF - 1, 1))


def store_planes(planes, n, b, r0, v):
    rows = v.shape[0]
    v = v.astype(bf16).astype(f32)
    for plane, value in (
        (EVEN + b, v),
        (ODD_LEFT if b == 1 else EVEN_RIGHT, shift_cols(v, 1 if b == 1 else -1)),
    ):
        planes[n, plane, pl.ds(r0 + 1, rows)] = value.astype(bf16)


def store_shifted(cells, n, r0, v):
    rows = v.shape[0]
    v = v.astype(bf16).astype(f32)
    for tap, value in ((0, shift_cols(v, 1)), (1, v), (2, shift_cols(v, -1))):
        cells[n, tap, pl.ds(r0 + 1, rows)] = value.astype(bf16)


def plane_block(planes, tap, jj):
    return planes[:, tap, pl.ds(jj, HALF, stride=2)].reshape(-1, planes.shape[-1])


def pair_input(planes, b, jjs):
    return jnp.concatenate([plane_block(planes, tap, jj) for jj in jjs for tap in TAPS[b]], axis=1)


def cell_input(cells, dys):
    return jnp.concatenate(
        [
            cells[:, tap, dy : dy + HALF].reshape(-1, cells.shape[-1])
            for dy in dys
            for tap in range(3)
        ],
        axis=1,
    )


def each(count, body, unroll=1):
    def step(i, carry):
        body(i)
        return carry

    lax.fori_loop(0, count, step, 0, unroll=unroll)


def prepare_weights(pair, down, wide, skip, attn, head, pair_fwd, pair_bwd, down_fwd, down_bwd, wide_fwd, wide_bwd, skip_low, attn_low, head_low):
    nothing = jnp.zeros((C1, C1), bf16)
    for member in range(2):
        for jj in range(4):
            for k in range(3):
                block = (jj * 3 + k) * C1
                for a in range(2):
                    dy = jj - a
                    inside = 0 <= dy < 3
                    row = (dy * 3 + k) * C1
                    back = ((2 - dy) * 3 + (2 - k)) * C1
                    pair_fwd[member, block : block + C1, a * C1 : a * C1 + C1] = (
                        pair[member][row : row + C1, :].astype(bf16) if inside else nothing
                    )
                    pair_bwd[member, a * C1 : a * C1 + C1, block : block + C1] = (
                        pair[member][back : back + C1, :].astype(bf16) if inside else nothing
                    )
    wide_channels = HALF_CHANNELS
    for tap in range(9):
        low = down[tap * C1 : tap * C1 + C1, :].astype(bf16)
        down_fwd[tap * C1 : tap * C1 + C1, :] = low
        down_bwd[:, (8 - tap) * wide_channels : (9 - tap) * wide_channels] = low
        low = wide[tap * wide_channels : (tap + 1) * wide_channels, :].astype(bf16)
        wide_fwd[tap * wide_channels : (tap + 1) * wide_channels, :] = low
        wide_bwd[:, (8 - tap) * wide_channels : (9 - tap) * wide_channels] = low
    skip_low[...] = skip[...].astype(bf16)
    attn_low[...] = attn[...].astype(bf16)
    head_low[...] = jnp.zeros(head_low.shape, f32)
    for tap in range(9):
        head_low[tap * 8 : tap * 8 + 3, :] = rounded(head[tap])


def split_three(v):
    high = v.astype(bf16)
    rest = v - high.astype(f32)
    middle = rest.astype(bf16)
    return high, middle, (rest - middle.astype(f32)).astype(bf16)


def lane_shift(v, step):
    lane = lax.broadcasted_iota(jnp.int32, v.shape, 1)
    j = lane & (HALF - 1)
    if step == 1:
        keep = j < HALF - 1
    elif step == -1:
        keep = j > 0
    elif step == HALF:
        keep = lane < HALF * (HALF - 1)
    else:
        keep = lane >= HALF
    return jnp.where(keep, pltpu.roll(v, (-step) % v.shape[-1], 1), 0.0)


def head_forward(table):
    cols = [
        [
            lane_shift(table[dy][0], -1) + table[dy][1] + table[dy][2],
            table[dy][0] + table[dy][1] + lane_shift(table[dy][2], 1),
        ]
        for dy in range(3)
    ]
    return [
        [
            lane_shift(cols[0][b], -HALF) + cols[1][b] + cols[2][b]
            if a == 0
            else cols[0][b] + cols[1][b] + lane_shift(cols[2][b], HALF)
            for b in range(2)
        ]
        for a in range(2)
    ]


def head_backward(grad):
    rows = [
        [
            lane_shift(grad[0][b], HALF) + grad[1][b],
            grad[0][b] + grad[1][b],
            grad[0][b] + lane_shift(grad[1][b], -HALF),
        ]
        for b in range(2)
    ]
    return [
        [
            lane_shift(rows[0][dy], 1) + rows[1][dy],
            rows[0][dy] + rows[1][dy],
            rows[0][dy] + lane_shift(rows[1][dy], -1),
        ]
        for dy in range(3)
    ]


def keep_columns(ref, row, v):
    for c in range(v.shape[1] // 128):
        ref[row + c * v.shape[0] : row + (c + 1) * v.shape[0], :] = v[:, c * 128 : (c + 1) * 128]


HEAD_ROWS = 72
WIDE_NORM_ROW = 72
LOSS_ROW = 78
TIME_WIDE_ROW = 80
SMALL_ROWS = 96
TIME_NARROW_ROW = 8
LATE_ROWS = 16
SKIP_ROW = 18 * C1
ATTN_ROWS = 8 * HALF_CHANNELS
WIDE_ROWS = 18 * HALF_CHANNELS
DOWN_ROWS = 20 * C1
PAIR_ROWS = 9 * C1
GRADS = (ATTN_ROWS, WIDE_ROWS, DOWN_ROWS, PAIR_ROWS, PAIR_ROWS)
TILE = 16


def padded(rows, devices, tile):
    return -(-rows // (devices * tile)) * devices * tile


def coded_rows(rows, devices):
    return padded(rows, devices, TILE) + devices * TILE


def main_kernel(
    dp_size,
    buckets, features, target_rows, mask_rows, pair_all, down_all, wide_all, skip_all, attn_all, head_all,
    narrow_all, gains_all, time_all,
    sum_attn, sum_wide, sum_down, sum_pair_b, sum_pair_a, sum_small, sum_late, counts,
    x_in, target, mask, down, wide, skip, attn, head, gains_narrow, gains_wide, time_bias, mask_local,
    g_attn, g_wide, g_down, g_pair_b, g_pair_a, g_rows,
    out_attn, out_wide, out_down, out_pair_b, out_pair_a,
    half_attn, half_wide, half_down, half_pair_b, half_pair_a,
    in_attn, in_wide, in_down, in_pair_b, in_pair_a, in_small,
    sems_attn, sems_wide, sems_down, sems_pair_b, sems_pair_a, sems_small,
    g_small, g_late,
    totals, arrived_totals, late_totals, arrived_late, image_sems, local_sems, count_sems, late_sems, weight_sems,
    pair_fwd, pair_bwd, down_fwd, down_bwd, wide_fwd, wide_bwd, skip_low, attn_low, head_low,
    x_full, h1_full, xs_full, dy_full, in_a, in_b, in_g, flat,
    cells_c, cells_d, cells_g, fs_low, dfs, h3, x2, x3, n5, qkv, probs, probs_low, att, a6, dwide, dout, dqkv, dnarrow,
    coef_n, coef_w,
):
    loads = [
        pltpu.make_async_copy(source, ref, weight_sems.at[i])
        for i, (source, ref) in enumerate(
            (
                (pair_all.at[:PAIR_ROWS], g_pair_a.at[:PAIR_ROWS]),
                (pair_all.at[PAIR_ROWS:], g_pair_b.at[:PAIR_ROWS]),
                (down_all, down),
                (wide_all, wide),
                (skip_all, skip),
                (attn_all, attn),
                (head_all, head),
                (narrow_all, gains_narrow),
                (gains_all, gains_wide),
                (time_all, time_bias),
                (mask_rows, mask_local),
            )
        )
    ]
    links = Links(dp_size)
    links.greet()
    for copy in loads[::-1]:
        copy.start()
    loads.pop().wait()
    counted = count_pixels(buckets, mask_local)
    links.meet()
    here = (lax.axis_index("dp"), 1 - lax.axis_index("sp"))
    moved = ((features, x_in), (target_rows, target), (mask_rows, mask))
    side = lax.axis_index("sp")
    arrivals = [
        send(source.at[1 - side], out.at[side], image_sems, i, i, here) for i, (source, out) in enumerate(moved)
    ]
    for copy in arrivals:
        copy.start()
    keeps = [
        pltpu.make_async_copy(source.at[side], out.at[side], local_sems.at[i])
        for i, (source, out) in enumerate(moved)
    ]
    for copy in keeps:
        copy.start()
    images = x_in.shape[1]
    position = lax.axis_index("sp")
    steps = RES // ROWS
    full_pixels = RES * RES
    half_pixels = HALF * HALF
    zero_n = jnp.zeros((8, C1), f32)
    zero_w = jnp.zeros((8, HALF_CHANNELS), f32)

    def bucket(n):
        return buckets[position * images + n]

    def gain_n(row):
        return jnp.broadcast_to(gains_narrow[row : row + 1, :], (8, C1))

    def gain_w(row):
        return jnp.broadcast_to(gains_wide[row : row + 1, :], (8, HALF_CHANNELS))

    def keep_coefs(ref, which, n, values):
        for kind in range(4):
            ref[which, n, kind] = values[kind]

    def row_of(ref, which, n, kind):
        return ref[which, n, kind, 0:1, :]

    counting = Exchange(counted, totals, arrived_totals, count_sems, links.brief)
    counting.step()
    sources = (g_attn, g_wide, g_down, g_pair_b, g_pair_a, g_rows)
    outgoing = (out_attn, out_wide, out_down, out_pair_b, out_pair_a, None)
    halves = (half_attn, half_wide, half_down, half_pair_b, half_pair_a, None)
    incoming = (in_attn, in_wide, in_down, in_pair_b, in_pair_a, in_small)
    outs = (sum_attn, sum_wide, sum_down, sum_pair_b, sum_pair_a, sum_small)
    sems = (sems_attn, sems_wide, sems_down, sems_pair_b, sems_pair_a, sems_small)
    orders = (links.brief, links.brief, links.brief, links.brief, links.brief, links.brief)
    pieces = dict(zip(PIECE_NAMES, (Piece(*parts) for parts in zip(sources, outgoing, halves, incoming, outs, sems, orders))))

    def advance(point):
        for name in SCHEDULE.get(point, ()):
            pieces[name].step()

    for rows, ref in zip(GRADS + (2 * SMALL_ROWS,), sources):
        if ref.shape[0] > rows:
            ref[rows:, :] = jnp.zeros((ref.shape[0] - rows, 128), f32)
    for copy in loads:
        copy.wait()
    prepare_weights((g_pair_a, g_pair_b), down, wide, skip, attn, head, pair_fwd, pair_bwd, down_fwd, down_bwd, wide_fwd, wide_bwd, skip_low, attn_low, head_low)
    g_small[...] = jnp.zeros(g_small.shape, f32)
    g_late[...] = jnp.zeros(g_late.shape, f32)
    for planes in (in_a, in_b, in_g):
        edge = jnp.zeros((images, 4, HALF, C1), bf16)
        planes[:, :, 0] = edge
        planes[:, :, RES + 1] = edge
    for cells in (cells_c, cells_d, cells_g):
        edge = jnp.zeros((images, 3, HALF, cells.shape[-1]), bf16)
        cells[:, :, 0] = edge
        cells[:, :, HALF + 1] = edge

    for copy in keeps + arrivals:
        copy.wait()
    counting.step()

    def load_image(n):
        def step(i, carry):
            sums, squares = carry
            half = i // 2
            v = x_in[half, n, pl.ds((i % 2) * ROWS, ROWS)].astype(f32)
            flat[...] = v.reshape(ROWS * RES, C1)
            for b in range(2):
                w = flat[pl.ds(b, ROWS * HALF, stride=2), :].reshape(ROWS, HALF, C1)
                x_full[n, b, pl.ds(i * ROWS, ROWS)] = w
                sums = sums + fold(w)
                squares = squares + fold(w * w)
            return sums, squares

        sums, squares = lax.fori_loop(0, steps, step, (zero_n, zero_n))
        keep_coefs(coef_n, 0, n, norm_coefs(sums, squares, gain_n(0), gain_n(1), full_pixels))

    each(images, load_image)

    def activate(values, planes, which):
        def image(n):
            scale = row_of(coef_n, which, n, 0)
            offset = row_of(coef_n, which, n, 1)

            def step(i):
                for b in range(2):
                    v = values[n, b, pl.ds(i * ROWS, ROWS)]
                    store_planes(planes, n, b, i * ROWS, silu(v * scale + offset))

            each(steps, step)

        each(images, image)

    def pair_rows(result, n):
        part = result[n * half_pixels : (n + 1) * half_pixels].reshape(HALF, 1, HALF, 2 * C1)
        return jnp.concatenate([part[..., :C1], part[..., C1:]], axis=1).reshape(RES, HALF, C1)

    activate(x_full, in_a, 0)
    counting.step()
    for b in range(2):
        out = mm(pair_input(in_a, b, range(4)), pair_fwd[0])
        for n in range(images):
            h1_full[n, b] = pair_rows(out, n)

    def first_hidden(n):
        bias = time_bias[pl.ds(bucket(n), 1), :][:, :C1]

        def step(i, carry):
            sums, squares = carry
            for b in range(2):
                v = h1_full[n, b, pl.ds(i * ROWS, ROWS)] + bias
                h1_full[n, b, pl.ds(i * ROWS, ROWS)] = v
                sums = sums + fold(v)
                squares = squares + fold(v * v)
            return sums, squares

        sums, squares = lax.fori_loop(0, steps, step, (zero_n, zero_n))
        keep_coefs(coef_n, 1, n, norm_coefs(sums, squares, gain_n(2), gain_n(3), full_pixels))

    each(images, first_hidden)
    activate(h1_full, in_b, 1)
    counting.step()
    for b in range(2):
        out = mm(pair_input(in_b, b, range(4)), pair_fwd[1])
        for n in range(images):
            xs_full[n, b] = pair_rows(out, n)

    def first_out(n):
        def step(i, carry):
            sums, squares = carry
            for b in range(2):
                v = xs_full[n, b, pl.ds(i * ROWS, ROWS)]
                v = rounded((x_full[n, b, pl.ds(i * ROWS, ROWS)] + v) * root_half)
                xs_full[n, b, pl.ds(i * ROWS, ROWS)] = v
                sums = sums + fold(v)
                squares = squares + fold(v * v)
            return sums, squares

        sums, squares = lax.fori_loop(0, steps, step, (zero_n, zero_n))
        keep_coefs(coef_n, 2, n, norm_coefs(sums, squares, gain_n(4), gain_n(5), full_pixels))

    each(images, first_out)

    counting.step()

    def fir_down_image(n):
        scale = row_of(coef_n, 2, n, 0)
        offset = row_of(coef_n, 2, n, 1)
        for b in range(2):
            dy_full[n, b, 0] = jnp.zeros((HALF, C1), f32)
            dy_full[n, b, RES + 1] = jnp.zeros((HALF, C1), f32)

        def act_step(i):
            for b in range(2):
                v = xs_full[n, b, pl.ds(i * ROWS, ROWS)]
                dy_full[n, b, pl.ds(i * ROWS + 1, ROWS)] = silu(v * scale + offset)

        each(steps, act_step)

        def columns(rows):
            even, odd = rows
            return (
                0.125 * (shift_cols(odd, 1) + shift_cols(even, -1)) + 0.375 * (even + odd)
            )

        def taps(ref, b, r0, size):
            return [ref[n, b, pl.ds(r0 + t, size, stride=2)] for t in range(4)]

        def down_step(i):
            size = HALF // 2
            rows = []
            for b in range(2):
                t = taps(dy_full, b, 2 * size * i, size)
                rows.append(0.125 * (t[0] + t[3]) + 0.375 * (t[1] + t[2]))
            store_shifted(cells_c, n, i * size, columns(rows))

        each(2, down_step)
        for b in range(2):
            dy_full[n, b, pl.ds(1, RES)] = xs_full[n, b]

        def skip_step(i):
            size = HALF // 2
            rows = []
            for b in range(2):
                t = taps(dy_full, b, 2 * size * i, size)
                rows.append(0.125 * (t[0] + t[3]) + 0.375 * (t[1] + t[2]))
            fs_low[n, pl.ds(i * size * HALF, size * HALF)] = (
                columns(rows).reshape(size * HALF, C1).astype(bf16)
            )

        each(2, skip_step)

    each(images, fir_down_image)

    def wide_stats(v, which, n, row):
        values = norm_coefs(fold(v), fold(v * v), gain_w(row), gain_w(row + 1), half_pixels)
        keep_coefs(coef_w, which, n, values)
        return values[0][0:1, :], values[1][0:1, :]

    out = mm(cell_input(cells_c, range(3)), down_fwd[...])
    for n in range(images):
        v = out[n * half_pixels : (n + 1) * half_pixels] + time_bias[pl.ds(bucket(n), 1), :][:, C1:]
        h3[n] = v
        scale, offset = wide_stats(v, 0, n, 0)
        store_shifted(cells_d, n, 0, silu(v * scale + offset).reshape(HALF, HALF, HALF_CHANNELS))
    out = mm(cell_input(cells_d, range(3)), wide_fwd[...])
    out = out + mm(fs_low[...].reshape(-1, C1), skip_low[...])
    for n in range(images):
        v = out[n * half_pixels : (n + 1) * half_pixels] * root_half
        x2[n] = v
        scale, offset = wide_stats(v, 1, n, 2)
        n5[n] = (v * scale + offset).astype(bf16)
        qkv[n] = mm(n5[n], attn_low[:, : 3 * HALF_CHANNELS]).astype(bf16)
        q = qkv[n, :, :HALF_CHANNELS]
        k = qkv[n, :, HALF_CHANNELS : 2 * HALF_CHANNELS]
        w = qkv[n, :, 2 * HALF_CHANNELS :]
        logits = mm_nt(q, k) * logit_scale
        powers = jnp.exp(logits - jnp.max(logits, axis=1, keepdims=True))
        weights = powers / jnp.sum(powers, axis=1, keepdims=True)
        probs[n] = weights
        probs_low[n] = weights.astype(bf16)
        att[n] = mm(probs_low[n], w).astype(bf16)
        v = (v + mm(att[n], attn_low[:, 3 * HALF_CHANNELS :])) * root_half
        x3[n] = v
        scale, offset = wide_stats(v, 2, n, 4)
        a6[n] = silu(v * scale + offset).astype(bf16)

    counting.finish(counts)

    lane = lax.broadcasted_iota(jnp.int32, (RES, 2 * half_pixels), 1)
    source = lax.broadcasted_iota(jnp.int32, (RES, 2 * half_pixels), 0)
    picks = (source == 2 * (lane & (HALF - 1)) + (lane >> 8)).astype(bf16)
    row_lane = (lax.broadcasted_iota(jnp.int32, (HALF, 2 * half_pixels), 1) & (half_pixels - 1)) >> 4
    row_source = lax.broadcasted_iota(jnp.int32, (HALF, 2 * half_pixels), 0)
    component = lax.broadcasted_iota(jnp.int32, (8, half_pixels), 0)

    def spread(halves):
        moved = [mm(half, picks) for half in halves]
        rows = []
        for a in range(2):
            picked = sum(
                jnp.where(2 * row_lane + a == row_source + HALF * h, moved[h], 0.0)
                for h in range(2)
            )
            row = jnp.sum(picked, axis=0, keepdims=True)
            rows.append([row[:, :half_pixels], row[:, half_pixels:]])
        return rows

    loss = jnp.zeros((1, half_pixels), f32)
    head_grad = jnp.zeros((HEAD_ROWS, HALF_CHANNELS), f32)
    for n in range(images):
        moved = mm_nt(head_low[...].astype(bf16), a6[n])
        pred = head_forward(
            [[moved[(dy * 3 + dx) * 8 : (dy * 3 + dx) * 8 + 8] for dx in range(3)] for dy in range(3)]
        )
        wanted = [spread([target[h, n, c] for h in range(2)]) for c in range(3)]
        counted = spread([mask[h, n].astype(f32).astype(bf16) for h in range(2)])
        per_image = 1.0 / counts[pl.ds(bucket(n), 1), :]
        per_image = jnp.concatenate([per_image, per_image], axis=1)
        grad_pred = [[None, None], [None, None]]
        for a in range(2):
            for b in range(2):
                goal = jnp.zeros((8, half_pixels), f32)
                for c in range(3):
                    goal = jnp.where(component == c, wanted[c][a][b], goal)
                error = pred[a][b] - goal
                weight = counted[a][b] * per_image
                loss = loss + weight * jnp.sum(error * error, axis=0, keepdims=True)
                grad_pred[a][b] = rounded(2.0 * error * weight)
        table = head_backward(grad_pred)
        table = jnp.concatenate([table[dy][dx] for dy in range(3) for dx in range(3)], axis=0)
        parts = split_three(table)
        for part in parts:
            head_grad = head_grad + mm(part, a6[n])
        head_rows = head_low[...].astype(bf16)
        grad = sum(mm_tn(part, head_rows) for part in parts)
        v = x3[n]
        values = [coef_w[2, n, kind] for kind in range(4)]
        dy = rounded(grad) * slope(v * values[0][0:1, :] + values[1][0:1, :])
        gain, shift, ca, cb, cd = norm_grad_coefs(
            fold(dy), fold(dy * v), gain_w(4), values[2], values[3], half_pixels
        )
        g_small[WIDE_NORM_ROW + 4 : WIDE_NORM_ROW + 5, :] += gain[0:1, :]
        g_small[WIDE_NORM_ROW + 5 : WIDE_NORM_ROW + 6, :] += shift[0:1, :]
        grad_third = dy * ca[0:1, :] + v * cb[0:1, :] + cd[0:1, :]
        dwide[n] = grad_third
    g_small[0:HEAD_ROWS, :] = head_grad
    g_small[LOSS_ROW : LOSS_ROW + 1, :] = jnp.broadcast_to(
        jnp.sum(loss, axis=1, keepdims=True), (1, HALF_CHANNELS)
    )

    for n in range(images):
        grad_attn = (dwide[n] * root_half).astype(bf16)
        dout[n] = grad_attn
        grad_att = mm_nt(grad_attn, attn_low[:, 3 * HALF_CHANNELS :]).astype(bf16)
        q = qkv[n, :, :HALF_CHANNELS]
        k = qkv[n, :, HALF_CHANNELS : 2 * HALF_CHANNELS]
        w = qkv[n, :, 2 * HALF_CHANNELS :]
        grad_probs = mm_nt(grad_att, w)
        weights = probs[n]
        inner = jnp.sum(weights * grad_probs, axis=1, keepdims=True)
        grad_scores = (weights * (grad_probs - inner)).astype(bf16)
        dqkv[n, :, :HALF_CHANNELS] = (mm(grad_scores, k) * logit_scale).astype(bf16)
        dqkv[n, :, HALF_CHANNELS : 2 * HALF_CHANNELS] = (mm_tn(grad_scores, q) * logit_scale).astype(bf16)
        dqkv[n, :, 2 * HALF_CHANNELS :] = mm_tn(probs_low[n], grad_att).astype(bf16)
    keep_columns(
        g_attn, 0, mm_tn(n5[...].reshape(-1, HALF_CHANNELS), dqkv[...].reshape(-1, 3 * HALF_CHANNELS))
    )
    keep_columns(
        g_attn,
        6 * HALF_CHANNELS,
        mm_tn(att[...].reshape(-1, HALF_CHANNELS), dout[...].reshape(-1, HALF_CHANNELS)),
    )
    advance("attn")
    for n in range(images):
        dy = mm_nt(dqkv[n], attn_low[:, : 3 * HALF_CHANNELS])
        v = x2[n]
        gain, shift, ca, cb, cd = norm_grad_coefs(
            fold(dy), fold(dy * v), gain_w(2), coef_w[1, n, 2], coef_w[1, n, 3], half_pixels
        )
        g_small[WIDE_NORM_ROW + 2 : WIDE_NORM_ROW + 3, :] += gain[0:1, :]
        g_small[WIDE_NORM_ROW + 3 : WIDE_NORM_ROW + 4, :] += shift[0:1, :]
        grad = dy * ca[0:1, :] + v * cb[0:1, :] + cd[0:1, :] + dwide[n] * root_half
        store_shifted(cells_g, n, 0, (grad * root_half).reshape(HALF, HALF, HALF_CHANNELS))
        advance("gn_e%d" % n)

    center = cells_g[:, 1, 1 : HALF + 1].reshape(-1, HALF_CHANNELS)
    for dy in range(3):
        product = mm_tn(cell_input(cells_d, [dy]), center)
        for k in range(3):
            keep_columns(
                g_wide,
                (dy * 3 + k) * 2 * HALF_CHANNELS,
                product[k * HALF_CHANNELS : (k + 1) * HALF_CHANNELS],
            )
    keep_columns(g_down, SKIP_ROW, mm_tn(fs_low[...].reshape(-1, C1), center))
    advance("wide")
    dfs[...] = mm_nt(center, skip_low[...]).reshape(dfs.shape)
    out = mm_nt(cell_input(cells_g, range(3)), wide_bwd[...])
    advance("conv_d")
    bucket_rows = lax.broadcasted_iota(jnp.int32, (NB, HALF_CHANNELS), 0)
    time_wide = jnp.zeros((NB, HALF_CHANNELS), f32)
    for n in range(images):
        v = h3[n]
        dy = out[n * half_pixels : (n + 1) * half_pixels] * slope(
            v * row_of(coef_w, 0, n, 0) + row_of(coef_w, 0, n, 1)
        )
        gain, shift, ca, cb, cd = norm_grad_coefs(
            fold(dy), fold(dy * v), gain_w(0), coef_w[0, n, 2], coef_w[0, n, 3], half_pixels
        )
        g_small[WIDE_NORM_ROW : WIDE_NORM_ROW + 1, :] += gain[0:1, :]
        g_small[WIDE_NORM_ROW + 1 : WIDE_NORM_ROW + 2, :] += shift[0:1, :]
        grad = dy * ca[0:1, :] + v * cb[0:1, :] + cd[0:1, :]
        time_wide = time_wide + jnp.where(bucket_rows == bucket(n), total(fold(grad)), 0.0)
        store_shifted(cells_g, n, 0, grad.reshape(HALF, HALF, HALF_CHANNELS))
        advance("gn_d%d" % n)
    g_small[TIME_WIDE_ROW : TIME_WIDE_ROW + NB, :] = time_wide

    for c in range(2):
        g_rows[c * SMALL_ROWS : (c + 1) * SMALL_ROWS, :] = g_small[:, c * 128 : (c + 1) * 128]
    advance("gn_d")

    center = cells_g[:, 1, 1 : HALF + 1].reshape(-1, HALF_CHANNELS)
    for dy in range(3):
        product = mm_tn(cell_input(cells_c, [dy]), center)
        for k in range(3):
            keep_columns(g_down, (dy * 3 + k) * 2 * C1, product[k * C1 : (k + 1) * C1])
    advance("down")
    dnarrow[...] = mm_nt(cell_input(cells_g, range(3)), down_bwd[...]).reshape(dnarrow.shape)

    def up_parts(ref, n, i, size):
        here = pl.ds(i * size * HALF, size * HALF)
        g = ref[n, here].reshape(size, HALF, C1)
        lane_rows = lax.broadcasted_iota(jnp.int32, g.shape, 0) + i * size
        above = ref[n, pl.ds(jnp.maximum(i * size - 1, 0) * HALF, HALF)].reshape(1, HALF, C1)
        below = ref[n, pl.ds(jnp.minimum((i + 1) * size, HALF - 1) * HALF, HALF)].reshape(1, HALF, C1)
        above = jnp.where(lane_rows == 0, 0.0, jnp.concatenate([above, g[:-1]], axis=0))
        below = jnp.where(lane_rows == HALF - 1, 0.0, jnp.concatenate([g[1:], below], axis=0))
        result = []
        for rows in (0.375 * g + 0.125 * above, 0.375 * g + 0.125 * below):
            result.append(
                (
                    0.375 * rows + 0.125 * shift_cols(rows, 1),
                    0.375 * rows + 0.125 * shift_cols(rows, -1),
                )
            )
        return result

    def third_norm(n):
        size = HALF // 4
        scale = row_of(coef_n, 2, n, 0)
        offset = row_of(coef_n, 2, n, 1)

        def step(i, carry):
            sum_dy, sum_dyv = carry
            parts = up_parts(dnarrow, n, i, size)
            for b in range(2):
                g = jnp.stack([parts[0][b], parts[1][b]], axis=1).reshape(2 * size, HALF, C1)
                v = xs_full[n, b, pl.ds(i * 2 * size, 2 * size)]
                dy = g * slope(v * scale + offset)
                dy_full[n, b, pl.ds(i * 2 * size, 2 * size)] = dy
                sum_dy = sum_dy + fold(dy)
                sum_dyv = sum_dyv + fold(dy * v)
            return sum_dy, sum_dyv

        carry = (zero_n, zero_n)
        for part in range(2):
            carry = lax.fori_loop(2 * part, 2 * part + 2, step, carry)
            if part == 0:
                advance("t%da0" % n)
        sum_dy, sum_dyv = carry
        gain, shift, ca, cb, cd = norm_grad_coefs(
            sum_dy, sum_dyv, gain_n(4), coef_n[2, n, 2], coef_n[2, n, 3], full_pixels
        )
        g_late[4:5, :] += gain[0:1, :]
        g_late[5:6, :] += shift[0:1, :]
        advance("t%da1" % n)

        def finish(i):
            parts = up_parts(dfs, n, i, size)
            for b in range(2):
                g = jnp.stack([parts[0][b], parts[1][b]], axis=1).reshape(2 * size, HALF, C1)
                here = pl.ds(i * 2 * size, 2 * size)
                v = xs_full[n, b, here]
                g = g + dy_full[n, b, here] * ca[0:1, :] + v * cb[0:1, :] + cd[0:1, :]
                store_planes(in_g, n, b, i * 2 * size, rounded(g) * root_half)

        for part in range(2):
            each(2, lambda i: finish(2 * part + i))
            advance("t%db%d" % (n, part))

    advance("narrow")
    for n in range(images):
        third_norm(n)

    def pair_gradient(planes, member):
        products = None
        for b in range(2):
            grads = jnp.concatenate([plane_block(in_g, EVEN + b, a + 1) for a in range(2)], axis=1)
            part = [mm_tn(grads, pair_input(planes, b, jjs)) for jjs in ((0, 1), (2, 3))]
            products = part if products is None else [p + q for p, q in zip(products, part)]
        for dy in range(3):
            blocks = []
            for a in range(2):
                jj = dy + a
                wide_part = products[jj // 2][a * C1 : (a + 1) * C1]
                blocks.append(wide_part[:, (jj % 2) * 3 * C1 : (jj % 2 + 1) * 3 * C1])
            both = blocks[0] + blocks[1]
            for k in range(3):
                row = (dy * 3 + k) * C1
                (g_pair_b if member else g_pair_a)[row : row + C1, :] = both[:, k * C1 : (k + 1) * C1].T

    def back_through(member, values, which, gain_row, last):
        for b in range(2):
            out = mm_nt(pair_input(in_g, b, range(4)), pair_bwd[member])
            for n in range(images):
                dy_full[n, b, pl.ds(0, RES)] = pair_rows(out, n)
            advance("b%dc" % member if b else "b%dc0" % member)
        bucket_rows = lax.broadcasted_iota(jnp.int32, (NB, C1), 0)

        def image(n):
            scale = row_of(coef_n, which, n, 0)
            offset = row_of(coef_n, which, n, 1)

            def step(i, carry):
                sum_dy, sum_dyv = carry
                here = pl.ds(i * ROWS, ROWS)
                for b in range(2):
                    v = values[n, b, here]
                    dy = dy_full[n, b, here] * slope(v * scale + offset)
                    if not last:
                        dy_full[n, b, here] = dy
                    sum_dy = sum_dy + fold(dy)
                    sum_dyv = sum_dyv + fold(dy * v)
                return sum_dy, sum_dyv

            sum_dy, sum_dyv = lax.fori_loop(0, steps, step, (zero_n, zero_n))
            gain, shift, ca, cb, cd = norm_grad_coefs(
                sum_dy, sum_dyv, gain_n(gain_row), coef_n[which, n, 2], coef_n[which, n, 3], full_pixels
            )
            g_late[gain_row : gain_row + 1, :] += gain[0:1, :]
            g_late[gain_row + 1 : gain_row + 2, :] += shift[0:1, :]
            if last:
                return
            advance("b%di%da" % (member, n))

            def finish(i, carry):
                here = pl.ds(i * ROWS, ROWS)
                for b in range(2):
                    v = values[n, b, here]
                    g = dy_full[n, b, here] * ca[0:1, :] + v * cb[0:1, :] + cd[0:1, :]
                    carry = carry + fold(g)
                    store_planes(in_g, n, b, i * ROWS, g)
                return carry

            sums = total(lax.fori_loop(0, steps, finish, zero_n))
            g_late[TIME_NARROW_ROW : TIME_NARROW_ROW + NB, :] += jnp.where(
                bucket_rows == bucket(n), sums, 0.0
            )

        for n in range(images):
            image(n)
            advance("b%di%d" % (member, n))

    pair_gradient(in_b, 1)
    advance("pair_b")
    back_through(1, h1_full, 1, 2, False)
    pair_gradient(in_a, 0)
    advance("pair_a")
    back_through(0, x_full, 0, 0, True)
    pieces["late"] = Exchange(g_late[...], late_totals, arrived_late, late_sems, links.brief)
    advance("end")
    while any(piece.left() for piece in pieces.values()):
        for name, piece in pieces.items():
            if piece.left():
                piece.step()
    sum_late[...] = late_totals[len(links.brief)]


def main_call(dp_size, *operands):
    n = operands[1].shape[1]
    devices = 2 * dp_size
    counts = group_sizes(dp_size)
    orders = (counts[1], counts[1], counts[1], counts[1], counts[1], counts[1])
    grads = [padded(rows, devices, TILE) for rows in GRADS]
    sums = [(coded_rows(rows, devices), jnp.int16) for rows in GRADS]
    sums.append((padded(2 * SMALL_ROWS, devices, 8), f32))
    spaces = [message_rows(rows // 2, order[1:], TILE) for rows, order in zip(grads, orders)]
    sent = [message_rows(rows // 2, order[1:], TILE, 1) for rows, order in zip(grads, orders)]
    small_space = message_rows(sums[-1][0], orders[-1], 0)
    stages = sum(size - 1 for size in counts[1])
    vm = pltpu.VMEM
    full = (n, 2, RES, HALF, C1)
    planes = (n, 4, RES + 2, HALF, C1)
    wide = HALF_CHANNELS
    square = (n, HALF * HALF, wide)
    moved = [vm(v.shape, v.dtype) for v in operands[1:4] + operands[5:] + operands[3:4]]
    scratch = moved + [vm((rows, 128), f32) for rows in grads + [sums[-1][0]]]
    scratch += [vm((rows, 128), jnp.int16) for rows in sent]
    scratch += [vm((rows // 2, 128), f32) for rows in grads]
    scratch += [vm((rows, 128), jnp.int16) for rows in spaces] + [vm((small_space, 128), f32)]
    scratch += [pltpu.SemaphoreType.DMA((2, 2 * sum(size - 1 for size in order))) for order in orders]
    scratch += [
        vm((SMALL_ROWS, wide), f32),
        vm((LATE_ROWS, C1), f32),
        vm((len(counts[1]) + 1, NB, 128), f32),
        vm((sum(counts[1]), NB, 128), f32),
        vm((len(counts[1]) + 1, LATE_ROWS, 128), f32),
        vm((sum(counts[1]), LATE_ROWS, 128), f32),
        pltpu.SemaphoreType.DMA((2, 3)),
        pltpu.SemaphoreType.DMA((3,)),
        pltpu.SemaphoreType.DMA((2, stages)),
        pltpu.SemaphoreType.DMA((2, stages)),
        pltpu.SemaphoreType.DMA((11,)),
        vm((2, 12 * C1, 2 * C1), bf16),
        vm((2, 2 * C1, 12 * C1), bf16),
        vm((9 * C1, wide), bf16),
        vm((C1, 9 * wide), bf16),
        vm((9 * wide, wide), bf16),
        vm((wide, 9 * wide), bf16),
        vm((C1, wide), bf16),
        vm((wide, 4 * wide), bf16),
        vm((HEAD_ROWS, wide), f32),
        vm(full, f32),
        vm(full, f32),
        vm(full, f32),
        vm((n, 2, RES + 2, HALF, C1), f32),
        vm(planes, bf16),
        vm(planes, bf16),
        vm(planes, bf16),
        vm((ROWS * RES, C1), f32),
        vm((n, 3, HALF + 2, HALF, C1), bf16),
        vm((n, 3, HALF + 2, HALF, wide), bf16),
        vm((n, 3, HALF + 2, HALF, wide), bf16),
        vm((n, HALF * HALF, C1), bf16),
        vm((n, HALF * HALF, C1), f32),
        vm(square, f32),
        vm(square, f32),
        vm(square, f32),
        vm(square, bf16),
        vm((n, HALF * HALF, 3 * wide), bf16),
        vm(square, f32),
        vm(square, bf16),
        vm(square, bf16),
        vm(square, bf16),
        vm(square, f32),
        vm(square, bf16),
        vm((n, HALF * HALF, 3 * wide), bf16),
        vm((n, HALF * HALF, C1), f32),
        vm((3, n, 4, 8, C1), f32),
        vm((3, n, 4, 8, wide), f32),
    ]
    whole = pl.BlockSpec(memory_space=pltpu.VMEM)
    anywhere = pl.BlockSpec(memory_space=pltpu.HBM)
    return pl.pallas_call(
        functools.partial(main_kernel, dp_size),
        out_shape=[jax.ShapeDtypeStruct((rows, 128), dtype) for rows, dtype in sums + [(LATE_ROWS, f32), (NB, f32)]],
        in_specs=[pl.BlockSpec(memory_space=pltpu.SMEM)] + [anywhere] * 12,
        out_specs=[whole] * (len(sums) + 2),
        scratch_shapes=scratch,
        compiler_params=pltpu.CompilerParams(
            collective_id=0, has_side_effects=True, vmem_limit_bytes=MAIN_LIMIT + 1536 * (sum(grads) - sum(GRADS))
        ),
        cost_estimate=pl.CostEstimate(flops=8 * 10**9, bytes_accessed=12 * 10**6, transcendentals=0),
    )(*[pltpu.with_memory_space_constraint(v, pltpu.HBM) for v in operands])


PIECE_NAMES = ("attn", "wide", "down", "pair_b", "pair_a", "small")
SCHEDULE = {
    "attn": ("attn",),
    "wide": ("wide",),
    "conv_d": ("attn",),
    "gn_d": ("small",),
    "down": ("down",),
    "t0a0": ("wide", "small",),
    "t0a1": ("down", "attn",),
    "pair_b": ("pair_b", "attn",),
    "b1i0a": ("wide", "small", "pair_b",),
    "b1i1a": ("attn",),
    "pair_a": ("pair_a", "down",),
    "b0c": ("wide", "small", "pair_b", "pair_a",),
    "end": (
        "late", "down", "attn", "late", "pair_a", "wide", "attn", "small",
        "pair_b", "late", "down", "pair_a", "pair_b", "late", "wide", "small",
        "pair_a", "wide", "small", "down", "down", "pair_b", "pair_b", "pair_a",
        "pair_a",
    ),
}


def group_sizes(dp_size):
    bits = (dp_size - 1).bit_length()
    far = []
    k = 2
    while k < bits:
        far.append(1 << min(2, bits - k))
        k += 2
    return [2, 2, 2] + far, [2, 4] + far, [2] + far + [4]


class Links:
    def __init__(self, dp_size):
        dp = lax.axis_index("dp")
        sp = lax.axis_index("sp")
        core = dp % 2
        near = (dp // 2) % 2

        def along(unit, size):
            place = (dp // unit) % size
            return place, [(dp + unit * ((place + r) % size - place), sp) for r in range(1, size)]

        def pick(first, other):
            return first + core * (other - first)

        across = (dp, 1 - sp)
        beside = (dp + 2 * (1 - 2 * near), sp)
        second = (pick(near, sp), [(pick(beside[0], dp), pick(sp, 1 - sp))])
        third = (pick(sp, near), [(pick(dp, beside[0]), pick(1 - sp, sp))])
        place = 2 * near + sp
        square = []
        for r in range(1, 4):
            member = (place + r) % 4
            square.append((dp + 2 * (member // 2 - near), member % 2))
        far = []
        unit = 4
        for size in group_sizes(dp_size)[1][2:]:
            far.append(along(unit, size))
            unit *= size
        self.full = [along(1, 2), second, third] + far
        self.brief = [along(1, 2), (place, square)] + far
        self.far_first = [along(1, 2)] + far + [(place, square)]
        self.all = [other for _, others in self.brief for other in others]

    def greet(self):
        barrier = pltpu.get_barrier_semaphore()
        for other in self.all:
            pl.semaphore_signal(barrier, inc=1, device_id=other, device_id_type=MESH)

    def meet(self):
        pl.semaphore_wait(pltpu.get_barrier_semaphore(), len(self.all))


def send(source, target, sems, index, landing, other):
    return pltpu.make_async_remote_copy(
        src_ref=source,
        dst_ref=target,
        send_sem=sems.at[0, index],
        recv_sem=sems.at[1, landing],
        device_id=other,
        device_id_type=MESH,
    )


class Exchange:
    def __init__(self, value, totals, arrived, sems, stages):
        totals[0] = value
        self.totals, self.arrived, self.sems, self.stages = totals, arrived, sems, stages
        self.t = self.base = self.index = 0
        self.copies = []

    def left(self):
        return self.t <= len(self.stages)

    def step(self):
        if self.copies:
            for copy in self.copies:
                copy.wait()
            size = len(self.copies) + 1
            total_now = self.arrived[self.base]
            for m in range(1, size):
                total_now = total_now + self.arrived[self.base + m]
            self.totals[self.t] = total_now
            self.base += size
            self.index += size - 1
            self.copies = []
        if self.t < len(self.stages):
            place, others = self.stages[self.t]
            mine = self.totals.at[self.t]
            landing = self.arrived.at[self.base + place]
            for r, other in enumerate(others):
                copy = send(mine, landing, self.sems, self.index + r, self.index + len(others) - 1 - r, other)
                copy.start()
                self.copies.append(copy)
            self.arrived[self.base + place] = self.totals[self.t]
        self.t += 1

    def finish(self, out):
        while self.left():
            self.step()
        out[...] = self.totals[len(self.stages)]


def count_pixels(buckets, mask):
    rows = lax.broadcasted_iota(jnp.int32, (NB, 128), 0)
    counted = jnp.zeros((NB, 128), f32)
    images = mask.shape[1]
    for i in range(2 * images):
        pixels = mask[i // images, i % images].astype(f32)
        number = jnp.sum(jnp.sum(pixels, axis=0, keepdims=True), axis=1, keepdims=True)
        counted = counted + jnp.where(rows == buckets[i], number, 0.0)
    return counted


def chunk_of(rows):
    return next(c for c in (128, 96, 80, 64, 48, 32, 16, 8) if rows % c == 0)


def aligned(row, tile):
    return row if isinstance(row, int) else pl.multiple_of(row, tile)


def encode(source, first, rows, parts, target, base):
    part = rows // parts
    size = chunk_of(part)
    per_part = part // size

    def largest(i, carry):
        v = jnp.abs(source[pl.ds(aligned(first + i * size, 8), size), :])
        return jnp.maximum(carry, jnp.max(v.reshape(-1, 8, 128), axis=0))

    bound = lax.fori_loop(0, rows // size, largest, jnp.zeros((8, 128), f32))
    bound = jnp.max(bound, axis=0, keepdims=True)
    power = jnp.floor(jnp.log2(jnp.maximum(bound, 1e-30))) + 1.0
    scale = jnp.exp2(15.0 - power)

    def step(i):
        v = source[pl.ds(aligned(first + i * size, 8), size), :] * scale
        v = jnp.clip(jnp.round(v), -32767.0, 32767.0).astype(jnp.int32).astype(jnp.int16)
        row = base + i * size + (i // per_part) * TILE
        target[pl.ds(aligned(row, TILE), size), :] = v

    each(rows // size, step)
    tile = jnp.broadcast_to(power.astype(jnp.int32), (TILE, 128)).astype(jnp.int16)
    for m in range(parts):
        target[pl.ds(aligned(base + m * (part + TILE) + part, TILE), TILE), :] = tile


def decode(source, base, rows):
    power = source[pl.ds(aligned(base + rows, TILE), TILE), :].astype(jnp.int32).astype(f32)
    return jnp.exp2(power[0:1, :] - 15.0)


def message_rows(rows, sizes, tile, own=0):
    needed = 0
    for size in sizes:
        rows //= size
        needed += (size - 1 + (own if size > 2 else 0)) * (rows + tile)
    return needed


class Piece:
    def __init__(self, source, outgoing, half, arrived, out, sems, stages):
        self.source, self.outgoing, self.half, self.arrived = source, outgoing, half, arrived
        self.out, self.sems = out, sems
        self.stages = stages
        self.tile = 0 if outgoing is None else TILE
        self.rows = source.shape[0]
        self.first = 0
        self.base = self.sent = self.index = self.t = 0
        self.copies = []
        self.share = self.rows
        for _, others in stages:
            self.share //= len(others) + 1

    def left(self):
        return self.t <= 2 * len(self.stages)

    def step(self):
        count = len(self.stages)
        if 0 < self.t <= count:
            self.scatter_end(self.stages[self.t - 1])
        elif self.t > count:
            self.gather_end(self.stages[2 * count - self.t])
        if self.t == count:
            self.keep()
        if self.t < count:
            self.scatter_start(self.stages[self.t])
        elif self.t < 2 * count:
            self.gather_start(self.stages[2 * count - 1 - self.t])
        self.t += 1

    def scatter_start(self, stage):
        place, others = stage
        size = len(others) + 1
        rows = self.rows // size
        raw = self.half is not None and self.t == 0
        tile = 0 if raw else self.tile
        block = rows + tile
        arrived = self.half if raw else self.arrived
        if tile and size > 2:
            encode(self.source, self.first, self.rows, size, self.outgoing, self.sent)
        for r, other in enumerate(others):
            member = (place + r + 1) % size
            part = self.first + member * rows
            if tile and size > 2:
                message = self.outgoing.at[pl.ds(aligned(self.sent + member * block, TILE), block)]
            elif tile:
                encode(self.source, part, rows, 1, self.outgoing, self.sent)
                message = self.outgoing.at[pl.ds(self.sent, block)]
            else:
                message = self.source.at[pl.ds(aligned(part, 8), rows)]
            landing = size - 2 - r
            copy = send(
                message,
                arrived.at[pl.ds(self.base + landing * block, block)],
                self.sems,
                self.index + r,
                self.index + landing,
                other,
            )
            copy.start()
            self.copies.append(copy)

    def scatter_end(self, stage):
        place, others = stage
        size = len(others) + 1
        rows = self.rows // size
        raw = self.half is not None and self.t == 1
        tile = 0 if raw else self.tile
        block = rows + tile
        arrived = self.half if raw else self.arrived
        for copy in self.copies:
            copy.wait()
        first = self.first + place * rows
        scales = [decode(arrived, self.base + r * block, rows) if tile else 1.0 for r in range(size - 1)]
        chunk = chunk_of(rows)

        def add(i):
            here = pl.ds(aligned(first + i * chunk, 8), chunk)
            v = self.source[here, :]
            for r, scale in enumerate(scales):
                more = arrived[pl.ds(aligned(self.base + r * block + i * chunk, tile or 8), chunk), :]
                v = v + (more.astype(jnp.int32).astype(f32) * scale if tile else more)
            self.source[here, :] = v

        each(rows // chunk, add)
        self.first, self.rows = first, rows
        if not raw:
            self.base += (size - 1) * block
            self.sent += (size if size > 2 else 1) * block
        self.index += size - 1
        self.copies = []

    def keep(self):
        block = self.share + self.tile
        self.place = 0
        for place, others in self.stages:
            self.place = self.place * (len(others) + 1) + place
        self.first = self.place * block
        self.rows = block
        if self.tile:
            encode(self.source, self.place * self.share, self.share, 1, self.out, self.first)
        else:
            self.out[pl.ds(aligned(self.first, 8), block), :] = self.source[
                pl.ds(aligned(self.first, 8), block), :
            ]

    def gather_start(self, stage):
        place, others = stage
        here = self.out.at[pl.ds(aligned(self.first, self.tile or 8), self.rows)]
        for r, other in enumerate(others):
            copy = send(here, here, self.sems, self.index + r, self.index + len(others) - 1 - r, other)
            copy.start()
            self.copies.append(copy)

    def gather_end(self, stage):
        place, others = stage
        size = len(others) + 1
        for copy in self.copies:
            copy.wait()
        self.copies = []
        self.index += size - 1
        self.first = self.first - place * self.rows
        self.rows = self.rows * size


def adamw(weight, grad, first, second, rate):
    first = beta_one * first + (1.0 - beta_one) * grad
    second = beta_two * second + (1.0 - beta_two) * grad * grad
    power = jnp.maximum(second * (1.0 / (1.0 - beta_two**STEP)), 1e-36)
    root = power * lax.rsqrt(power) + adam_epsilon
    scale = rate / (1.0 - beta_one**STEP)
    return weight * (1.0 - rate * decay_rate) - scale * first / root, first, second


PARTS = (
    (2, 1, HALF_CHANNELS, 0, 3, 0),
    (2, 1, HALF_CHANNELS, 6 * HALF_CHANNELS, 3, 3 * HALF_CHANNELS),
    (2, 1, HALF_CHANNELS, 12 * HALF_CHANNELS, 3, 6 * HALF_CHANNELS),
    (4, 0, HALF_CHANNELS, 0, 1, 0),
    (1, 2, C1, 0, 9, 0),
    (3, 2, C1, 18 * C1, 1, 0),
    (0, 3, C1, 0, 9, 9 * C1),
    (0, 4, C1, 0, 9, 0),
)
LARGE = 5


def update_kernel(devices, *refs):
    count = len(GRADS)
    coded, (g_small, g_late, counts), refs = refs[:count], refs[count : count + 3], refs[count + 3 :]
    members = [refs[3 * i : 3 + 3 * i] for i in range(9)]
    outs = [refs[27 + 3 * i : 30 + 3 * i] for i in range(9)]
    loss_out, counts_out = refs[54:56]
    refs = refs[56:]
    grads, refs = refs[:count], refs[count:]
    staged = [refs[3 * i : 3 * i + 3] for i in range(LARGE)]
    store_sems = refs[3 * LARGE]

    def small(row, rows, lanes):
        parts = [g_small[c * SMALL_ROWS + row : c * SMALL_ROWS + row + rows, :] for c in range(lanes // 128)]
        return parts[0] if len(parts) == 1 else jnp.concatenate(parts, axis=1)

    def single(member, index, grad, rate):
        w, m, v = (ref[index] for ref in members[member])
        for out, value in zip(outs[member], adamw(w, grad, m, v, rate)):
            out[index] = value

    def unpack(source, grad):
        share = grad.shape[0] // devices

        def shares(i):
            base = i * (share + TILE)
            v = source[pl.ds(aligned(base, TILE), share), :].astype(jnp.int32).astype(f32)
            grad[pl.ds(aligned(i * share, 8), share), :] = v * decode(source, base, share)

        each(devices, shares, 4)

    def update(part):
        member, which, block_rows, base, blocks, start = part
        size = 128
        grad = grads[which]
        columns = staged[member][0].shape[1] // 128

        def step(i):
            block = i // (block_rows // size)
            row = (i % (block_rows // size)) * size
            here = pl.ds(aligned(start + block * block_rows + row, 8), size)
            for c in range(columns):
                lanes = slice(c * 128, (c + 1) * 128)
                g = grad[pl.ds(aligned(base + (block * columns + c) * block_rows + row, 8), size), :]
                w, m, v = (ref[here, lanes] for ref in members[member])
                for out, value in zip(staged[member], adamw(w, g, m, v, rate_matrix)):
                    out[here, lanes] = value

        each(blocks * block_rows // size, step)

    stores = []
    seen = set()
    for i, part in enumerate(PARTS):
        member, which, block_rows, _, blocks, start = part
        if which not in seen:
            unpack(coded[which], grads[which])
            seen.add(which)
        update(part)
        here = pl.ds(start, block_rows * blocks)
        for kind in range(3):
            copy = pltpu.make_async_copy(
                staged[member][kind].at[here], outs[member][kind].at[here], store_sems.at[i, kind]
            )
            copy.start()
            stores.append(copy)
    for tap in range(9):
        single(5, (tap,), small(tap * 8, 3, HALF_CHANNELS), rate_matrix)
    every = slice(None)
    single(6, (every, every), g_late[:6, :], rate_vector)
    single(7, (every, every), small(WIDE_NORM_ROW, 6, HALF_CHANNELS), rate_vector)
    single(8, (every, slice(0, C1)), g_late[TIME_NARROW_ROW : TIME_NARROW_ROW + NB, :], rate_vector)
    single(8, (every, slice(C1, None)), small(TIME_WIDE_ROW, NB, HALF_CHANNELS), rate_vector)
    loss_out[...] = g_small[LOSS_ROW : LOSS_ROW + 1, :]
    diagonal = lax.broadcasted_iota(jnp.int32, (NB, 128), 0) == lax.broadcasted_iota(jnp.int32, (NB, 128), 1)
    counts_out[...] = jnp.sum(jnp.where(diagonal, counts[...], 0.0), axis=0, keepdims=True)[:, :NB]
    for copy in stores:
        copy.wait()


def update_call(devices, grads, members):
    whole = pl.BlockSpec(memory_space=pltpu.VMEM)
    outside = pl.BlockSpec(memory_space=pltpu.HBM)
    flat = [v for member in members for v in member]
    large = [v.shape for v in flat[: 3 * LARGE]]
    return pl.pallas_call(
        functools.partial(update_kernel, devices),
        out_shape=[jax.ShapeDtypeStruct(v.shape, f32) for v in flat]
        + [jax.ShapeDtypeStruct((1, 128), f32), jax.ShapeDtypeStruct((1, NB), f32)],
        in_specs=[whole] * (len(grads) + len(flat)),
        out_specs=[outside] * (3 * LARGE) + [whole] * (len(flat) - 3 * LARGE + 2),
        scratch_shapes=[pltpu.VMEM((padded(rows, devices, TILE), 128), f32) for rows in GRADS]
        + [pltpu.VMEM(shape, f32) for shape in large]
        + [pltpu.SemaphoreType.DMA((len(PARTS), 3))],
        compiler_params=pltpu.CompilerParams(vmem_limit_bytes=UPDATE_LIMIT),
        cost_estimate=pl.CostEstimate(flops=30 * 10**6, bytes_accessed=40 * 10**6, transcendentals=0),
    )(*grads, *flat)


def on_device(
    features,
    target,
    pixel_mask,
    buckets,
    conv_pair,
    down_conv,
    conv_wide,
    skip_proj,
    attn_proj,
    head_conv,
    norm_narrow,
    norm_wide,
    time_bias,
    conv_pair_mom,
    down_conv_mom,
    conv_wide_mom,
    skip_proj_mom,
    attn_proj_mom,
    head_conv_mom,
    norm_narrow_mom,
    norm_wide_mom,
    time_bias_mom,
    conv_pair_sq,
    down_conv_sq,
    conv_wide_sq,
    skip_proj_sq,
    attn_proj_sq,
    head_conv_sq,
    norm_narrow_sq,
    norm_wide_sq,
    time_bias_sq,
):
    dp_size = lax.axis_size("dp")
    images = features.shape[0] // 2

    def halves(tensor):
        return tensor.reshape((2, images) + tensor.shape[1:])

    def flat(tensor):
        return tensor.reshape(-1, tensor.shape[-1])

    def head_rows(tensor):
        return jnp.transpose(tensor, (0, 1, 3, 2)).reshape(9, 3, HALF_CHANNELS)

    params = (
        flat(conv_pair),
        flat(down_conv),
        flat(conv_wide),
        skip_proj,
        attn_proj,
        head_rows(head_conv),
        norm_narrow,
        norm_wide,
        time_bias,
    )
    firsts = (
        flat(conv_pair_mom),
        flat(down_conv_mom),
        flat(conv_wide_mom),
        skip_proj_mom,
        attn_proj_mom,
        head_rows(head_conv_mom),
        norm_narrow_mom,
        norm_wide_mom,
        time_bias_mom,
    )
    seconds = (
        flat(conv_pair_sq),
        flat(down_conv_sq),
        flat(conv_wide_sq),
        skip_proj_sq,
        attn_proj_sq,
        head_rows(head_conv_sq),
        norm_narrow_sq,
        norm_wide_sq,
        time_bias_sq,
    )
    summed = main_call(
        dp_size,
        buckets,
        halves(features),
        halves(jnp.transpose(target, (0, 3, 1, 2))),
        halves(pixel_mask),
        *params,
    )
    results = update_call(2 * dp_size, summed, list(zip(params, firsts, seconds)))
    shaped = []
    for member, like in enumerate((conv_pair, down_conv, conv_wide, skip_proj, attn_proj)):
        shaped.extend(v.reshape(like.shape) for v in results[3 * member : 3 * member + 3])
    for v in results[15:18]:
        shaped.append(jnp.transpose(v.reshape(3, 3, 3, HALF_CHANNELS), (0, 1, 3, 2)))
    shaped.extend(results[18:27])
    return (results[27][0, 0], results[28].reshape(NB)) + tuple(shaped)


def solution(mesh):
    placed = (
        P("dp", "sp", None, None),
        P("dp", "sp", None, None),
        P("dp", "sp", None),
        P("dp"),
        P(),
        P(),
        P(),
        P(),
        P(),
        P(),
        P(),
        P(),
        P(),
        P(),
        P(),
        P(),
        P(),
        P(),
        P(),
        P(),
        P(),
        P(),
        P(),
        P(),
        P(),
        P(),
        P(),
        P(),
        P(),
        P(),
        P(),
    )
    return jax.shard_map(
        on_device,
        mesh=mesh,
        in_specs=placed,
        out_specs=(
            P(),
            P(),
            P(),
            P(),
            P(),
            P(),
            P(),
            P(),
            P(),
            P(),
            P(),
            P(),
            P(),
            P(),
            P(),
            P(),
            P(),
            P(),
            P(),
            P(),
            P(),
            P(),
            P(),
            P(),
            P(),
            P(),
            P(),
            P(),
            P(),
        ),
        check_vma=False,
    )
```

```python
import functools

import jax
import jax.numpy as jnp
from jax import lax
from jax.experimental import pallas as pl
from jax.experimental.pallas import tpu as pltpu
from jax.sharding import PartitionSpec as P

C1 = 128
HALF_CHANNELS = 256
GROUPS = 32
RES = 32
HALF = 16
NB = 8
STEP = 10
MESH = pl.DeviceIdType.MESH
MAIN_LIMIT = 41 * 1024 * 1024
UPDATE_LIMIT = 26 * 1024 * 1024

epsilon = 1e-05
root_half = 0.7071067811865476
beta_one = 0.9
beta_two = 0.999
adam_epsilon = 1e-08
decay_rate = 0.1
rate_matrix = 0.03
rate_vector = 0.5
logit_scale = HALF_CHANNELS ** (-0.5)
ROWS = 8

bf16 = jnp.bfloat16
f32 = jnp.float32

EVEN, ODD, ODD_LEFT, EVEN_RIGHT = 0, 1, 2, 3
TAPS = ((ODD_LEFT, EVEN, ODD), (EVEN, ODD, EVEN_RIGHT))


def rounded(v):
    return v.astype(bf16).astype(f32)


def silu(t):
    return t * jax.nn.sigmoid(t)


def slope(t):
    s = jax.nn.sigmoid(t)
    return s * (1.0 + t * (1.0 - s))


def mm(a, b):
    return lax.dot_general(a, b, (((1,), (0,)), ((), ())), preferred_element_type=f32)


def mm_nt(a, b):
    return lax.dot_general(a, b, (((1,), (1,)), ((), ())), preferred_element_type=f32)


def mm_tn(a, b):
    return lax.dot_general(a, b, (((0,), (0,)), ((), ())), preferred_element_type=f32)


def fold(v):
    return jnp.sum(v.reshape(-1, 8, v.shape[-1]), axis=0)


def total(v):
    return jnp.broadcast_to(jnp.sum(v, axis=0, keepdims=True), v.shape)


def group_sum(v, size):
    lanes = v.shape[-1]
    lane = lax.broadcasted_iota(jnp.int32, v.shape, 1)
    step = 1
    while step < size:
        other = jnp.where(
            (lane & step) == 0, pltpu.roll(v, lanes - step, 1), pltpu.roll(v, step, 1)
        )
        v = v + other
        step *= 2
    return v


def norm_coefs(sums, squares, gain, shift, pixels):
    size = sums.shape[-1] // GROUPS
    count = pixels * size
    mean = group_sum(total(sums), size) / count
    power = group_sum(total(squares), size) / count
    inv = lax.rsqrt(power - mean * mean + epsilon)
    scale = inv * gain
    return scale, shift - mean * scale, mean, inv


def norm_grad_coefs(sum_dy, sum_dyv, gain, mean, inv, pixels):
    size = sum_dy.shape[-1] // GROUPS
    count = pixels * size
    first = total(sum_dy)
    second = (total(sum_dyv) - mean * first) * inv
    one = group_sum(first * gain, size) / count
    two = group_sum(second * gain, size) / count
    b = -inv * inv * two
    return second, first, inv * gain, b, -inv * one - mean * b


def shift_cols(v, step):
    col = lax.broadcasted_iota(jnp.int32, v.shape, 1)
    if step == 1:
        return jnp.where(col == 0, 0.0, pltpu.roll(v, 1, 1))
    return jnp.where(col == HALF - 1, 0.0, pltpu.roll(v, HALF - 1, 1))


def store_planes(planes, n, b, r0, v):
    rows = v.shape[0]
    v = v.astype(bf16).astype(f32)
    for plane, value in (
        (EVEN + b, v),
        (ODD_LEFT if b == 1 else EVEN_RIGHT, shift_cols(v, 1 if b == 1 else -1)),
    ):
        planes[n, plane, pl.ds(r0 + 1, rows)] = value.astype(bf16)


def store_shifted(cells, n, r0, v):
    rows = v.shape[0]
    v = v.astype(bf16).astype(f32)
    for tap, value in ((0, shift_cols(v, 1)), (1, v), (2, shift_cols(v, -1))):
        cells[n, tap, pl.ds(r0 + 1, rows)] = value.astype(bf16)


def plane_block(planes, tap, jj):
    return planes[:, tap, pl.ds(jj, HALF, stride=2)].reshape(-1, planes.shape[-1])


def pair_input(planes, b, jjs):
    return jnp.concatenate([plane_block(planes, tap, jj) for jj in jjs for tap in TAPS[b]], axis=1)


def cell_input(cells, dys):
    return jnp.concatenate(
        [
            cells[:, tap, dy : dy + HALF].reshape(-1, cells.shape[-1])
            for dy in dys
            for tap in range(3)
        ],
        axis=1,
    )


def each(count, body, unroll=1):
    def step(i, carry):
        body(i)
        return carry

    lax.fori_loop(0, count, step, 0, unroll=unroll)


def prepare_weights(pair, down, wide, skip, attn, head, pair_fwd, pair_bwd, down_fwd, down_bwd, wide_fwd, wide_bwd, skip_low, attn_low, head_low):
    nothing = jnp.zeros((C1, C1), bf16)
    for member in range(2):
        for jj in range(4):
            for k in range(3):
                block = (jj * 3 + k) * C1
                for a in range(2):
                    dy = jj - a
                    inside = 0 <= dy < 3
                    row = (dy * 3 + k) * C1
                    back = ((2 - dy) * 3 + (2 - k)) * C1
                    pair_fwd[member, block : block + C1, a * C1 : a * C1 + C1] = (
                        pair[member][row : row + C1, :].astype(bf16) if inside else nothing
                    )
                    pair_bwd[member, a * C1 : a * C1 + C1, block : block + C1] = (
                        pair[member][back : back + C1, :].astype(bf16) if inside else nothing
                    )
    wide_channels = HALF_CHANNELS
    for tap in range(9):
        low = down[tap * C1 : tap * C1 + C1, :].astype(bf16)
        down_fwd[tap * C1 : tap * C1 + C1, :] = low
        down_bwd[:, (8 - tap) * wide_channels : (9 - tap) * wide_channels] = low
        low = wide[tap * wide_channels : (tap + 1) * wide_channels, :].astype(bf16)
        wide_fwd[tap * wide_channels : (tap + 1) * wide_channels, :] = low
        wide_bwd[:, (8 - tap) * wide_channels : (9 - tap) * wide_channels] = low
    skip_low[...] = skip[...].astype(bf16)
    attn_low[...] = attn[...].astype(bf16)
    head_low[...] = jnp.zeros(head_low.shape, f32)
    for tap in range(9):
        head_low[tap * 8 : tap * 8 + 3, :] = rounded(head[tap])


def split_three(v):
    high = v.astype(bf16)
    rest = v - high.astype(f32)
    middle = rest.astype(bf16)
    return high, middle, (rest - middle.astype(f32)).astype(bf16)


def lane_shift(v, step):
    lane = lax.broadcasted_iota(jnp.int32, v.shape, 1)
    j = lane & (HALF - 1)
    if step == 1:
        keep = j < HALF - 1
    elif step == -1:
        keep = j > 0
    elif step == HALF:
        keep = lane < HALF * (HALF - 1)
    else:
        keep = lane >= HALF
    return jnp.where(keep, pltpu.roll(v, (-step) % v.shape[-1], 1), 0.0)


def head_forward(table):
    cols = [
        [
            lane_shift(table[dy][0], -1) + table[dy][1] + table[dy][2],
            table[dy][0] + table[dy][1] + lane_shift(table[dy][2], 1),
        ]
        for dy in range(3)
    ]
    return [
        [
            lane_shift(cols[0][b], -HALF) + cols[1][b] + cols[2][b]
            if a == 0
            else cols[0][b] + cols[1][b] + lane_shift(cols[2][b], HALF)
            for b in range(2)
        ]
        for a in range(2)
    ]


def head_backward(grad):
    rows = [
        [
            lane_shift(grad[0][b], HALF) + grad[1][b],
            grad[0][b] + grad[1][b],
            grad[0][b] + lane_shift(grad[1][b], -HALF),
        ]
        for b in range(2)
    ]
    return [
        [
            lane_shift(rows[0][dy], 1) + rows[1][dy],
            rows[0][dy] + rows[1][dy],
            rows[0][dy] + lane_shift(rows[1][dy], -1),
        ]
        for dy in range(3)
    ]


def keep_columns(ref, row, v):
    for c in range(v.shape[1] // 128):
        ref[row + c * v.shape[0] : row + (c + 1) * v.shape[0], :] = v[:, c * 128 : (c + 1) * 128]


HEAD_ROWS = 72
WIDE_NORM_ROW = 72
LOSS_ROW = 78
TIME_WIDE_ROW = 80
SMALL_ROWS = 96
TIME_NARROW_ROW = 8
LATE_ROWS = 16
SKIP_ROW = 18 * C1
ATTN_ROWS = 8 * HALF_CHANNELS
WIDE_ROWS = 18 * HALF_CHANNELS
DOWN_ROWS = 20 * C1
PAIR_ROWS = 9 * C1
GRADS = (ATTN_ROWS, WIDE_ROWS, DOWN_ROWS, PAIR_ROWS, PAIR_ROWS)
TILE = 16


def padded(rows, devices, tile):
    return -(-rows // (devices * tile)) * devices * tile


def coded_rows(rows, devices):
    return padded(rows, devices, TILE) + devices * TILE


def main_kernel(
    dp_size,
    buckets, features, target_rows, mask_rows, pair_all, down_all, wide_all, skip_all, attn_all, head_all,
    narrow_all, gains_all, time_all,
    sum_attn, sum_wide, sum_down, sum_pair_b, sum_pair_a, sum_small, sum_late, counts,
    x_in, target, mask, down, wide, skip, attn, head, gains_narrow, gains_wide, time_bias, mask_local,
    g_attn, g_wide, g_down, g_pair_b, g_pair_a, g_rows,
    out_attn, out_wide, out_down, out_pair_b, out_pair_a,
    half_attn, half_wide, half_down, half_pair_b, half_pair_a,
    in_attn, in_wide, in_down, in_pair_b, in_pair_a, in_small,
    sems_attn, sems_wide, sems_down, sems_pair_b, sems_pair_a, sems_small,
    g_small, g_late,
    totals, arrived_totals, late_totals, arrived_late, image_sems, local_sems, count_sems, late_sems, weight_sems,
    pair_fwd, pair_bwd, down_fwd, down_bwd, wide_fwd, wide_bwd, skip_low, attn_low, head_low,
    x_full, h1_full, xs_full, dy_full, in_a, in_b, in_g, flat,
    cells_c, cells_d, cells_g, fs_low, dfs, h3, x2, x3, n5, qkv, probs, probs_low, att, a6, dwide, dout, dqkv, dnarrow,
    coef_n, coef_w,
):
    loads = [
        pltpu.make_async_copy(source, ref, weight_sems.at[i])
        for i, (source, ref) in enumerate(
            (
                (pair_all.at[:PAIR_ROWS], g_pair_a.at[:PAIR_ROWS]),
                (pair_all.at[PAIR_ROWS:], g_pair_b.at[:PAIR_ROWS]),
                (down_all, down),
                (wide_all, wide),
                (skip_all, skip),
                (attn_all, attn),
                (head_all, head),
                (narrow_all, gains_narrow),
                (gains_all, gains_wide),
                (time_all, time_bias),
                (mask_rows, mask_local),
            )
        )
    ]
    links = Links(dp_size)
    links.greet()
    for copy in loads[::-1]:
        copy.start()
    loads.pop().wait()
    counted = count_pixels(buckets, mask_local)
    links.meet()
    here = (lax.axis_index("dp"), 1 - lax.axis_index("sp"))
    moved = ((features, x_in), (target_rows, target), (mask_rows, mask))
    side = lax.axis_index("sp")
    arrivals = [
        send(source.at[1 - side], out.at[side], image_sems, i, i, here) for i, (source, out) in enumerate(moved)
    ]
    for copy in arrivals:
        copy.start()
    keeps = [
        pltpu.make_async_copy(source.at[side], out.at[side], local_sems.at[i])
        for i, (source, out) in enumerate(moved)
    ]
    for copy in keeps:
        copy.start()
    images = x_in.shape[1]
    position = lax.axis_index("sp")
    steps = RES // ROWS
    full_pixels = RES * RES
    half_pixels = HALF * HALF
    zero_n = jnp.zeros((8, C1), f32)
    zero_w = jnp.zeros((8, HALF_CHANNELS), f32)

    def bucket(n):
        return buckets[position * images + n]

    def gain_n(row):
        return jnp.broadcast_to(gains_narrow[row : row + 1, :], (8, C1))

    def gain_w(row):
        return jnp.broadcast_to(gains_wide[row : row + 1, :], (8, HALF_CHANNELS))

    def keep_coefs(ref, which, n, values):
        for kind in range(4):
            ref[which, n, kind] = values[kind]

    def row_of(ref, which, n, kind):
        return ref[which, n, kind, 0:1, :]

    counting = Exchange(counted, totals, arrived_totals, count_sems, links.brief)
    counting.step()
    sources = (g_attn, g_wide, g_down, g_pair_b, g_pair_a, g_rows)
    outgoing = (out_attn, out_wide, out_down, out_pair_b, out_pair_a, None)
    halves = (half_attn, half_wide, half_down, half_pair_b, half_pair_a, None)
    incoming = (in_attn, in_wide, in_down, in_pair_b, in_pair_a, in_small)
    outs = (sum_attn, sum_wide, sum_down, sum_pair_b, sum_pair_a, sum_small)
    sems = (sems_attn, sems_wide, sems_down, sems_pair_b, sems_pair_a, sems_small)
    orders = (links.brief, links.brief, links.brief, links.brief, links.brief, links.brief)
    pieces = dict(zip(PIECE_NAMES, (Piece(*parts) for parts in zip(sources, outgoing, halves, incoming, outs, sems, orders))))

    def advance(point):
        for name in SCHEDULE.get(point, ()):
            pieces[name].step()

    for rows, ref in zip(GRADS + (2 * SMALL_ROWS,), sources):
        if ref.shape[0] > rows:
            ref[rows:, :] = jnp.zeros((ref.shape[0] - rows, 128), f32)
    for copy in loads:
        copy.wait()
    prepare_weights((g_pair_a, g_pair_b), down, wide, skip, attn, head, pair_fwd, pair_bwd, down_fwd, down_bwd, wide_fwd, wide_bwd, skip_low, attn_low, head_low)
    g_small[...] = jnp.zeros(g_small.shape, f32)
    g_late[...] = jnp.zeros(g_late.shape, f32)
    for planes in (in_a, in_b, in_g):
        edge = jnp.zeros((images, 4, HALF, C1), bf16)
        planes[:, :, 0] = edge
        planes[:, :, RES + 1] = edge
    for cells in (cells_c, cells_d, cells_g):
        edge = jnp.zeros((images, 3, HALF, cells.shape[-1]), bf16)
        cells[:, :, 0] = edge
        cells[:, :, HALF + 1] = edge

    for copy in keeps + arrivals:
        copy.wait()
    counting.step()

    def load_image(n):
        def step(i, carry):
            sums, squares = carry
            half = i // 2
            v = x_in[half, n, pl.ds((i % 2) * ROWS, ROWS)].astype(f32)
            flat[...] = v.reshape(ROWS * RES, C1)
            for b in range(2):
                w = flat[pl.ds(b, ROWS * HALF, stride=2), :].reshape(ROWS, HALF, C1)
                x_full[n, b, pl.ds(i * ROWS, ROWS)] = w
                sums = sums + fold(w)
                squares = squares + fold(w * w)
            return sums, squares

        sums, squares = lax.fori_loop(0, steps, step, (zero_n, zero_n))
        keep_coefs(coef_n, 0, n, norm_coefs(sums, squares, gain_n(0), gain_n(1), full_pixels))

    each(images, load_image)

    def activate(values, planes, which):
        def image(n):
            scale = row_of(coef_n, which, n, 0)
            offset = row_of(coef_n, which, n, 1)

            def step(i):
                for b in range(2):
                    v = values[n, b, pl.ds(i * ROWS, ROWS)]
                    store_planes(planes, n, b, i * ROWS, silu(v * scale + offset))

            each(steps, step)

        each(images, image)

    def pair_rows(result, n):
        part = result[n * half_pixels : (n + 1) * half_pixels].reshape(HALF, 1, HALF, 2 * C1)
        return jnp.concatenate([part[..., :C1], part[..., C1:]], axis=1).reshape(RES, HALF, C1)

    activate(x_full, in_a, 0)
    counting.step()
    for b in range(2):
        out = mm(pair_input(in_a, b, range(4)), pair_fwd[0])
        for n in range(images):
            h1_full[n, b] = pair_rows(out, n)

    def first_hidden(n):
        bias = time_bias[pl.ds(bucket(n), 1), :][:, :C1]

        def step(i, carry):
            sums, squares = carry
            for b in range(2):
                v = h1_full[n, b, pl.ds(i * ROWS, ROWS)] + bias
                h1_full[n, b, pl.ds(i * ROWS, ROWS)] = v
                sums = sums + fold(v)
                squares = squares + fold(v * v)
            return sums, squares

        sums, squares = lax.fori_loop(0, steps, step, (zero_n, zero_n))
        keep_coefs(coef_n, 1, n, norm_coefs(sums, squares, gain_n(2), gain_n(3), full_pixels))

    each(images, first_hidden)
    activate(h1_full, in_b, 1)
    counting.step()
    for b in range(2):
        out = mm(pair_input(in_b, b, range(4)), pair_fwd[1])
        for n in range(images):
            xs_full[n, b] = pair_rows(out, n)

    def first_out(n):
        def step(i, carry):
            sums, squares = carry
            for b in range(2):
                v = xs_full[n, b, pl.ds(i * ROWS, ROWS)]
                v = rounded((x_full[n, b, pl.ds(i * ROWS, ROWS)] + v) * root_half)
                xs_full[n, b, pl.ds(i * ROWS, ROWS)] = v
                sums = sums + fold(v)
                squares = squares + fold(v * v)
            return sums, squares

        sums, squares = lax.fori_loop(0, steps, step, (zero_n, zero_n))
        keep_coefs(coef_n, 2, n, norm_coefs(sums, squares, gain_n(4), gain_n(5), full_pixels))

    each(images, first_out)

    counting.step()

    def fir_down_image(n):
        scale = row_of(coef_n, 2, n, 0)
        offset = row_of(coef_n, 2, n, 1)
        for b in range(2):
            dy_full[n, b, 0] = jnp.zeros((HALF, C1), f32)
            dy_full[n, b, RES + 1] = jnp.zeros((HALF, C1), f32)

        def act_step(i):
            for b in range(2):
                v = xs_full[n, b, pl.ds(i * ROWS, ROWS)]
                dy_full[n, b, pl.ds(i * ROWS + 1, ROWS)] = silu(v * scale + offset)

        each(steps, act_step)

        def columns(rows):
            even, odd = rows
            return (
                0.125 * (shift_cols(odd, 1) + shift_cols(even, -1)) + 0.375 * (even + odd)
            )

        def taps(ref, b, r0, size):
            return [ref[n, b, pl.ds(r0 + t, size, stride=2)] for t in range(4)]

        def down_step(i):
            size = HALF // 2
            rows = []
            for b in range(2):
                t = taps(dy_full, b, 2 * size * i, size)
                rows.append(0.125 * (t[0] + t[3]) + 0.375 * (t[1] + t[2]))
            store_shifted(cells_c, n, i * size, columns(rows))

        each(2, down_step)
        for b in range(2):
            dy_full[n, b, pl.ds(1, RES)] = xs_full[n, b]

        def skip_step(i):
            size = HALF // 2
            rows = []
            for b in range(2):
                t = taps(dy_full, b, 2 * size * i, size)
                rows.append(0.125 * (t[0] + t[3]) + 0.375 * (t[1] + t[2]))
            fs_low[n, pl.ds(i * size * HALF, size * HALF)] = (
                columns(rows).reshape(size * HALF, C1).astype(bf16)
            )

        each(2, skip_step)

    each(images, fir_down_image)

    def wide_stats(v, which, n, row):
        values = norm_coefs(fold(v), fold(v * v), gain_w(row), gain_w(row + 1), half_pixels)
        keep_coefs(coef_w, which, n, values)
        return values[0][0:1, :], values[1][0:1, :]

    out = mm(cell_input(cells_c, range(3)), down_fwd[...])
    for n in range(images):
        v = out[n * half_pixels : (n + 1) * half_pixels] + time_bias[pl.ds(bucket(n), 1), :][:, C1:]
        h3[n] = v
        scale, offset = wide_stats(v, 0, n, 0)
        store_shifted(cells_d, n, 0, silu(v * scale + offset).reshape(HALF, HALF, HALF_CHANNELS))
    out = mm(cell_input(cells_d, range(3)), wide_fwd[...])
    out = out + mm(fs_low[...].reshape(-1, C1), skip_low[...])
    for n in range(images):
        v = out[n * half_pixels : (n + 1) * half_pixels] * root_half
        x2[n] = v
        scale, offset = wide_stats(v, 1, n, 2)
        n5[n] = (v * scale + offset).astype(bf16)
        qkv[n] = mm(n5[n], attn_low[:, : 3 * HALF_CHANNELS]).astype(bf16)
        q = qkv[n, :, :HALF_CHANNELS]
        k = qkv[n, :, HALF_CHANNELS : 2 * HALF_CHANNELS]
        w = qkv[n, :, 2 * HALF_CHANNELS :]
        logits = mm_nt(q, k) * logit_scale
        powers = jnp.exp(logits - jnp.max(logits, axis=1, keepdims=True))
        weights = powers / jnp.sum(powers, axis=1, keepdims=True)
        probs[n] = weights
        probs_low[n] = weights.astype(bf16)
        att[n] = mm(probs_low[n], w).astype(bf16)
        v = (v + mm(att[n], attn_low[:, 3 * HALF_CHANNELS :])) * root_half
        x3[n] = v
        scale, offset = wide_stats(v, 2, n, 4)
        a6[n] = silu(v * scale + offset).astype(bf16)

    counting.finish(counts)

    lane = lax.broadcasted_iota(jnp.int32, (RES, 2 * half_pixels), 1)
    source = lax.broadcasted_iota(jnp.int32, (RES, 2 * half_pixels), 0)
    picks = (source == 2 * (lane & (HALF - 1)) + (lane >> 8)).astype(bf16)
    row_lane = (lax.broadcasted_iota(jnp.int32, (HALF, 2 * half_pixels), 1) & (half_pixels - 1)) >> 4
    row_source = lax.broadcasted_iota(jnp.int32, (HALF, 2 * half_pixels), 0)
    component = lax.broadcasted_iota(jnp.int32, (8, half_pixels), 0)

    def spread(halves):
        moved = [mm(half, picks) for half in halves]
        rows = []
        for a in range(2):
            picked = sum(
                jnp.where(2 * row_lane + a == row_source + HALF * h, moved[h], 0.0)
                for h in range(2)
            )
            row = jnp.sum(picked, axis=0, keepdims=True)
            rows.append([row[:, :half_pixels], row[:, half_pixels:]])
        return rows

    loss = jnp.zeros((1, half_pixels), f32)
    head_grad = jnp.zeros((HEAD_ROWS, HALF_CHANNELS), f32)
    for n in range(images):
        moved = mm_nt(head_low[...].astype(bf16), a6[n])
        pred = head_forward(
            [[moved[(dy * 3 + dx) * 8 : (dy * 3 + dx) * 8 + 8] for dx in range(3)] for dy in range(3)]
        )
        wanted = [spread([target[h, n, c] for h in range(2)]) for c in range(3)]
        counted = spread([mask[h, n].astype(f32).astype(bf16) for h in range(2)])
        per_image = 1.0 / counts[pl.ds(bucket(n), 1), :]
        per_image = jnp.concatenate([per_image, per_image], axis=1)
        grad_pred = [[None, None], [None, None]]
        for a in range(2):
            for b in range(2):
                goal = jnp.zeros((8, half_pixels), f32)
                for c in range(3):
                    goal = jnp.where(component == c, wanted[c][a][b], goal)
                error = pred[a][b] - goal
                weight = counted[a][b] * per_image
                loss = loss + weight * jnp.sum(error * error, axis=0, keepdims=True)
                grad_pred[a][b] = rounded(2.0 * error * weight)
        table = head_backward(grad_pred)
        table = jnp.concatenate([table[dy][dx] for dy in range(3) for dx in range(3)], axis=0)
        parts = split_three(table)
        for part in parts:
            head_grad = head_grad + mm(part, a6[n])
        head_rows = head_low[...].astype(bf16)
        grad = sum(mm_tn(part, head_rows) for part in parts)
        v = x3[n]
        values = [coef_w[2, n, kind] for kind in range(4)]
        dy = rounded(grad) * slope(v * values[0][0:1, :] + values[1][0:1, :])
        gain, shift, ca, cb, cd = norm_grad_coefs(
            fold(dy), fold(dy * v), gain_w(4), values[2], values[3], half_pixels
        )
        g_small[WIDE_NORM_ROW + 4 : WIDE_NORM_ROW + 5, :] += gain[0:1, :]
        g_small[WIDE_NORM_ROW + 5 : WIDE_NORM_ROW + 6, :] += shift[0:1, :]
        grad_third = dy * ca[0:1, :] + v * cb[0:1, :] + cd[0:1, :]
        dwide[n] = grad_third
    g_small[0:HEAD_ROWS, :] = head_grad
    g_small[LOSS_ROW : LOSS_ROW + 1, :] = jnp.broadcast_to(
        jnp.sum(loss, axis=1, keepdims=True), (1, HALF_CHANNELS)
    )

    for n in range(images):
        grad_attn = (dwide[n] * root_half).astype(bf16)
        dout[n] = grad_attn
        grad_att = mm_nt(grad_attn, attn_low[:, 3 * HALF_CHANNELS :]).astype(bf16)
        q = qkv[n, :, :HALF_CHANNELS]
        k = qkv[n, :, HALF_CHANNELS : 2 * HALF_CHANNELS]
        w = qkv[n, :, 2 * HALF_CHANNELS :]
        grad_probs = mm_nt(grad_att, w)
        weights = probs[n]
        inner = jnp.sum(weights * grad_probs, axis=1, keepdims=True)
        grad_scores = (weights * (grad_probs - inner)).astype(bf16)
        dqkv[n, :, :HALF_CHANNELS] = (mm(grad_scores, k) * logit_scale).astype(bf16)
        dqkv[n, :, HALF_CHANNELS : 2 * HALF_CHANNELS] = (mm_tn(grad_scores, q) * logit_scale).astype(bf16)
        dqkv[n, :, 2 * HALF_CHANNELS :] = mm_tn(probs_low[n], grad_att).astype(bf16)
    keep_columns(
        g_attn, 0, mm_tn(n5[...].reshape(-1, HALF_CHANNELS), dqkv[...].reshape(-1, 3 * HALF_CHANNELS))
    )
    keep_columns(
        g_attn,
        6 * HALF_CHANNELS,
        mm_tn(att[...].reshape(-1, HALF_CHANNELS), dout[...].reshape(-1, HALF_CHANNELS)),
    )
    advance("attn")
    for n in range(images):
        dy = mm_nt(dqkv[n], attn_low[:, : 3 * HALF_CHANNELS])
        v = x2[n]
        gain, shift, ca, cb, cd = norm_grad_coefs(
            fold(dy), fold(dy * v), gain_w(2), coef_w[1, n, 2], coef_w[1, n, 3], half_pixels
        )
        g_small[WIDE_NORM_ROW + 2 : WIDE_NORM_ROW + 3, :] += gain[0:1, :]
        g_small[WIDE_NORM_ROW + 3 : WIDE_NORM_ROW + 4, :] += shift[0:1, :]
        grad = dy * ca[0:1, :] + v * cb[0:1, :] + cd[0:1, :] + dwide[n] * root_half
        store_shifted(cells_g, n, 0, (grad * root_half).reshape(HALF, HALF, HALF_CHANNELS))
        advance("gn_e%d" % n)

    center = cells_g[:, 1, 1 : HALF + 1].reshape(-1, HALF_CHANNELS)
    for dy in range(3):
        product = mm_tn(cell_input(cells_d, [dy]), center)
        for k in range(3):
            keep_columns(
                g_wide,
                (dy * 3 + k) * 2 * HALF_CHANNELS,
                product[k * HALF_CHANNELS : (k + 1) * HALF_CHANNELS],
            )
    keep_columns(g_down, SKIP_ROW, mm_tn(fs_low[...].reshape(-1, C1), center))
    advance("wide")
    dfs[...] = mm_nt(center, skip_low[...]).reshape(dfs.shape)
    out = mm_nt(cell_input(cells_g, range(3)), wide_bwd[...])
    advance("conv_d")
    bucket_rows = lax.broadcasted_iota(jnp.int32, (NB, HALF_CHANNELS), 0)
    time_wide = jnp.zeros((NB, HALF_CHANNELS), f32)
    for n in range(images):
        v = h3[n]
        dy = out[n * half_pixels : (n + 1) * half_pixels] * slope(
            v * row_of(coef_w, 0, n, 0) + row_of(coef_w, 0, n, 1)
        )
        gain, shift, ca, cb, cd = norm_grad_coefs(
            fold(dy), fold(dy * v), gain_w(0), coef_w[0, n, 2], coef_w[0, n, 3], half_pixels
        )
        g_small[WIDE_NORM_ROW : WIDE_NORM_ROW + 1, :] += gain[0:1, :]
        g_small[WIDE_NORM_ROW + 1 : WIDE_NORM_ROW + 2, :] += shift[0:1, :]
        grad = dy * ca[0:1, :] + v * cb[0:1, :] + cd[0:1, :]
        time_wide = time_wide + jnp.where(bucket_rows == bucket(n), total(fold(grad)), 0.0)
        store_shifted(cells_g, n, 0, grad.reshape(HALF, HALF, HALF_CHANNELS))
        advance("gn_d%d" % n)
    g_small[TIME_WIDE_ROW : TIME_WIDE_ROW + NB, :] = time_wide

    for c in range(2):
        g_rows[c * SMALL_ROWS : (c + 1) * SMALL_ROWS, :] = g_small[:, c * 128 : (c + 1) * 128]
    advance("gn_d")

    center = cells_g[:, 1, 1 : HALF + 1].reshape(-1, HALF_CHANNELS)
    for dy in range(3):
        product = mm_tn(cell_input(cells_c, [dy]), center)
        for k in range(3):
            keep_columns(g_down, (dy * 3 + k) * 2 * C1, product[k * C1 : (k + 1) * C1])
    advance("down")
    dnarrow[...] = mm_nt(cell_input(cells_g, range(3)), down_bwd[...]).reshape(dnarrow.shape)

    def up_parts(ref, n, i, size):
        here = pl.ds(i * size * HALF, size * HALF)
        g = ref[n, here].reshape(size, HALF, C1)
        lane_rows = lax.broadcasted_iota(jnp.int32, g.shape, 0) + i * size
        above = ref[n, pl.ds(jnp.maximum(i * size - 1, 0) * HALF, HALF)].reshape(1, HALF, C1)
        below = ref[n, pl.ds(jnp.minimum((i + 1) * size, HALF - 1) * HALF, HALF)].reshape(1, HALF, C1)
        above = jnp.where(lane_rows == 0, 0.0, jnp.concatenate([above, g[:-1]], axis=0))
        below = jnp.where(lane_rows == HALF - 1, 0.0, jnp.concatenate([g[1:], below], axis=0))
        result = []
        for rows in (0.375 * g + 0.125 * above, 0.375 * g + 0.125 * below):
            result.append(
                (
                    0.375 * rows + 0.125 * shift_cols(rows, 1),
                    0.375 * rows + 0.125 * shift_cols(rows, -1),
                )
            )
        return result

    def third_norm(n):
        size = HALF // 4
        scale = row_of(coef_n, 2, n, 0)
        offset = row_of(coef_n, 2, n, 1)

        def step(i, carry):
            sum_dy, sum_dyv = carry
            parts = up_parts(dnarrow, n, i, size)
            for b in range(2):
                g = jnp.stack([parts[0][b], parts[1][b]], axis=1).reshape(2 * size, HALF, C1)
                v = xs_full[n, b, pl.ds(i * 2 * size, 2 * size)]
                dy = g * slope(v * scale + offset)
                dy_full[n, b, pl.ds(i * 2 * size, 2 * size)] = dy
                sum_dy = sum_dy + fold(dy)
                sum_dyv = sum_dyv + fold(dy * v)
            return sum_dy, sum_dyv

        carry = (zero_n, zero_n)
        for part in range(2):
            carry = lax.fori_loop(2 * part, 2 * part + 2, step, carry)
            if part == 0:
                advance("t%da0" % n)
        sum_dy, sum_dyv = carry
        gain, shift, ca, cb, cd = norm_grad_coefs(
            sum_dy, sum_dyv, gain_n(4), coef_n[2, n, 2], coef_n[2, n, 3], full_pixels
        )
        g_late[4:5, :] += gain[0:1, :]
        g_late[5:6, :] += shift[0:1, :]
        advance("t%da1" % n)

        def finish(i):
            parts = up_parts(dfs, n, i, size)
            for b in range(2):
                g = jnp.stack([parts[0][b], parts[1][b]], axis=1).reshape(2 * size, HALF, C1)
                here = pl.ds(i * 2 * size, 2 * size)
                v = xs_full[n, b, here]
                g = g + dy_full[n, b, here] * ca[0:1, :] + v * cb[0:1, :] + cd[0:1, :]
                store_planes(in_g, n, b, i * 2 * size, rounded(g) * root_half)

        for part in range(2):
            each(2, lambda i: finish(2 * part + i))
            advance("t%db%d" % (n, part))

    advance("narrow")
    for n in range(images):
        third_norm(n)

    def pair_gradient(planes, member):
        products = None
        for b in range(2):
            grads = jnp.concatenate([plane_block(in_g, EVEN + b, a + 1) for a in range(2)], axis=1)
            part = [mm_tn(grads, pair_input(planes, b, jjs)) for jjs in ((0, 1), (2, 3))]
            products = part if products is None else [p + q for p, q in zip(products, part)]
        for dy in range(3):
            blocks = []
            for a in range(2):
                jj = dy + a
                wide_part = products[jj // 2][a * C1 : (a + 1) * C1]
                blocks.append(wide_part[:, (jj % 2) * 3 * C1 : (jj % 2 + 1) * 3 * C1])
            both = blocks[0] + blocks[1]
            for k in range(3):
                row = (dy * 3 + k) * C1
                (g_pair_b if member else g_pair_a)[row : row + C1, :] = both[:, k * C1 : (k + 1) * C1].T

    def back_through(member, values, which, gain_row, last):
        for b in range(2):
            out = mm_nt(pair_input(in_g, b, range(4)), pair_bwd[member])
            for n in range(images):
                dy_full[n, b, pl.ds(0, RES)] = pair_rows(out, n)
            advance("b%dc" % member if b else "b%dc0" % member)
        bucket_rows = lax.broadcasted_iota(jnp.int32, (NB, C1), 0)

        def image(n):
            scale = row_of(coef_n, which, n, 0)
            offset = row_of(coef_n, which, n, 1)

            def step(i, carry):
                sum_dy, sum_dyv = carry
                here = pl.ds(i * ROWS, ROWS)
                for b in range(2):
                    v = values[n, b, here]
                    dy = dy_full[n, b, here] * slope(v * scale + offset)
                    if not last:
                        dy_full[n, b, here] = dy
                    sum_dy = sum_dy + fold(dy)
                    sum_dyv = sum_dyv + fold(dy * v)
                return sum_dy, sum_dyv

            sum_dy, sum_dyv = lax.fori_loop(0, steps, step, (zero_n, zero_n))
            gain, shift, ca, cb, cd = norm_grad_coefs(
                sum_dy, sum_dyv, gain_n(gain_row), coef_n[which, n, 2], coef_n[which, n, 3], full_pixels
            )
            g_late[gain_row : gain_row + 1, :] += gain[0:1, :]
            g_late[gain_row + 1 : gain_row + 2, :] += shift[0:1, :]
            if last:
                return
            advance("b%di%da" % (member, n))

            def finish(i, carry):
                here = pl.ds(i * ROWS, ROWS)
                for b in range(2):
                    v = values[n, b, here]
                    g = dy_full[n, b, here] * ca[0:1, :] + v * cb[0:1, :] + cd[0:1, :]
                    carry = carry + fold(g)
                    store_planes(in_g, n, b, i * ROWS, g)
                return carry

            sums = total(lax.fori_loop(0, steps, finish, zero_n))
            g_late[TIME_NARROW_ROW : TIME_NARROW_ROW + NB, :] += jnp.where(
                bucket_rows == bucket(n), sums, 0.0
            )

        for n in range(images):
            image(n)
            advance("b%di%d" % (member, n))

    pair_gradient(in_b, 1)
    advance("pair_b")
    back_through(1, h1_full, 1, 2, False)
    pair_gradient(in_a, 0)
    advance("pair_a")
    back_through(0, x_full, 0, 0, True)
    pieces["late"] = Exchange(g_late[...], late_totals, arrived_late, late_sems, links.brief)
    advance("end")
    while any(piece.left() for piece in pieces.values()):
        for name, piece in pieces.items():
            if piece.left():
                piece.step()
    sum_late[...] = late_totals[len(links.brief)]


def main_call(dp_size, *operands):
    n = operands[1].shape[1]
    devices = 2 * dp_size
    counts = group_sizes(dp_size)
    orders = (counts[1], counts[1], counts[1], counts[1], counts[1], counts[1])
    grads = [padded(rows, devices, TILE) for rows in GRADS]
    sums = [(coded_rows(rows, devices), jnp.int16) for rows in GRADS]
    sums.append((padded(2 * SMALL_ROWS, devices, 8), f32))
    spaces = [message_rows(rows // 2, order[1:], TILE) for rows, order in zip(grads, orders)]
    sent = [message_rows(rows // 2, order[1:], TILE, 1) for rows, order in zip(grads, orders)]
    small_space = message_rows(sums[-1][0], orders[-1], 0)
    stages = sum(size - 1 for size in counts[1])
    vm = pltpu.VMEM
    full = (n, 2, RES, HALF, C1)
    planes = (n, 4, RES + 2, HALF, C1)
    wide = HALF_CHANNELS
    square = (n, HALF * HALF, wide)
    moved = [vm(v.shape, v.dtype) for v in operands[1:4] + operands[5:] + operands[3:4]]
    scratch = moved + [vm((rows, 128), f32) for rows in grads + [sums[-1][0]]]
    scratch += [vm((rows, 128), jnp.int16) for rows in sent]
    scratch += [vm((rows // 2, 128), f32) for rows in grads]
    scratch += [vm((rows, 128), jnp.int16) for rows in spaces] + [vm((small_space, 128), f32)]
    scratch += [pltpu.SemaphoreType.DMA((2, 2 * sum(size - 1 for size in order))) for order in orders]
    scratch += [
        vm((SMALL_ROWS, wide), f32),
        vm((LATE_ROWS, C1), f32),
        vm((len(counts[1]) + 1, NB, 128), f32),
        vm((sum(counts[1]), NB, 128), f32),
        vm((len(counts[1]) + 1, LATE_ROWS, 128), f32),
        vm((sum(counts[1]), LATE_ROWS, 128), f32),
        pltpu.SemaphoreType.DMA((2, 3)),
        pltpu.SemaphoreType.DMA((3,)),
        pltpu.SemaphoreType.DMA((2, stages)),
        pltpu.SemaphoreType.DMA((2, stages)),
        pltpu.SemaphoreType.DMA((11,)),
        vm((2, 12 * C1, 2 * C1), bf16),
        vm((2, 2 * C1, 12 * C1), bf16),
        vm((9 * C1, wide), bf16),
        vm((C1, 9 * wide), bf16),
        vm((9 * wide, wide), bf16),
        vm((wide, 9 * wide), bf16),
        vm((C1, wide), bf16),
        vm((wide, 4 * wide), bf16),
        vm((HEAD_ROWS, wide), f32),
        vm(full, f32),
        vm(full, f32),
        vm(full, f32),
        vm((n, 2, RES + 2, HALF, C1), f32),
        vm(planes, bf16),
        vm(planes, bf16),
        vm(planes, bf16),
        vm((ROWS * RES, C1), f32),
        vm((n, 3, HALF + 2, HALF, C1), bf16),
        vm((n, 3, HALF + 2, HALF, wide), bf16),
        vm((n, 3, HALF + 2, HALF, wide), bf16),
        vm((n, HALF * HALF, C1), bf16),
        vm((n, HALF * HALF, C1), f32),
        vm(square, f32),
        vm(square, f32),
        vm(square, f32),
        vm(square, bf16),
        vm((n, HALF * HALF, 3 * wide), bf16),
        vm(square, f32),
        vm(square, bf16),
        vm(square, bf16),
        vm(square, bf16),
        vm(square, f32),
        vm(square, bf16),
        vm((n, HALF * HALF, 3 * wide), bf16),
        vm((n, HALF * HALF, C1), f32),
        vm((3, n, 4, 8, C1), f32),
        vm((3, n, 4, 8, wide), f32),
    ]
    whole = pl.BlockSpec(memory_space=pltpu.VMEM)
    anywhere = pl.BlockSpec(memory_space=pltpu.HBM)
    return pl.pallas_call(
        functools.partial(main_kernel, dp_size),
        out_shape=[jax.ShapeDtypeStruct((rows, 128), dtype) for rows, dtype in sums + [(LATE_ROWS, f32), (NB, f32)]],
        in_specs=[pl.BlockSpec(memory_space=pltpu.SMEM)] + [anywhere] * 12,
        out_specs=[whole] * (len(sums) + 2),
        scratch_shapes=scratch,
        compiler_params=pltpu.CompilerParams(
            collective_id=0, has_side_effects=True, vmem_limit_bytes=MAIN_LIMIT + 1536 * (sum(grads) - sum(GRADS))
        ),
        cost_estimate=pl.CostEstimate(flops=8 * 10**9, bytes_accessed=12 * 10**6, transcendentals=0),
    )(*[pltpu.with_memory_space_constraint(v, pltpu.HBM) for v in operands])


PIECE_NAMES = ("attn", "wide", "down", "pair_b", "pair_a", "small")
SCHEDULE = {
    "attn": ("attn",),
    "wide": ("wide",),
    "conv_d": ("attn",),
    "gn_d": ("small",),
    "down": ("down",),
    "t0a0": ("small", "wide",),
    "t0a1": ("attn", "down",),
    "t0b1": ("small",),
    "t1b1": ("attn",),
    "pair_b": ("pair_b",),
    "b1c": ("small", "wide",),
    "b1i0a": ("pair_b",),
    "b1i0": ("attn",),
    "b1i1a": ("down",),
    "b1i1": ("small",),
    "pair_a": ("pair_a",),
    "b0c0": ("wide", "pair_b",),
    "b0i0": ("pair_a", "down",),
    "end": (
        "late", "small", "attn", "wide", "late", "small", "pair_b", "attn",
        "pair_a", "down", "pair_b", "pair_a", "wide", "late", "pair_a", "wide",
        "down", "late", "down", "pair_b", "pair_b", "pair_a", "pair_a",
    ),
}


def group_sizes(dp_size):
    bits = (dp_size - 1).bit_length()
    far = []
    k = 2
    while k < bits:
        far.append(1 << min(2, bits - k))
        k += 2
    return [2, 2, 2] + far, [2, 4] + far, [2] + far + [4]


class Links:
    def __init__(self, dp_size):
        dp = lax.axis_index("dp")
        sp = lax.axis_index("sp")
        core = dp % 2
        near = (dp // 2) % 2

        def along(unit, size):
            place = (dp // unit) % size
            return place, [(dp + unit * ((place + r) % size - place), sp) for r in range(1, size)]

        def pick(first, other):
            return first + core * (other - first)

        across = (dp, 1 - sp)
        beside = (dp + 2 * (1 - 2 * near), sp)
        second = (pick(near, sp), [(pick(beside[0], dp), pick(sp, 1 - sp))])
        third = (pick(sp, near), [(pick(dp, beside[0]), pick(1 - sp, sp))])
        place = 2 * near + sp
        square = []
        for r in range(1, 4):
            member = (place + r) % 4
            square.append((dp + 2 * (member // 2 - near), member % 2))
        far = []
        unit = 4
        for size in group_sizes(dp_size)[1][2:]:
            far.append(along(unit, size))
            unit *= size
        self.full = [along(1, 2), second, third] + far
        self.brief = [along(1, 2), (place, square)] + far
        self.far_first = [along(1, 2)] + far + [(place, square)]
        self.all = [other for _, others in self.brief for other in others]

    def greet(self):
        barrier = pltpu.get_barrier_semaphore()
        for other in self.all:
            pl.semaphore_signal(barrier, inc=1, device_id=other, device_id_type=MESH)

    def meet(self):
        pl.semaphore_wait(pltpu.get_barrier_semaphore(), len(self.all))


def send(source, target, sems, index, landing, other):
    return pltpu.make_async_remote_copy(
        src_ref=source,
        dst_ref=target,
        send_sem=sems.at[0, index],
        recv_sem=sems.at[1, landing],
        device_id=other,
        device_id_type=MESH,
    )


class Exchange:
    def __init__(self, value, totals, arrived, sems, stages):
        totals[0] = value
        self.totals, self.arrived, self.sems, self.stages = totals, arrived, sems, stages
        self.t = self.base = self.index = 0
        self.copies = []

    def left(self):
        return self.t <= len(self.stages)

    def step(self):
        if self.copies:
            for copy in self.copies:
                copy.wait()
            size = len(self.copies) + 1
            total_now = self.arrived[self.base]
            for m in range(1, size):
                total_now = total_now + self.arrived[self.base + m]
            self.totals[self.t] = total_now
            self.base += size
            self.index += size - 1
            self.copies = []
        if self.t < len(self.stages):
            place, others = self.stages[self.t]
            mine = self.totals.at[self.t]
            landing = self.arrived.at[self.base + place]
            for r, other in enumerate(others):
                copy = send(mine, landing, self.sems, self.index + r, self.index + len(others) - 1 - r, other)
                copy.start()
                self.copies.append(copy)
            self.arrived[self.base + place] = self.totals[self.t]
        self.t += 1

    def finish(self, out):
        while self.left():
            self.step()
        out[...] = self.totals[len(self.stages)]


def count_pixels(buckets, mask):
    rows = lax.broadcasted_iota(jnp.int32, (NB, 128), 0)
    counted = jnp.zeros((NB, 128), f32)
    images = mask.shape[1]
    for i in range(2 * images):
        pixels = mask[i // images, i % images].astype(f32)
        number = jnp.sum(jnp.sum(pixels, axis=0, keepdims=True), axis=1, keepdims=True)
        counted = counted + jnp.where(rows == buckets[i], number, 0.0)
    return counted


def chunk_of(rows):
    return next(c for c in (128, 96, 80, 64, 48, 32, 16, 8) if rows % c == 0)


def aligned(row, tile):
    return row if isinstance(row, int) else pl.multiple_of(row, tile)


def encode(source, first, rows, parts, target, base):
    part = rows // parts
    size = chunk_of(part)
    per_part = part // size

    def largest(i, carry):
        v = jnp.abs(source[pl.ds(aligned(first + i * size, 8), size), :])
        return jnp.maximum(carry, jnp.max(v.reshape(-1, 8, 128), axis=0))

    bound = lax.fori_loop(0, rows // size, largest, jnp.zeros((8, 128), f32))
    bound = jnp.max(bound, axis=0, keepdims=True)
    power = jnp.floor(jnp.log2(jnp.maximum(bound, 1e-30))) + 1.0
    scale = jnp.exp2(15.0 - power)

    def step(i):
        v = source[pl.ds(aligned(first + i * size, 8), size), :] * scale
        v = jnp.clip(jnp.round(v), -32767.0, 32767.0).astype(jnp.int32).astype(jnp.int16)
        row = base + i * size + (i // per_part) * TILE
        target[pl.ds(aligned(row, TILE), size), :] = v

    each(rows // size, step)
    tile = jnp.broadcast_to(power.astype(jnp.int32), (TILE, 128)).astype(jnp.int16)
    for m in range(parts):
        target[pl.ds(aligned(base + m * (part + TILE) + part, TILE), TILE), :] = tile


def decode(source, base, rows):
    power = source[pl.ds(aligned(base + rows, TILE), TILE), :].astype(jnp.int32).astype(f32)
    return jnp.exp2(power[0:1, :] - 15.0)


def message_rows(rows, sizes, tile, own=0):
    needed = 0
    for size in sizes:
        rows //= size
        needed += (size - 1 + (own if size > 2 else 0)) * (rows + tile)
    return needed


class Piece:
    def __init__(self, source, outgoing, half, arrived, out, sems, stages):
        self.source, self.outgoing, self.half, self.arrived = source, outgoing, half, arrived
        self.out, self.sems = out, sems
        self.stages = stages
        self.tile = 0 if outgoing is None else TILE
        self.rows = source.shape[0]
        self.first = 0
        self.base = self.sent = self.index = self.t = 0
        self.copies = []
        self.share = self.rows
        for _, others in stages:
            self.share //= len(others) + 1

    def left(self):
        return self.t <= 2 * len(self.stages)

    def step(self):
        count = len(self.stages)
        if 0 < self.t <= count:
            self.scatter_end(self.stages[self.t - 1])
        elif self.t > count:
            self.gather_end(self.stages[2 * count - self.t])
        if self.t == count:
            self.keep()
        if self.t < count:
            self.scatter_start(self.stages[self.t])
        elif self.t < 2 * count:
            self.gather_start(self.stages[2 * count - 1 - self.t])
        self.t += 1

    def scatter_start(self, stage):
        place, others = stage
        size = len(others) + 1
        rows = self.rows // size
        raw = self.half is not None and self.t == 0
        tile = 0 if raw else self.tile
        block = rows + tile
        arrived = self.half if raw else self.arrived
        if tile and size > 2:
            encode(self.source, self.first, self.rows, size, self.outgoing, self.sent)
        for r, other in enumerate(others):
            member = (place + r + 1) % size
            part = self.first + member * rows
            if tile and size > 2:
                message = self.outgoing.at[pl.ds(aligned(self.sent + member * block, TILE), block)]
            elif tile:
                encode(self.source, part, rows, 1, self.outgoing, self.sent)
                message = self.outgoing.at[pl.ds(self.sent, block)]
            else:
                message = self.source.at[pl.ds(aligned(part, 8), rows)]
            landing = size - 2 - r
            copy = send(
                message,
                arrived.at[pl.ds(self.base + landing * block, block)],
                self.sems,
                self.index + r,
                self.index + landing,
                other,
            )
            copy.start()
            self.copies.append(copy)

    def scatter_end(self, stage):
        place, others = stage
        size = len(others) + 1
        rows = self.rows // size
        raw = self.half is not None and self.t == 1
        tile = 0 if raw else self.tile
        block = rows + tile
        arrived = self.half if raw else self.arrived
        for copy in self.copies:
            copy.wait()
        first = self.first + place * rows
        scales = [decode(arrived, self.base + r * block, rows) if tile else 1.0 for r in range(size - 1)]
        chunk = chunk_of(rows)

        def add(i):
            here = pl.ds(aligned(first + i * chunk, 8), chunk)
            v = self.source[here, :]
            for r, scale in enumerate(scales):
                more = arrived[pl.ds(aligned(self.base + r * block + i * chunk, tile or 8), chunk), :]
                v = v + (more.astype(jnp.int32).astype(f32) * scale if tile else more)
            self.source[here, :] = v

        each(rows // chunk, add)
        self.first, self.rows = first, rows
        if not raw:
            self.base += (size - 1) * block
            self.sent += (size if size > 2 else 1) * block
        self.index += size - 1
        self.copies = []

    def keep(self):
        block = self.share + self.tile
        self.place = 0
        for place, others in self.stages:
            self.place = self.place * (len(others) + 1) + place
        self.first = self.place * block
        self.rows = block
        if self.tile:
            encode(self.source, self.place * self.share, self.share, 1, self.out, self.first)
        else:
            self.out[pl.ds(aligned(self.first, 8), block), :] = self.source[
                pl.ds(aligned(self.first, 8), block), :
            ]

    def gather_start(self, stage):
        place, others = stage
        here = self.out.at[pl.ds(aligned(self.first, self.tile or 8), self.rows)]
        for r, other in enumerate(others):
            copy = send(here, here, self.sems, self.index + r, self.index + len(others) - 1 - r, other)
            copy.start()
            self.copies.append(copy)

    def gather_end(self, stage):
        place, others = stage
        size = len(others) + 1
        for copy in self.copies:
            copy.wait()
        self.copies = []
        self.index += size - 1
        self.first = self.first - place * self.rows
        self.rows = self.rows * size


def adamw(weight, grad, first, second, rate):
    first = beta_one * first + (1.0 - beta_one) * grad
    second = beta_two * second + (1.0 - beta_two) * grad * grad
    power = jnp.maximum(second * (1.0 / (1.0 - beta_two**STEP)), 1e-36)
    root = power * lax.rsqrt(power) + adam_epsilon
    scale = rate / (1.0 - beta_one**STEP)
    return weight * (1.0 - rate * decay_rate) - scale * first / root, first, second


PARTS = (
    (2, 1, HALF_CHANNELS, 0, 3, 0),
    (2, 1, HALF_CHANNELS, 6 * HALF_CHANNELS, 3, 3 * HALF_CHANNELS),
    (2, 1, HALF_CHANNELS, 12 * HALF_CHANNELS, 3, 6 * HALF_CHANNELS),
    (4, 0, HALF_CHANNELS, 0, 1, 0),
    (1, 2, C1, 0, 9, 0),
    (3, 2, C1, 18 * C1, 1, 0),
    (0, 3, C1, 0, 9, 9 * C1),
    (0, 4, C1, 0, 9, 0),
)
LARGE = 5


def update_kernel(devices, *refs):
    count = len(GRADS)
    coded, (g_small, g_late, counts), refs = refs[:count], refs[count : count + 3], refs[count + 3 :]
    members = [refs[3 * i : 3 + 3 * i] for i in range(9)]
    outs = [refs[27 + 3 * i : 30 + 3 * i] for i in range(9)]
    loss_out, counts_out = refs[54:56]
    refs = refs[56:]
    grads, refs = refs[:count], refs[count:]
    staged = [refs[3 * i : 3 * i + 3] for i in range(LARGE)]
    store_sems = refs[3 * LARGE]

    def small(row, rows, lanes):
        parts = [g_small[c * SMALL_ROWS + row : c * SMALL_ROWS + row + rows, :] for c in range(lanes // 128)]
        return parts[0] if len(parts) == 1 else jnp.concatenate(parts, axis=1)

    def single(member, index, grad, rate):
        w, m, v = (ref[index] for ref in members[member])
        for out, value in zip(outs[member], adamw(w, grad, m, v, rate)):
            out[index] = value

    def unpack(source, grad):
        share = grad.shape[0] // devices

        def shares(i):
            base = i * (share + TILE)
            v = source[pl.ds(aligned(base, TILE), share), :].astype(jnp.int32).astype(f32)
            grad[pl.ds(aligned(i * share, 8), share), :] = v * decode(source, base, share)

        each(devices, shares, 4)

    def update(part):
        member, which, block_rows, base, blocks, start = part
        size = 128
        grad = grads[which]
        columns = staged[member][0].shape[1] // 128

        def step(i):
            block = i // (block_rows // size)
            row = (i % (block_rows // size)) * size
            here = pl.ds(aligned(start + block * block_rows + row, 8), size)
            for c in range(columns):
                lanes = slice(c * 128, (c + 1) * 128)
                g = grad[pl.ds(aligned(base + (block * columns + c) * block_rows + row, 8), size), :]
                w, m, v = (ref[here, lanes] for ref in members[member])
                for out, value in zip(staged[member], adamw(w, g, m, v, rate_matrix)):
                    out[here, lanes] = value

        each(blocks * block_rows // size, step)

    stores = []
    seen = set()
    for i, part in enumerate(PARTS):
        member, which, block_rows, _, blocks, start = part
        if which not in seen:
            unpack(coded[which], grads[which])
            seen.add(which)
        update(part)
        here = pl.ds(start, block_rows * blocks)
        for kind in range(3):
            copy = pltpu.make_async_copy(
                staged[member][kind].at[here], outs[member][kind].at[here], store_sems.at[i, kind]
            )
            copy.start()
            stores.append(copy)
    for tap in range(9):
        single(5, (tap,), small(tap * 8, 3, HALF_CHANNELS), rate_matrix)
    every = slice(None)
    single(6, (every, every), g_late[:6, :], rate_vector)
    single(7, (every, every), small(WIDE_NORM_ROW, 6, HALF_CHANNELS), rate_vector)
    single(8, (every, slice(0, C1)), g_late[TIME_NARROW_ROW : TIME_NARROW_ROW + NB, :], rate_vector)
    single(8, (every, slice(C1, None)), small(TIME_WIDE_ROW, NB, HALF_CHANNELS), rate_vector)
    loss_out[...] = g_small[LOSS_ROW : LOSS_ROW + 1, :]
    diagonal = lax.broadcasted_iota(jnp.int32, (NB, 128), 0) == lax.broadcasted_iota(jnp.int32, (NB, 128), 1)
    counts_out[...] = jnp.sum(jnp.where(diagonal, counts[...], 0.0), axis=0, keepdims=True)[:, :NB]
    for copy in stores:
        copy.wait()


def update_call(devices, grads, members):
    whole = pl.BlockSpec(memory_space=pltpu.VMEM)
    outside = pl.BlockSpec(memory_space=pltpu.HBM)
    flat = [v for member in members for v in member]
    large = [v.shape for v in flat[: 3 * LARGE]]
    return pl.pallas_call(
        functools.partial(update_kernel, devices),
        out_shape=[jax.ShapeDtypeStruct(v.shape, f32) for v in flat]
        + [jax.ShapeDtypeStruct((1, 128), f32), jax.ShapeDtypeStruct((1, NB), f32)],
        in_specs=[whole] * (len(grads) + len(flat)),
        out_specs=[outside] * (3 * LARGE) + [whole] * (len(flat) - 3 * LARGE + 2),
        scratch_shapes=[pltpu.VMEM((padded(rows, devices, TILE), 128), f32) for rows in GRADS]
        + [pltpu.VMEM(shape, f32) for shape in large]
        + [pltpu.SemaphoreType.DMA((len(PARTS), 3))],
        compiler_params=pltpu.CompilerParams(vmem_limit_bytes=UPDATE_LIMIT),
        cost_estimate=pl.CostEstimate(flops=30 * 10**6, bytes_accessed=40 * 10**6, transcendentals=0),
    )(*grads, *flat)


def on_device(
    features,
    target,
    pixel_mask,
    buckets,
    conv_pair,
    down_conv,
    conv_wide,
    skip_proj,
    attn_proj,
    head_conv,
    norm_narrow,
    norm_wide,
    time_bias,
    conv_pair_mom,
    down_conv_mom,
    conv_wide_mom,
    skip_proj_mom,
    attn_proj_mom,
    head_conv_mom,
    norm_narrow_mom,
    norm_wide_mom,
    time_bias_mom,
    conv_pair_sq,
    down_conv_sq,
    conv_wide_sq,
    skip_proj_sq,
    attn_proj_sq,
    head_conv_sq,
    norm_narrow_sq,
    norm_wide_sq,
    time_bias_sq,
):
    dp_size = lax.axis_size("dp")
    images = features.shape[0] // 2

    def halves(tensor):
        return tensor.reshape((2, images) + tensor.shape[1:])

    def flat(tensor):
        return tensor.reshape(-1, tensor.shape[-1])

    def head_rows(tensor):
        return jnp.transpose(tensor, (0, 1, 3, 2)).reshape(9, 3, HALF_CHANNELS)

    params = (
        flat(conv_pair),
        flat(down_conv),
        flat(conv_wide),
        skip_proj,
        attn_proj,
        head_rows(head_conv),
        norm_narrow,
        norm_wide,
        time_bias,
    )
    firsts = (
        flat(conv_pair_mom),
        flat(down_conv_mom),
        flat(conv_wide_mom),
        skip_proj_mom,
        attn_proj_mom,
        head_rows(head_conv_mom),
        norm_narrow_mom,
        norm_wide_mom,
        time_bias_mom,
    )
    seconds = (
        flat(conv_pair_sq),
        flat(down_conv_sq),
        flat(conv_wide_sq),
        skip_proj_sq,
        attn_proj_sq,
        head_rows(head_conv_sq),
        norm_narrow_sq,
        norm_wide_sq,
        time_bias_sq,
    )
    summed = main_call(
        dp_size,
        buckets,
        halves(features),
        halves(jnp.transpose(target, (0, 3, 1, 2))),
        halves(pixel_mask),
        *params,
    )
    results = update_call(2 * dp_size, summed, list(zip(params, firsts, seconds)))
    shaped = []
    for member, like in enumerate((conv_pair, down_conv, conv_wide, skip_proj, attn_proj)):
        shaped.extend(v.reshape(like.shape) for v in results[3 * member : 3 * member + 3])
    for v in results[15:18]:
        shaped.append(jnp.transpose(v.reshape(3, 3, 3, HALF_CHANNELS), (0, 1, 3, 2)))
    shaped.extend(results[18:27])
    return (results[27][0, 0], results[28].reshape(NB)) + tuple(shaped)


def solution(mesh):
    placed = (
        P("dp", "sp", None, None),
        P("dp", "sp", None, None),
        P("dp", "sp", None),
        P("dp"),
        P(),
        P(),
        P(),
        P(),
        P(),
        P(),
        P(),
        P(),
        P(),
        P(),
        P(),
        P(),
        P(),
        P(),
        P(),
        P(),
        P(),
        P(),
        P(),
        P(),
        P(),
        P(),
        P(),
        P(),
        P(),
        P(),
        P(),
    )
    return jax.shard_map(
        on_device,
        mesh=mesh,
        in_specs=placed,
        out_specs=(
            P(),
            P(),
            P(),
            P(),
            P(),
            P(),
            P(),
            P(),
            P(),
            P(),
            P(),
            P(),
            P(),
            P(),
            P(),
            P(),
            P(),
            P(),
            P(),
            P(),
            P(),
            P(),
            P(),
            P(),
            P(),
            P(),
            P(),
            P(),
            P(),
        ),
        check_vma=False,
    )
```
